32 devices in a mesh: gx: 8 (over z, y), gy: 4 (over x, core).
Axes of the slice: x: 2, y: 2, z: 4, core: 2. Of those that a mesh axis runs over, the one named last changes fastest.
Arguments:
- ref_image: bfloat16 [8, 512, 512], P(None, 'gx', 'gy'), may hold values from -6 to 6
- def_image: bfloat16 [8, 512, 512], P(None, 'gx', 'gy'), may hold values from -6 to 6
- shift_xy: int32 [2, 4096], P(None, ('gx', 'gy')), may hold values from -64 to 63, as said below
- shift_z: int32 [4096], P(('gx', 'gy')), may hold values from -2 to 1, as said below
- frac: float32 [3, 4096], P(None, ('gx', 'gy')), may hold values from 0 to 1
- connectivity: int32 [8, 4096], P(None, ('gx', 'gy')), may hold values from 0 to 305, as said below
Outputs:
- residual: bfloat16 [8, 512, 512], P(None, 'gx', 'gy')
- step_disp: float32 [3, 2, 64, 64], P(None, None, 'gx', 'gy')
- gn_product: float32 [3, 2, 64, 64], P(None, None, 'gx', 'gy')
- misfit: float32 [], replicated
The draws below stay inside these ranges and needn't reach their ends.
Inputs may be any that keep to these rules, and one draw needn't show every extreme that they name: `connectivity`: each device's elements appear in a shuffled order; corner c = 4 cz + 2 cx + cy of an element with lower-corner node (a, b, c0) is node ((a + cz) (64/8+1) + b + cx) (128/8+1) + c0 + cy of the device's node grid, and every element of the device's brick is listed once. `shift_xy`: the in-plane shifts follow a continuous displacement field over the slab: elements side by side differ by a few voxels. `shift_z`: the plane shifts follow a continuous field over the slab.
All inputs are finite; a program needn't handle non-finite values.
Results may differ from the reference program's by a relative error of at most 0.0004.
Values may be sent and summed in bfloat16 or wider, within the bound.
No kernel may reach another device: no remote copies, remote signals or barrier semaphores. Data moves between devices by JAX's collectives and lax.ppermute only.
A program may use at most 64 MiB of HBM per device.

```python
import jax
import jax.numpy as jnp
from jax import lax

BX = 64
BY = 128
Z = 8
HALO = 64
NX = 512
NY = 512
EX = 64
EY = 64
ELEMS = 4096
N_GX = 8
N_GY = 4


def element_layout(key):
    base = jax.random.fold_in(key, 7)
    ez_n = Z // 8
    ex_n = BX // 8
    ey_n = BY // 8
    count = ez_n * ex_n * ey_n
    device_total = ELEMS // count
    per_row = NY // BY

    def one_device(dev):
        order = jax.random.permutation(jax.random.fold_in(base, dev), count).astype(jnp.int32)
        layer_z = order // (ex_n * ey_n)
        col_x = order // ey_n % ex_n
        col_y = order % ey_n
        glob_x = dev // per_row * ex_n + col_x
        glob_y = dev % per_row * ey_n + col_y
        return (layer_z, col_x, col_y, glob_x, glob_y)
    parts = jax.vmap(one_device)(jnp.arange(device_total, dtype=jnp.int32))
    return [p.reshape(-1).astype(jnp.int32) for p in parts]


def smooth_ramp(key, glob_x, glob_y, low, span):
    weights = jax.random.randint(jax.random.fold_in(key, 1), (2,), 1, 5).astype(jnp.int32)
    flips = jax.random.randint(jax.random.fold_in(key, 2), (2,), 0, 2).astype(jnp.int32)
    pos_x = jnp.where(flips[0] == 1, EX - 1 - glob_x, glob_x)
    pos_y = jnp.where(flips[1] == 1, EY - 1 - glob_y, glob_y)
    denom = weights[0] * (EX - 1) + weights[1] * (EY - 1)
    return (low + span * (weights[0] * pos_x + weights[1] * pos_y) // denom, pos_x)


def draw_connectivity(key, part):
    layer_z, col_x, col_y, glob_x, glob_y = element_layout(key)
    ex_n = BX // 8
    ey_n = BY // 8
    corner = jnp.arange(8, dtype=jnp.int32)
    offset = (corner // 4 * (ex_n + 1) + corner // 2 % 2) * (ey_n + 1) + corner % 2
    first = (layer_z * (ex_n + 1) + col_x) * (ey_n + 1) + col_y
    return (offset[:, None] + first[None, :]).astype(jnp.int32)


def draw_shift_xy(key, part):
    layer_z, col_x, col_y, glob_x, glob_y = element_layout(key)
    key = jax.random.fold_in(key, 3)
    rows = []
    for comp in range(2):
        sub = jax.random.fold_in(key, comp)
        ramp, pos_x = smooth_ramp(sub, glob_x, glob_y, 0 - HALO, 2 * HALO - 1)
        amp = jax.random.randint(jax.random.fold_in(sub, 9), (), 0, 9).astype(jnp.int32)
        bump = amp * 4 * pos_x * (EX - 1 - pos_x) // ((EX - 1) * (EX - 1))
        rows.append(jnp.clip(ramp + bump, 0 - HALO, HALO - 1))
    return jnp.stack(rows).astype(jnp.int32)


def draw_shift_z(key, part):
    layer_z, col_x, col_y, glob_x, glob_y = element_layout(key)
    key = jax.random.fold_in(key, 4)
    ramp, pos_x = smooth_ramp(key, glob_x, glob_y, -2, 3)
    return jnp.clip(ramp, -2, 1).astype(jnp.int32)


def steps_of(stream_key, shape, split, low, high):
    def one(position, blocks):
        steps = jax.random.uniform(jax.random.fold_in(jax.random.fold_in(stream_key, 6), position), (blocks,), jnp.float32, low / len(split), high / len(split))
        return jnp.repeat(jnp.exp(steps), shape[position] // blocks).reshape((-1,) + (1,) * (len(shape) - position - 1))

    loudness = one(*split[0])
    for cut in split[1:]:
        loudness = loudness * one(*cut)
    return loudness


def scatter_about(stream_key, shape, width, most, shards=(), kind=jnp.bfloat16):
    level = steps_of(stream_key, shape, shards, -0.22, 0.18) if shards else 1.0
    values = jax.random.normal(stream_key, shape, jnp.float32) * width * level
    return jnp.minimum(jnp.maximum(values, -most), most).astype(kind)


def setup_inputs(seed: int = 0) -> dict:
    streams_of = jax.random.split(jax.random.key(seed), 7)
    ref_image = scatter_about(streams_of[0], (Z, NX, NY), 1.0, 6.0, ((1, 8), (2, 4)))
    def_image = scatter_about(streams_of[1], (Z, NX, NY), 1.0, 6.0, ((1, 8), (2, 4)))
    shift_xy = draw_shift_xy(jax.random.fold_in(streams_of[6], 71), 0)
    shift_z = draw_shift_z(jax.random.fold_in(streams_of[6], 71), 0)
    frac = jnp.clip(1.0 * jax.random.uniform(streams_of[4], (3, ELEMS), jnp.float32) ** steps_of(streams_of[4], (3, ELEMS), ((1, 32),), -0.2, 0.2), 0.0, 1.0)
    connectivity = draw_connectivity(jax.random.fold_in(streams_of[6], 71), 0)
    return dict(ref_image=ref_image, def_image=def_image, shift_xy=shift_xy, shift_z=shift_z, frac=frac, connectivity=connectivity)


def basis():
    lane = jnp.arange(512, dtype=jnp.int32)
    coords = [((lane // 64) % 8).astype(jnp.float32), ((lane // 8) % 8).astype(jnp.float32), (lane % 8).astype(jnp.float32)]
    coords = [(v + 0.5) / 8.0 for v in coords]
    rows = []
    for corner in range(8):
        bits = [(corner // 4) % 2, (corner // 2) % 2, corner % 2]
        prod = jnp.ones((512,), jnp.float32)
        for bit, pos in zip(bits, coords):
            prod = prod * (pos if bit == 1 else 1.0 - pos)
        rows.append(prod)
    return jnp.stack(rows)


def interpolate(tile, frac):
    wz, wx, wy = frac[0], frac[1], frac[2]
    low_z = tile[:8] * (1.0 - wz) + tile[1:] * wz
    dif_z = tile[1:] - tile[:8]

    def along_x(a):
        return a[:, :8] * (1.0 - wx) + a[:, 1:] * wx

    def along_y(a):
        return a[:, :, :8] * (1.0 - wy) + a[:, :, 1:] * wy

    low_zx = along_x(low_z)
    dif_zx = along_x(dif_z)
    dif_xl = low_z[:, 1:] - low_z[:, :8]
    value = along_y(low_zx)
    slope_z = along_y(dif_zx)
    slope_x = along_y(dif_xl)
    slope_y = low_zx[:, :, 1:] - low_zx[:, :, :8]
    count = tile.shape[-1]
    return value.reshape(512, count), jnp.stack([slope_z, slope_x, slope_y]).reshape(3, 512, count)


def as_index(value):
    return jnp.asarray(value).astype(jnp.int32)


def reference(ref_image, def_image, shift_xy, shift_z, frac, connectivity):
    ez_n = Z // 8
    ex_n = BX // 8
    ey_n = BY // 8
    count = ez_n * ex_n * ey_n
    nx_n = ex_n + 1
    ny_n = ey_n + 1
    device_total = N_GX * N_GY
    padded = jnp.pad(def_image, ((2, 2), (HALO, HALO), (HALO, HALO)))
    shape_tab = basis()
    high = lax.Precision.HIGHEST
    zero_index = as_index(0)

    def fields(dev):
        dev = as_index(dev)
        col_i = dev // N_GY
        col_j = dev % N_GY
        conn = lax.dynamic_slice_in_dim(connectivity, as_index(dev * count), count, 1)
        moves = lax.dynamic_slice_in_dim(shift_xy, as_index(dev * count), count, 1)
        planes = lax.dynamic_slice_in_dim(shift_z, as_index(dev * count), count, 0)
        parts = lax.dynamic_slice_in_dim(frac, as_index(dev * count), count, 1)
        first = conn[0]
        layer_z = first // (nx_n * ny_n)
        col_x = (first // ny_n) % nx_n
        col_y = first % ny_n
        start_z = as_index(8 * layer_z + planes + 2)
        start_x = as_index(col_i * BX + 8 * col_x + moves[0] + HALO)
        start_y = as_index(col_j * BY + 8 * col_y + moves[1] + HALO)
        tiles = jax.vmap(lambda a, b, c: lax.dynamic_slice(padded, (a, b, c), (9, 9, 9)))(start_z, start_x, start_y)
        tiles = jnp.transpose(tiles, (1, 2, 3, 0)).astype(jnp.float32)
        ref_z = as_index(8 * layer_z)
        ref_x = as_index(col_i * BX + 8 * col_x)
        ref_y = as_index(col_j * BY + 8 * col_y)
        refs = jax.vmap(lambda a, b, c: lax.dynamic_slice(ref_image, (a, b, c), (8, 8, 8)))(ref_z, ref_x, ref_y)
        refs = jnp.transpose(refs, (1, 2, 3, 0)).reshape(512, count).astype(jnp.float32)
        value, slopes = interpolate(tiles, parts)
        misfit_el = refs - value
        struct_id = ((layer_z * ex_n + col_x) * ey_n + col_y).astype(jnp.int32)
        return conn, misfit_el, slopes, struct_id

    def scatter_nodes(conn, terms):
        acc = jnp.zeros((3, (ez_n + 1) * nx_n * ny_n), jnp.float32)
        acc = acc.at[:, conn.reshape(-1)].add(terms.reshape(3, -1))
        return acc.reshape(3, ez_n + 1, nx_n, ny_n)

    def first_pass(dev):
        conn, misfit_el, slopes, struct_id = fields(dev)
        weighted = slopes * misfit_el[None] * (1.0 / 512.0)
        terms = jnp.einsum("cv,kve->kce", shape_tab, weighted, precision=high)
        inverse = jnp.zeros((count,), jnp.int32).at[struct_id].set(jnp.arange(count, dtype=jnp.int32))
        brick = jnp.take(misfit_el, inverse, axis=1).astype(jnp.bfloat16)
        brick = brick.reshape(8, 8, 8, ez_n, ex_n, ey_n).transpose(3, 0, 4, 1, 5, 2).reshape(Z, BX, BY)
        return scatter_nodes(conn, terms), brick, jnp.sum(misfit_el * misfit_el)

    def assemble(accs):
        def add_one(dev, total):
            dev = as_index(dev)
            col_i = dev // N_GY
            col_j = dev % N_GY
            where = (zero_index, zero_index, as_index(col_i * ex_n), as_index(col_j * ey_n))
            cur = lax.dynamic_slice(total, where, (3, ez_n + 1, nx_n, ny_n))
            return lax.dynamic_update_slice(total, cur + accs[dev], where)

        total = lax.fori_loop(jnp.int32(0), jnp.int32(device_total), add_one, jnp.zeros((3, ez_n + 1, EX + 1, EY + 1), jnp.float32))
        return total.at[:, :, EX, :].set(0.0).at[:, :, :, EY].set(0.0)

    ids = jnp.arange(device_total, dtype=jnp.int32)
    accs, bricks, squares = lax.map(first_pass, ids)
    grad_nodes = assemble(accs)

    def second_pass(dev):
        conn, misfit_el, slopes, struct_id = fields(dev)
        dev = as_index(dev)
        col_i = dev // N_GY
        col_j = dev % N_GY
        where = (zero_index, zero_index, as_index(col_i * ex_n), as_index(col_j * ey_n))
        local = lax.dynamic_slice(grad_nodes, where, (3, ez_n + 1, nx_n, ny_n)).reshape(3, -1)
        corner_vals = jnp.take(local, conn.reshape(-1), axis=1).reshape(3, 8, count)
        moved = jnp.einsum("cv,kce->kve", shape_tab, corner_vals, precision=high)
        along = jnp.sum(slopes * moved, axis=0)
        terms = jnp.einsum("cv,kve->kce", shape_tab, slopes * along[None] * (1.0 / 512.0), precision=high)
        return scatter_nodes(conn, terms)

    hess_nodes = assemble(lax.map(second_pass, ids))
    own_grad = grad_nodes[:, :, :EX, :EY]
    own_hess = hess_nodes[:, :, :EX, :EY]
    alpha = jnp.sum(own_grad * own_grad) / jnp.sum(own_grad * own_hess)
    residual = bricks.reshape(N_GX, N_GY, Z, BX, BY).transpose(2, 0, 3, 1, 4).reshape(Z, NX, NY)
    misfit = jnp.sum(squares) / (Z * NX * NY)
    return residual, alpha * own_grad, own_hess, misfit
```

```python
import jax
import jax.numpy as jnp
import numpy as np
from jax import lax
from jax.experimental import pallas as pl
from jax.experimental.pallas import tpu as pltpu
from jax.sharding import PartitionSpec as P

HALO = 64
F32 = jnp.float32
BF16 = jnp.bfloat16
SPAN = 192
TILE_ROWS = 12 * SPAN
VMEM = pl.BlockSpec(memory_space=pltpu.VMEM)
SMEM = pl.BlockSpec(memory_space=pltpu.SMEM)
PARAMS = pltpu.CompilerParams(vmem_limit_bytes=40 * 1024 * 1024)


def node_weights(count):
    w = np.zeros((count + 1, 8 * count), np.float32)
    for v in range(8 * count):
        s = (v % 8 + 0.5) / 8.0
        w[v // 8, v] = 1.0 - s
        w[v // 8 + 1, v] = s
    return w


def tables():
    wx = node_weights(8)
    left = np.zeros((64, 6, 64), np.float32)
    for kc in range(6):
        left[kc * 8 : kc * 8 + 8, kc] = wx[:8]
        left[48 + kc, kc] = wx[8]
        left[56 + kc, kc] = wx[0]
    left = left.reshape(64, 384)
    expand = left.T.copy()
    expand[:, 56:] = 0.0
    wy = np.zeros((128, 128), np.float32)
    wy[:, :17] = node_weights(16).T
    as_bf = lambda a: jnp.asarray(a, BF16)
    return as_bf(left / 512.0), as_bf(wy), as_bf(expand), as_bf(wy.T)


def split(x):
    hi = x.astype(BF16)
    return hi, (x - hi.astype(F32)).astype(BF16)


def dot(a, b):
    return jnp.dot(a, b, preferred_element_type=F32)


def dot_right(w, x):
    hi, lo = split(x)
    return dot(w, hi) + dot(w, lo)


def dot_left(x, w):
    hi, lo = split(x)
    return dot(hi, w) + dot(lo, w)


def pack_kernel(up_ref, own_ref, down_ref, right_ref, left_ref):
    left = lax.broadcasted_iota(jnp.int32, (64, 128), 1) < 64
    for p in range(4):
        for s, ref in enumerate((up_ref, own_ref, down_ref)):
            a = ref[p].astype(F32)
            c = ref[p + 4].astype(F32)
            ra = pltpu.roll(a, 64, 1)
            rc = pltpu.roll(c, 64, 1)
            rows = pl.ds(s * 64, 64)
            right_ref[p, rows] = jnp.where(left, ra, c).astype(BF16)
            left_ref[p, rows] = jnp.where(left, a, rc).astype(BF16)


def column_block(rows, face, lane_from):
    lane = lax.broadcasted_iota(jnp.int32, (8, 128), 1)
    out = jnp.where(lane == 8, jnp.broadcast_to(face[:, lane_from : lane_from + 1], (8, 128)), 0.0)
    for kc in range(6):
        col = rows[kc][:, lane_from : lane_from + 1]
        out = jnp.where(lane == kc, jnp.broadcast_to(col, (8, 128)), out)
    return out


def sample_kernel(
    nx, ny, idx_ref, frac_ref, up_ref, own_ref, down_ref, lo_ref, hi_ref, ref_ref, left_ref, wy_ref,
    res_ref, slope_ref, node_ref, send_ref, sq_ref, img, arr, wgt, rsc, gsc,
):
    half = lax.broadcasted_iota(jnp.int32, (64, 128), 1) < 64
    zero = jnp.zeros((2 * SPAN, 128), F32)
    for k in range(3):
        img[pl.ds(k * TILE_ROWS, 2 * SPAN)] = zero
        img[pl.ds(k * TILE_ROWS + 10 * SPAN, 2 * SPAN)] = zero
    for p in range(4):
        for s, ref in enumerate((up_ref, own_ref, down_ref)):
            a = ref[p].astype(F32)
            c = ref[p + 4].astype(F32)
            ra = pltpu.roll(a, 64, 1)
            rc = pltpu.roll(c, 64, 1)
            rows = pl.ds(s * 64, 64)
            lo = lo_ref[p, rows].astype(F32)
            hi = hi_ref[p, rows].astype(F32)
            rlo = pltpu.roll(lo, 64, 1)
            rhi = pltpu.roll(hi, 64, 1)
            at = lambda k, q: pl.ds(k * TILE_ROWS + (q + 2) * SPAN + s * 64, 64)
            img[at(0, p)] = jnp.where(half, lo, ra)
            img[at(1, p)] = a
            img[at(2, p)] = jnp.where(half, ra, rhi)
            img[at(0, p + 4)] = jnp.where(half, rlo, rc)
            img[at(1, p + 4)] = c
            img[at(2, p + 4)] = jnp.where(half, rc, hi)
    for z in range(8):
        rsc[z] = ref_ref[z].astype(F32).reshape(8, 8, 128)

    lane = lax.broadcasted_iota(jnp.int32, (8, 128), 1)

    def element(e, carry):
        base = idx_ref[0, e]
        shift = idx_ref[1, e]
        place = idx_ref[2, e]
        first = idx_ref[3, e]
        where_to = (lane - first) & 127
        mask = where_to < 9
        for z in range(9):
            for q in range(2):
                v = img[pl.ds(base + (z * SPAN + q), 8), :]
                v = pltpu.roll(v, shift, 1)
                pltpu.store(arr.at[place, z * 2 + q], v, mask=mask)
        mask = where_to < 8
        row = place & 7
        for c in range(3):
            pltpu.store(wgt.at[c, row], jnp.full((8, 128), frac_ref[c, e], F32), mask=mask)
        return carry

    lax.fori_loop(0, 128, element, 0, unroll=4)

    phase = lane & 15
    even = phase < 8
    even_next = (phase >= 1) & (phase <= 8)

    def interpolate(cx, square):
        wz, wx, wy = wgt[0, cx], wgt[1, cx], wgt[2, cx]

        def pair(z, q):
            ev = arr[cx, z * 2 + q]
            od = arr[cx + 8, z * 2 + q]
            near = jnp.where(even, ev, od)
            far = pltpu.roll(jnp.where(even_next, ev, od), 127, 1)
            return near, far

        total = [None] * 3
        upper = [None] * 3
        prev = [pair(0, 0), pair(0, 1)]
        for z in range(8):
            cur = [pair(z + 1, 0), pair(z + 1, 1)]
            low, dzx, dx = [], [], []
            for y in range(2):
                d0 = cur[0][y] - prev[0][y]
                d1 = cur[1][y] - prev[1][y]
                l0 = prev[0][y] + wz * d0
                l1 = prev[1][y] + wz * d1
                dx.append(l1 - l0)
                low.append(l0 + wx * dx[y])
                dzx.append(d0 + wx * (d1 - d0))
            prev = cur
            slope_y = low[1] - low[0]
            value = low[0] + wy * slope_y
            slope_z = dzx[0] + wy * (dzx[1] - dzx[0])
            slope_x = dx[0] + wy * (dx[1] - dx[0])
            r = rsc[z, cx] - value
            rsc[z, cx] = r
            square = square + r * r
            for k, s in enumerate((slope_z, slope_x, slope_y)):
                slope_ref[k, z, cx] = s
                w = s * r
                u = w * ((z + 0.5) / 8.0)
                total[k] = w if z == 0 else total[k] + w
                upper[k] = u if z == 0 else upper[k] + u
        for k in range(3):
            gsc[2 * k, cx] = total[k] - upper[k]
            gsc[2 * k + 1, cx] = upper[k]
        return square

    sq_ref[...] = lax.fori_loop(0, 8, interpolate, jnp.zeros((8, 128), F32))
    res_ref[...] = rsc[...].reshape(8, 64, 128).astype(BF16)
    nodes = dot_left(dot_right(left_ref[...], gsc[...].reshape(384, 128)), wy_ref[...])
    node_ref[...] = nodes
    rows = [nodes[kc * 8 : kc * 8 + 8] for kc in range(6)]
    high, low = nodes[48:56], nodes[56:64]
    col_high = column_block(rows, high, 16)
    col_low = column_block(rows, high, 0)
    gx, gy = lax.axis_index("gx"), lax.axis_index("gy")
    send_ref[...] = jnp.zeros(send_ref.shape, F32)
    for dx in (-1, 0, 1):
        for dy in (-1, 0, 1):
            if dx == 0 and dy == 0:
                continue
            block = high if dx == 1 else low if dx == -1 else col_high if dy == 1 else col_low
            px, py = gx + dx, gy + dy

            @pl.when((px >= 0) & (px < nx) & (py >= 0) & (py < ny))
            def _():
                send_ref[px * ny + py] = block


def product_kernel(
    nx, ny, recv_ref, node_ref, slope_ref, sq_ref, expand_ref, wyt_ref, left_ref, wy_ref,
    grad_ref, hess_ref, send_ref, msc, gsc,
):
    gx, gy = lax.axis_index("gx"), lax.axis_index("gy")
    own = gx * ny + gy
    lane = lax.broadcasted_iota(jnp.int32, (8, 128), 1)
    sub = lax.broadcasted_iota(jnp.int32, (8, 128), 0)

    def block(dx, dy):
        px, py = gx + dx, gy + dy
        there = (px >= 0) & (px < nx) & (py >= 0) & (py < ny)
        return recv_ref[jnp.where(there, px * ny + py, own)]

    def column(x, at):
        return jnp.broadcast_to(x[:, at : at + 1], (8, 128))

    def with_corners(dx):
        mid = block(dx, 0)
        mid = mid + jnp.where(lane == 0, column(block(dx, -1), 16), 0.0)
        return mid + jnp.where(lane == 16, column(block(dx, 1), 0), 0.0)

    keep_x = jnp.where(gx == nx - 1, 0.0, 1.0).astype(F32)
    keep_y = jnp.where(gy == ny - 1, 0.0, 1.0).astype(F32)
    keep_lane = jnp.where(lane == 16, keep_y, 1.0)
    row_low = with_corners(-1)
    row_high = with_corners(1)
    col_low = block(0, -1)
    col_high = block(0, 1)
    grads = []
    square = jnp.zeros((8, 128), F32)
    for kc in range(6):
        g = node_ref[kc * 8 : kc * 8 + 8]
        g = g + jnp.where(sub == 0, jnp.broadcast_to(row_low[kc : kc + 1], (8, 128)), 0.0)
        g = g + jnp.where(lane == 0, column(col_low, kc), 0.0)
        g = g + jnp.where(lane == 16, column(col_high, kc), 0.0)
        g = g * keep_lane
        grads.append(g)
        grad_ref[kc] = g
        own_g = jnp.where(lane < 16, g, 0.0)
        square = square + own_g * own_g
    face = node_ref[48:56] + row_high
    face = face + jnp.where(lane == 0, column(col_low, 8), 0.0)
    face = face + jnp.where(lane == 16, column(col_high, 8), 0.0)
    face = jnp.where(sub < 6, face * keep_lane * keep_x, 0.0)
    full = jnp.concatenate(grads + [face, jnp.zeros((8, 128), F32)], axis=0)
    moved = dot_right(expand_ref[...], dot_left(full, wyt_ref[...]))
    msc[...] = moved.reshape(6, 8, 8, 128)

    def apply(cx, curve):
        m0 = [msc[2 * k, cx] for k in range(3)]
        dm = [msc[2 * k + 1, cx] - m0[k] for k in range(3)]
        total = [None] * 3
        upper = [None] * 3
        for z in range(8):
            sz = (z + 0.5) / 8.0
            s = [slope_ref[k, z, cx] for k in range(3)]
            along = s[0] * (m0[0] + sz * dm[0])
            for k in (1, 2):
                along = along + s[k] * (m0[k] + sz * dm[k])
            curve = curve + along * along
            for k in range(3):
                w = s[k] * along
                u = w * sz
                total[k] = w if z == 0 else total[k] + w
                upper[k] = u if z == 0 else upper[k] + u
        for k in range(3):
            gsc[2 * k, cx] = total[k] - upper[k]
            gsc[2 * k + 1, cx] = upper[k]
        return curve

    curve = lax.fori_loop(0, 8, apply, jnp.zeros((8, 128), F32))
    nodes = dot_left(dot_right(left_ref[...], gsc[...].reshape(384, 128)), wy_ref[...])
    rows = [nodes[kc * 8 : kc * 8 + 8] for kc in range(6)]
    for kc in range(6):
        hess_ref[kc] = rows[kc]
    high = nodes[48:56]
    col_high = column_block(rows, high, 16)
    sums = jnp.where(lane == 32, jnp.sum(sq_ref[...]), 0.0)
    sums = jnp.where(lane == 33, jnp.sum(square), sums)
    sums = jnp.where(lane == 34, jnp.sum(curve) * (1.0 / 512.0), sums)
    tail = lane >= 32
    send_ref[...] = jnp.broadcast_to(sums[None], send_ref.shape)
    for dx, dy, data in ((1, 0, high), (1, 1, high), (0, 1, col_high)):
        px, py = gx + dx, gy + dy

        @pl.when((px < nx) & (py < ny))
        def _():
            send_ref[px * ny + py] = jnp.where(tail, sums, data)


def finish_kernel(nx, ny, voxels, recv_ref, grad_ref, hess_ref, step_ref, prod_ref, misfit_ref):
    gx, gy = lax.axis_index("gx"), lax.axis_index("gy")
    own = gx * ny + gy
    lane = lax.broadcasted_iota(jnp.int32, (8, 128), 1)
    sub = lax.broadcasted_iota(jnp.int32, (8, 128), 0)

    def block(dx, dy):
        px, py = gx + dx, gy + dy
        there = (px >= 0) & (py >= 0)
        data = recv_ref[jnp.where(there, px * ny + py, own)]
        return jnp.where(there, data, 0.0)

    def column(x, at):
        return jnp.broadcast_to(x[:, at : at + 1], (8, 128))

    total = jnp.sum(recv_ref[...], axis=0)
    misfit_ref[...] = total[0:1, 32:33] * (1.0 / voxels)
    alpha = column(total, 33) / column(total, 34)
    row_low = block(-1, 0) + jnp.where(lane == 0, column(block(-1, -1), 16), 0.0)
    col_low = block(0, -1)
    for kc in range(6):
        h = hess_ref[kc]
        h = h + jnp.where(sub == 0, jnp.broadcast_to(row_low[kc : kc + 1], (8, 128)), 0.0)
        h = h + jnp.where(lane == 0, column(col_low, kc), 0.0)
        prod_ref[kc // 2, kc % 2] = h[:, :16]
        step_ref[kc // 2, kc % 2] = (alpha * grad_ref[kc])[:, :16]


def on_device(ref_image, def_image, shift_xy, shift_z, frac, connectivity):
    nx, ny = lax.axis_size("gx"), lax.axis_size("gy")
    peers = nx * ny
    sds = jax.ShapeDtypeStruct
    up = [(i, i + 1) for i in range(nx - 1)]
    below = lax.ppermute(def_image, "gx", up)
    above = lax.ppermute(def_image, "gx", [(j, i) for i, j in up])
    to_right, to_left = pl.pallas_call(
        pack_kernel,
        out_shape=(sds((4, SPAN, 128), BF16), sds((4, SPAN, 128), BF16)),
        in_specs=[VMEM] * 3,
        out_specs=(VMEM, VMEM),
        compiler_params=PARAMS,
        name="pack_halo",
    )(below, def_image, above)
    up = [(i, i + 1) for i in range(ny - 1)]
    lo = lax.ppermute(to_right, "gy", up)
    hi = lax.ppermute(to_left, "gy", [(j, i) for i, j in up])

    first = connectivity[0]
    col_x = first // 17 % 9
    col_y = first % 17
    start_x = 8 * col_x + shift_xy[0] + HALO
    start_y = 8 * col_y + shift_xy[1] + HALO
    tile = jnp.minimum(start_y // 64, 2)
    base = tile * TILE_ROWS + (shift_z + 2) * SPAN + start_x
    shift = (8 * col_y - (start_y - 64 * tile)) & 127
    place = (col_y & 1) * 8 + col_x
    idx = jnp.stack([base, shift, place, 8 * col_y])

    left, wy, expand, wyt = tables()
    residual, slopes, nodes, send, square = pl.pallas_call(
        lambda *refs: sample_kernel(nx, ny, *refs),
        out_shape=(
            sds((8, 64, 128), BF16),
            sds((3, 8, 8, 8, 128), F32),
            sds((64, 128), F32),
            sds((peers, 8, 128), F32),
            sds((8, 128), F32),
        ),
        in_specs=[SMEM, SMEM] + [VMEM] * 8,
        out_specs=(VMEM,) * 5,
        scratch_shapes=[
            pltpu.VMEM((3 * TILE_ROWS, 128), F32),
            pltpu.VMEM((16, 18, 8, 128), F32),
            pltpu.VMEM((3, 8, 8, 128), F32),
            pltpu.VMEM((8, 8, 8, 128), F32),
            pltpu.VMEM((6, 8, 8, 128), F32),
        ],
        compiler_params=PARAMS,
        name="sample_and_gradient",
    )(idx, frac, below, def_image, above, lo, hi, ref_image, left, wy)
    recv = lax.all_to_all(send, ("gx", "gy"), 0, 0, tiled=True)
    grads, hess, send = pl.pallas_call(
        lambda *refs: product_kernel(nx, ny, *refs),
        out_shape=(sds((6, 8, 128), F32), sds((6, 8, 128), F32), sds((peers, 8, 128), F32)),
        in_specs=[VMEM] * 8,
        out_specs=(VMEM,) * 3,
        scratch_shapes=[pltpu.VMEM((6, 8, 8, 128), F32), pltpu.VMEM((6, 8, 8, 128), F32)],
        compiler_params=PARAMS,
        name="gauss_newton_product",
    )(recv, nodes, slopes, square, expand, wyt, left, wy)
    recv = lax.all_to_all(send, ("gx", "gy"), 0, 0, tiled=True)
    voxels = 8 * 64 * 128 * peers
    step, product, misfit = pl.pallas_call(
        lambda *refs: finish_kernel(nx, ny, voxels, *refs),
        out_shape=(sds((3, 2, 8, 16), F32), sds((3, 2, 8, 16), F32), sds((1, 1), F32)),
        in_specs=[VMEM] * 3,
        out_specs=(VMEM,) * 3,
        compiler_params=PARAMS,
        name="finish",
    )(recv, grads, hess)
    return (residual, step, product, misfit[0, 0])


def solution(mesh):
    in_specs = (
        P(None, "gx", "gy"),
        P(None, "gx", "gy"),
        P(None, ("gx", "gy")),
        P(("gx", "gy")),
        P(None, ("gx", "gy")),
        P(None, ("gx", "gy")),
    )
    out_specs = (P(None, "gx", "gy"), P(None, None, "gx", "gy"), P(None, None, "gx", "gy"), P())
    return jax.shard_map(
        on_device, mesh=mesh, in_specs=in_specs, out_specs=out_specs, check_vma=False
    )
```

```python
import jax
import jax.numpy as jnp
import numpy as np
from jax import lax
from jax.experimental import pallas as pl
from jax.experimental.pallas import tpu as pltpu
from jax.sharding import PartitionSpec as P

HALO = 64
F32 = jnp.float32
BF16 = jnp.bfloat16
SPAN = 192
TILE_ROWS = 12 * SPAN
VMEM = pl.BlockSpec(memory_space=pltpu.VMEM)
SMEM = pl.BlockSpec(memory_space=pltpu.SMEM)
PARAMS = pltpu.CompilerParams(vmem_limit_bytes=40 * 1024 * 1024)


def node_weights(count):
    w = np.zeros((count + 1, 8 * count), np.float32)
    for v in range(8 * count):
        s = (v % 8 + 0.5) / 8.0
        w[v // 8, v] = 1.0 - s
        w[v // 8 + 1, v] = s
    return w


def tables():
    wx = node_weights(8)
    left = np.zeros((64, 6, 64), np.float32)
    for kc in range(6):
        left[kc * 8 : kc * 8 + 8, kc] = wx[:8]
        left[48 + kc, kc] = wx[8]
        left[56 + kc, kc] = wx[0]
    left = left.reshape(64, 384)
    expand = left.T.copy()
    expand[:, 56:] = 0.0
    wy = np.zeros((128, 128), np.float32)
    wy[:, :17] = node_weights(16).T
    as_bf = lambda a: jnp.asarray(a, BF16)
    return as_bf(left / 512.0), as_bf(wy), as_bf(expand), as_bf(wy.T)


def split(x):
    hi = x.astype(BF16)
    return hi, (x - hi.astype(F32)).astype(BF16)


def dot(a, b):
    return jnp.dot(a, b, preferred_element_type=F32)


def dot_right(w, x):
    hi, lo = split(x)
    return dot(w, hi) + dot(w, lo)


def dot_left(x, w):
    hi, lo = split(x)
    return dot(hi, w) + dot(lo, w)


def pack_kernel(up_ref, own_ref, down_ref, right_ref, left_ref):
    left = lax.broadcasted_iota(jnp.int32, (64, 128), 1) < 64
    for p in range(4):
        for s, ref in enumerate((up_ref, own_ref, down_ref)):
            a = ref[p].astype(F32)
            c = ref[p + 4].astype(F32)
            ra = pltpu.roll(a, 64, 1)
            rc = pltpu.roll(c, 64, 1)
            rows = pl.ds(s * 64, 64)
            right_ref[p, rows] = jnp.where(left, ra, c).astype(BF16)
            left_ref[p, rows] = jnp.where(left, a, rc).astype(BF16)


def over_sublanes(x):
    return jnp.sum(x, axis=0, keepdims=True)


def lanes_of(x, idx):
    return jnp.take_along_axis(x, idx & 127, axis=1, mode="promise_in_bounds")


def face_row(face):
    return over_sublanes(pltpu.roll(face, 0, 1, stride=17, stride_axis=0))


def face_of(row):
    lane = lax.broadcasted_iota(jnp.int32, (8, 128), 1)
    sub = lax.broadcasted_iota(jnp.int32, (8, 128), 0)
    back = lanes_of(jnp.broadcast_to(row, (8, 128)), lane + 17 * sub)
    return jnp.where((lane < 17) & (sub < 6), back, 0.0)


def column_row(rows, face, at):
    lane = lax.broadcasted_iota(jnp.int32, (8, 128), 1)
    block = jnp.zeros((8, 128), F32)
    for kc in range(6):
        block = jnp.where(lane == kc, jnp.broadcast_to(rows[kc][:, at : at + 1], (8, 128)), block)
    edge = jnp.where(lane == 64, jnp.broadcast_to(face[:, at : at + 1], (8, 128)), 0.0)
    block = pltpu.roll(block, 0, 1, stride=8, stride_axis=0)
    edge = pltpu.roll(edge, 0, 1, stride=1, stride_axis=0)
    return over_sublanes(block + edge)


def column_of(row):
    lane = lax.broadcasted_iota(jnp.int32, (8, 128), 1)
    sub = lax.broadcasted_iota(jnp.int32, (8, 128), 0)
    row = jnp.broadcast_to(row, (8, 128))
    return lanes_of(row, lane + 8 * sub), lanes_of(row, lane + 64 + sub)


def sample_kernel(
    nx, ny, idx_ref, frac_ref, up_ref, own_ref, down_ref, lo_ref, hi_ref, ref_ref, left_ref, wy_ref,
    res_ref, slope_ref, node_ref, send_ref, sq_ref, img, arr, wgt, rsc, gsc,
):
    half = lax.broadcasted_iota(jnp.int32, (64, 128), 1) < 64
    zero = jnp.zeros((2 * SPAN, 128), F32)
    for k in range(3):
        img[pl.ds(k * TILE_ROWS, 2 * SPAN)] = zero
        img[pl.ds(k * TILE_ROWS + 10 * SPAN, 2 * SPAN)] = zero
    for p in range(4):
        for s, ref in enumerate((up_ref, own_ref, down_ref)):
            a = ref[p].astype(F32)
            c = ref[p + 4].astype(F32)
            ra = pltpu.roll(a, 64, 1)
            rc = pltpu.roll(c, 64, 1)
            rows = pl.ds(s * 64, 64)
            lo = lo_ref[p, rows].astype(F32)
            hi = hi_ref[p, rows].astype(F32)
            rlo = pltpu.roll(lo, 64, 1)
            rhi = pltpu.roll(hi, 64, 1)
            at = lambda k, q: pl.ds(k * TILE_ROWS + (q + 2) * SPAN + s * 64, 64)
            img[at(0, p)] = jnp.where(half, lo, ra)
            img[at(1, p)] = a
            img[at(2, p)] = jnp.where(half, ra, rhi)
            img[at(0, p + 4)] = jnp.where(half, rlo, rc)
            img[at(1, p + 4)] = c
            img[at(2, p + 4)] = jnp.where(half, rc, hi)
    for z in range(8):
        rsc[z] = ref_ref[z].astype(F32).reshape(8, 8, 128)

    lane = lax.broadcasted_iota(jnp.int32, (8, 128), 1)

    def element(e, carry):
        base = idx_ref[0, e]
        shift = idx_ref[1, e]
        place = idx_ref[2, e]
        first = idx_ref[3, e]
        where_to = (lane - first) & 127
        mask = where_to < 9
        for z in range(9):
            for q in range(2):
                v = img[pl.ds(base + (z * SPAN + q), 8), :]
                v = pltpu.roll(v, shift, 1)
                pltpu.store(arr.at[place, z * 2 + q], v, mask=mask)
        mask = where_to < 8
        row = place & 7
        for c in range(3):
            pltpu.store(wgt.at[c, row], jnp.full((8, 128), frac_ref[c, e], F32), mask=mask)
        return carry

    lax.fori_loop(0, 128, element, 0, unroll=16)

    phase = lane & 15
    even = phase < 8
    even_next = (phase >= 1) & (phase <= 8)

    def interpolate(cx, square):
        wz, wx, wy = wgt[0, cx], wgt[1, cx], wgt[2, cx]

        def pair(z, q):
            ev = arr[cx, z * 2 + q]
            od = arr[cx + 8, z * 2 + q]
            near = jnp.where(even, ev, od)
            far = pltpu.roll(jnp.where(even_next, ev, od), 127, 1)
            return near, far

        total = [None] * 3
        upper = [None] * 3
        prev = [pair(0, 0), pair(0, 1)]
        for z in range(8):
            cur = [pair(z + 1, 0), pair(z + 1, 1)]
            low, dzx, dx = [], [], []
            for y in range(2):
                d0 = cur[0][y] - prev[0][y]
                d1 = cur[1][y] - prev[1][y]
                l0 = prev[0][y] + wz * d0
                l1 = prev[1][y] + wz * d1
                dx.append(l1 - l0)
                low.append(l0 + wx * dx[y])
                dzx.append(d0 + wx * (d1 - d0))
            prev = cur
            slope_y = low[1] - low[0]
            value = low[0] + wy * slope_y
            slope_z = dzx[0] + wy * (dzx[1] - dzx[0])
            slope_x = dx[0] + wy * (dx[1] - dx[0])
            r = rsc[z, cx] - value
            rsc[z, cx] = r
            square = square + r * r
            for k, s in enumerate((slope_z, slope_x, slope_y)):
                slope_ref[k, z, cx] = s
                w = s * r
                u = w * ((z + 0.5) / 8.0)
                total[k] = w if z == 0 else total[k] + w
                upper[k] = u if z == 0 else upper[k] + u
        for k in range(3):
            gsc[2 * k, cx] = total[k] - upper[k]
            gsc[2 * k + 1, cx] = upper[k]
        return square

    sq_ref[...] = lax.fori_loop(0, 8, interpolate, jnp.zeros((8, 128), F32))
    res_ref[...] = rsc[...].reshape(8, 64, 128).astype(BF16)
    nodes = dot_left(dot_right(left_ref[...], gsc[...].reshape(384, 128)), wy_ref[...])
    node_ref[...] = nodes
    rows = [nodes[kc * 8 : kc * 8 + 8] for kc in range(6)]
    high, low = nodes[48:56], nodes[56:64]
    col_high = column_row(rows, high, 16)
    col_low = column_row(rows, high, 0)
    high, low = face_row(high), face_row(low)
    gx, gy = lax.axis_index("gx"), lax.axis_index("gy")
    send_ref[...] = jnp.zeros(send_ref.shape, F32)
    for dx in (-1, 0, 1):
        for dy in (-1, 0, 1):
            if dx == 0 and dy == 0:
                continue
            block = high if dx == 1 else low if dx == -1 else col_high if dy == 1 else col_low
            px, py = gx + dx, gy + dy

            @pl.when((px >= 0) & (px < nx) & (py >= 0) & (py < ny))
            def _():
                send_ref[px * ny + py] = block


def product_kernel(
    nx, ny, recv_ref, node_ref, slope_ref, sq_ref, expand_ref, wyt_ref, left_ref, wy_ref,
    grad_ref, hess_ref, send_ref, msc, gsc,
):
    gx, gy = lax.axis_index("gx"), lax.axis_index("gy")
    own = gx * ny + gy
    lane = lax.broadcasted_iota(jnp.int32, (8, 128), 1)
    sub = lax.broadcasted_iota(jnp.int32, (8, 128), 0)

    def block(dx, dy):
        px, py = gx + dx, gy + dy
        there = (px >= 0) & (px < nx) & (py >= 0) & (py < ny)
        return recv_ref[jnp.where(there, px * ny + py, own)]

    def column(x, at):
        return jnp.broadcast_to(x[:, at : at + 1], (8, 128))

    def with_corners(dx):
        mid = face_of(block(dx, 0))
        mid = mid + jnp.where(lane == 0, column(face_of(block(dx, -1)), 16), 0.0)
        return mid + jnp.where(lane == 16, column(face_of(block(dx, 1)), 0), 0.0)

    keep_x = jnp.where(gx == nx - 1, 0.0, 1.0).astype(F32)
    keep_y = jnp.where(gy == ny - 1, 0.0, 1.0).astype(F32)
    keep_lane = jnp.where(lane == 16, keep_y, 1.0)
    row_low = with_corners(-1)
    row_high = with_corners(1)
    col_low, edge_low = column_of(block(0, -1))
    col_high, edge_high = column_of(block(0, 1))
    grads = []
    square = jnp.zeros((8, 128), F32)
    for kc in range(6):
        g = node_ref[kc * 8 : kc * 8 + 8]
        g = g + jnp.where(sub == 0, jnp.broadcast_to(row_low[kc : kc + 1], (8, 128)), 0.0)
        g = g + jnp.where(lane == 0, column(col_low, kc), 0.0)
        g = g + jnp.where(lane == 16, column(col_high, kc), 0.0)
        g = g * keep_lane
        grads.append(g)
        grad_ref[kc] = g
        own_g = jnp.where(lane < 16, g, 0.0)
        square = square + own_g * own_g
    face = node_ref[48:56] + row_high
    face = face + jnp.where(lane == 0, column(edge_low, 0), 0.0)
    face = face + jnp.where(lane == 16, column(edge_high, 0), 0.0)
    face = jnp.where(sub < 6, face * keep_lane * keep_x, 0.0)
    full = jnp.concatenate(grads + [face, jnp.zeros((8, 128), F32)], axis=0)
    moved = dot_right(expand_ref[...], dot_left(full, wyt_ref[...]))
    msc[...] = moved.reshape(6, 8, 8, 128)

    def apply(cx, curve):
        m0 = [msc[2 * k, cx] for k in range(3)]
        dm = [msc[2 * k + 1, cx] - m0[k] for k in range(3)]
        total = [None] * 3
        upper = [None] * 3
        for z in range(8):
            sz = (z + 0.5) / 8.0
            s = [slope_ref[k, z, cx] for k in range(3)]
            along = s[0] * (m0[0] + sz * dm[0])
            for k in (1, 2):
                along = along + s[k] * (m0[k] + sz * dm[k])
            curve = curve + along * along
            for k in range(3):
                w = s[k] * along
                u = w * sz
                total[k] = w if z == 0 else total[k] + w
                upper[k] = u if z == 0 else upper[k] + u
        for k in range(3):
            gsc[2 * k, cx] = total[k] - upper[k]
            gsc[2 * k + 1, cx] = upper[k]
        return curve

    curve = lax.fori_loop(0, 8, apply, jnp.zeros((8, 128), F32))
    nodes = dot_left(dot_right(left_ref[...], gsc[...].reshape(384, 128)), wy_ref[...])
    rows = [nodes[kc * 8 : kc * 8 + 8] for kc in range(6)]
    for kc in range(6):
        hess_ref[kc] = rows[kc]
    col_high = column_row(rows, nodes[48:56], 16)
    high = face_row(nodes[48:56])
    spot = lane[:1]
    sums = jnp.where(spot == 104, jnp.sum(sq_ref[...]), 0.0)
    sums = jnp.where(spot == 105, jnp.sum(square), sums)
    sums = jnp.where(spot == 106, jnp.sum(curve) * (1.0 / 512.0), sums)
    tail = spot >= 104
    send_ref[...] = jnp.broadcast_to(sums[None], send_ref.shape)
    for dx, dy, data in ((1, 0, high), (1, 1, high), (0, 1, col_high)):
        px, py = gx + dx, gy + dy

        @pl.when((px < nx) & (py < ny))
        def _():
            send_ref[px * ny + py] = jnp.where(tail, sums, data)


def finish_kernel(nx, ny, voxels, recv_ref, grad_ref, hess_ref, step_ref, prod_ref, misfit_ref):
    gx, gy = lax.axis_index("gx"), lax.axis_index("gy")
    own = gx * ny + gy
    lane = lax.broadcasted_iota(jnp.int32, (8, 128), 1)
    sub = lax.broadcasted_iota(jnp.int32, (8, 128), 0)

    def block(dx, dy):
        px, py = gx + dx, gy + dy
        there = (px >= 0) & (py >= 0)
        data = recv_ref[jnp.where(there, px * ny + py, own)]
        return jnp.where(there, data, 0.0)

    def column(x, at):
        return jnp.broadcast_to(x[:, at : at + 1], (8, 128))

    total = jnp.sum(recv_ref[...], axis=0)
    misfit_ref[...] = total[:, 104:105] * (1.0 / voxels)
    total = jnp.broadcast_to(total, (8, 128))
    alpha = column(total, 105) / column(total, 106)
    row_low = face_of(block(-1, 0)) + jnp.where(lane == 0, column(face_of(block(-1, -1)), 16), 0.0)
    col_low = column_of(block(0, -1))[0]
    for kc in range(6):
        h = hess_ref[kc]
        h = h + jnp.where(sub == 0, jnp.broadcast_to(row_low[kc : kc + 1], (8, 128)), 0.0)
        h = h + jnp.where(lane == 0, column(col_low, kc), 0.0)
        prod_ref[kc // 2, kc % 2] = h[:, :16]
        step_ref[kc // 2, kc % 2] = (alpha * grad_ref[kc])[:, :16]


def on_device(ref_image, def_image, shift_xy, shift_z, frac, connectivity):
    nx, ny = lax.axis_size("gx"), lax.axis_size("gy")
    peers = nx * ny
    sds = jax.ShapeDtypeStruct
    up = [(i, i + 1) for i in range(nx - 1)]
    below = lax.ppermute(def_image, "gx", up)
    above = lax.ppermute(def_image, "gx", [(j, i) for i, j in up])
    to_right, to_left = pl.pallas_call(
        pack_kernel,
        out_shape=(sds((4, SPAN, 128), BF16), sds((4, SPAN, 128), BF16)),
        in_specs=[VMEM] * 3,
        out_specs=(VMEM, VMEM),
        compiler_params=PARAMS,
        name="pack_halo",
    )(below, def_image, above)
    up = [(i, i + 1) for i in range(ny - 1)]
    lo = lax.ppermute(to_right, "gy", up)
    hi = lax.ppermute(to_left, "gy", [(j, i) for i, j in up])

    first = connectivity[0]
    col_x = first // 17 % 9
    col_y = first % 17
    start_x = 8 * col_x + shift_xy[0] + HALO
    start_y = 8 * col_y + shift_xy[1] + HALO
    tile = jnp.minimum(start_y // 64, 2)
    base = tile * TILE_ROWS + (shift_z + 2) * SPAN + start_x
    shift = (8 * col_y - (start_y - 64 * tile)) & 127
    place = (col_y & 1) * 8 + col_x
    idx = jnp.stack([base, shift, place, 8 * col_y])

    left, wy, expand, wyt = tables()
    residual, slopes, nodes, send, square = pl.pallas_call(
        lambda *refs: sample_kernel(nx, ny, *refs),
        out_shape=(
            sds((8, 64, 128), BF16),
            sds((3, 8, 8, 8, 128), F32),
            sds((64, 128), F32),
            sds((peers, 1, 128), F32),
            sds((8, 128), F32),
        ),
        in_specs=[SMEM, SMEM] + [VMEM] * 8,
        out_specs=(VMEM,) * 5,
        scratch_shapes=[
            pltpu.VMEM((3 * TILE_ROWS, 128), F32),
            pltpu.VMEM((16, 18, 8, 128), F32),
            pltpu.VMEM((3, 8, 8, 128), F32),
            pltpu.VMEM((8, 8, 8, 128), F32),
            pltpu.VMEM((6, 8, 8, 128), F32),
        ],
        compiler_params=PARAMS,
        name="sample_and_gradient",
    )(idx, frac, below, def_image, above, lo, hi, ref_image, left, wy)
    recv = lax.all_to_all(send, ("gx", "gy"), 0, 0, tiled=True)
    grads, hess, send = pl.pallas_call(
        lambda *refs: product_kernel(nx, ny, *refs),
        out_shape=(sds((6, 8, 128), F32), sds((6, 8, 128), F32), sds((peers, 1, 128), F32)),
        in_specs=[VMEM] * 8,
        out_specs=(VMEM,) * 3,
        scratch_shapes=[pltpu.VMEM((6, 8, 8, 128), F32), pltpu.VMEM((6, 8, 8, 128), F32)],
        compiler_params=PARAMS,
        name="gauss_newton_product",
    )(recv, nodes, slopes, square, expand, wyt, left, wy)
    recv = lax.all_to_all(send, ("gx", "gy"), 0, 0, tiled=True)
    voxels = 8 * 64 * 128 * peers
    step, product, misfit = pl.pallas_call(
        lambda *refs: finish_kernel(nx, ny, voxels, *refs),
        out_shape=(sds((3, 2, 8, 16), F32), sds((3, 2, 8, 16), F32), sds((1, 1), F32)),
        in_specs=[VMEM] * 3,
        out_specs=(VMEM,) * 3,
        compiler_params=PARAMS,
        name="finish",
    )(recv, grads, hess)
    return (residual, step, product, misfit[0, 0])


def solution(mesh):
    in_specs = (
        P(None, "gx", "gy"),
        P(None, "gx", "gy"),
        P(None, ("gx", "gy")),
        P(("gx", "gy")),
        P(None, ("gx", "gy")),
        P(None, ("gx", "gy")),
    )
    out_specs = (P(None, "gx", "gy"), P(None, None, "gx", "gy"), P(None, None, "gx", "gy"), P())
    return jax.shard_map(
        on_device, mesh=mesh, in_specs=in_specs, out_specs=out_specs, check_vma=False
    )
```

```python
import jax
import jax.numpy as jnp
import numpy as np
from jax import lax
from jax.experimental import pallas as pl
from jax.experimental.pallas import tpu as pltpu
from jax.sharding import PartitionSpec as P

HALO = 64
F32 = jnp.float32
BF16 = jnp.bfloat16
SPAN = 192
TILE_ROWS = 12 * SPAN
VMEM = pl.BlockSpec(memory_space=pltpu.VMEM)
SMEM = pl.BlockSpec(memory_space=pltpu.SMEM)
PARAMS = pltpu.CompilerParams(vmem_limit_bytes=40 * 1024 * 1024)


def node_weights(count):
    w = np.zeros((count + 1, 8 * count), np.float32)
    for v in range(8 * count):
        s = (v % 8 + 0.5) / 8.0
        w[v // 8, v] = 1.0 - s
        w[v // 8 + 1, v] = s
    return w


def tables():
    wx = node_weights(8)
    left = np.zeros((64, 6, 64), np.float32)
    for kc in range(6):
        left[kc * 8 : kc * 8 + 8, kc] = wx[:8]
        left[48 + kc, kc] = wx[8]
        left[56 + kc, kc] = wx[0]
    left = left.reshape(64, 384)
    expand = left.T.copy()
    expand[:, 56:] = 0.0
    wy = np.zeros((128, 128), np.float32)
    wy[:, :17] = node_weights(16).T
    as_bf = lambda a: jnp.asarray(a, BF16)
    return as_bf(left / 512.0), as_bf(wy), as_bf(expand), as_bf(wy.T)


def split(x):
    hi = x.astype(BF16)
    return hi, (x - hi.astype(F32)).astype(BF16)


def dot(a, b):
    return jnp.dot(a, b, preferred_element_type=F32)


def dot_right(w, x):
    hi, lo = split(x)
    return dot(w, hi) + dot(w, lo)


def dot_left(x, w):
    hi, lo = split(x)
    return dot(hi, w) + dot(lo, w)


def pack_kernel(up_ref, own_ref, down_ref, right_ref, left_ref):
    left = lax.broadcasted_iota(jnp.int32, (64, 128), 1) < 64
    for p in range(4):
        for s, ref in enumerate((up_ref, own_ref, down_ref)):
            a = ref[p].astype(F32)
            c = ref[p + 4].astype(F32)
            ra = pltpu.roll(a, 64, 1)
            rc = pltpu.roll(c, 64, 1)
            rows = pl.ds(s * 64, 64)
            right_ref[p, rows] = jnp.where(left, ra, c).astype(BF16)
            left_ref[p, rows] = jnp.where(left, a, rc).astype(BF16)


def over_sublanes(x):
    return jnp.sum(x, axis=0, keepdims=True)


def lanes_of(x, idx):
    return jnp.take_along_axis(x, idx & 127, axis=1, mode="promise_in_bounds")


def face_row(face):
    return over_sublanes(pltpu.roll(face, 0, 1, stride=17, stride_axis=0))


def face_of(row):
    lane = lax.broadcasted_iota(jnp.int32, (8, 128), 1)
    sub = lax.broadcasted_iota(jnp.int32, (8, 128), 0)
    back = lanes_of(jnp.broadcast_to(row, (8, 128)), lane + 17 * sub)
    return jnp.where((lane < 17) & (sub < 6), back, 0.0)


def column_row(rows, face, at):
    lane = lax.broadcasted_iota(jnp.int32, (8, 128), 1)
    block = jnp.zeros((8, 128), F32)
    for kc in range(6):
        block = jnp.where(lane == kc, jnp.broadcast_to(rows[kc][:, at : at + 1], (8, 128)), block)
    edge = jnp.where(lane == 64, jnp.broadcast_to(face[:, at : at + 1], (8, 128)), 0.0)
    block = pltpu.roll(block, 0, 1, stride=8, stride_axis=0)
    edge = pltpu.roll(edge, 0, 1, stride=1, stride_axis=0)
    return over_sublanes(block + edge)


def column_of(row):
    lane = lax.broadcasted_iota(jnp.int32, (8, 128), 1)
    sub = lax.broadcasted_iota(jnp.int32, (8, 128), 0)
    row = jnp.broadcast_to(row, (8, 128))
    return lanes_of(row, lane + 8 * sub), lanes_of(row, lane + 64 + sub)


def sample_kernel(
    nx, ny, idx_ref, frac_ref, up_ref, own_ref, down_ref, lo_ref, hi_ref, ref_ref, left_ref, wy_ref,
    res_ref, slope_ref, node_ref, send_ref, sq_ref, img, arr, wgt, rsc, gsc,
):
    half = lax.broadcasted_iota(jnp.int32, (64, 128), 1) < 64
    zero = jnp.zeros((2 * SPAN, 128), F32)
    for k in range(3):
        img[pl.ds(k * TILE_ROWS, 2 * SPAN)] = zero
        img[pl.ds(k * TILE_ROWS + 10 * SPAN, 2 * SPAN)] = zero
    for p in range(4):
        for s, ref in enumerate((up_ref, own_ref, down_ref)):
            a = ref[p].astype(F32)
            c = ref[p + 4].astype(F32)
            ra = pltpu.roll(a, 64, 1)
            rc = pltpu.roll(c, 64, 1)
            rows = pl.ds(s * 64, 64)
            lo = lo_ref[p, rows].astype(F32)
            hi = hi_ref[p, rows].astype(F32)
            rlo = pltpu.roll(lo, 64, 1)
            rhi = pltpu.roll(hi, 64, 1)
            at = lambda k, q: pl.ds(k * TILE_ROWS + (q + 2) * SPAN + s * 64, 64)
            img[at(0, p)] = jnp.where(half, lo, ra)
            img[at(1, p)] = a
            img[at(2, p)] = jnp.where(half, ra, rhi)
            img[at(0, p + 4)] = jnp.where(half, rlo, rc)
            img[at(1, p + 4)] = c
            img[at(2, p + 4)] = jnp.where(half, rc, hi)
    for z in range(8):
        rsc[z] = ref_ref[z].astype(F32).reshape(8, 8, 128)

    lane = lax.broadcasted_iota(jnp.int32, (8, 128), 1)

    def element(e, carry):
        base = idx_ref[0, e]
        shift = idx_ref[1, e]
        place = idx_ref[2, e]
        first = idx_ref[3, e]
        where_to = (lane - first) & 127
        mask = where_to < 9
        for z in range(9):
            for q in range(2):
                v = img[pl.ds(base + (z * SPAN + q), 8), :]
                v = pltpu.roll(v, shift, 1)
                pltpu.store(arr.at[place, z * 2 + q], v, mask=mask)
        mask = where_to < 8
        row = place & 7
        for c in range(3):
            pltpu.store(wgt.at[c, row], jnp.full((8, 128), frac_ref[c, e], F32), mask=mask)
        return carry

    lax.fori_loop(0, 128, element, 0, unroll=16)

    phase = lane & 15
    even = phase < 8
    even_next = (phase >= 1) & (phase <= 8)

    def interpolate(cx, square):
        wz, wx, wy = wgt[0, cx], wgt[1, cx], wgt[2, cx]

        def pair(z, q):
            ev = arr[cx, z * 2 + q]
            od = arr[cx + 8, z * 2 + q]
            near = jnp.where(even, ev, od)
            far = pltpu.roll(jnp.where(even_next, ev, od), 127, 1)
            return near, far

        total = [None] * 3
        upper = [None] * 3
        prev = [pair(0, 0), pair(0, 1)]
        for z in range(8):
            cur = [pair(z + 1, 0), pair(z + 1, 1)]
            low, dzx, dx = [], [], []
            for y in range(2):
                d0 = cur[0][y] - prev[0][y]
                d1 = cur[1][y] - prev[1][y]
                l0 = prev[0][y] + wz * d0
                l1 = prev[1][y] + wz * d1
                dx.append(l1 - l0)
                low.append(l0 + wx * dx[y])
                dzx.append(d0 + wx * (d1 - d0))
            prev = cur
            slope_y = low[1] - low[0]
            value = low[0] + wy * slope_y
            slope_z = dzx[0] + wy * (dzx[1] - dzx[0])
            slope_x = dx[0] + wy * (dx[1] - dx[0])
            r = rsc[z, cx] - value
            rsc[z, cx] = r
            square = square + r * r
            for k, s in enumerate((slope_z, slope_x, slope_y)):
                slope_ref[k, z, cx] = s
                w = s * r
                u = w * ((z + 0.5) / 8.0)
                total[k] = w if z == 0 else total[k] + w
                upper[k] = u if z == 0 else upper[k] + u
        for k in range(3):
            gsc[2 * k, cx] = total[k] - upper[k]
            gsc[2 * k + 1, cx] = upper[k]
        return square

    sq_ref[...] = lax.fori_loop(0, 8, interpolate, jnp.zeros((8, 128), F32))
    res_ref[...] = rsc[...].reshape(8, 64, 128).astype(BF16)
    nodes = dot_left(dot_right(left_ref[...], gsc[...].reshape(384, 128)), wy_ref[...])
    node_ref[...] = nodes
    rows = [nodes[kc * 8 : kc * 8 + 8] for kc in range(6)]
    high, low = nodes[48:56], nodes[56:64]
    col_high = column_row(rows, high, 16)
    col_low = column_row(rows, high, 0)
    high, low = face_row(high), face_row(low)
    for n, row in enumerate((high, low, col_high, col_low)):
        send_ref[n : n + 1] = row


def product_kernel(
    nx, ny, recv_ref, node_ref, slope_ref, sq_ref, expand_ref, wyt_ref, left_ref, wy_ref,
    grad_ref, hess_ref, send_ref, msc, gsc,
):
    gx, gy = lax.axis_index("gx"), lax.axis_index("gy")
    own = gx * ny + gy
    lane = lax.broadcasted_iota(jnp.int32, (8, 128), 1)
    sub = lax.broadcasted_iota(jnp.int32, (8, 128), 0)

    def block(dx, dy):
        px, py = gx + dx, gy + dy
        there = (px >= 0) & (px < nx) & (py >= 0) & (py < ny)
        n = 0 if dx == -1 else 1 if dx == 1 else 2 if dy == -1 else 3
        return jnp.where(there, recv_ref[jnp.where(there, px * ny + py, own), n : n + 1], 0.0)

    def column(x, at):
        return jnp.broadcast_to(x[:, at : at + 1], (8, 128))

    def with_corners(dx):
        mid = face_of(block(dx, 0))
        mid = mid + jnp.where(lane == 0, column(face_of(block(dx, -1)), 16), 0.0)
        return mid + jnp.where(lane == 16, column(face_of(block(dx, 1)), 0), 0.0)

    keep_x = jnp.where(gx == nx - 1, 0.0, 1.0).astype(F32)
    keep_y = jnp.where(gy == ny - 1, 0.0, 1.0).astype(F32)
    keep_lane = jnp.where(lane == 16, keep_y, 1.0)
    row_low = with_corners(-1)
    row_high = with_corners(1)
    col_low, edge_low = column_of(block(0, -1))
    col_high, edge_high = column_of(block(0, 1))
    grads = []
    square = jnp.zeros((8, 128), F32)
    for kc in range(6):
        g = node_ref[kc * 8 : kc * 8 + 8]
        g = g + jnp.where(sub == 0, jnp.broadcast_to(row_low[kc : kc + 1], (8, 128)), 0.0)
        g = g + jnp.where(lane == 0, column(col_low, kc), 0.0)
        g = g + jnp.where(lane == 16, column(col_high, kc), 0.0)
        g = g * keep_lane
        grads.append(g)
        grad_ref[kc] = g
        own_g = jnp.where(lane < 16, g, 0.0)
        square = square + own_g * own_g
    face = node_ref[48:56] + row_high
    face = face + jnp.where(lane == 0, column(edge_low, 0), 0.0)
    face = face + jnp.where(lane == 16, column(edge_high, 0), 0.0)
    face = jnp.where(sub < 6, face * keep_lane * keep_x, 0.0)
    full = jnp.concatenate(grads + [face, jnp.zeros((8, 128), F32)], axis=0)
    moved = dot_right(expand_ref[...], dot_left(full, wyt_ref[...]))
    msc[...] = moved.reshape(6, 8, 8, 128)

    def apply(cx, curve):
        m0 = [msc[2 * k, cx] for k in range(3)]
        dm = [msc[2 * k + 1, cx] - m0[k] for k in range(3)]
        total = [None] * 3
        upper = [None] * 3
        for z in range(8):
            sz = (z + 0.5) / 8.0
            s = [slope_ref[k, z, cx] for k in range(3)]
            along = s[0] * (m0[0] + sz * dm[0])
            for k in (1, 2):
                along = along + s[k] * (m0[k] + sz * dm[k])
            curve = curve + along * along
            for k in range(3):
                w = s[k] * along
                u = w * sz
                total[k] = w if z == 0 else total[k] + w
                upper[k] = u if z == 0 else upper[k] + u
        for k in range(3):
            gsc[2 * k, cx] = total[k] - upper[k]
            gsc[2 * k + 1, cx] = upper[k]
        return curve

    curve = lax.fori_loop(0, 8, apply, jnp.zeros((8, 128), F32))
    nodes = dot_left(dot_right(left_ref[...], gsc[...].reshape(384, 128)), wy_ref[...])
    rows = [nodes[kc * 8 : kc * 8 + 8] for kc in range(6)]
    for kc in range(6):
        hess_ref[kc] = rows[kc]
    col_high = column_row(rows, nodes[48:56], 16)
    high = face_row(nodes[48:56])
    spot = lane[:1]
    sums = jnp.where(spot == 104, jnp.sum(sq_ref[...]), 0.0)
    sums = jnp.where(spot == 105, jnp.sum(square), sums)
    sums = jnp.where(spot == 106, jnp.sum(curve) * (1.0 / 512.0), sums)
    send_ref[0:1] = jnp.where(spot >= 104, sums, high)
    send_ref[1:2] = col_high


def finish_kernel(nx, ny, voxels, recv_ref, grad_ref, hess_ref, step_ref, prod_ref, misfit_ref):
    gx, gy = lax.axis_index("gx"), lax.axis_index("gy")
    own = gx * ny + gy
    lane = lax.broadcasted_iota(jnp.int32, (8, 128), 1)
    sub = lax.broadcasted_iota(jnp.int32, (8, 128), 0)

    def block(dx, dy):
        px, py = gx + dx, gy + dy
        there = (px >= 0) & (py >= 0)
        n = 0 if dx == -1 else 1
        data = recv_ref[jnp.where(there, px * ny + py, own), n : n + 1]
        return jnp.where(there, data, 0.0)

    def column(x, at):
        return jnp.broadcast_to(x[:, at : at + 1], (8, 128))

    total = jnp.sum(recv_ref[...], axis=0)[0:1]
    misfit_ref[...] = total[:, 104:105] * (1.0 / voxels)
    total = jnp.broadcast_to(total, (8, 128))
    alpha = column(total, 105) / column(total, 106)
    row_low = face_of(block(-1, 0)) + jnp.where(lane == 0, column(face_of(block(-1, -1)), 16), 0.0)
    col_low = column_of(block(0, -1))[0]
    for kc in range(6):
        h = hess_ref[kc]
        h = h + jnp.where(sub == 0, jnp.broadcast_to(row_low[kc : kc + 1], (8, 128)), 0.0)
        h = h + jnp.where(lane == 0, column(col_low, kc), 0.0)
        prod_ref[kc // 2, kc % 2] = h[:, :16]
        step_ref[kc // 2, kc % 2] = (alpha * grad_ref[kc])[:, :16]


def on_device(ref_image, def_image, shift_xy, shift_z, frac, connectivity):
    nx, ny = lax.axis_size("gx"), lax.axis_size("gy")
    peers = nx * ny
    sds = jax.ShapeDtypeStruct
    up = [(i, i + 1) for i in range(nx - 1)]
    below = lax.ppermute(def_image, "gx", up)
    above = lax.ppermute(def_image, "gx", [(j, i) for i, j in up])
    to_right, to_left = pl.pallas_call(
        pack_kernel,
        out_shape=(sds((4, SPAN, 128), BF16), sds((4, SPAN, 128), BF16)),
        in_specs=[VMEM] * 3,
        out_specs=(VMEM, VMEM),
        compiler_params=PARAMS,
        name="pack_halo",
    )(below, def_image, above)
    up = [(i, i + 1) for i in range(ny - 1)]
    lo = lax.ppermute(to_right, "gy", up)
    hi = lax.ppermute(to_left, "gy", [(j, i) for i, j in up])

    first = connectivity[0]
    col_x = first // 17 % 9
    col_y = first % 17
    start_x = 8 * col_x + shift_xy[0] + HALO
    start_y = 8 * col_y + shift_xy[1] + HALO
    tile = jnp.minimum(start_y // 64, 2)
    base = tile * TILE_ROWS + (shift_z + 2) * SPAN + start_x
    shift = (8 * col_y - (start_y - 64 * tile)) & 127
    place = (col_y & 1) * 8 + col_x
    idx = jnp.stack([base, shift, place, 8 * col_y])

    left, wy, expand, wyt = tables()
    residual, slopes, nodes, send, square = pl.pallas_call(
        lambda *refs: sample_kernel(nx, ny, *refs),
        out_shape=(
            sds((8, 64, 128), BF16),
            sds((3, 8, 8, 8, 128), F32),
            sds((64, 128), F32),
            sds((4, 128), F32),
            sds((8, 128), F32),
        ),
        in_specs=[SMEM, SMEM] + [VMEM] * 8,
        out_specs=(VMEM,) * 5,
        scratch_shapes=[
            pltpu.VMEM((3 * TILE_ROWS, 128), F32),
            pltpu.VMEM((16, 18, 8, 128), F32),
            pltpu.VMEM((3, 8, 8, 128), F32),
            pltpu.VMEM((8, 8, 8, 128), F32),
            pltpu.VMEM((6, 8, 8, 128), F32),
        ],
        compiler_params=PARAMS,
        name="sample_and_gradient",
    )(idx, frac, below, def_image, above, lo, hi, ref_image, left, wy)
    recv = lax.all_gather(send, ("gx", "gy"))
    grads, hess, send = pl.pallas_call(
        lambda *refs: product_kernel(nx, ny, *refs),
        out_shape=(sds((6, 8, 128), F32), sds((6, 8, 128), F32), sds((2, 128), F32)),
        in_specs=[VMEM] * 8,
        out_specs=(VMEM,) * 3,
        scratch_shapes=[pltpu.VMEM((6, 8, 8, 128), F32), pltpu.VMEM((6, 8, 8, 128), F32)],
        compiler_params=PARAMS,
        name="gauss_newton_product",
    )(recv, nodes, slopes, square, expand, wyt, left, wy)
    recv = lax.all_gather(send, ("gx", "gy"))
    voxels = 8 * 64 * 128 * peers
    step, product, misfit = pl.pallas_call(
        lambda *refs: finish_kernel(nx, ny, voxels, *refs),
        out_shape=(sds((3, 2, 8, 16), F32), sds((3, 2, 8, 16), F32), sds((1, 1), F32)),
        in_specs=[VMEM] * 3,
        out_specs=(VMEM,) * 3,
        compiler_params=PARAMS,
        name="finish",
    )(recv, grads, hess)
    return (residual, step, product, misfit[0, 0])


def solution(mesh):
    in_specs = (
        P(None, "gx", "gy"),
        P(None, "gx", "gy"),
        P(None, ("gx", "gy")),
        P(("gx", "gy")),
        P(None, ("gx", "gy")),
        P(None, ("gx", "gy")),
    )
    out_specs = (P(None, "gx", "gy"), P(None, None, "gx", "gy"), P(None, None, "gx", "gy"), P())
    return jax.shard_map(
        on_device, mesh=mesh, in_specs=in_specs, out_specs=out_specs, check_vma=False
    )
```

```python
import jax
import jax.numpy as jnp
import numpy as np
from jax import lax
from jax.experimental import pallas as pl
from jax.experimental.pallas import tpu as pltpu
from jax.sharding import PartitionSpec as P

HALO = 64
F32 = jnp.float32
BF16 = jnp.bfloat16
SPAN = 192
TILE_ROWS = 12 * SPAN
VMEM = pl.BlockSpec(memory_space=pltpu.VMEM)
SMEM = pl.BlockSpec(memory_space=pltpu.SMEM)
PARAMS = pltpu.CompilerParams(vmem_limit_bytes=40 * 1024 * 1024)


def node_weights(count):
    w = np.zeros((count + 1, 8 * count), np.float32)
    for v in range(8 * count):
        s = (v % 8 + 0.5) / 8.0
        w[v // 8, v] = 1.0 - s
        w[v // 8 + 1, v] = s
    return w


def tables():
    wx = node_weights(8)
    left = np.zeros((64, 6, 64), np.float32)
    for kc in range(6):
        left[kc * 8 : kc * 8 + 8, kc] = wx[:8]
        left[48 + kc, kc] = wx[8]
        left[56 + kc, kc] = wx[0]
    left = left.reshape(64, 384)
    expand = left.T.copy()
    expand[:, 56:] = 0.0
    wy = np.zeros((128, 128), np.float32)
    wy[:, :17] = node_weights(16).T
    as_bf = lambda a: jnp.asarray(a, BF16)
    return as_bf(left / 512.0), as_bf(wy), as_bf(expand), as_bf(wy.T)


def split(x):
    hi = x.astype(BF16)
    return hi, (x - hi.astype(F32)).astype(BF16)


def dot(a, b):
    return jnp.dot(a, b, preferred_element_type=F32)


def dot_right(w, x):
    hi, lo = split(x)
    return dot(w, hi) + dot(w, lo)


def dot_left(x, w):
    hi, lo = split(x)
    return dot(hi, w) + dot(lo, w)


def pack_rows(src, dst_a, dst_b, at, even):
    left = lax.broadcasted_iota(jnp.int32, (64, 128), 1) < 64
    for p in range(4):
        a = src[p].astype(F32)
        c = src[p + 4].astype(F32)
        right = jnp.where(left, pltpu.roll(a, 64, 1), c)
        other = jnp.where(left, a, pltpu.roll(c, 64, 1))
        dst_a[p, pl.ds(at, 64)] = jnp.where(even, right, other).astype(BF16)
        dst_b[p, pl.ds(at, 64)] = jnp.where(even, other, right).astype(BF16)


def pack_own_kernel(own_ref, a_ref, b_ref):
    even = lax.axis_index("gy") % 2 == 0
    pack_rows(own_ref, a_ref, b_ref, 0, even)


def pack_corner_kernel(xa_ref, xb_ref, a_ref, b_ref):
    even = lax.axis_index("gy") % 2 == 0
    pack_rows(xa_ref, a_ref, b_ref, 0, even)
    pack_rows(xb_ref, a_ref, b_ref, 64, even)


def over_sublanes(x):
    return jnp.sum(x, axis=0, keepdims=True)


def lanes_of(x, idx):
    return jnp.take_along_axis(x, idx & 127, axis=1, mode="promise_in_bounds")


def face_row(face):
    return over_sublanes(pltpu.roll(face, 0, 1, stride=17, stride_axis=0))


def face_of(row):
    lane = lax.broadcasted_iota(jnp.int32, (8, 128), 1)
    sub = lax.broadcasted_iota(jnp.int32, (8, 128), 0)
    back = lanes_of(jnp.broadcast_to(row, (8, 128)), lane + 17 * sub)
    return jnp.where((lane < 17) & (sub < 6), back, 0.0)


def column_row(rows, face, at):
    lane = lax.broadcasted_iota(jnp.int32, (8, 128), 1)
    block = jnp.zeros((8, 128), F32)
    for kc in range(6):
        block = jnp.where(lane == kc, jnp.broadcast_to(rows[kc][:, at : at + 1], (8, 128)), block)
    edge = jnp.where(lane == 64, jnp.broadcast_to(face[:, at : at + 1], (8, 128)), 0.0)
    block = pltpu.roll(block, 0, 1, stride=8, stride_axis=0)
    edge = pltpu.roll(edge, 0, 1, stride=1, stride_axis=0)
    return over_sublanes(block + edge)


def column_of(row):
    lane = lax.broadcasted_iota(jnp.int32, (8, 128), 1)
    sub = lax.broadcasted_iota(jnp.int32, (8, 128), 0)
    row = jnp.broadcast_to(row, (8, 128))
    return lanes_of(row, lane + 8 * sub), lanes_of(row, lane + 64 + sub)


def sample_kernel(
    nx, ny, idx_ref, frac_ref, xa_ref, own_ref, xb_ref, ya_ref, yb_ref, ca_ref, cb_ref, ref_ref, left_ref, wy_ref,
    res_ref, slope_ref, node_ref, send_ref, sq_ref, img, arr, wgt, rsc, gsc,
):
    half = lax.broadcasted_iota(jnp.int32, (64, 128), 1) < 64
    zero = jnp.zeros((2 * SPAN, 128), F32)
    for k in range(3):
        img[pl.ds(k * TILE_ROWS, 2 * SPAN)] = zero
        img[pl.ds(k * TILE_ROWS + 10 * SPAN, 2 * SPAN)] = zero
    odd_x = lax.axis_index("gx") % 2 == 1
    odd_y = lax.axis_index("gy") % 2 == 1
    at_a = jnp.where(odd_x, 0, 128)
    segments = (
        (xa_ref, ca_ref, cb_ref, 0, pl.multiple_of(at_a, 64)),
        (own_ref, ya_ref, yb_ref, 0, 64),
        (xb_ref, ca_ref, cb_ref, 64, pl.multiple_of(128 - at_a, 64)),
    )
    for p in range(4):
        for ref, pair_a, pair_b, at, row in segments:
            a = ref[p].astype(F32)
            c = ref[p + 4].astype(F32)
            ra = pltpu.roll(a, 64, 1)
            rc = pltpu.roll(c, 64, 1)
            from_a = pair_a[p, pl.ds(at, 64)].astype(F32)
            from_b = pair_b[p, pl.ds(at, 64)].astype(F32)
            lo = jnp.where(odd_y, from_a, from_b)
            hi = jnp.where(odd_y, from_b, from_a)
            rlo = pltpu.roll(lo, 64, 1)
            rhi = pltpu.roll(hi, 64, 1)
            at_row = lambda k, q: pl.ds(pl.multiple_of(k * TILE_ROWS + (q + 2) * SPAN + row, 8), 64)
            img[at_row(0, p)] = jnp.where(half, lo, ra)
            img[at_row(1, p)] = a
            img[at_row(2, p)] = jnp.where(half, ra, rhi)
            img[at_row(0, p + 4)] = jnp.where(half, rlo, rc)
            img[at_row(1, p + 4)] = c
            img[at_row(2, p + 4)] = jnp.where(half, rc, hi)
    for z in range(8):
        rsc[z] = ref_ref[z].astype(F32).reshape(8, 8, 128)

    lane = lax.broadcasted_iota(jnp.int32, (8, 128), 1)

    def element(e, carry):
        base = idx_ref[0, e]
        shift = idx_ref[1, e]
        place = idx_ref[2, e]
        first = idx_ref[3, e]
        where_to = (lane - first) & 127
        mask = where_to < 9
        for z in range(9):
            for q in range(2):
                v = img[pl.ds(base + (z * SPAN + q), 8), :]
                v = pltpu.roll(v, shift, 1)
                pltpu.store(arr.at[place, z * 2 + q], v, mask=mask)
        mask = where_to < 8
        row = place & 7
        for c in range(3):
            pltpu.store(wgt.at[c, row], jnp.full((8, 128), frac_ref[c, e], F32), mask=mask)
        return carry

    lax.fori_loop(0, 128, element, 0, unroll=16)

    phase = lane & 15
    even = phase < 8
    even_next = (phase >= 1) & (phase <= 8)

    def interpolate(cx, square):
        wz, wx, wy = wgt[0, cx], wgt[1, cx], wgt[2, cx]

        def pair(z, q):
            ev = arr[cx, z * 2 + q]
            od = arr[cx + 8, z * 2 + q]
            near = jnp.where(even, ev, od)
            far = pltpu.roll(jnp.where(even_next, ev, od), 127, 1)
            return near, far

        total = [None] * 3
        upper = [None] * 3
        prev = [pair(0, 0), pair(0, 1)]
        for z in range(8):
            cur = [pair(z + 1, 0), pair(z + 1, 1)]
            low, dzx, dx = [], [], []
            for y in range(2):
                d0 = cur[0][y] - prev[0][y]
                d1 = cur[1][y] - prev[1][y]
                l0 = prev[0][y] + wz * d0
                l1 = prev[1][y] + wz * d1
                dx.append(l1 - l0)
                low.append(l0 + wx * dx[y])
                dzx.append(d0 + wx * (d1 - d0))
            prev = cur
            slope_y = low[1] - low[0]
            value = low[0] + wy * slope_y
            slope_z = dzx[0] + wy * (dzx[1] - dzx[0])
            slope_x = dx[0] + wy * (dx[1] - dx[0])
            r = rsc[z, cx] - value
            rsc[z, cx] = r
            square = square + r * r
            for k, s in enumerate((slope_z, slope_x, slope_y)):
                slope_ref[k, z, cx] = s
                w = s * r
                u = w * ((z + 0.5) / 8.0)
                total[k] = w if z == 0 else total[k] + w
                upper[k] = u if z == 0 else upper[k] + u
        for k in range(3):
            gsc[2 * k, cx] = total[k] - upper[k]
            gsc[2 * k + 1, cx] = upper[k]
        return square

    sq_ref[...] = lax.fori_loop(0, 8, interpolate, jnp.zeros((8, 128), F32))
    res_ref[...] = rsc[...].reshape(8, 64, 128).astype(BF16)
    nodes = dot_left(dot_right(left_ref[...], gsc[...].reshape(384, 128)), wy_ref[...])
    node_ref[...] = nodes
    rows = [nodes[kc * 8 : kc * 8 + 8] for kc in range(6)]
    high, low = nodes[48:56], nodes[56:64]
    col_high = column_row(rows, high, 16)
    col_low = column_row(rows, high, 0)
    high, low = face_row(high), face_row(low)
    gx, gy = lax.axis_index("gx"), lax.axis_index("gy")
    send_ref[...] = jnp.zeros(send_ref.shape, F32)
    for dx in (-1, 0, 1):
        for dy in (-1, 0, 1):
            if dx == 0 and dy == 0:
                continue
            block = high if dx == 1 else low if dx == -1 else col_high if dy == 1 else col_low
            px, py = gx + dx, gy + dy

            @pl.when((px >= 0) & (px < nx) & (py >= 0) & (py < ny))
            def _():
                send_ref[px * ny + py] = block


def product_kernel(
    nx, ny, recv_ref, node_ref, slope_ref, sq_ref, expand_ref, wyt_ref, left_ref, wy_ref,
    grad_ref, hess_ref, send_ref, msc, gsc,
):
    gx, gy = lax.axis_index("gx"), lax.axis_index("gy")
    own = gx * ny + gy
    lane = lax.broadcasted_iota(jnp.int32, (8, 128), 1)
    sub = lax.broadcasted_iota(jnp.int32, (8, 128), 0)

    def block(dx, dy):
        px, py = gx + dx, gy + dy
        there = (px >= 0) & (px < nx) & (py >= 0) & (py < ny)
        return recv_ref[jnp.where(there, px * ny + py, own)]

    def column(x, at):
        return jnp.broadcast_to(x[:, at : at + 1], (8, 128))

    def with_corners(dx):
        mid = face_of(block(dx, 0))
        mid = mid + jnp.where(lane == 0, column(face_of(block(dx, -1)), 16), 0.0)
        return mid + jnp.where(lane == 16, column(face_of(block(dx, 1)), 0), 0.0)

    keep_x = jnp.where(gx == nx - 1, 0.0, 1.0).astype(F32)
    keep_y = jnp.where(gy == ny - 1, 0.0, 1.0).astype(F32)
    keep_lane = jnp.where(lane == 16, keep_y, 1.0)
    row_low = with_corners(-1)
    row_high = with_corners(1)
    col_low, edge_low = column_of(block(0, -1))
    col_high, edge_high = column_of(block(0, 1))
    grads = []
    square = jnp.zeros((8, 128), F32)
    for kc in range(6):
        g = node_ref[kc * 8 : kc * 8 + 8]
        g = g + jnp.where(sub == 0, jnp.broadcast_to(row_low[kc : kc + 1], (8, 128)), 0.0)
        g = g + jnp.where(lane == 0, column(col_low, kc), 0.0)
        g = g + jnp.where(lane == 16, column(col_high, kc), 0.0)
        g = g * keep_lane
        grads.append(g)
        grad_ref[kc] = g
        own_g = jnp.where(lane < 16, g, 0.0)
        square = square + own_g * own_g
    face = node_ref[48:56] + row_high
    face = face + jnp.where(lane == 0, column(edge_low, 0), 0.0)
    face = face + jnp.where(lane == 16, column(edge_high, 0), 0.0)
    face = jnp.where(sub < 6, face * keep_lane * keep_x, 0.0)
    full = jnp.concatenate(grads + [face, jnp.zeros((8, 128), F32)], axis=0)
    moved = dot_right(expand_ref[...], dot_left(full, wyt_ref[...]))
    msc[...] = moved.reshape(6, 8, 8, 128)

    def apply(cx, curve):
        m0 = [msc[2 * k, cx] for k in range(3)]
        dm = [msc[2 * k + 1, cx] - m0[k] for k in range(3)]
        total = [None] * 3
        upper = [None] * 3
        for z in range(8):
            sz = (z + 0.5) / 8.0
            s = [slope_ref[k, z, cx] for k in range(3)]
            along = s[0] * (m0[0] + sz * dm[0])
            for k in (1, 2):
                along = along + s[k] * (m0[k] + sz * dm[k])
            curve = curve + along * along
            for k in range(3):
                w = s[k] * along
                u = w * sz
                total[k] = w if z == 0 else total[k] + w
                upper[k] = u if z == 0 else upper[k] + u
        for k in range(3):
            gsc[2 * k, cx] = total[k] - upper[k]
            gsc[2 * k + 1, cx] = upper[k]
        return curve

    curve = lax.fori_loop(0, 8, apply, jnp.zeros((8, 128), F32))
    nodes = dot_left(dot_right(left_ref[...], gsc[...].reshape(384, 128)), wy_ref[...])
    rows = [nodes[kc * 8 : kc * 8 + 8] for kc in range(6)]
    for kc in range(6):
        hess_ref[kc] = rows[kc]
    col_high = column_row(rows, nodes[48:56], 16)
    high = face_row(nodes[48:56])
    spot = lane[:1]
    sums = jnp.where(spot == 104, jnp.sum(sq_ref[...]), 0.0)
    sums = jnp.where(spot == 105, jnp.sum(square), sums)
    sums = jnp.where(spot == 106, jnp.sum(curve) * (1.0 / 512.0), sums)
    tail = spot >= 104
    send_ref[...] = jnp.broadcast_to(sums[None], send_ref.shape)
    for dx, dy, data in ((1, 0, high), (1, 1, high), (0, 1, col_high)):
        px, py = gx + dx, gy + dy

        @pl.when((px < nx) & (py < ny))
        def _():
            send_ref[px * ny + py] = jnp.where(tail, sums, data)


def finish_kernel(nx, ny, voxels, recv_ref, grad_ref, hess_ref, step_ref, prod_ref, misfit_ref):
    gx, gy = lax.axis_index("gx"), lax.axis_index("gy")
    own = gx * ny + gy
    lane = lax.broadcasted_iota(jnp.int32, (8, 128), 1)
    sub = lax.broadcasted_iota(jnp.int32, (8, 128), 0)

    def block(dx, dy):
        px, py = gx + dx, gy + dy
        there = (px >= 0) & (py >= 0)
        data = recv_ref[jnp.where(there, px * ny + py, own)]
        return jnp.where(there, data, 0.0)

    def column(x, at):
        return jnp.broadcast_to(x[:, at : at + 1], (8, 128))

    total = jnp.sum(recv_ref[...], axis=0)
    misfit_ref[...] = total[:, 104:105] * (1.0 / voxels)
    total = jnp.broadcast_to(total, (8, 128))
    alpha = column(total, 105) / column(total, 106)
    row_low = face_of(block(-1, 0)) + jnp.where(lane == 0, column(face_of(block(-1, -1)), 16), 0.0)
    col_low = column_of(block(0, -1))[0]
    for kc in range(6):
        h = hess_ref[kc]
        h = h + jnp.where(sub == 0, jnp.broadcast_to(row_low[kc : kc + 1], (8, 128)), 0.0)
        h = h + jnp.where(lane == 0, column(col_low, kc), 0.0)
        prod_ref[kc // 2, kc % 2] = h[:, :16]
        step_ref[kc // 2, kc % 2] = (alpha * grad_ref[kc])[:, :16]


def swaps(count, first):
    pairs = [(i, i + 1) for i in range(first, count - 1, 2)]
    return pairs + [(j, i) for i, j in pairs]


def on_device(ref_image, def_image, shift_xy, shift_z, frac, connectivity):
    nx, ny = lax.axis_size("gx"), lax.axis_size("gy")
    peers = nx * ny
    sds = jax.ShapeDtypeStruct
    xa = lax.ppermute(def_image, "gx", swaps(nx, 0))
    xb = lax.ppermute(def_image, "gx", swaps(nx, 1))
    half = sds((4, 64, 128), BF16)
    to_a, to_b = pl.pallas_call(
        pack_own_kernel,
        out_shape=(half, half),
        in_specs=[VMEM],
        out_specs=(VMEM, VMEM),
        compiler_params=PARAMS,
        cost_estimate=pl.CostEstimate(flops=300000, bytes_accessed=262144, transcendentals=0),
        name="pack_own_halo",
    )(def_image)
    ya = lax.ppermute(to_a, "gy", swaps(ny, 0))
    yb = lax.ppermute(to_b, "gy", swaps(ny, 1))
    corner = sds((4, 128, 128), BF16)
    to_a, to_b = pl.pallas_call(
        pack_corner_kernel,
        out_shape=(corner, corner),
        in_specs=[VMEM] * 2,
        out_specs=(VMEM, VMEM),
        compiler_params=PARAMS,
        cost_estimate=pl.CostEstimate(flops=300000, bytes_accessed=524288, transcendentals=0),
        name="pack_corner_halo",
    )(xa, xb)
    ca = lax.ppermute(to_a, "gy", swaps(ny, 0))
    cb = lax.ppermute(to_b, "gy", swaps(ny, 1))

    first = connectivity[0]
    col_x = first // 17 % 9
    col_y = first % 17
    start_x = 8 * col_x + shift_xy[0] + HALO
    start_y = 8 * col_y + shift_xy[1] + HALO
    tile = jnp.minimum(start_y // 64, 2)
    base = tile * TILE_ROWS + (shift_z + 2) * SPAN + start_x
    shift = (8 * col_y - (start_y - 64 * tile)) & 127
    place = (col_y & 1) * 8 + col_x
    idx = jnp.stack([base, shift, place, 8 * col_y])

    left, wy, expand, wyt = tables()
    residual, slopes, nodes, send, square = pl.pallas_call(
        lambda *refs: sample_kernel(nx, ny, *refs),
        out_shape=(
            sds((8, 64, 128), BF16),
            sds((3, 8, 8, 8, 128), F32),
            sds((64, 128), F32),
            sds((peers, 1, 128), F32),
            sds((8, 128), F32),
        ),
        in_specs=[SMEM, SMEM] + [VMEM] * 10,
        out_specs=(VMEM,) * 5,
        scratch_shapes=[
            pltpu.VMEM((3 * TILE_ROWS, 128), F32),
            pltpu.VMEM((16, 18, 8, 128), F32),
            pltpu.VMEM((3, 8, 8, 128), F32),
            pltpu.VMEM((8, 8, 8, 128), F32),
            pltpu.VMEM((6, 8, 8, 128), F32),
        ],
        compiler_params=PARAMS,
        name="sample_and_gradient",
    )(idx, frac, xa, def_image, xb, ya, yb, ca, cb, ref_image, left, wy)
    recv = lax.all_to_all(send, ("gx", "gy"), 0, 0, tiled=True)
    grads, hess, send = pl.pallas_call(
        lambda *refs: product_kernel(nx, ny, *refs),
        out_shape=(sds((6, 8, 128), F32), sds((6, 8, 128), F32), sds((peers, 1, 128), F32)),
        in_specs=[VMEM] * 8,
        out_specs=(VMEM,) * 3,
        scratch_shapes=[pltpu.VMEM((6, 8, 8, 128), F32), pltpu.VMEM((6, 8, 8, 128), F32)],
        compiler_params=PARAMS,
        name="gauss_newton_product",
    )(recv, nodes, slopes, square, expand, wyt, left, wy)
    recv = lax.all_to_all(send, ("gx", "gy"), 0, 0, tiled=True)
    voxels = 8 * 64 * 128 * peers
    step, product, misfit = pl.pallas_call(
        lambda *refs: finish_kernel(nx, ny, voxels, *refs),
        out_shape=(sds((3, 2, 8, 16), F32), sds((3, 2, 8, 16), F32), sds((1, 1), F32)),
        in_specs=[VMEM] * 3,
        out_specs=(VMEM,) * 3,
        compiler_params=PARAMS,
        name="finish",
    )(recv, grads, hess)
    return (residual, step, product, misfit[0, 0])


def solution(mesh):
    in_specs = (
        P(None, "gx", "gy"),
        P(None, "gx", "gy"),
        P(None, ("gx", "gy")),
        P(("gx", "gy")),
        P(None, ("gx", "gy")),
        P(None, ("gx", "gy")),
    )
    out_specs = (P(None, "gx", "gy"), P(None, None, "gx", "gy"), P(None, None, "gx", "gy"), P())
    return jax.shard_map(
        on_device, mesh=mesh, in_specs=in_specs, out_specs=out_specs, check_vma=False
    )
```

```python
import jax
import jax.numpy as jnp
import numpy as np
from jax import lax
from jax.experimental import pallas as pl
from jax.experimental.pallas import tpu as pltpu
from jax.sharding import PartitionSpec as P

HALO = 64
F32 = jnp.float32
BF16 = jnp.bfloat16
SPAN = 192
TILE_ROWS = 12 * SPAN
CHUNK = 16
VMEM = pl.BlockSpec(memory_space=pltpu.VMEM)
SMEM = pl.BlockSpec(memory_space=pltpu.SMEM)
PARAMS = pltpu.CompilerParams(vmem_limit_bytes=24 * 1024 * 1024)


def node_weights(count):
    w = np.zeros((count + 1, 8 * count), np.float32)
    for v in range(8 * count):
        s = (v % 8 + 0.5) / 8.0
        w[v // 8, v] = 1.0 - s
        w[v // 8 + 1, v] = s
    return w


def tables():
    wx = node_weights(8)
    left = np.zeros((64, 6, 64), np.float32)
    for kc in range(6):
        left[kc * 8 : kc * 8 + 8, kc] = wx[:8]
        left[48 + kc, kc] = wx[8]
        left[56 + kc, kc] = wx[0]
    left = left.reshape(64, 384)
    expand = left.T.copy()
    expand[:, 56:] = 0.0
    wy = np.zeros((128, 128), np.float32)
    wy[:, :17] = node_weights(16).T
    as_bf = lambda a: jnp.asarray(a, BF16)
    return as_bf(left / 512.0), as_bf(wy), as_bf(expand), as_bf(wy.T)


def split(x):
    hi = x.astype(BF16)
    return hi, (x - hi.astype(F32)).astype(BF16)


def dot(a, b):
    return jnp.dot(a, b, preferred_element_type=F32)


def dot_right(w, x):
    hi, lo = split(x)
    return dot(w, hi) + dot(w, lo)


def dot_left(x, w):
    hi, lo = split(x)
    return dot(hi, w) + dot(lo, w)


def pack_rows(src, dst_a, dst_b, at, even):
    left = lax.broadcasted_iota(jnp.int32, (64, 128), 1) < 64
    for p in range(4):
        a = src[p].astype(F32)
        c = src[p + 4].astype(F32)
        right = jnp.where(left, pltpu.roll(a, 64, 1), c)
        other = jnp.where(left, a, pltpu.roll(c, 64, 1))
        dst_a[p, pl.ds(at, 64)] = jnp.where(even, right, other).astype(BF16)
        dst_b[p, pl.ds(at, 64)] = jnp.where(even, other, right).astype(BF16)


def dot_rows(a, b):
    return lax.dot_general(a, b, (((1,), (1,)), ((), ())), preferred_element_type=F32)


def as_rows(rows):
    sub = lax.broadcasted_iota(jnp.int32, (8, 128), 0)
    out = jnp.zeros((8, 128), F32)
    for n, row in enumerate(rows):
        out = jnp.where(sub == n, jnp.broadcast_to(row.astype(F32), (8, 128)), out)
    return out


def prepare_kernel(*refs):
    sources, (b_ref, a_ref, idx_ref, wgt_ref), scratch, sems = refs[:5], refs[5:9], refs[9:14], refs[14]
    copies = [pltpu.make_async_copy(sources[n], scratch[n], sems.at[n]) for n in range(5)]
    for copy in copies:
        copy.start()
    for copy in copies:
        copy.wait()
    own_ref, conn_ref, xy_ref, z_ref, frac_ref = scratch
    pack_rows(own_ref, a_ref, b_ref, 0, lax.axis_index("gy") % 2 == 0)
    first = conn_ref[0:1]
    col_x = (first * 241) >> 12
    col_y = first - 17 * col_x
    start_x = 8 * col_x + xy_ref[0:1] + HALO
    start_y = 8 * col_y + xy_ref[1:2] + HALO
    early = (start_y >= 64) & (start_y < 184)
    below = start_y < 64
    offset = jnp.where(early, start_y - 64, jnp.where(below, start_y, start_y - 128))
    base = (z_ref[...] + 2) * SPAN + start_x
    tile = jnp.where(early | below, 0, TILE_ROWS)
    shift = (8 * col_y - offset) & 127
    place = (col_y & 1) * 8 + col_x
    width = jnp.where(early, 0, 9)
    flag = early.astype(F32)
    row = lax.broadcasted_iota(jnp.int32, (128, 128), 0)
    lane = lax.broadcasted_iota(jnp.int32, (128, 128), 1)
    upto = dot(as_rows([flag]).astype(BF16), (row <= lane).astype(F32).astype(BF16))[0:1]
    count = jnp.sum(flag, axis=1, keepdims=True)
    rank = jnp.where(early, upto - 1.0, count + lane[0:1].astype(F32) - upto)
    order = (jnp.broadcast_to(rank, (128, 128)) == row.astype(F32)).astype(F32).astype(BF16)
    hi, lo = split(as_rows([base, shift, place, 8 * col_y, tile, width]))
    table = dot_rows(hi, order) + dot_rows(lo, order)
    sub = lax.broadcasted_iota(jnp.int32, (8, 128), 0)
    table = jnp.where(sub == 6, jnp.broadcast_to(count, (8, 128)), table)
    idx_ref[...] = table.astype(jnp.int32)
    value = as_rows([frac_ref[c : c + 1] for c in range(3)])
    hi, lo = split(value)
    rest = (value - hi.astype(F32) - lo.astype(F32)).astype(BF16)
    element = jnp.broadcast_to(col_x * 16 + col_y, (128, 128))
    for cx in range(8):
        spread = (element == cx * 16 + (row >> 3)).astype(F32).astype(BF16)
        wgt_ref[cx] = dot_rows(hi, spread) + dot_rows(lo, spread) + dot_rows(rest, spread)


def pack_corner_kernel(xa_ref, xb_ref, own_b_ref, own_a_ref, b_ref, a_ref):
    even = lax.axis_index("gy") % 2 == 0
    pack_rows(xa_ref, a_ref, b_ref, 0, even)
    pack_rows(xb_ref, a_ref, b_ref, 64, even)


def over_sublanes(x):
    return jnp.sum(x, axis=0, keepdims=True)


def lanes_of(x, idx):
    return jnp.take_along_axis(x, idx & 127, axis=1, mode="promise_in_bounds")


def face_row(face):
    return over_sublanes(pltpu.roll(face, 0, 1, stride=17, stride_axis=0))


def face_of(row):
    lane = lax.broadcasted_iota(jnp.int32, (8, 128), 1)
    sub = lax.broadcasted_iota(jnp.int32, (8, 128), 0)
    back = lanes_of(jnp.broadcast_to(row, (8, 128)), lane + 17 * sub)
    return jnp.where((lane < 17) & (sub < 6), back, 0.0)


def column_row(rows, face, at):
    lane = lax.broadcasted_iota(jnp.int32, (8, 128), 1)
    block = jnp.zeros((8, 128), F32)
    for kc in range(6):
        block = jnp.where(lane == kc, jnp.broadcast_to(rows[kc][:, at : at + 1], (8, 128)), block)
    edge = jnp.where(lane == 64, jnp.broadcast_to(face[:, at : at + 1], (8, 128)), 0.0)
    block = pltpu.roll(block, 0, 1, stride=8, stride_axis=0)
    edge = pltpu.roll(edge, 0, 1, stride=1, stride_axis=0)
    return over_sublanes(block + edge)


def column_of(row):
    lane = lax.broadcasted_iota(jnp.int32, (8, 128), 1)
    sub = lax.broadcasted_iota(jnp.int32, (8, 128), 0)
    row = jnp.broadcast_to(row, (8, 128))
    return lanes_of(row, lane + 8 * sub), lanes_of(row, lane + 64 + sub)


def place_of_a():
    return pl.multiple_of(jnp.where(lax.axis_index("gx") % 2 == 1, 0, 128), 64)


def clear_outside(img, tiles):
    zero = jnp.zeros((2 * SPAN, 128), F32)
    for k in range(tiles):
        img[pl.ds(k * TILE_ROWS, 2 * SPAN)] = zero
        img[pl.ds(k * TILE_ROWS + 10 * SPAN, 2 * SPAN)] = zero


def sample_element(img, arr, base, shift, place, first, width):
    lane = lax.broadcasted_iota(jnp.int32, (8, 128), 1)
    mask = ((lane - first) & 127) < width
    for z in range(9):
        for q in range(2):
            v = img[pl.ds(base + (z * SPAN + q), 8), :]
            pltpu.store(arr.at[place, z * 2 + q], pltpu.roll(v, shift, 1), mask=mask)


def early_kernel(idx_ref, xa_ref, own_ref, xb_ref, arr_ref, img):
    clear_outside(img, 1)
    at_a = place_of_a()
    for z in range(8):
        for ref, row in ((xa_ref, at_a), (own_ref, 64), (xb_ref, 128 - at_a)):
            img[pl.ds(pl.multiple_of((z + 2) * SPAN + row, 8), 64)] = ref[z].astype(F32)

    def chunk(n, carry):
        for m in range(CHUNK):
            e = n * CHUNK + m
            sample_element(
                img, arr_ref, idx_ref[0, e], idx_ref[1, e], idx_ref[2, e], idx_ref[3, e], 9
            )
        return carry

    lax.fori_loop(0, (idx_ref[6, 0] + (CHUNK - 1)) // CHUNK, chunk, 0)


def late_kernel(
    nx, ny, idx_ref, wgt, xa_ref, own_ref, xb_ref, yb_ref, ya_ref, cb_ref, ca_ref, arr_ref, ref_ref,
    left_ref, wy_ref, res_ref, slope_ref, node_ref, send_ref, sq_ref, img, arr, rsc, gsc,
):
    half = lax.broadcasted_iota(jnp.int32, (64, 128), 1) < 64
    clear_outside(img, 2)
    odd_y = lax.axis_index("gy") % 2 == 1
    at_a = place_of_a()
    segments = (
        (xa_ref, ca_ref, cb_ref, 0, at_a),
        (own_ref, ya_ref, yb_ref, 0, 64),
        (xb_ref, ca_ref, cb_ref, 64, 128 - at_a),
    )
    for p in range(4):
        for ref, pair_a, pair_b, at, row in segments:
            ra = pltpu.roll(ref[p].astype(F32), 64, 1)
            rc = pltpu.roll(ref[p + 4].astype(F32), 64, 1)
            from_a = pair_a[p, pl.ds(at, 64)].astype(F32)
            from_b = pair_b[p, pl.ds(at, 64)].astype(F32)
            lo = jnp.where(odd_y, from_a, from_b)
            hi = jnp.where(odd_y, from_b, from_a)
            at_row = lambda k, q: pl.ds(pl.multiple_of(k * TILE_ROWS + (q + 2) * SPAN + row, 8), 64)
            img[at_row(0, p)] = jnp.where(half, lo, ra)
            img[at_row(1, p)] = jnp.where(half, ra, pltpu.roll(hi, 64, 1))
            img[at_row(0, p + 4)] = jnp.where(half, pltpu.roll(lo, 64, 1), rc)
            img[at_row(1, p + 4)] = jnp.where(half, rc, hi)
    for z in range(8):
        rsc[z] = ref_ref[z].astype(F32).reshape(8, 8, 128)
    arr[...] = arr_ref[...]

    def chunk(n, carry):
        for m in range(CHUNK):
            e = n * CHUNK + m
            base = idx_ref[0, e] + idx_ref[4, e]
            sample_element(
                img, arr, base, idx_ref[1, e], idx_ref[2, e], idx_ref[3, e], idx_ref[5, e]
            )
        return carry

    lax.fori_loop(idx_ref[6, 0] // CHUNK, 128 // CHUNK, chunk, 0)

    lane = lax.broadcasted_iota(jnp.int32, (8, 128), 1)
    phase = lane & 15
    even = phase < 8
    even_next = (phase >= 1) & (phase <= 8)

    def interpolate(cx, square):
        wz, wx, wy = (jnp.broadcast_to(wgt[cx, c : c + 1], (8, 128)) for c in range(3))

        def pair(z, q):
            ev = arr[cx, z * 2 + q]
            od = arr[cx + 8, z * 2 + q]
            near = jnp.where(even, ev, od)
            far = pltpu.roll(jnp.where(even_next, ev, od), 127, 1)
            return near, far

        total = [None] * 3
        upper = [None] * 3
        prev = [pair(0, 0), pair(0, 1)]
        for z in range(8):
            cur = [pair(z + 1, 0), pair(z + 1, 1)]
            low, dzx, dx = [], [], []
            for y in range(2):
                d0 = cur[0][y] - prev[0][y]
                d1 = cur[1][y] - prev[1][y]
                l0 = prev[0][y] + wz * d0
                l1 = prev[1][y] + wz * d1
                dx.append(l1 - l0)
                low.append(l0 + wx * dx[y])
                dzx.append(d0 + wx * (d1 - d0))
            prev = cur
            slope_y = low[1] - low[0]
            value = low[0] + wy * slope_y
            slope_z = dzx[0] + wy * (dzx[1] - dzx[0])
            slope_x = dx[0] + wy * (dx[1] - dx[0])
            r = rsc[z, cx] - value
            rsc[z, cx] = r
            square = square + r * r
            for k, s in enumerate((slope_z, slope_x, slope_y)):
                slope_ref[k, z, cx] = s
                w = s * r
                u = w * ((z + 0.5) / 8.0)
                total[k] = w if z == 0 else total[k] + w
                upper[k] = u if z == 0 else upper[k] + u
        for k in range(3):
            gsc[2 * k, cx] = total[k] - upper[k]
            gsc[2 * k + 1, cx] = upper[k]
        return square

    sq_ref[...] = lax.fori_loop(0, 8, interpolate, jnp.zeros((8, 128), F32))
    res_ref[...] = rsc[...].reshape(8, 64, 128).astype(BF16)
    nodes = dot_left(dot_right(left_ref[...], gsc[...].reshape(384, 128)), wy_ref[...])
    node_ref[...] = nodes
    rows = [nodes[kc * 8 : kc * 8 + 8] for kc in range(6)]
    high, low = nodes[48:56], nodes[56:64]
    col_high = column_row(rows, high, 16)
    col_low = column_row(rows, high, 0)
    high, low = face_row(high), face_row(low)
    gx, gy = lax.axis_index("gx"), lax.axis_index("gy")
    send_ref[...] = jnp.zeros(send_ref.shape, F32)
    for dx in (-1, 0, 1):
        for dy in (-1, 0, 1):
            if dx == 0 and dy == 0:
                continue
            block = high if dx == 1 else low if dx == -1 else col_high if dy == 1 else col_low
            px, py = gx + dx, gy + dy

            @pl.when((px >= 0) & (px < nx) & (py >= 0) & (py < ny))
            def _():
                send_ref[px * ny + py] = block


def product_kernel(
    nx, ny, recv_ref, node_ref, slope_ref, sq_ref, expand_ref, wyt_ref, left_ref, wy_ref,
    grad_ref, hess_ref, send_ref, msc, gsc,
):
    gx, gy = lax.axis_index("gx"), lax.axis_index("gy")
    own = gx * ny + gy
    lane = lax.broadcasted_iota(jnp.int32, (8, 128), 1)
    sub = lax.broadcasted_iota(jnp.int32, (8, 128), 0)

    def block(dx, dy):
        px, py = gx + dx, gy + dy
        there = (px >= 0) & (px < nx) & (py >= 0) & (py < ny)
        return recv_ref[jnp.where(there, px * ny + py, own)]

    def column(x, at):
        return jnp.broadcast_to(x[:, at : at + 1], (8, 128))

    def with_corners(dx):
        mid = face_of(block(dx, 0))
        mid = mid + jnp.where(lane == 0, column(face_of(block(dx, -1)), 16), 0.0)
        return mid + jnp.where(lane == 16, column(face_of(block(dx, 1)), 0), 0.0)

    keep_x = jnp.where(gx == nx - 1, 0.0, 1.0).astype(F32)
    keep_y = jnp.where(gy == ny - 1, 0.0, 1.0).astype(F32)
    keep_lane = jnp.where(lane == 16, keep_y, 1.0)
    row_low = with_corners(-1)
    row_high = with_corners(1)
    col_low, edge_low = column_of(block(0, -1))
    col_high, edge_high = column_of(block(0, 1))
    grads = []
    square = jnp.zeros((8, 128), F32)
    for kc in range(6):
        g = node_ref[kc * 8 : kc * 8 + 8]
        g = g + jnp.where(sub == 0, jnp.broadcast_to(row_low[kc : kc + 1], (8, 128)), 0.0)
        g = g + jnp.where(lane == 0, column(col_low, kc), 0.0)
        g = g + jnp.where(lane == 16, column(col_high, kc), 0.0)
        g = g * keep_lane
        grads.append(g)
        grad_ref[kc] = g
        own_g = jnp.where(lane < 16, g, 0.0)
        square = square + own_g * own_g
    face = node_ref[48:56] + row_high
    face = face + jnp.where(lane == 0, column(edge_low, 0), 0.0)
    face = face + jnp.where(lane == 16, column(edge_high, 0), 0.0)
    face = jnp.where(sub < 6, face * keep_lane * keep_x, 0.0)
    full = jnp.concatenate(grads + [face, jnp.zeros((8, 128), F32)], axis=0)
    moved = dot_right(expand_ref[...], dot_left(full, wyt_ref[...]))
    msc[...] = moved.reshape(6, 8, 8, 128)

    def apply(cx, curve):
        m0 = [msc[2 * k, cx] for k in range(3)]
        dm = [msc[2 * k + 1, cx] - m0[k] for k in range(3)]
        total = [None] * 3
        upper = [None] * 3
        for z in range(8):
            sz = (z + 0.5) / 8.0
            s = [slope_ref[k, z, cx] for k in range(3)]
            along = s[0] * (m0[0] + sz * dm[0])
            for k in (1, 2):
                along = along + s[k] * (m0[k] + sz * dm[k])
            curve = curve + along * along
            for k in range(3):
                w = s[k] * along
                u = w * sz
                total[k] = w if z == 0 else total[k] + w
                upper[k] = u if z == 0 else upper[k] + u
        for k in range(3):
            gsc[2 * k, cx] = total[k] - upper[k]
            gsc[2 * k + 1, cx] = upper[k]
        return curve

    curve = lax.fori_loop(0, 8, apply, jnp.zeros((8, 128), F32))
    nodes = dot_left(dot_right(left_ref[...], gsc[...].reshape(384, 128)), wy_ref[...])
    rows = [nodes[kc * 8 : kc * 8 + 8] for kc in range(6)]
    for kc in range(6):
        hess_ref[kc] = rows[kc]
    col_high = column_row(rows, nodes[48:56], 16)
    high = face_row(nodes[48:56])
    spot = lane[:1]
    sums = jnp.where(spot == 104, jnp.sum(sq_ref[...]), 0.0)
    sums = jnp.where(spot == 105, jnp.sum(square), sums)
    sums = jnp.where(spot == 106, jnp.sum(curve) * (1.0 / 512.0), sums)
    tail = spot >= 104
    send_ref[...] = jnp.broadcast_to(sums[None], send_ref.shape)
    for dx, dy, data in ((1, 0, high), (1, 1, high), (0, 1, col_high)):
        px, py = gx + dx, gy + dy

        @pl.when((px < nx) & (py < ny))
        def _():
            send_ref[px * ny + py] = jnp.where(tail, sums, data)


def finish_kernel(nx, ny, voxels, recv_ref, grad_ref, hess_ref, step_ref, prod_ref, misfit_ref):
    gx, gy = lax.axis_index("gx"), lax.axis_index("gy")
    own = gx * ny + gy
    lane = lax.broadcasted_iota(jnp.int32, (8, 128), 1)
    sub = lax.broadcasted_iota(jnp.int32, (8, 128), 0)

    def block(dx, dy):
        px, py = gx + dx, gy + dy
        there = (px >= 0) & (py >= 0)
        data = recv_ref[jnp.where(there, px * ny + py, own)]
        return jnp.where(there, data, 0.0)

    def column(x, at):
        return jnp.broadcast_to(x[:, at : at + 1], (8, 128))

    total = jnp.sum(recv_ref[...], axis=0)
    misfit_ref[...] = total[:, 104:105] * (1.0 / voxels)
    total = jnp.broadcast_to(total, (8, 128))
    alpha = column(total, 105) / column(total, 106)
    row_low = face_of(block(-1, 0)) + jnp.where(lane == 0, column(face_of(block(-1, -1)), 16), 0.0)
    col_low = column_of(block(0, -1))[0]
    for kc in range(6):
        h = hess_ref[kc]
        h = h + jnp.where(sub == 0, jnp.broadcast_to(row_low[kc : kc + 1], (8, 128)), 0.0)
        h = h + jnp.where(lane == 0, column(col_low, kc), 0.0)
        prod_ref[kc // 2, kc % 2] = h[:, :16]
        step_ref[kc // 2, kc % 2] = (alpha * grad_ref[kc])[:, :16]


def swaps(count, first):
    pairs = [(i, i + 1) for i in range(first, count - 1, 2)]
    return pairs + [(j, i) for i, j in pairs]


def on_device(ref_image, def_image, shift_xy, shift_z, frac, connectivity):
    nx, ny = lax.axis_size("gx"), lax.axis_size("gy")
    peers = nx * ny
    sds = jax.ShapeDtypeStruct
    xa = lax.ppermute(def_image, "gx", swaps(nx, 0))
    xb = lax.ppermute(def_image, "gx", swaps(nx, 1))
    half = sds((4, 64, 128), BF16)
    to_b, to_a, idx, wgt = pl.pallas_call(
        prepare_kernel,
        out_shape=(half, half, sds((8, 128), jnp.int32), sds((8, 8, 128), F32)),
        in_specs=[pl.BlockSpec(memory_space=pltpu.HBM)] * 5,
        out_specs=(VMEM,) * 4,
        scratch_shapes=[
            pltpu.VMEM((8, 64, 128), BF16),
            pltpu.VMEM((8, 128), jnp.int32),
            pltpu.VMEM((2, 128), jnp.int32),
            pltpu.VMEM((1, 128), jnp.int32),
            pltpu.VMEM((3, 128), F32),
            pltpu.SemaphoreType.DMA((5,)),
        ],
        compiler_params=PARAMS,
        cost_estimate=pl.CostEstimate(flops=300000, bytes_accessed=262144, transcendentals=0),
        name="prepare",
    )(def_image, connectivity, shift_xy, shift_z.reshape(1, 128), frac)
    yb = lax.ppermute(to_b, "gy", swaps(ny, 1))
    ya = lax.ppermute(to_a, "gy", swaps(ny, 0))
    corner = sds((4, 128, 128), BF16)
    corner_b, corner_a = pl.pallas_call(
        pack_corner_kernel,
        out_shape=(corner, corner),
        in_specs=[VMEM, VMEM] + [pl.BlockSpec(memory_space=pl.ANY)] * 2,
        out_specs=(VMEM, VMEM),
        compiler_params=PARAMS,
        cost_estimate=pl.CostEstimate(flops=300000, bytes_accessed=524288, transcendentals=0),
        name="pack_corner_halo",
    )(xa, xb, yb, ya)
    cb = lax.ppermute(corner_b, "gy", swaps(ny, 1))
    ca = lax.ppermute(corner_a, "gy", swaps(ny, 0))

    left, wy, expand, wyt = tables()
    arr = pl.pallas_call(
        early_kernel,
        out_shape=sds((16, 18, 8, 128), F32),
        in_specs=[SMEM] + [VMEM] * 3,
        out_specs=VMEM,
        scratch_shapes=[pltpu.VMEM((TILE_ROWS, 128), F32)],
        compiler_params=PARAMS,
        cost_estimate=pl.CostEstimate(flops=4000000, bytes_accessed=2000000, transcendentals=0),
        name="sample_early",
    )(idx, xa, def_image, xb)
    residual, slopes, nodes, send, square = pl.pallas_call(
        lambda *refs: late_kernel(nx, ny, *refs),
        out_shape=(
            sds((8, 64, 128), BF16),
            sds((3, 8, 8, 8, 128), F32),
            sds((64, 128), F32),
            sds((peers, 1, 128), F32),
            sds((8, 128), F32),
        ),
        in_specs=[SMEM] + [VMEM] * 12,
        out_specs=(VMEM,) * 5,
        scratch_shapes=[
            pltpu.VMEM((2 * TILE_ROWS, 128), F32),
            pltpu.VMEM((16, 18, 8, 128), F32),
            pltpu.VMEM((8, 8, 8, 128), F32),
            pltpu.VMEM((6, 8, 8, 128), F32),
        ],
        compiler_params=PARAMS,
        name="sample_and_gradient",
    )(idx, wgt, xa, def_image, xb, yb, ya, cb, ca, arr, ref_image, left, wy)
    recv = lax.all_to_all(send, ("gx", "gy"), 0, 0, tiled=True)
    grads, hess, send = pl.pallas_call(
        lambda *refs: product_kernel(nx, ny, *refs),
        out_shape=(sds((6, 8, 128), F32), sds((6, 8, 128), F32), sds((peers, 1, 128), F32)),
        in_specs=[VMEM] * 8,
        out_specs=(VMEM,) * 3,
        scratch_shapes=[pltpu.VMEM((6, 8, 8, 128), F32), pltpu.VMEM((6, 8, 8, 128), F32)],
        compiler_params=PARAMS,
        name="gauss_newton_product",
    )(recv, nodes, slopes, square, expand, wyt, left, wy)
    recv = lax.all_to_all(send, ("gx", "gy"), 0, 0, tiled=True)
    voxels = 8 * 64 * 128 * peers
    step, product, misfit = pl.pallas_call(
        lambda *refs: finish_kernel(nx, ny, voxels, *refs),
        out_shape=(sds((3, 2, 8, 16), F32), sds((3, 2, 8, 16), F32), sds((1, 1), F32)),
        in_specs=[VMEM] * 3,
        out_specs=(VMEM,) * 3,
        compiler_params=PARAMS,
        name="finish",
    )(recv, grads, hess)
    return (residual, step, product, misfit[0, 0])


def solution(mesh):
    in_specs = (
        P(None, "gx", "gy"),
        P(None, "gx", "gy"),
        P(None, ("gx", "gy")),
        P(("gx", "gy")),
        P(None, ("gx", "gy")),
        P(None, ("gx", "gy")),
    )
    out_specs = (P(None, "gx", "gy"), P(None, None, "gx", "gy"), P(None, None, "gx", "gy"), P())
    return jax.shard_map(
        on_device, mesh=mesh, in_specs=in_specs, out_specs=out_specs, check_vma=False
    )
```

```python
import jax
import jax.numpy as jnp
import numpy as np
from jax import lax
from jax.experimental import pallas as pl
from jax.experimental.pallas import tpu as pltpu
from jax.sharding import PartitionSpec as P

HALO = 64
F32 = jnp.float32
BF16 = jnp.bfloat16
SPAN = 192
TILE_ROWS = 12 * SPAN
CHUNK = 16
VMEM = pl.BlockSpec(memory_space=pltpu.VMEM)
SMEM = pl.BlockSpec(memory_space=pltpu.SMEM)
PARAMS = pltpu.CompilerParams(vmem_limit_bytes=24 * 1024 * 1024)


def node_weights(count):
    w = np.zeros((count + 1, 8 * count), np.float32)
    for v in range(8 * count):
        s = (v % 8 + 0.5) / 8.0
        w[v // 8, v] = 1.0 - s
        w[v // 8 + 1, v] = s
    return w


def tables():
    wx = node_weights(8)
    left = np.zeros((64, 6, 64), np.float32)
    for kc in range(6):
        left[kc * 8 : kc * 8 + 8, kc] = wx[:8]
        left[48 + kc, kc] = wx[8]
        left[56 + kc, kc] = wx[0]
    left = left.reshape(64, 384)
    expand = left.T.copy()
    expand[:, 56:] = 0.0
    wy = np.zeros((128, 128), np.float32)
    wy[:, :17] = node_weights(16).T
    as_bf = lambda a: jnp.asarray(a, BF16)
    return as_bf(left / 512.0), as_bf(wy), as_bf(expand), as_bf(wy.T)


def split(x):
    hi = x.astype(BF16)
    return hi, (x - hi.astype(F32)).astype(BF16)


def dot(a, b):
    return jnp.dot(a, b, preferred_element_type=F32)


def dot_right(w, x):
    hi, lo = split(x)
    return dot(w, hi) + dot(w, lo)


def dot_left(x, w):
    hi, lo = split(x)
    return dot(hi, w) + dot(lo, w)


def pack_rows(src, dst_a, dst_b, at, even):
    left = lax.broadcasted_iota(jnp.int32, (64, 128), 1) < 64
    for p in range(4):
        a = src[p].astype(F32)
        c = src[p + 4].astype(F32)
        right = jnp.where(left, pltpu.roll(a, 64, 1), c)
        other = jnp.where(left, a, pltpu.roll(c, 64, 1))
        dst_a[p, pl.ds(at, 64)] = jnp.where(even, right, other).astype(BF16)
        dst_b[p, pl.ds(at, 64)] = jnp.where(even, other, right).astype(BF16)


def dot_rows(a, b):
    return lax.dot_general(a, b, (((1,), (1,)), ((), ())), preferred_element_type=F32)


def as_rows(rows):
    sub = lax.broadcasted_iota(jnp.int32, (8, 128), 0)
    out = jnp.zeros((8, 128), F32)
    for n, row in enumerate(rows):
        out = jnp.where(sub == n, jnp.broadcast_to(row.astype(F32), (8, 128)), out)
    return out


def pack_own_kernel(own_ref, b_ref, a_ref, keep_ref):
    keep_ref[...] = own_ref[...]
    pack_rows(own_ref, a_ref, b_ref, 0, lax.axis_index("gy") % 2 == 0)


def index_kernel(row_ref, idx_ref, wgt_ref):
    first = row_ref[0:1].astype(jnp.int32)
    col_x = (first * 241) >> 12
    col_y = first - 17 * col_x
    start_x = 8 * col_x + row_ref[1:2].astype(jnp.int32) + HALO
    start_y = 8 * col_y + row_ref[2:3].astype(jnp.int32) + HALO
    early = (start_y >= 64) & (start_y < 184)
    below = start_y < 64
    offset = jnp.where(early, start_y - 64, jnp.where(below, start_y, start_y - 128))
    base = (row_ref[3:4].astype(jnp.int32) + 2) * SPAN + start_x
    tile = jnp.where(early | below, 0, TILE_ROWS)
    shift = (8 * col_y - offset) & 127
    place = (col_y & 1) * 8 + col_x
    width = jnp.where(early, 0, 9)
    flag = early.astype(F32)
    row = lax.broadcasted_iota(jnp.int32, (128, 128), 0)
    lane = lax.broadcasted_iota(jnp.int32, (128, 128), 1)
    upto = dot(as_rows([flag]).astype(BF16), (row <= lane).astype(F32).astype(BF16))[0:1]
    count = jnp.sum(flag, axis=1, keepdims=True)
    rank = jnp.where(early, upto - 1.0, count + lane[0:1].astype(F32) - upto)
    order = (jnp.broadcast_to(rank, (128, 128)) == row.astype(F32)).astype(F32).astype(BF16)
    hi, lo = split(as_rows([base, shift, place, 8 * col_y, tile, width]))
    table = dot_rows(hi, order) + dot_rows(lo, order)
    sub = lax.broadcasted_iota(jnp.int32, (8, 128), 0)
    table = jnp.where(sub == 6, jnp.broadcast_to(count, (8, 128)), table)
    idx_ref[...] = table.astype(jnp.int32)
    value = as_rows([row_ref[4 + c : 5 + c] for c in range(3)])
    hi, lo = split(value)
    rest = (value - hi.astype(F32) - lo.astype(F32)).astype(BF16)
    element = jnp.broadcast_to(col_x * 16 + col_y, (128, 128))
    for cx in range(8):
        spread = (element == cx * 16 + (row >> 3)).astype(F32).astype(BF16)
        wgt_ref[cx] = dot_rows(hi, spread) + dot_rows(lo, spread) + dot_rows(rest, spread)


def pack_corner_kernel(xa_ref, xb_ref, own_b_ref, own_a_ref, idx_ref, b_ref, a_ref):
    even = lax.axis_index("gy") % 2 == 0
    pack_rows(xa_ref, a_ref, b_ref, 0, even)
    pack_rows(xb_ref, a_ref, b_ref, 64, even)


def over_sublanes(x):
    return jnp.sum(x, axis=0, keepdims=True)


def lanes_of(x, idx):
    return jnp.take_along_axis(x, idx & 127, axis=1, mode="promise_in_bounds")


def face_row(face):
    return over_sublanes(pltpu.roll(face, 0, 1, stride=17, stride_axis=0))


def face_of(row):
    lane = lax.broadcasted_iota(jnp.int32, (8, 128), 1)
    sub = lax.broadcasted_iota(jnp.int32, (8, 128), 0)
    back = lanes_of(jnp.broadcast_to(row, (8, 128)), lane + 17 * sub)
    return jnp.where((lane < 17) & (sub < 6), back, 0.0)


def column_row(rows, face, at):
    lane = lax.broadcasted_iota(jnp.int32, (8, 128), 1)
    block = jnp.zeros((8, 128), F32)
    for kc in range(6):
        block = jnp.where(lane == kc, jnp.broadcast_to(rows[kc][:, at : at + 1], (8, 128)), block)
    edge = jnp.where(lane == 64, jnp.broadcast_to(face[:, at : at + 1], (8, 128)), 0.0)
    block = pltpu.roll(block, 0, 1, stride=8, stride_axis=0)
    edge = pltpu.roll(edge, 0, 1, stride=1, stride_axis=0)
    return over_sublanes(block + edge)


def column_of(row):
    lane = lax.broadcasted_iota(jnp.int32, (8, 128), 1)
    sub = lax.broadcasted_iota(jnp.int32, (8, 128), 0)
    row = jnp.broadcast_to(row, (8, 128))
    return lanes_of(row, lane + 8 * sub), lanes_of(row, lane + 64 + sub)


def place_of_a():
    return pl.multiple_of(jnp.where(lax.axis_index("gx") % 2 == 1, 0, 128), 64)


def clear_outside(img, tiles):
    zero = jnp.zeros((2 * SPAN, 128), F32)
    for k in range(tiles):
        img[pl.ds(k * TILE_ROWS, 2 * SPAN)] = zero
        img[pl.ds(k * TILE_ROWS + 10 * SPAN, 2 * SPAN)] = zero


def sample_element(img, arr, base, shift, place, first, width):
    lane = lax.broadcasted_iota(jnp.int32, (8, 128), 1)
    mask = ((lane - first) & 127) < width
    for z in range(9):
        for q in range(2):
            v = img[pl.ds(base + (z * SPAN + q), 8), :]
            pltpu.store(arr.at[place, z * 2 + q], pltpu.roll(v, shift, 1), mask=mask)


def early_kernel(idx_ref, xa_ref, own_ref, xb_ref, arr_ref, img):
    clear_outside(img, 1)
    at_a = place_of_a()
    for z in range(8):
        for ref, row in ((xa_ref, at_a), (own_ref, 64), (xb_ref, 128 - at_a)):
            img[pl.ds(pl.multiple_of((z + 2) * SPAN + row, 8), 64)] = ref[z].astype(F32)

    def chunk(n, carry):
        for m in range(CHUNK):
            e = n * CHUNK + m
            sample_element(
                img, arr_ref, idx_ref[0, e], idx_ref[1, e], idx_ref[2, e], idx_ref[3, e], 9
            )
        return carry

    lax.fori_loop(0, (idx_ref[6, 0] + (CHUNK - 1)) // CHUNK, chunk, 0)


def late_kernel(
    nx, ny, idx_ref, wgt, xa_ref, own_ref, xb_ref, yb_ref, ya_ref, cb_ref, ca_ref, arr_ref, ref_ref,
    left_ref, wy_ref, res_ref, slope_ref, node_ref, send_ref, sq_ref, img, arr, rsc, gsc,
):
    half = lax.broadcasted_iota(jnp.int32, (64, 128), 1) < 64
    clear_outside(img, 2)
    odd_y = lax.axis_index("gy") % 2 == 1
    at_a = place_of_a()
    segments = (
        (xa_ref, ca_ref, cb_ref, 0, at_a),
        (own_ref, ya_ref, yb_ref, 0, 64),
        (xb_ref, ca_ref, cb_ref, 64, 128 - at_a),
    )
    for p in range(4):
        for ref, pair_a, pair_b, at, row in segments:
            ra = pltpu.roll(ref[p].astype(F32), 64, 1)
            rc = pltpu.roll(ref[p + 4].astype(F32), 64, 1)
            from_a = pair_a[p, pl.ds(at, 64)].astype(F32)
            from_b = pair_b[p, pl.ds(at, 64)].astype(F32)
            lo = jnp.where(odd_y, from_a, from_b)
            hi = jnp.where(odd_y, from_b, from_a)
            at_row = lambda k, q: pl.ds(pl.multiple_of(k * TILE_ROWS + (q + 2) * SPAN + row, 8), 64)
            img[at_row(0, p)] = jnp.where(half, lo, ra)
            img[at_row(1, p)] = jnp.where(half, ra, pltpu.roll(hi, 64, 1))
            img[at_row(0, p + 4)] = jnp.where(half, pltpu.roll(lo, 64, 1), rc)
            img[at_row(1, p + 4)] = jnp.where(half, rc, hi)
    for z in range(8):
        rsc[z] = ref_ref[z].astype(F32).reshape(8, 8, 128)
    arr[...] = arr_ref[...]

    def chunk(n, carry):
        for m in range(CHUNK):
            e = n * CHUNK + m
            base = idx_ref[0, e] + idx_ref[4, e]
            sample_element(
                img, arr, base, idx_ref[1, e], idx_ref[2, e], idx_ref[3, e], idx_ref[5, e]
            )
        return carry

    lax.fori_loop(idx_ref[6, 0] // CHUNK, 128 // CHUNK, chunk, 0)

    lane = lax.broadcasted_iota(jnp.int32, (8, 128), 1)
    phase = lane & 15
    even = phase < 8
    even_next = (phase >= 1) & (phase <= 8)

    def interpolate(cx, square):
        wz, wx, wy = (jnp.broadcast_to(wgt[cx, c : c + 1], (8, 128)) for c in range(3))

        def pair(z, q):
            ev = arr[cx, z * 2 + q]
            od = arr[cx + 8, z * 2 + q]
            near = jnp.where(even, ev, od)
            far = pltpu.roll(jnp.where(even_next, ev, od), 127, 1)
            return near, far

        total = [None] * 3
        upper = [None] * 3
        prev = [pair(0, 0), pair(0, 1)]
        for z in range(8):
            cur = [pair(z + 1, 0), pair(z + 1, 1)]
            low, dzx, dx = [], [], []
            for y in range(2):
                d0 = cur[0][y] - prev[0][y]
                d1 = cur[1][y] - prev[1][y]
                l0 = prev[0][y] + wz * d0
                l1 = prev[1][y] + wz * d1
                dx.append(l1 - l0)
                low.append(l0 + wx * dx[y])
                dzx.append(d0 + wx * (d1 - d0))
            prev = cur
            slope_y = low[1] - low[0]
            value = low[0] + wy * slope_y
            slope_z = dzx[0] + wy * (dzx[1] - dzx[0])
            slope_x = dx[0] + wy * (dx[1] - dx[0])
            r = rsc[z, cx] - value
            rsc[z, cx] = r
            square = square + r * r
            for k, s in enumerate((slope_z, slope_x, slope_y)):
                slope_ref[k, z, cx] = s
                w = s * r
                u = w * ((z + 0.5) / 8.0)
                total[k] = w if z == 0 else total[k] + w
                upper[k] = u if z == 0 else upper[k] + u
        for k in range(3):
            gsc[2 * k, cx] = total[k] - upper[k]
            gsc[2 * k + 1, cx] = upper[k]
        return square

    sq_ref[...] = lax.fori_loop(0, 8, interpolate, jnp.zeros((8, 128), F32))
    res_ref[...] = rsc[...].reshape(8, 64, 128).astype(BF16)
    nodes = dot_left(dot_right(left_ref[...], gsc[...].reshape(384, 128)), wy_ref[...])
    node_ref[...] = nodes
    rows = [nodes[kc * 8 : kc * 8 + 8] for kc in range(6)]
    high, low = nodes[48:56], nodes[56:64]
    col_high = column_row(rows, high, 16)
    col_low = column_row(rows, high, 0)
    high, low = face_row(high), face_row(low)
    gx, gy = lax.axis_index("gx"), lax.axis_index("gy")
    send_ref[...] = jnp.zeros(send_ref.shape, F32)
    for dx in (-1, 0, 1):
        for dy in (-1, 0, 1):
            if dx == 0 and dy == 0:
                continue
            block = high if dx == 1 else low if dx == -1 else col_high if dy == 1 else col_low
            px, py = gx + dx, gy + dy

            @pl.when((px >= 0) & (px < nx) & (py >= 0) & (py < ny))
            def _():
                send_ref[px * ny + py] = block


def product_kernel(
    nx, ny, recv_ref, node_ref, slope_ref, sq_ref, expand_ref, wyt_ref, left_ref, wy_ref, res_ref,
    grad_ref, hess_ref, send_ref, out_ref, msc, gsc, sem,
):
    copy_out = pltpu.make_async_copy(res_ref, out_ref, sem)
    copy_out.start()
    gx, gy = lax.axis_index("gx"), lax.axis_index("gy")
    own = gx * ny + gy
    lane = lax.broadcasted_iota(jnp.int32, (8, 128), 1)
    sub = lax.broadcasted_iota(jnp.int32, (8, 128), 0)

    def block(dx, dy):
        px, py = gx + dx, gy + dy
        there = (px >= 0) & (px < nx) & (py >= 0) & (py < ny)
        return recv_ref[jnp.where(there, px * ny + py, own)]

    def column(x, at):
        return jnp.broadcast_to(x[:, at : at + 1], (8, 128))

    def with_corners(dx):
        mid = face_of(block(dx, 0))
        mid = mid + jnp.where(lane == 0, column(face_of(block(dx, -1)), 16), 0.0)
        return mid + jnp.where(lane == 16, column(face_of(block(dx, 1)), 0), 0.0)

    keep_x = jnp.where(gx == nx - 1, 0.0, 1.0).astype(F32)
    keep_y = jnp.where(gy == ny - 1, 0.0, 1.0).astype(F32)
    keep_lane = jnp.where(lane == 16, keep_y, 1.0)
    row_low = with_corners(-1)
    row_high = with_corners(1)
    col_low, edge_low = column_of(block(0, -1))
    col_high, edge_high = column_of(block(0, 1))
    grads = []
    square = jnp.zeros((8, 128), F32)
    for kc in range(6):
        g = node_ref[kc * 8 : kc * 8 + 8]
        g = g + jnp.where(sub == 0, jnp.broadcast_to(row_low[kc : kc + 1], (8, 128)), 0.0)
        g = g + jnp.where(lane == 0, column(col_low, kc), 0.0)
        g = g + jnp.where(lane == 16, column(col_high, kc), 0.0)
        g = g * keep_lane
        grads.append(g)
        grad_ref[kc] = g
        own_g = jnp.where(lane < 16, g, 0.0)
        square = square + own_g * own_g
    face = node_ref[48:56] + row_high
    face = face + jnp.where(lane == 0, column(edge_low, 0), 0.0)
    face = face + jnp.where(lane == 16, column(edge_high, 0), 0.0)
    face = jnp.where(sub < 6, face * keep_lane * keep_x, 0.0)
    full = jnp.concatenate(grads + [face, jnp.zeros((8, 128), F32)], axis=0)
    moved = dot_right(expand_ref[...], dot_left(full, wyt_ref[...]))
    msc[...] = moved.reshape(6, 8, 8, 128)

    def apply(cx, curve):
        m0 = [msc[2 * k, cx] for k in range(3)]
        dm = [msc[2 * k + 1, cx] - m0[k] for k in range(3)]
        total = [None] * 3
        upper = [None] * 3
        for z in range(8):
            sz = (z + 0.5) / 8.0
            s = [slope_ref[k, z, cx] for k in range(3)]
            along = s[0] * (m0[0] + sz * dm[0])
            for k in (1, 2):
                along = along + s[k] * (m0[k] + sz * dm[k])
            curve = curve + along * along
            for k in range(3):
                w = s[k] * along
                u = w * sz
                total[k] = w if z == 0 else total[k] + w
                upper[k] = u if z == 0 else upper[k] + u
        for k in range(3):
            gsc[2 * k, cx] = total[k] - upper[k]
            gsc[2 * k + 1, cx] = upper[k]
        return curve

    curve = lax.fori_loop(0, 8, apply, jnp.zeros((8, 128), F32))
    nodes = dot_left(dot_right(left_ref[...], gsc[...].reshape(384, 128)), wy_ref[...])
    rows = [nodes[kc * 8 : kc * 8 + 8] for kc in range(6)]
    for kc in range(6):
        hess_ref[kc] = rows[kc]
    col_high = column_row(rows, nodes[48:56], 16)
    high = face_row(nodes[48:56])
    spot = lane[:1]
    sums = jnp.where(spot == 104, jnp.sum(sq_ref[...]), 0.0)
    sums = jnp.where(spot == 105, jnp.sum(square), sums)
    sums = jnp.where(spot == 106, jnp.sum(curve) * (1.0 / 512.0), sums)
    tail = spot >= 104
    send_ref[...] = jnp.broadcast_to(sums[None], send_ref.shape)
    for dx, dy, data in ((1, 0, high), (1, 1, high), (0, 1, col_high)):
        px, py = gx + dx, gy + dy

        @pl.when((px < nx) & (py < ny))
        def _():
            send_ref[px * ny + py] = jnp.where(tail, sums, data)

    copy_out.wait()


def finish_kernel(nx, ny, voxels, recv_ref, grad_ref, hess_ref, step_ref, prod_ref, misfit_ref):
    gx, gy = lax.axis_index("gx"), lax.axis_index("gy")
    own = gx * ny + gy
    lane = lax.broadcasted_iota(jnp.int32, (8, 128), 1)
    sub = lax.broadcasted_iota(jnp.int32, (8, 128), 0)

    def block(dx, dy):
        px, py = gx + dx, gy + dy
        there = (px >= 0) & (py >= 0)
        data = recv_ref[jnp.where(there, px * ny + py, own)]
        return jnp.where(there, data, 0.0)

    def column(x, at):
        return jnp.broadcast_to(x[:, at : at + 1], (8, 128))

    total = jnp.sum(recv_ref[...], axis=0)
    misfit_ref[...] = total[:, 104:105] * (1.0 / voxels)
    total = jnp.broadcast_to(total, (8, 128))
    alpha = column(total, 105) / column(total, 106)
    row_low = face_of(block(-1, 0)) + jnp.where(lane == 0, column(face_of(block(-1, -1)), 16), 0.0)
    col_low = column_of(block(0, -1))[0]
    for kc in range(6):
        h = hess_ref[kc]
        h = h + jnp.where(sub == 0, jnp.broadcast_to(row_low[kc : kc + 1], (8, 128)), 0.0)
        h = h + jnp.where(lane == 0, column(col_low, kc), 0.0)
        prod_ref[kc // 2, kc % 2] = h[:, :16]
        step_ref[kc // 2, kc % 2] = (alpha * grad_ref[kc])[:, :16]


def swaps(count, first):
    pairs = [(i, i + 1) for i in range(first, count - 1, 2)]
    return pairs + [(j, i) for i, j in pairs]


def on_device(ref_image, def_image, shift_xy, shift_z, frac, connectivity):
    nx, ny = lax.axis_size("gx"), lax.axis_size("gy")
    peers = nx * ny
    sds = jax.ShapeDtypeStruct
    xa = lax.ppermute(def_image, "gx", swaps(nx, 0))
    xb = lax.ppermute(def_image, "gx", swaps(nx, 1))
    half = sds((4, 64, 128), BF16)
    to_b, to_a, own = pl.pallas_call(
        pack_own_kernel,
        out_shape=(half, half, sds((8, 64, 128), BF16)),
        in_specs=[VMEM],
        out_specs=(VMEM,) * 3,
        compiler_params=PARAMS,
        cost_estimate=pl.CostEstimate(flops=300000, bytes_accessed=262144, transcendentals=0),
        name="pack_own_halo",
    )(def_image)
    yb = lax.ppermute(to_b, "gy", swaps(ny, 1))
    ya = lax.ppermute(to_a, "gy", swaps(ny, 0))
    table = [connectivity[:1], shift_xy, shift_z[None]]
    table = [row.astype(F32) for row in table] + [frac, jnp.zeros((1, 128), F32)]
    idx, wgt = pl.pallas_call(
        index_kernel,
        out_shape=(sds((8, 128), jnp.int32), sds((8, 8, 128), F32)),
        in_specs=[VMEM],
        out_specs=(VMEM, VMEM),
        compiler_params=PARAMS,
        cost_estimate=pl.CostEstimate(flops=300000, bytes_accessed=262144, transcendentals=0),
        name="order_elements",
    )(jnp.concatenate(table))
    corner = sds((4, 128, 128), BF16)
    corner_b, corner_a = pl.pallas_call(
        pack_corner_kernel,
        out_shape=(corner, corner),
        in_specs=[VMEM, VMEM] + [pl.BlockSpec(memory_space=pl.ANY)] * 3,
        out_specs=(VMEM, VMEM),
        compiler_params=PARAMS,
        cost_estimate=pl.CostEstimate(flops=300000, bytes_accessed=524288, transcendentals=0),
        name="pack_corner_halo",
    )(xa, xb, yb, ya, idx)
    cb = lax.ppermute(corner_b, "gy", swaps(ny, 1))
    ca = lax.ppermute(corner_a, "gy", swaps(ny, 0))

    left, wy, expand, wyt = tables()
    arr = pl.pallas_call(
        early_kernel,
        out_shape=sds((16, 18, 8, 128), F32),
        in_specs=[SMEM] + [VMEM] * 3,
        out_specs=VMEM,
        scratch_shapes=[pltpu.VMEM((TILE_ROWS, 128), F32)],
        compiler_params=PARAMS,
        cost_estimate=pl.CostEstimate(flops=4000000, bytes_accessed=2000000, transcendentals=0),
        name="sample_early",
    )(idx, xa, own, xb)
    residual, slopes, nodes, send, square = pl.pallas_call(
        lambda *refs: late_kernel(nx, ny, *refs),
        out_shape=(
            sds((8, 64, 128), BF16),
            sds((3, 8, 8, 8, 128), F32),
            sds((64, 128), F32),
            sds((peers, 1, 128), F32),
            sds((8, 128), F32),
        ),
        in_specs=[SMEM] + [VMEM] * 12,
        out_specs=(VMEM,) * 5,
        scratch_shapes=[
            pltpu.VMEM((2 * TILE_ROWS, 128), F32),
            pltpu.VMEM((16, 18, 8, 128), F32),
            pltpu.VMEM((8, 8, 8, 128), F32),
            pltpu.VMEM((6, 8, 8, 128), F32),
        ],
        compiler_params=PARAMS,
        name="sample_and_gradient",
    )(idx, wgt, xa, own, xb, yb, ya, cb, ca, arr, ref_image, left, wy)
    recv = lax.all_to_all(send, ("gx", "gy"), 0, 0, tiled=True)
    grads, hess, send, residual = pl.pallas_call(
        lambda *refs: product_kernel(nx, ny, *refs),
        out_shape=(
            sds((6, 8, 128), F32),
            sds((6, 8, 128), F32),
            sds((peers, 1, 128), F32),
            sds((8, 64, 128), BF16),
        ),
        in_specs=[VMEM] * 9,
        out_specs=(VMEM,) * 3 + (pl.BlockSpec(memory_space=pl.ANY),),
        scratch_shapes=[
            pltpu.VMEM((6, 8, 8, 128), F32),
            pltpu.VMEM((6, 8, 8, 128), F32),
            pltpu.SemaphoreType.DMA,
        ],
        compiler_params=PARAMS,
        name="gauss_newton_product",
    )(recv, nodes, slopes, square, expand, wyt, left, wy, residual)
    recv = lax.all_to_all(send, ("gx", "gy"), 0, 0, tiled=True)
    voxels = 8 * 64 * 128 * peers
    step, product, misfit = pl.pallas_call(
        lambda *refs: finish_kernel(nx, ny, voxels, *refs),
        out_shape=(sds((3, 2, 8, 16), F32), sds((3, 2, 8, 16), F32), sds((1, 1), F32)),
        in_specs=[VMEM] * 3,
        out_specs=(VMEM,) * 3,
        compiler_params=PARAMS,
        name="finish",
    )(recv, grads, hess)
    return (residual, step, product, misfit[0, 0])


def solution(mesh):
    in_specs = (
        P(None, "gx", "gy"),
        P(None, "gx", "gy"),
        P(None, ("gx", "gy")),
        P(("gx", "gy")),
        P(None, ("gx", "gy")),
        P(None, ("gx", "gy")),
    )
    out_specs = (P(None, "gx", "gy"), P(None, None, "gx", "gy"), P(None, None, "gx", "gy"), P())
    return jax.shard_map(
        on_device, mesh=mesh, in_specs=in_specs, out_specs=out_specs, check_vma=False
    )
```

```python
import jax
import jax.numpy as jnp
import numpy as np
from jax import lax
from jax.experimental import pallas as pl
from jax.experimental.pallas import tpu as pltpu
from jax.sharding import PartitionSpec as P

HALO = 64
F32 = jnp.float32
BF16 = jnp.bfloat16
SPAN = 192
TILE_ROWS = 12 * SPAN
CHUNK = 16
VMEM = pl.BlockSpec(memory_space=pltpu.VMEM)
SMEM = pl.BlockSpec(memory_space=pltpu.SMEM)
PARAMS = pltpu.CompilerParams(vmem_limit_bytes=24 * 1024 * 1024)


def node_weights(count):
    w = np.zeros((count + 1, 8 * count), np.float32)
    for v in range(8 * count):
        s = (v % 8 + 0.5) / 8.0
        w[v // 8, v] = 1.0 - s
        w[v // 8 + 1, v] = s
    return w


def tables():
    wx = node_weights(8)
    left = np.zeros((64, 6, 64), np.float32)
    for kc in range(6):
        left[kc * 8 : kc * 8 + 8, kc] = wx[:8]
        left[48 + kc, kc] = wx[8]
        left[56 + kc, kc] = wx[0]
    left = left.reshape(64, 384)
    expand = left.T.copy()
    expand[:, 56:] = 0.0
    wy = np.zeros((128, 128), np.float32)
    wy[:, :17] = node_weights(16).T
    as_bf = lambda a: jnp.asarray(a, BF16)
    return as_bf(left / 512.0), as_bf(wy), as_bf(expand), as_bf(wy.T)


def split(x):
    hi = x.astype(BF16)
    return hi, (x - hi.astype(F32)).astype(BF16)


def dot(a, b):
    return jnp.dot(a, b, preferred_element_type=F32)


def dot_right(w, x):
    hi, lo = split(x)
    return dot(w, hi) + dot(w, lo)


def dot_left(x, w):
    hi, lo = split(x)
    return dot(hi, w) + dot(lo, w)


def pack_rows(src, dst_a, dst_b, at, even):
    left = lax.broadcasted_iota(jnp.int32, (64, 128), 1) < 64
    for p in range(4):
        a = src[p].astype(F32)
        c = src[p + 4].astype(F32)
        right = jnp.where(left, pltpu.roll(a, 64, 1), c)
        other = jnp.where(left, a, pltpu.roll(c, 64, 1))
        dst_a[p, pl.ds(at, 64)] = jnp.where(even, right, other).astype(BF16)
        dst_b[p, pl.ds(at, 64)] = jnp.where(even, other, right).astype(BF16)


def dot_rows(a, b):
    return lax.dot_general(a, b, (((1,), (1,)), ((), ())), preferred_element_type=F32)


def as_rows(rows):
    sub = lax.broadcasted_iota(jnp.int32, (8, 128), 0)
    out = jnp.zeros((8, 128), F32)
    for n, row in enumerate(rows):
        out = jnp.where(sub == n, jnp.broadcast_to(row.astype(F32), (8, 128)), out)
    return out


def pack_own_kernel(own_ref, b_ref, a_ref, keep_ref):
    keep_ref[...] = own_ref[...]
    pack_rows(own_ref, a_ref, b_ref, 0, lax.axis_index("gy") % 2 == 0)


def index_kernel(row_ref, idx_ref, wgt_ref):
    first = row_ref[0:1].astype(jnp.int32)
    col_x = (first * 241) >> 12
    col_y = first - 17 * col_x
    start_x = 8 * col_x + row_ref[8:9].astype(jnp.int32) + HALO
    start_y = 8 * col_y + row_ref[9:10].astype(jnp.int32) + HALO
    early = (start_y >= 64) & (start_y < 184)
    below = start_y < 64
    offset = jnp.where(early, start_y - 64, jnp.where(below, start_y, start_y - 128))
    base = (row_ref[10:11].astype(jnp.int32) + 2) * SPAN + start_x
    tile = jnp.where(early | below, 0, TILE_ROWS)
    shift = (8 * col_y - offset) & 127
    place = (col_y & 1) * 8 + col_x
    width = jnp.where(early, 0, 9)
    flag = early.astype(F32)
    row = lax.broadcasted_iota(jnp.int32, (128, 128), 0)
    lane = lax.broadcasted_iota(jnp.int32, (128, 128), 1)
    upto = dot(as_rows([flag]).astype(BF16), (row <= lane).astype(F32).astype(BF16))[0:1]
    count = jnp.sum(flag, axis=1, keepdims=True)
    rank = jnp.where(early, upto - 1.0, count + lane[0:1].astype(F32) - upto)
    order = (jnp.broadcast_to(rank, (128, 128)) == row.astype(F32)).astype(F32).astype(BF16)
    hi, lo = split(as_rows([base, shift, place, 8 * col_y, tile, width]))
    table = dot_rows(hi, order) + dot_rows(lo, order)
    sub = lax.broadcasted_iota(jnp.int32, (8, 128), 0)
    table = jnp.where(sub == 6, jnp.broadcast_to(count, (8, 128)), table)
    idx_ref[...] = table.astype(jnp.int32)
    value = as_rows([row_ref[11 + c : 12 + c] for c in range(3)])
    hi, lo = split(value)
    rest = (value - hi.astype(F32) - lo.astype(F32)).astype(BF16)
    element = jnp.broadcast_to(col_x * 16 + col_y, (128, 128))
    for cx in range(8):
        spread = (element == cx * 16 + (row >> 3)).astype(F32).astype(BF16)
        wgt_ref[cx] = dot_rows(hi, spread) + dot_rows(lo, spread) + dot_rows(rest, spread)


def pack_corner_kernel(xa_ref, xb_ref, own_b_ref, own_a_ref, idx_ref, b_ref, a_ref):
    even = lax.axis_index("gy") % 2 == 0
    pack_rows(xa_ref, a_ref, b_ref, 0, even)
    pack_rows(xb_ref, a_ref, b_ref, 64, even)


def over_sublanes(x):
    return jnp.sum(x, axis=0, keepdims=True)


def lanes_of(x, idx):
    return jnp.take_along_axis(x, idx & 127, axis=1, mode="promise_in_bounds")


def face_row(face):
    return over_sublanes(pltpu.roll(face, 0, 1, stride=17, stride_axis=0))


def face_of(row):
    lane = lax.broadcasted_iota(jnp.int32, (8, 128), 1)
    sub = lax.broadcasted_iota(jnp.int32, (8, 128), 0)
    back = lanes_of(jnp.broadcast_to(row, (8, 128)), lane + 17 * sub)
    return jnp.where((lane < 17) & (sub < 6), back, 0.0)


def column_row(rows, face, at):
    lane = lax.broadcasted_iota(jnp.int32, (8, 128), 1)
    block = jnp.zeros((8, 128), F32)
    for kc in range(6):
        block = jnp.where(lane == kc, jnp.broadcast_to(rows[kc][:, at : at + 1], (8, 128)), block)
    edge = jnp.where(lane == 64, jnp.broadcast_to(face[:, at : at + 1], (8, 128)), 0.0)
    block = pltpu.roll(block, 0, 1, stride=8, stride_axis=0)
    edge = pltpu.roll(edge, 0, 1, stride=1, stride_axis=0)
    return over_sublanes(block + edge)


def column_of(row):
    lane = lax.broadcasted_iota(jnp.int32, (8, 128), 1)
    sub = lax.broadcasted_iota(jnp.int32, (8, 128), 0)
    row = jnp.broadcast_to(row, (8, 128))
    return lanes_of(row, lane + 8 * sub), lanes_of(row, lane + 64 + sub)


def place_of_a():
    return pl.multiple_of(jnp.where(lax.axis_index("gx") % 2 == 1, 0, 128), 64)


def clear_outside(img, tiles):
    zero = jnp.zeros((2 * SPAN, 128), F32)
    for k in range(tiles):
        img[pl.ds(k * TILE_ROWS, 2 * SPAN)] = zero
        img[pl.ds(k * TILE_ROWS + 10 * SPAN, 2 * SPAN)] = zero


def sample_element(img, arr, base, shift, place, first, width):
    lane = lax.broadcasted_iota(jnp.int32, (8, 128), 1)
    mask = ((lane - first) & 127) < width
    for z in range(9):
        for q in range(2):
            v = img[pl.ds(base + (z * SPAN + q), 8), :]
            pltpu.store(arr.at[place, z * 2 + q], pltpu.roll(v, shift, 1), mask=mask)


def early_kernel(idx_ref, xa_ref, own_ref, xb_ref, arr_ref, img):
    clear_outside(img, 1)
    at_a = place_of_a()
    for z in range(8):
        for ref, row in ((xa_ref, at_a), (own_ref, 64), (xb_ref, 128 - at_a)):
            img[pl.ds(pl.multiple_of((z + 2) * SPAN + row, 8), 64)] = ref[z].astype(F32)

    def chunk(n, carry):
        for m in range(CHUNK):
            e = n * CHUNK + m
            sample_element(
                img, arr_ref, idx_ref[0, e], idx_ref[1, e], idx_ref[2, e], idx_ref[3, e], 9
            )
        return carry

    lax.fori_loop(0, (idx_ref[6, 0] + (CHUNK - 1)) // CHUNK, chunk, 0)


def late_kernel(
    nx, ny, idx_ref, wgt, xa_ref, own_ref, xb_ref, yb_ref, ya_ref, cb_ref, ca_ref, arr_ref, ref_ref,
    left_ref, wy_ref, res_ref, slope_ref, node_ref, send_ref, sq_ref, img, arr, rsc, gsc,
):
    half = lax.broadcasted_iota(jnp.int32, (64, 128), 1) < 64
    clear_outside(img, 2)
    odd_y = lax.axis_index("gy") % 2 == 1
    at_a = place_of_a()
    segments = (
        (xa_ref, ca_ref, cb_ref, 0, at_a),
        (own_ref, ya_ref, yb_ref, 0, 64),
        (xb_ref, ca_ref, cb_ref, 64, 128 - at_a),
    )
    for p in range(4):
        for ref, pair_a, pair_b, at, row in segments:
            ra = pltpu.roll(ref[p].astype(F32), 64, 1)
            rc = pltpu.roll(ref[p + 4].astype(F32), 64, 1)
            from_a = pair_a[p, pl.ds(at, 64)].astype(F32)
            from_b = pair_b[p, pl.ds(at, 64)].astype(F32)
            lo = jnp.where(odd_y, from_a, from_b)
            hi = jnp.where(odd_y, from_b, from_a)
            at_row = lambda k, q: pl.ds(pl.multiple_of(k * TILE_ROWS + (q + 2) * SPAN + row, 8), 64)
            img[at_row(0, p)] = jnp.where(half, lo, ra)
            img[at_row(1, p)] = jnp.where(half, ra, pltpu.roll(hi, 64, 1))
            img[at_row(0, p + 4)] = jnp.where(half, pltpu.roll(lo, 64, 1), rc)
            img[at_row(1, p + 4)] = jnp.where(half, rc, hi)
    for z in range(8):
        rsc[z] = ref_ref[z].astype(F32).reshape(8, 8, 128)
    arr[...] = arr_ref[...]

    def chunk(n, carry):
        for m in range(CHUNK):
            e = n * CHUNK + m
            base = idx_ref[0, e] + idx_ref[4, e]
            sample_element(
                img, arr, base, idx_ref[1, e], idx_ref[2, e], idx_ref[3, e], idx_ref[5, e]
            )
        return carry

    lax.fori_loop(idx_ref[6, 0] // CHUNK, 128 // CHUNK, chunk, 0)

    lane = lax.broadcasted_iota(jnp.int32, (8, 128), 1)
    phase = lane & 15
    even = phase < 8
    even_next = (phase >= 1) & (phase <= 8)

    def interpolate(cx, square):
        wz, wx, wy = (jnp.broadcast_to(wgt[cx, c : c + 1], (8, 128)) for c in range(3))

        def pair(z, q):
            ev = arr[cx, z * 2 + q]
            od = arr[cx + 8, z * 2 + q]
            near = jnp.where(even, ev, od)
            far = pltpu.roll(jnp.where(even_next, ev, od), 127, 1)
            return near, far

        total = [None] * 3
        upper = [None] * 3
        prev = [pair(0, 0), pair(0, 1)]
        for z in range(8):
            cur = [pair(z + 1, 0), pair(z + 1, 1)]
            low, dzx, dx = [], [], []
            for y in range(2):
                d0 = cur[0][y] - prev[0][y]
                d1 = cur[1][y] - prev[1][y]
                l0 = prev[0][y] + wz * d0
                l1 = prev[1][y] + wz * d1
                dx.append(l1 - l0)
                low.append(l0 + wx * dx[y])
                dzx.append(d0 + wx * (d1 - d0))
            prev = cur
            slope_y = low[1] - low[0]
            value = low[0] + wy * slope_y
            slope_z = dzx[0] + wy * (dzx[1] - dzx[0])
            slope_x = dx[0] + wy * (dx[1] - dx[0])
            r = rsc[z, cx] - value
            rsc[z, cx] = r
            square = square + r * r
            for k, s in enumerate((slope_z, slope_x, slope_y)):
                slope_ref[k, z, cx] = s
                w = s * r
                u = w * ((z + 0.5) / 8.0)
                total[k] = w if z == 0 else total[k] + w
                upper[k] = u if z == 0 else upper[k] + u
        for k in range(3):
            gsc[2 * k, cx] = total[k] - upper[k]
            gsc[2 * k + 1, cx] = upper[k]
        return square

    sq_ref[...] = lax.fori_loop(0, 8, interpolate, jnp.zeros((8, 128), F32), unroll=4)
    res_ref[...] = rsc[...].reshape(8, 64, 128).astype(BF16)
    nodes = dot_left(dot_right(left_ref[...], gsc[...].reshape(384, 128)), wy_ref[...])
    node_ref[...] = nodes
    rows = [nodes[kc * 8 : kc * 8 + 8] for kc in range(6)]
    high, low = nodes[48:56], nodes[56:64]
    col_high = column_row(rows, high, 16)
    col_low = column_row(rows, high, 0)
    high, low = face_row(high), face_row(low)
    gx, gy = lax.axis_index("gx"), lax.axis_index("gy")
    send_ref[...] = jnp.zeros(send_ref.shape, F32)
    for dx in (-1, 0, 1):
        for dy in (-1, 0, 1):
            if dx == 0 and dy == 0:
                continue
            block = high if dx == 1 else low if dx == -1 else col_high if dy == 1 else col_low
            px, py = gx + dx, gy + dy

            @pl.when((px >= 0) & (px < nx) & (py >= 0) & (py < ny))
            def _():
                send_ref[px * ny + py] = block


def product_kernel(
    nx, ny, recv_ref, node_ref, slope_ref, sq_ref, expand_ref, wyt_ref, left_ref, wy_ref, res_ref,
    grad_ref, hess_ref, send_ref, out_ref, msc, gsc, sem,
):
    copy_out = pltpu.make_async_copy(res_ref, out_ref, sem)
    copy_out.start()
    gx, gy = lax.axis_index("gx"), lax.axis_index("gy")
    own = gx * ny + gy
    lane = lax.broadcasted_iota(jnp.int32, (8, 128), 1)
    sub = lax.broadcasted_iota(jnp.int32, (8, 128), 0)

    def block(dx, dy):
        px, py = gx + dx, gy + dy
        there = (px >= 0) & (px < nx) & (py >= 0) & (py < ny)
        return recv_ref[jnp.where(there, px * ny + py, own)]

    def column(x, at):
        return jnp.broadcast_to(x[:, at : at + 1], (8, 128))

    def with_corners(dx):
        mid = face_of(block(dx, 0))
        mid = mid + jnp.where(lane == 0, column(face_of(block(dx, -1)), 16), 0.0)
        return mid + jnp.where(lane == 16, column(face_of(block(dx, 1)), 0), 0.0)

    keep_x = jnp.where(gx == nx - 1, 0.0, 1.0).astype(F32)
    keep_y = jnp.where(gy == ny - 1, 0.0, 1.0).astype(F32)
    keep_lane = jnp.where(lane == 16, keep_y, 1.0)
    row_low = with_corners(-1)
    row_high = with_corners(1)
    col_low, edge_low = column_of(block(0, -1))
    col_high, edge_high = column_of(block(0, 1))
    grads = []
    square = jnp.zeros((8, 128), F32)
    for kc in range(6):
        g = node_ref[kc * 8 : kc * 8 + 8]
        g = g + jnp.where(sub == 0, jnp.broadcast_to(row_low[kc : kc + 1], (8, 128)), 0.0)
        g = g + jnp.where(lane == 0, column(col_low, kc), 0.0)
        g = g + jnp.where(lane == 16, column(col_high, kc), 0.0)
        g = g * keep_lane
        grads.append(g)
        grad_ref[kc] = g
        own_g = jnp.where(lane < 16, g, 0.0)
        square = square + own_g * own_g
    face = node_ref[48:56] + row_high
    face = face + jnp.where(lane == 0, column(edge_low, 0), 0.0)
    face = face + jnp.where(lane == 16, column(edge_high, 0), 0.0)
    face = jnp.where(sub < 6, face * keep_lane * keep_x, 0.0)
    full = jnp.concatenate(grads + [face, jnp.zeros((8, 128), F32)], axis=0)
    moved = dot_right(expand_ref[...], dot_left(full, wyt_ref[...]))
    msc[...] = moved.reshape(6, 8, 8, 128)

    def apply(cx, curve):
        m0 = [msc[2 * k, cx] for k in range(3)]
        dm = [msc[2 * k + 1, cx] - m0[k] for k in range(3)]
        total = [None] * 3
        upper = [None] * 3
        for z in range(8):
            sz = (z + 0.5) / 8.0
            s = [slope_ref[k, z, cx] for k in range(3)]
            along = s[0] * (m0[0] + sz * dm[0])
            for k in (1, 2):
                along = along + s[k] * (m0[k] + sz * dm[k])
            curve = curve + along * along
            for k in range(3):
                w = s[k] * along
                u = w * sz
                total[k] = w if z == 0 else total[k] + w
                upper[k] = u if z == 0 else upper[k] + u
        for k in range(3):
            gsc[2 * k, cx] = total[k] - upper[k]
            gsc[2 * k + 1, cx] = upper[k]
        return curve

    curve = lax.fori_loop(0, 8, apply, jnp.zeros((8, 128), F32), unroll=4)
    nodes = dot_left(dot_right(left_ref[...], gsc[...].reshape(384, 128)), wy_ref[...])
    rows = [nodes[kc * 8 : kc * 8 + 8] for kc in range(6)]
    for kc in range(6):
        hess_ref[kc] = rows[kc]
    col_high = column_row(rows, nodes[48:56], 16)
    high = face_row(nodes[48:56])
    spot = lane[:1]
    sums = jnp.where(spot == 104, jnp.sum(sq_ref[...]), 0.0)
    sums = jnp.where(spot == 105, jnp.sum(square), sums)
    sums = jnp.where(spot == 106, jnp.sum(curve) * (1.0 / 512.0), sums)
    tail = spot >= 104
    send_ref[...] = jnp.broadcast_to(sums[None], send_ref.shape)
    for dx, dy, data in ((1, 0, high), (1, 1, high), (0, 1, col_high)):
        px, py = gx + dx, gy + dy

        @pl.when((px < nx) & (py < ny))
        def _():
            send_ref[px * ny + py] = jnp.where(tail, sums, data)

    copy_out.wait()


def finish_kernel(nx, ny, voxels, recv_ref, grad_ref, hess_ref, step_ref, prod_ref, misfit_ref):
    gx, gy = lax.axis_index("gx"), lax.axis_index("gy")
    own = gx * ny + gy
    lane = lax.broadcasted_iota(jnp.int32, (8, 128), 1)
    sub = lax.broadcasted_iota(jnp.int32, (8, 128), 0)

    def block(dx, dy):
        px, py = gx + dx, gy + dy
        there = (px >= 0) & (py >= 0)
        data = recv_ref[jnp.where(there, px * ny + py, own)]
        return jnp.where(there, data, 0.0)

    def column(x, at):
        return jnp.broadcast_to(x[:, at : at + 1], (8, 128))

    total = jnp.sum(recv_ref[...], axis=0)
    misfit_ref[...] = total[:, 104:105] * (1.0 / voxels)
    total = jnp.broadcast_to(total, (8, 128))
    alpha = column(total, 105) / column(total, 106)
    row_low = face_of(block(-1, 0)) + jnp.where(lane == 0, column(face_of(block(-1, -1)), 16), 0.0)
    col_low = column_of(block(0, -1))[0]
    for kc in range(6):
        h = hess_ref[kc]
        h = h + jnp.where(sub == 0, jnp.broadcast_to(row_low[kc : kc + 1], (8, 128)), 0.0)
        h = h + jnp.where(lane == 0, column(col_low, kc), 0.0)
        prod_ref[kc // 2, kc % 2] = h[:, :16]
        step_ref[kc // 2, kc % 2] = (alpha * grad_ref[kc])[:, :16]


def swaps(count, first):
    pairs = [(i, i + 1) for i in range(first, count - 1, 2)]
    return pairs + [(j, i) for i, j in pairs]


def on_device(ref_image, def_image, shift_xy, shift_z, frac, connectivity):
    nx, ny = lax.axis_size("gx"), lax.axis_size("gy")
    peers = nx * ny
    sds = jax.ShapeDtypeStruct
    xa = lax.ppermute(def_image, "gx", swaps(nx, 0))
    xb = lax.ppermute(def_image, "gx", swaps(nx, 1))
    half = sds((4, 64, 128), BF16)
    to_b, to_a, own = pl.pallas_call(
        pack_own_kernel,
        out_shape=(half, half, sds((8, 64, 128), BF16)),
        in_specs=[VMEM],
        out_specs=(VMEM,) * 3,
        compiler_params=PARAMS,
        cost_estimate=pl.CostEstimate(flops=300000, bytes_accessed=262144, transcendentals=0),
        name="pack_own_halo",
    )(def_image)
    yb = lax.ppermute(to_b, "gy", swaps(ny, 1))
    ya = lax.ppermute(to_a, "gy", swaps(ny, 0))
    row = lax.broadcasted_iota(jnp.int32, (16, 128), 0)
    table = jnp.where(row == 10, shift_z[None], 0).astype(F32)
    for rows, at in ((connectivity, 0), (shift_xy, 8), (frac, 11)):
        table = table + jnp.pad(rows.astype(F32), ((at, 16 - at - rows.shape[0]), (0, 0)))
    idx, wgt = pl.pallas_call(
        index_kernel,
        out_shape=(sds((8, 128), jnp.int32), sds((8, 8, 128), F32)),
        in_specs=[VMEM],
        out_specs=(VMEM, VMEM),
        compiler_params=PARAMS,
        cost_estimate=pl.CostEstimate(flops=300000, bytes_accessed=262144, transcendentals=0),
        name="order_elements",
    )(table)
    corner = sds((4, 128, 128), BF16)
    corner_b, corner_a = pl.pallas_call(
        pack_corner_kernel,
        out_shape=(corner, corner),
        in_specs=[VMEM, VMEM] + [pl.BlockSpec(memory_space=pl.ANY)] * 3,
        out_specs=(VMEM, VMEM),
        compiler_params=PARAMS,
        cost_estimate=pl.CostEstimate(flops=300000, bytes_accessed=524288, transcendentals=0),
        name="pack_corner_halo",
    )(xa, xb, yb, ya, idx)
    cb = lax.ppermute(corner_b, "gy", swaps(ny, 1))
    ca = lax.ppermute(corner_a, "gy", swaps(ny, 0))

    left, wy, expand, wyt = tables()
    arr = pl.pallas_call(
        early_kernel,
        out_shape=sds((16, 18, 8, 128), F32),
        in_specs=[SMEM] + [VMEM] * 3,
        out_specs=VMEM,
        scratch_shapes=[pltpu.VMEM((TILE_ROWS, 128), F32)],
        compiler_params=PARAMS,
        cost_estimate=pl.CostEstimate(flops=4000000, bytes_accessed=2000000, transcendentals=0),
        name="sample_early",
    )(idx, xa, own, xb)
    residual, slopes, nodes, send, square = pl.pallas_call(
        lambda *refs: late_kernel(nx, ny, *refs),
        out_shape=(
            sds((8, 64, 128), BF16),
            sds((3, 8, 8, 8, 128), F32),
            sds((64, 128), F32),
            sds((peers, 1, 128), F32),
            sds((8, 128), F32),
        ),
        in_specs=[SMEM] + [VMEM] * 12,
        out_specs=(VMEM,) * 5,
        scratch_shapes=[
            pltpu.VMEM((2 * TILE_ROWS, 128), F32),
            pltpu.VMEM((16, 18, 8, 128), F32),
            pltpu.VMEM((8, 8, 8, 128), F32),
            pltpu.VMEM((6, 8, 8, 128), F32),
        ],
        compiler_params=PARAMS,
        name="sample_and_gradient",
    )(idx, wgt, xa, own, xb, yb, ya, cb, ca, arr, ref_image, left, wy)
    recv = lax.all_to_all(send, ("gx", "gy"), 0, 0, tiled=True)
    grads, hess, send, residual = pl.pallas_call(
        lambda *refs: product_kernel(nx, ny, *refs),
        out_shape=(
            sds((6, 8, 128), F32),
            sds((6, 8, 128), F32),
            sds((peers, 1, 128), F32),
            sds((8, 64, 128), BF16),
        ),
        in_specs=[VMEM] * 9,
        out_specs=(VMEM,) * 3 + (pl.BlockSpec(memory_space=pl.ANY),),
        scratch_shapes=[
            pltpu.VMEM((6, 8, 8, 128), F32),
            pltpu.VMEM((6, 8, 8, 128), F32),
            pltpu.SemaphoreType.DMA,
        ],
        compiler_params=PARAMS,
        name="gauss_newton_product",
    )(recv, nodes, slopes, square, expand, wyt, left, wy, residual)
    recv = lax.all_to_all(send, ("gx", "gy"), 0, 0, tiled=True)
    voxels = 8 * 64 * 128 * peers
    step, product, misfit = pl.pallas_call(
        lambda *refs: finish_kernel(nx, ny, voxels, *refs),
        out_shape=(sds((3, 2, 8, 16), F32), sds((3, 2, 8, 16), F32), sds((1, 1), F32)),
        in_specs=[VMEM] * 3,
        out_specs=(VMEM,) * 3,
        compiler_params=PARAMS,
        name="finish",
    )(recv, grads, hess)
    return (residual, step, product, misfit[0, 0])


def solution(mesh):
    in_specs = (
        P(None, "gx", "gy"),
        P(None, "gx", "gy"),
        P(None, ("gx", "gy")),
        P(("gx", "gy")),
        P(None, ("gx", "gy")),
        P(None, ("gx", "gy")),
    )
    out_specs = (P(None, "gx", "gy"), P(None, None, "gx", "gy"), P(None, None, "gx", "gy"), P())
    return jax.shard_map(
        on_device, mesh=mesh, in_specs=in_specs, out_specs=out_specs, check_vma=False
    )
```

```python
import jax
import jax.numpy as jnp
import numpy as np
from jax import lax
from jax.experimental import pallas as pl
from jax.experimental.pallas import tpu as pltpu
from jax.sharding import PartitionSpec as P

HALO = 64
F32 = jnp.float32
BF16 = jnp.bfloat16
SPAN = 192
TILE_ROWS = 12 * SPAN
CHUNK = 16
VMEM = pl.BlockSpec(memory_space=pltpu.VMEM)
SMEM = pl.BlockSpec(memory_space=pltpu.SMEM)
PARAMS = pltpu.CompilerParams(vmem_limit_bytes=24 * 1024 * 1024)


def node_weights(count):
    w = np.zeros((count + 1, 8 * count), np.float32)
    for v in range(8 * count):
        s = (v % 8 + 0.5) / 8.0
        w[v // 8, v] = 1.0 - s
        w[v // 8 + 1, v] = s
    return w


def tables():
    wx = node_weights(8)
    left = np.zeros((64, 6, 64), np.float32)
    for kc in range(6):
        left[kc * 8 : kc * 8 + 8, kc] = wx[:8]
        left[48 + kc, kc] = wx[8]
        left[56 + kc, kc] = wx[0]
    left = left.reshape(64, 384)
    expand = left.T.copy()
    expand[:, 56:] = 0.0
    wy = np.zeros((128, 128), np.float32)
    wy[:, :17] = node_weights(16).T
    as_bf = lambda a: jnp.asarray(a, BF16)
    return as_bf(left / 512.0), as_bf(wy), as_bf(expand), as_bf(wy.T)


def split(x):
    hi = x.astype(BF16)
    return hi, (x - hi.astype(F32)).astype(BF16)


def dot(a, b):
    return jnp.dot(a, b, preferred_element_type=F32)


def dot_right(w, x):
    hi, lo = split(x)
    return dot(w, hi) + dot(w, lo)


def dot_left(x, w):
    hi, lo = split(x)
    return dot(hi, w) + dot(lo, w)


def pack_rows(src, dst_a, dst_b, at, even):
    left = lax.broadcasted_iota(jnp.int32, (64, 128), 1) < 64
    for p in range(4):
        a = src[p].astype(F32)
        c = src[p + 4].astype(F32)
        right = jnp.where(left, pltpu.roll(a, 64, 1), c)
        other = jnp.where(left, a, pltpu.roll(c, 64, 1))
        dst_a[p, pl.ds(at, 64)] = jnp.where(even, right, other).astype(BF16)
        dst_b[p, pl.ds(at, 64)] = jnp.where(even, other, right).astype(BF16)


def dot_rows(a, b):
    return lax.dot_general(a, b, (((1,), (1,)), ((), ())), preferred_element_type=F32)


def as_rows(rows):
    sub = lax.broadcasted_iota(jnp.int32, (8, 128), 0)
    out = jnp.zeros((8, 128), F32)
    for n, row in enumerate(rows):
        out = jnp.where(sub == n, jnp.broadcast_to(row.astype(F32), (8, 128)), out)
    return out


def index_kernel(row_ref, own_ref, idx_ref, wgt_ref, keep_ref):
    keep_ref[...] = own_ref[...]
    first = row_ref[0:1].astype(jnp.int32)
    col_x = (first * 241) >> 12
    col_y = first - 17 * col_x
    start_x = 8 * col_x + row_ref[8:9].astype(jnp.int32) + HALO
    start_y = 8 * col_y + row_ref[9:10].astype(jnp.int32) + HALO
    early = (start_y >= 64) & (start_y < 184)
    below = start_y < 64
    offset = jnp.where(early, start_y - 64, jnp.where(below, start_y, start_y - 128))
    base = (row_ref[10:11].astype(jnp.int32) + 2) * SPAN + start_x
    tile = jnp.where(early | below, 0, TILE_ROWS)
    shift = (8 * col_y - offset) & 127
    place = (col_y & 1) * 8 + col_x
    width = jnp.where(early, 0, 9)
    flag = early.astype(F32)
    row = lax.broadcasted_iota(jnp.int32, (128, 128), 0)
    lane = lax.broadcasted_iota(jnp.int32, (128, 128), 1)
    upto = dot(as_rows([flag]).astype(BF16), (row <= lane).astype(F32).astype(BF16))[0:1]
    count = jnp.sum(flag, axis=1, keepdims=True)
    rank = jnp.where(early, upto - 1.0, count + lane[0:1].astype(F32) - upto)
    order = (jnp.broadcast_to(rank, (128, 128)) == row.astype(F32)).astype(F32).astype(BF16)
    hi, lo = split(as_rows([base, shift, place, 8 * col_y, tile, width]))
    table = dot_rows(hi, order) + dot_rows(lo, order)
    sub = lax.broadcasted_iota(jnp.int32, (8, 128), 0)
    table = jnp.where(sub == 6, jnp.broadcast_to(count, (8, 128)), table)
    idx_ref[...] = table.astype(jnp.int32)
    value = as_rows([row_ref[11 + c : 12 + c] for c in range(3)])
    hi, lo = split(value)
    rest = (value - hi.astype(F32) - lo.astype(F32)).astype(BF16)
    element = jnp.broadcast_to(col_x * 16 + col_y, (128, 128))
    for cx in range(8):
        spread = (element == cx * 16 + (row >> 3)).astype(F32).astype(BF16)
        wgt_ref[cx] = dot_rows(hi, spread) + dot_rows(lo, spread) + dot_rows(rest, spread)


def pack_kernel(xa_ref, own_ref, xb_ref, b_ref, a_ref):
    even = lax.axis_index("gy") % 2 == 0
    for n, ref in enumerate((xa_ref, own_ref, xb_ref)):
        pack_rows(ref, a_ref, b_ref, 64 * n, even)


def over_sublanes(x):
    return jnp.sum(x, axis=0, keepdims=True)


def lanes_of(x, idx):
    return jnp.take_along_axis(x, idx & 127, axis=1, mode="promise_in_bounds")


def face_row(face):
    return over_sublanes(pltpu.roll(face, 0, 1, stride=17, stride_axis=0))


def face_of(row):
    lane = lax.broadcasted_iota(jnp.int32, (8, 128), 1)
    sub = lax.broadcasted_iota(jnp.int32, (8, 128), 0)
    back = lanes_of(jnp.broadcast_to(row, (8, 128)), lane + 17 * sub)
    return jnp.where((lane < 17) & (sub < 6), back, 0.0)


def column_row(rows, face, at):
    lane = lax.broadcasted_iota(jnp.int32, (8, 128), 1)
    block = jnp.zeros((8, 128), F32)
    for kc in range(6):
        block = jnp.where(lane == kc, jnp.broadcast_to(rows[kc][:, at : at + 1], (8, 128)), block)
    edge = jnp.where(lane == 64, jnp.broadcast_to(face[:, at : at + 1], (8, 128)), 0.0)
    block = pltpu.roll(block, 0, 1, stride=8, stride_axis=0)
    edge = pltpu.roll(edge, 0, 1, stride=1, stride_axis=0)
    return over_sublanes(block + edge)


def column_of(row):
    lane = lax.broadcasted_iota(jnp.int32, (8, 128), 1)
    sub = lax.broadcasted_iota(jnp.int32, (8, 128), 0)
    row = jnp.broadcast_to(row, (8, 128))
    return lanes_of(row, lane + 8 * sub), lanes_of(row, lane + 64 + sub)


def place_of_a():
    return pl.multiple_of(jnp.where(lax.axis_index("gx") % 2 == 1, 0, 128), 64)


def clear_outside(img, tiles):
    zero = jnp.zeros((2 * SPAN, 128), F32)
    for k in range(tiles):
        img[pl.ds(k * TILE_ROWS, 2 * SPAN)] = zero
        img[pl.ds(k * TILE_ROWS + 10 * SPAN, 2 * SPAN)] = zero


def sample_element(img, arr, base, shift, place, first, width):
    lane = lax.broadcasted_iota(jnp.int32, (8, 128), 1)
    mask = ((lane - first) & 127) < width
    for z in range(9):
        for q in range(2):
            v = img[pl.ds(base + (z * SPAN + q), 8), :]
            pltpu.store(arr.at[place, z * 2 + q], pltpu.roll(v, shift, 1), mask=mask)


def early_kernel(idx_ref, xa_ref, own_ref, xb_ref, arr_ref, img):
    clear_outside(img, 1)
    at_a = place_of_a()
    for z in range(8):
        for ref, row in ((xa_ref, at_a), (own_ref, 64), (xb_ref, 128 - at_a)):
            img[pl.ds(pl.multiple_of((z + 2) * SPAN + row, 8), 64)] = ref[z].astype(F32)

    def chunk(n, carry):
        for m in range(CHUNK):
            e = n * CHUNK + m
            sample_element(
                img, arr_ref, idx_ref[0, e], idx_ref[1, e], idx_ref[2, e], idx_ref[3, e], 9
            )
        return carry

    lax.fori_loop(0, (idx_ref[6, 0] + (CHUNK - 1)) // CHUNK, chunk, 0)


def late_kernel(
    nx, ny, idx_ref, wgt, xa_ref, own_ref, xb_ref, yb_ref, ya_ref, arr_ref, ref_ref,
    left_ref, wy_ref, res_ref, slope_ref, node_ref, send_ref, sq_ref, img, arr, rsc, gsc,
):
    half = lax.broadcasted_iota(jnp.int32, (64, 128), 1) < 64
    clear_outside(img, 2)
    odd_y = lax.axis_index("gy") % 2 == 1
    at_a = place_of_a()
    segments = (
        (xa_ref, 0, at_a),
        (own_ref, 64, 64),
        (xb_ref, 128, 128 - at_a),
    )
    for p in range(4):
        for ref, at, row in segments:
            ra = pltpu.roll(ref[p].astype(F32), 64, 1)
            rc = pltpu.roll(ref[p + 4].astype(F32), 64, 1)
            from_a = ya_ref[p, pl.ds(at, 64)].astype(F32)
            from_b = yb_ref[p, pl.ds(at, 64)].astype(F32)
            lo = jnp.where(odd_y, from_a, from_b)
            hi = jnp.where(odd_y, from_b, from_a)
            at_row = lambda k, q: pl.ds(pl.multiple_of(k * TILE_ROWS + (q + 2) * SPAN + row, 8), 64)
            img[at_row(0, p)] = jnp.where(half, lo, ra)
            img[at_row(1, p)] = jnp.where(half, ra, pltpu.roll(hi, 64, 1))
            img[at_row(0, p + 4)] = jnp.where(half, pltpu.roll(lo, 64, 1), rc)
            img[at_row(1, p + 4)] = jnp.where(half, rc, hi)
    for z in range(8):
        rsc[z] = ref_ref[z].astype(F32).reshape(8, 8, 128)
    arr[...] = arr_ref[...]

    def chunk(n, carry):
        for m in range(CHUNK):
            e = n * CHUNK + m
            base = idx_ref[0, e] + idx_ref[4, e]
            sample_element(
                img, arr, base, idx_ref[1, e], idx_ref[2, e], idx_ref[3, e], idx_ref[5, e]
            )
        return carry

    lax.fori_loop(idx_ref[6, 0] // CHUNK, 128 // CHUNK, chunk, 0)

    lane = lax.broadcasted_iota(jnp.int32, (8, 128), 1)
    phase = lane & 15
    even = phase < 8
    even_next = (phase >= 1) & (phase <= 8)

    def interpolate(cx, square):
        wz, wx, wy = (jnp.broadcast_to(wgt[cx, c : c + 1], (8, 128)) for c in range(3))

        def pair(z, q):
            ev = arr[cx, z * 2 + q]
            od = arr[cx + 8, z * 2 + q]
            near = jnp.where(even, ev, od)
            far = pltpu.roll(jnp.where(even_next, ev, od), 127, 1)
            return near, far

        total = [None] * 3
        upper = [None] * 3
        prev = [pair(0, 0), pair(0, 1)]
        for z in range(8):
            cur = [pair(z + 1, 0), pair(z + 1, 1)]
            low, dzx, dx = [], [], []
            for y in range(2):
                d0 = cur[0][y] - prev[0][y]
                d1 = cur[1][y] - prev[1][y]
                l0 = prev[0][y] + wz * d0
                l1 = prev[1][y] + wz * d1
                dx.append(l1 - l0)
                low.append(l0 + wx * dx[y])
                dzx.append(d0 + wx * (d1 - d0))
            prev = cur
            slope_y = low[1] - low[0]
            value = low[0] + wy * slope_y
            slope_z = dzx[0] + wy * (dzx[1] - dzx[0])
            slope_x = dx[0] + wy * (dx[1] - dx[0])
            r = rsc[z, cx] - value
            rsc[z, cx] = r
            square = square + r * r
            for k, s in enumerate((slope_z, slope_x, slope_y)):
                slope_ref[k, z, cx] = s
                w = s * r
                u = w * ((z + 0.5) / 8.0)
                total[k] = w if z == 0 else total[k] + w
                upper[k] = u if z == 0 else upper[k] + u
        for k in range(3):
            gsc[2 * k, cx] = total[k] - upper[k]
            gsc[2 * k + 1, cx] = upper[k]
        return square

    sq_ref[...] = lax.fori_loop(0, 8, interpolate, jnp.zeros((8, 128), F32), unroll=4)
    res_ref[...] = rsc[...].reshape(8, 64, 128).astype(BF16)
    nodes = dot_left(dot_right(left_ref[...], gsc[...].reshape(384, 128)), wy_ref[...])
    node_ref[...] = nodes
    rows = [nodes[kc * 8 : kc * 8 + 8] for kc in range(6)]
    high, low = nodes[48:56], nodes[56:64]
    col_high = column_row(rows, high, 16)
    col_low = column_row(rows, high, 0)
    high, low = face_row(high), face_row(low)
    gx, gy = lax.axis_index("gx"), lax.axis_index("gy")
    send_ref[...] = jnp.zeros(send_ref.shape, F32)
    for dx in (-1, 0, 1):
        for dy in (-1, 0, 1):
            if dx == 0 and dy == 0:
                continue
            block = high if dx == 1 else low if dx == -1 else col_high if dy == 1 else col_low
            px, py = gx + dx, gy + dy

            @pl.when((px >= 0) & (px < nx) & (py >= 0) & (py < ny))
            def _():
                send_ref[px * ny + py] = block


def product_kernel(
    nx, ny, recv_ref, node_ref, slope_ref, sq_ref, expand_ref, wyt_ref, left_ref, wy_ref, res_ref,
    grad_ref, hess_ref, send_ref, out_ref, msc, gsc, sem,
):
    copy_out = pltpu.make_async_copy(res_ref, out_ref, sem)
    copy_out.start()
    gx, gy = lax.axis_index("gx"), lax.axis_index("gy")
    own = gx * ny + gy
    lane = lax.broadcasted_iota(jnp.int32, (8, 128), 1)
    sub = lax.broadcasted_iota(jnp.int32, (8, 128), 0)

    def block(dx, dy):
        px, py = gx + dx, gy + dy
        there = (px >= 0) & (px < nx) & (py >= 0) & (py < ny)
        return recv_ref[jnp.where(there, px * ny + py, own)]

    def column(x, at):
        return jnp.broadcast_to(x[:, at : at + 1], (8, 128))

    def with_corners(dx):
        mid = face_of(block(dx, 0))
        mid = mid + jnp.where(lane == 0, column(face_of(block(dx, -1)), 16), 0.0)
        return mid + jnp.where(lane == 16, column(face_of(block(dx, 1)), 0), 0.0)

    keep_x = jnp.where(gx == nx - 1, 0.0, 1.0).astype(F32)
    keep_y = jnp.where(gy == ny - 1, 0.0, 1.0).astype(F32)
    keep_lane = jnp.where(lane == 16, keep_y, 1.0)
    row_low = with_corners(-1)
    row_high = with_corners(1)
    col_low, edge_low = column_of(block(0, -1))
    col_high, edge_high = column_of(block(0, 1))
    grads = []
    square = jnp.zeros((8, 128), F32)
    for kc in range(6):
        g = node_ref[kc * 8 : kc * 8 + 8]
        g = g + jnp.where(sub == 0, jnp.broadcast_to(row_low[kc : kc + 1], (8, 128)), 0.0)
        g = g + jnp.where(lane == 0, column(col_low, kc), 0.0)
        g = g + jnp.where(lane == 16, column(col_high, kc), 0.0)
        g = g * keep_lane
        grads.append(g)
        grad_ref[kc] = g
        own_g = jnp.where(lane < 16, g, 0.0)
        square = square + own_g * own_g
    face = node_ref[48:56] + row_high
    face = face + jnp.where(lane == 0, column(edge_low, 0), 0.0)
    face = face + jnp.where(lane == 16, column(edge_high, 0), 0.0)
    face = jnp.where(sub < 6, face * keep_lane * keep_x, 0.0)
    full = jnp.concatenate(grads + [face, jnp.zeros((8, 128), F32)], axis=0)
    moved = dot_right(expand_ref[...], dot_left(full, wyt_ref[...]))
    msc[...] = moved.reshape(6, 8, 8, 128)

    def apply(cx, curve):
        m0 = [msc[2 * k, cx] for k in range(3)]
        dm = [msc[2 * k + 1, cx] - m0[k] for k in range(3)]
        total = [None] * 3
        upper = [None] * 3
        for z in range(8):
            sz = (z + 0.5) / 8.0
            s = [slope_ref[k, z, cx] for k in range(3)]
            along = s[0] * (m0[0] + sz * dm[0])
            for k in (1, 2):
                along = along + s[k] * (m0[k] + sz * dm[k])
            curve = curve + along * along
            for k in range(3):
                w = s[k] * along
                u = w * sz
                total[k] = w if z == 0 else total[k] + w
                upper[k] = u if z == 0 else upper[k] + u
        for k in range(3):
            gsc[2 * k, cx] = total[k] - upper[k]
            gsc[2 * k + 1, cx] = upper[k]
        return curve

    curve = lax.fori_loop(0, 8, apply, jnp.zeros((8, 128), F32), unroll=4)
    nodes = dot_left(dot_right(left_ref[...], gsc[...].reshape(384, 128)), wy_ref[...])
    rows = [nodes[kc * 8 : kc * 8 + 8] for kc in range(6)]
    for kc in range(6):
        hess_ref[kc] = rows[kc]
    col_high = column_row(rows, nodes[48:56], 16)
    high = face_row(nodes[48:56])
    spot = lane[:1]
    sums = jnp.where(spot == 104, jnp.sum(sq_ref[...]), 0.0)
    sums = jnp.where(spot == 105, jnp.sum(square), sums)
    sums = jnp.where(spot == 106, jnp.sum(curve) * (1.0 / 512.0), sums)
    tail = spot >= 104
    send_ref[...] = jnp.broadcast_to(sums[None], send_ref.shape)
    for dx, dy, data in ((1, 0, high), (1, 1, high), (0, 1, col_high)):
        px, py = gx + dx, gy + dy

        @pl.when((px < nx) & (py < ny))
        def _():
            send_ref[px * ny + py] = jnp.where(tail, sums, data)

    copy_out.wait()


def finish_kernel(nx, ny, voxels, recv_ref, grad_ref, hess_ref, step_ref, prod_ref, misfit_ref):
    gx, gy = lax.axis_index("gx"), lax.axis_index("gy")
    own = gx * ny + gy
    lane = lax.broadcasted_iota(jnp.int32, (8, 128), 1)
    sub = lax.broadcasted_iota(jnp.int32, (8, 128), 0)

    def block(dx, dy):
        px, py = gx + dx, gy + dy
        there = (px >= 0) & (py >= 0)
        data = recv_ref[jnp.where(there, px * ny + py, own)]
        return jnp.where(there, data, 0.0)

    def column(x, at):
        return jnp.broadcast_to(x[:, at : at + 1], (8, 128))

    total = jnp.sum(recv_ref[...], axis=0)
    misfit_ref[...] = total[:, 104:105] * (1.0 / voxels)
    total = jnp.broadcast_to(total, (8, 128))
    alpha = column(total, 105) / column(total, 106)
    row_low = face_of(block(-1, 0)) + jnp.where(lane == 0, column(face_of(block(-1, -1)), 16), 0.0)
    col_low = column_of(block(0, -1))[0]
    for kc in range(6):
        h = hess_ref[kc]
        h = h + jnp.where(sub == 0, jnp.broadcast_to(row_low[kc : kc + 1], (8, 128)), 0.0)
        h = h + jnp.where(lane == 0, column(col_low, kc), 0.0)
        prod_ref[kc // 2, kc % 2] = h[:, :16]
        step_ref[kc // 2, kc % 2] = (alpha * grad_ref[kc])[:, :16]


def swaps(count, first):
    pairs = [(i, i + 1) for i in range(first, count - 1, 2)]
    return pairs + [(j, i) for i, j in pairs]


def on_device(ref_image, def_image, shift_xy, shift_z, frac, connectivity):
    nx, ny = lax.axis_size("gx"), lax.axis_size("gy")
    peers = nx * ny
    sds = jax.ShapeDtypeStruct
    xa = lax.ppermute(def_image, "gx", swaps(nx, 0))
    xb = lax.ppermute(def_image, "gx", swaps(nx, 1))
    row = lax.broadcasted_iota(jnp.int32, (16, 128), 0)
    table = jnp.where(row == 10, shift_z[None], 0).astype(F32)
    for rows, at in ((connectivity, 0), (shift_xy, 8), (frac, 11)):
        table = table + jnp.pad(rows.astype(F32), ((at, 16 - at - rows.shape[0]), (0, 0)))
    idx, wgt, own = pl.pallas_call(
        index_kernel,
        out_shape=(sds((8, 128), jnp.int32), sds((8, 8, 128), F32), sds((8, 64, 128), BF16)),
        in_specs=[VMEM, VMEM],
        out_specs=(VMEM,) * 3,
        compiler_params=PARAMS,
        cost_estimate=pl.CostEstimate(flops=300000, bytes_accessed=262144, transcendentals=0),
        name="order_elements",
    )(table, def_image)
    packed = sds((4, SPAN, 128), BF16)
    to_b, to_a = pl.pallas_call(
        pack_kernel,
        out_shape=(packed, packed),
        in_specs=[VMEM] * 3,
        out_specs=(VMEM, VMEM),
        compiler_params=PARAMS,
        cost_estimate=pl.CostEstimate(flops=300000, bytes_accessed=524288, transcendentals=0),
        name="pack_halo",
    )(xa, own, xb)
    yb = lax.ppermute(to_b, "gy", swaps(ny, 1))
    ya = lax.ppermute(to_a, "gy", swaps(ny, 0))

    left, wy, expand, wyt = tables()
    arr = pl.pallas_call(
        early_kernel,
        out_shape=sds((16, 18, 8, 128), F32),
        in_specs=[SMEM] + [VMEM] * 3,
        out_specs=VMEM,
        scratch_shapes=[pltpu.VMEM((TILE_ROWS, 128), F32)],
        compiler_params=PARAMS,
        cost_estimate=pl.CostEstimate(flops=4000000, bytes_accessed=2000000, transcendentals=0),
        name="sample_early",
    )(idx, xa, own, xb)
    residual, slopes, nodes, send, square = pl.pallas_call(
        lambda *refs: late_kernel(nx, ny, *refs),
        out_shape=(
            sds((8, 64, 128), BF16),
            sds((3, 8, 8, 8, 128), F32),
            sds((64, 128), F32),
            sds((peers, 1, 128), F32),
            sds((8, 128), F32),
        ),
        in_specs=[SMEM] + [VMEM] * 10,
        out_specs=(VMEM,) * 5,
        scratch_shapes=[
            pltpu.VMEM((2 * TILE_ROWS, 128), F32),
            pltpu.VMEM((16, 18, 8, 128), F32),
            pltpu.VMEM((8, 8, 8, 128), F32),
            pltpu.VMEM((6, 8, 8, 128), F32),
        ],
        compiler_params=PARAMS,
        name="sample_and_gradient",
    )(idx, wgt, xa, own, xb, yb, ya, arr, ref_image, left, wy)
    recv = lax.all_to_all(send, ("gx", "gy"), 0, 0, tiled=True)
    grads, hess, send, residual = pl.pallas_call(
        lambda *refs: product_kernel(nx, ny, *refs),
        out_shape=(
            sds((6, 8, 128), F32),
            sds((6, 8, 128), F32),
            sds((peers, 1, 128), F32),
            sds((8, 64, 128), BF16),
        ),
        in_specs=[VMEM] * 9,
        out_specs=(VMEM,) * 3 + (pl.BlockSpec(memory_space=pl.ANY),),
        scratch_shapes=[
            pltpu.VMEM((6, 8, 8, 128), F32),
            pltpu.VMEM((6, 8, 8, 128), F32),
            pltpu.SemaphoreType.DMA,
        ],
        compiler_params=PARAMS,
        name="gauss_newton_product",
    )(recv, nodes, slopes, square, expand, wyt, left, wy, residual)
    recv = lax.all_to_all(send, ("gx", "gy"), 0, 0, tiled=True)
    voxels = 8 * 64 * 128 * peers
    step, product, misfit = pl.pallas_call(
        lambda *refs: finish_kernel(nx, ny, voxels, *refs),
        out_shape=(sds((3, 2, 8, 16), F32), sds((3, 2, 8, 16), F32), sds((1, 1), F32)),
        in_specs=[VMEM] * 3,
        out_specs=(VMEM,) * 3,
        compiler_params=PARAMS,
        name="finish",
    )(recv, grads, hess)
    return (residual, step, product, misfit[0, 0])


def solution(mesh):
    in_specs = (
        P(None, "gx", "gy"),
        P(None, "gx", "gy"),
        P(None, ("gx", "gy")),
        P(("gx", "gy")),
        P(None, ("gx", "gy")),
        P(None, ("gx", "gy")),
    )
    out_specs = (P(None, "gx", "gy"), P(None, None, "gx", "gy"), P(None, None, "gx", "gy"), P())
    return jax.shard_map(
        on_device, mesh=mesh, in_specs=in_specs, out_specs=out_specs, check_vma=False
    )
```

```python
import jax
import jax.numpy as jnp
import numpy as np
from jax import lax
from jax.experimental import pallas as pl
from jax.experimental.pallas import tpu as pltpu
from jax.sharding import PartitionSpec as P

HALO = 64
F32 = jnp.float32
BF16 = jnp.bfloat16
SPAN = 192
TILE_ROWS = 12 * SPAN
CHUNK = 16
VMEM = pl.BlockSpec(memory_space=pltpu.VMEM)
SMEM = pl.BlockSpec(memory_space=pltpu.SMEM)
PARAMS = pltpu.CompilerParams(vmem_limit_bytes=24 * 1024 * 1024)


def node_weights(count):
    w = np.zeros((count + 1, 8 * count), np.float32)
    for v in range(8 * count):
        s = (v % 8 + 0.5) / 8.0
        w[v // 8, v] = 1.0 - s
        w[v // 8 + 1, v] = s
    return w


def tables():
    wx = node_weights(8)
    left = np.zeros((64, 6, 64), np.float32)
    for kc in range(6):
        left[kc * 8 : kc * 8 + 8, kc] = wx[:8]
        left[48 + kc, kc] = wx[8]
        left[56 + kc, kc] = wx[0]
    left = left.reshape(64, 384)
    expand = left.T.copy()
    expand[:, 56:] = 0.0
    wy = np.zeros((128, 128), np.float32)
    wy[:, :17] = node_weights(16).T
    as_bf = lambda a: jnp.asarray(a, BF16)
    return as_bf(left / 512.0), as_bf(wy), as_bf(expand), as_bf(wy.T)


def split(x):
    hi = x.astype(BF16)
    return hi, (x - hi.astype(F32)).astype(BF16)


def dot(a, b):
    return jnp.dot(a, b, preferred_element_type=F32)


def dot_right(w, x):
    hi, lo = split(x)
    return dot(w, hi) + dot(w, lo)


def dot_left(x, w):
    hi, lo = split(x)
    return dot(hi, w) + dot(lo, w)


def pack_rows(src, dst_a, dst_b, at, even):
    left = lax.broadcasted_iota(jnp.int32, (64, 128), 1) < 64
    for p in range(4):
        a = src[p].astype(F32)
        c = src[p + 4].astype(F32)
        right = jnp.where(left, pltpu.roll(a, 64, 1), c)
        other = jnp.where(left, a, pltpu.roll(c, 64, 1))
        dst_a[p, pl.ds(at, 64)] = jnp.where(even, right, other).astype(BF16)
        dst_b[p, pl.ds(at, 64)] = jnp.where(even, other, right).astype(BF16)


def dot_rows(a, b):
    return lax.dot_general(a, b, (((1,), (1,)), ((), ())), preferred_element_type=F32)


def as_rows(rows):
    sub = lax.broadcasted_iota(jnp.int32, (8, 128), 0)
    out = jnp.zeros((8, 128), F32)
    for n, row in enumerate(rows):
        out = jnp.where(sub == n, jnp.broadcast_to(row.astype(F32), (8, 128)), out)
    return out


def index_kernel(row_ref, own_ref, idx_ref, wgt_ref, keep_ref):
    keep_ref[...] = own_ref[...]
    first = row_ref[0:1].astype(jnp.int32)
    col_x = (first * 241) >> 12
    col_y = first - 17 * col_x
    start_x = 8 * col_x + row_ref[8:9].astype(jnp.int32) + HALO
    start_y = 8 * col_y + row_ref[9:10].astype(jnp.int32) + HALO
    early = (start_y >= 64) & (start_y < 184)
    below = start_y < 64
    offset = jnp.where(early, start_y - 64, jnp.where(below, start_y, start_y - 128))
    base = (row_ref[10:11].astype(jnp.int32) + 2) * SPAN + start_x
    tile = jnp.where(early | below, 0, TILE_ROWS)
    shift = (8 * col_y - offset) & 127
    place = (col_y & 1) * 8 + col_x
    width = jnp.where(early, 0, 9)
    flag = early.astype(F32)
    row = lax.broadcasted_iota(jnp.int32, (128, 128), 0)
    lane = lax.broadcasted_iota(jnp.int32, (128, 128), 1)
    upto = dot(as_rows([flag]).astype(BF16), (row <= lane).astype(F32).astype(BF16))[0:1]
    count = jnp.sum(flag, axis=1, keepdims=True)
    rank = jnp.where(early, upto - 1.0, count + lane[0:1].astype(F32) - upto)
    order = (jnp.broadcast_to(rank, (128, 128)) == row.astype(F32)).astype(F32).astype(BF16)
    hi, lo = split(as_rows([base, shift, place, 8 * col_y, tile, width]))
    table = dot_rows(hi, order) + dot_rows(lo, order)
    sub = lax.broadcasted_iota(jnp.int32, (8, 128), 0)
    table = jnp.where(sub == 6, jnp.broadcast_to(count, (8, 128)), table)
    idx_ref[...] = table.astype(jnp.int32)
    value = as_rows([row_ref[11 + c : 12 + c] for c in range(3)])
    hi, lo = split(value)
    rest = (value - hi.astype(F32) - lo.astype(F32)).astype(BF16)
    element = jnp.broadcast_to(col_x * 16 + col_y, (128, 128))
    for cx in range(8):
        spread = (element == cx * 16 + (row >> 3)).astype(F32).astype(BF16)
        wgt_ref[cx] = dot_rows(hi, spread) + dot_rows(lo, spread) + dot_rows(rest, spread)


def pack_kernel(xb_ref, own_ref, xa_ref, b_ref, a_ref):
    even = lax.axis_index("gy") % 2 == 0
    for n, ref in enumerate((xa_ref, own_ref, xb_ref)):
        pack_rows(ref, a_ref, b_ref, 64 * n, even)


def over_sublanes(x):
    return jnp.sum(x, axis=0, keepdims=True)


def lanes_of(x, idx):
    return jnp.take_along_axis(x, idx & 127, axis=1, mode="promise_in_bounds")


def face_row(face):
    return over_sublanes(pltpu.roll(face, 0, 1, stride=17, stride_axis=0))


def face_of(row):
    lane = lax.broadcasted_iota(jnp.int32, (8, 128), 1)
    sub = lax.broadcasted_iota(jnp.int32, (8, 128), 0)
    back = lanes_of(jnp.broadcast_to(row, (8, 128)), lane + 17 * sub)
    return jnp.where((lane < 17) & (sub < 6), back, 0.0)


def column_row(rows, face, at):
    lane = lax.broadcasted_iota(jnp.int32, (8, 128), 1)
    block = jnp.zeros((8, 128), F32)
    for kc in range(6):
        block = jnp.where(lane == kc, jnp.broadcast_to(rows[kc][:, at : at + 1], (8, 128)), block)
    edge = jnp.where(lane == 64, jnp.broadcast_to(face[:, at : at + 1], (8, 128)), 0.0)
    block = pltpu.roll(block, 0, 1, stride=8, stride_axis=0)
    edge = pltpu.roll(edge, 0, 1, stride=1, stride_axis=0)
    return over_sublanes(block + edge)


def column_of(row):
    lane = lax.broadcasted_iota(jnp.int32, (8, 128), 1)
    sub = lax.broadcasted_iota(jnp.int32, (8, 128), 0)
    row = jnp.broadcast_to(row, (8, 128))
    return lanes_of(row, lane + 8 * sub), lanes_of(row, lane + 64 + sub)


def place_of_a():
    return pl.multiple_of(jnp.where(lax.axis_index("gx") % 2 == 1, 0, 128), 64)


def clear_outside(img, tiles):
    zero = jnp.zeros((2 * SPAN, 128), F32)
    for k in range(tiles):
        img[pl.ds(k * TILE_ROWS, 2 * SPAN)] = zero
        img[pl.ds(k * TILE_ROWS + 10 * SPAN, 2 * SPAN)] = zero


def sample_element(img, arr, base, shift, place, first, width):
    lane = lax.broadcasted_iota(jnp.int32, (8, 128), 1)
    mask = ((lane - first) & 127) < width
    for z in range(9):
        for q in range(2):
            v = img[pl.ds(base + (z * SPAN + q), 8), :]
            pltpu.store(arr.at[place, z * 2 + q], pltpu.roll(v, shift, 1), mask=mask)


def early_kernel(idx_ref, xb_ref, own_ref, xa_ref, arr_ref, img):
    clear_outside(img, 1)
    at_a = place_of_a()
    for z in range(8):
        for ref, row in ((xa_ref, at_a), (own_ref, 64), (xb_ref, 128 - at_a)):
            img[pl.ds(pl.multiple_of((z + 2) * SPAN + row, 8), 64)] = ref[z].astype(F32)

    def chunk(n, carry):
        for m in range(CHUNK):
            e = n * CHUNK + m
            sample_element(
                img, arr_ref, idx_ref[0, e], idx_ref[1, e], idx_ref[2, e], idx_ref[3, e], 9
            )
        return carry

    lax.fori_loop(0, (idx_ref[6, 0] + (CHUNK - 1)) // CHUNK, chunk, 0)


def late_kernel(
    nx, ny, idx_ref, wgt, xb_ref, own_ref, xa_ref, yb_ref, ya_ref, arr_ref, ref_ref,
    left_ref, wy_ref, res_ref, slope_ref, node_ref, send_ref, sq_ref, img, arr, rsc, gsc,
):
    half = lax.broadcasted_iota(jnp.int32, (64, 128), 1) < 64
    clear_outside(img, 2)
    odd_y = lax.axis_index("gy") % 2 == 1
    at_a = place_of_a()
    segments = (
        (xa_ref, 0, at_a),
        (own_ref, 64, 64),
        (xb_ref, 128, 128 - at_a),
    )
    for p in range(4):
        for ref, at, row in segments:
            ra = pltpu.roll(ref[p].astype(F32), 64, 1)
            rc = pltpu.roll(ref[p + 4].astype(F32), 64, 1)
            from_a = ya_ref[p, pl.ds(at, 64)].astype(F32)
            from_b = yb_ref[p, pl.ds(at, 64)].astype(F32)
            lo = jnp.where(odd_y, from_a, from_b)
            hi = jnp.where(odd_y, from_b, from_a)
            at_row = lambda k, q: pl.ds(pl.multiple_of(k * TILE_ROWS + (q + 2) * SPAN + row, 8), 64)
            img[at_row(0, p)] = jnp.where(half, lo, ra)
            img[at_row(1, p)] = jnp.where(half, ra, pltpu.roll(hi, 64, 1))
            img[at_row(0, p + 4)] = jnp.where(half, pltpu.roll(lo, 64, 1), rc)
            img[at_row(1, p + 4)] = jnp.where(half, rc, hi)
    for z in range(8):
        rsc[z] = ref_ref[z].astype(F32).reshape(8, 8, 128)
    arr[...] = arr_ref[...]

    def chunk(n, carry):
        for m in range(CHUNK):
            e = n * CHUNK + m
            base = idx_ref[0, e] + idx_ref[4, e]
            sample_element(
                img, arr, base, idx_ref[1, e], idx_ref[2, e], idx_ref[3, e], idx_ref[5, e]
            )
        return carry

    lax.fori_loop(idx_ref[6, 0] // CHUNK, 128 // CHUNK, chunk, 0)

    lane = lax.broadcasted_iota(jnp.int32, (8, 128), 1)
    phase = lane & 15
    even = phase < 8
    even_next = (phase >= 1) & (phase <= 8)

    def interpolate(cx, square):
        wz, wx, wy = (jnp.broadcast_to(wgt[cx, c : c + 1], (8, 128)) for c in range(3))

        def pair(z, q):
            ev = arr[cx, z * 2 + q]
            od = arr[cx + 8, z * 2 + q]
            near = jnp.where(even, ev, od)
            far = pltpu.roll(jnp.where(even_next, ev, od), 127, 1)
            return near, far

        total = [None] * 3
        upper = [None] * 3
        prev = [pair(0, 0), pair(0, 1)]
        for z in range(8):
            cur = [pair(z + 1, 0), pair(z + 1, 1)]
            low, dzx, dx = [], [], []
            for y in range(2):
                d0 = cur[0][y] - prev[0][y]
                d1 = cur[1][y] - prev[1][y]
                l0 = prev[0][y] + wz * d0
                l1 = prev[1][y] + wz * d1
                dx.append(l1 - l0)
                low.append(l0 + wx * dx[y])
                dzx.append(d0 + wx * (d1 - d0))
            prev = cur
            slope_y = low[1] - low[0]
            value = low[0] + wy * slope_y
            slope_z = dzx[0] + wy * (dzx[1] - dzx[0])
            slope_x = dx[0] + wy * (dx[1] - dx[0])
            r = rsc[z, cx] - value
            rsc[z, cx] = r
            square = square + r * r
            for k, s in enumerate((slope_z, slope_x, slope_y)):
                slope_ref[k, z, cx] = s
                w = s * r
                u = w * ((z + 0.5) / 8.0)
                total[k] = w if z == 0 else total[k] + w
                upper[k] = u if z == 0 else upper[k] + u
        for k in range(3):
            gsc[2 * k, cx] = total[k] - upper[k]
            gsc[2 * k + 1, cx] = upper[k]
        return square

    sq_ref[...] = lax.fori_loop(0, 8, interpolate, jnp.zeros((8, 128), F32), unroll=4)
    res_ref[...] = rsc[...].reshape(8, 64, 128).astype(BF16)
    nodes = dot_left(dot_right(left_ref[...], gsc[...].reshape(384, 128)), wy_ref[...])
    node_ref[...] = nodes
    rows = [nodes[kc * 8 : kc * 8 + 8] for kc in range(6)]
    high, low = nodes[48:56], nodes[56:64]
    col_high = column_row(rows, high, 16)
    col_low = column_row(rows, high, 0)
    high, low = face_row(high), face_row(low)
    gx, gy = lax.axis_index("gx"), lax.axis_index("gy")
    send_ref[...] = jnp.zeros(send_ref.shape, F32)
    for dx in (-1, 0, 1):
        for dy in (-1, 0, 1):
            if dx == 0 and dy == 0:
                continue
            block = high if dx == 1 else low if dx == -1 else col_high if dy == 1 else col_low
            px, py = gx + dx, gy + dy

            @pl.when((px >= 0) & (px < nx) & (py >= 0) & (py < ny))
            def _():
                send_ref[px * ny + py] = block


def product_kernel(
    nx, ny, recv_ref, node_ref, slope_ref, sq_ref, expand_ref, wyt_ref, left_ref, wy_ref, res_ref,
    grad_ref, hess_ref, send_ref, out_ref, msc, gsc, sem,
):
    copy_out = pltpu.make_async_copy(res_ref, out_ref, sem)
    copy_out.start()
    gx, gy = lax.axis_index("gx"), lax.axis_index("gy")
    own = gx * ny + gy
    lane = lax.broadcasted_iota(jnp.int32, (8, 128), 1)
    sub = lax.broadcasted_iota(jnp.int32, (8, 128), 0)

    def block(dx, dy):
        px, py = gx + dx, gy + dy
        there = (px >= 0) & (px < nx) & (py >= 0) & (py < ny)
        return recv_ref[jnp.where(there, px * ny + py, own)]

    def column(x, at):
        return jnp.broadcast_to(x[:, at : at + 1], (8, 128))

    def with_corners(dx):
        mid = face_of(block(dx, 0))
        mid = mid + jnp.where(lane == 0, column(face_of(block(dx, -1)), 16), 0.0)
        return mid + jnp.where(lane == 16, column(face_of(block(dx, 1)), 0), 0.0)

    keep_x = jnp.where(gx == nx - 1, 0.0, 1.0).astype(F32)
    keep_y = jnp.where(gy == ny - 1, 0.0, 1.0).astype(F32)
    keep_lane = jnp.where(lane == 16, keep_y, 1.0)
    row_low = with_corners(-1)
    row_high = with_corners(1)
    col_low, edge_low = column_of(block(0, -1))
    col_high, edge_high = column_of(block(0, 1))
    grads = []
    square = jnp.zeros((8, 128), F32)
    for kc in range(6):
        g = node_ref[kc * 8 : kc * 8 + 8]
        g = g + jnp.where(sub == 0, jnp.broadcast_to(row_low[kc : kc + 1], (8, 128)), 0.0)
        g = g + jnp.where(lane == 0, column(col_low, kc), 0.0)
        g = g + jnp.where(lane == 16, column(col_high, kc), 0.0)
        g = g * keep_lane
        grads.append(g)
        grad_ref[kc] = g
        own_g = jnp.where(lane < 16, g, 0.0)
        square = square + own_g * own_g
    face = node_ref[48:56] + row_high
    face = face + jnp.where(lane == 0, column(edge_low, 0), 0.0)
    face = face + jnp.where(lane == 16, column(edge_high, 0), 0.0)
    face = jnp.where(sub < 6, face * keep_lane * keep_x, 0.0)
    full = jnp.concatenate(grads + [face, jnp.zeros((8, 128), F32)], axis=0)
    moved = dot_right(expand_ref[...], dot_left(full, wyt_ref[...]))
    msc[...] = moved.reshape(6, 8, 8, 128)

    def apply(cx, curve):
        m0 = [msc[2 * k, cx] for k in range(3)]
        dm = [msc[2 * k + 1, cx] - m0[k] for k in range(3)]
        total = [None] * 3
        upper = [None] * 3
        for z in range(8):
            sz = (z + 0.5) / 8.0
            s = [slope_ref[k, z, cx] for k in range(3)]
            along = s[0] * (m0[0] + sz * dm[0])
            for k in (1, 2):
                along = along + s[k] * (m0[k] + sz * dm[k])
            curve = curve + along * along
            for k in range(3):
                w = s[k] * along
                u = w * sz
                total[k] = w if z == 0 else total[k] + w
                upper[k] = u if z == 0 else upper[k] + u
        for k in range(3):
            gsc[2 * k, cx] = total[k] - upper[k]
            gsc[2 * k + 1, cx] = upper[k]
        return curve

    curve = lax.fori_loop(0, 8, apply, jnp.zeros((8, 128), F32), unroll=4)
    nodes = dot_left(dot_right(left_ref[...], gsc[...].reshape(384, 128)), wy_ref[...])
    rows = [nodes[kc * 8 : kc * 8 + 8] for kc in range(6)]
    for kc in range(6):
        hess_ref[kc] = rows[kc]
    col_high = column_row(rows, nodes[48:56], 16)
    high = face_row(nodes[48:56])
    spot = lane[:1]
    sums = jnp.where(spot == 104, jnp.sum(sq_ref[...]), 0.0)
    sums = jnp.where(spot == 105, jnp.sum(square), sums)
    sums = jnp.where(spot == 106, jnp.sum(curve) * (1.0 / 512.0), sums)
    tail = spot >= 104
    send_ref[...] = jnp.broadcast_to(sums[None], send_ref.shape)
    for dx, dy, data in ((1, 0, high), (1, 1, high), (0, 1, col_high)):
        px, py = gx + dx, gy + dy

        @pl.when((px < nx) & (py < ny))
        def _():
            send_ref[px * ny + py] = jnp.where(tail, sums, data)

    copy_out.wait()


def finish_kernel(nx, ny, voxels, recv_ref, grad_ref, hess_ref, step_ref, prod_ref, misfit_ref):
    gx, gy = lax.axis_index("gx"), lax.axis_index("gy")
    own = gx * ny + gy
    lane = lax.broadcasted_iota(jnp.int32, (8, 128), 1)
    sub = lax.broadcasted_iota(jnp.int32, (8, 128), 0)

    def block(dx, dy):
        px, py = gx + dx, gy + dy
        there = (px >= 0) & (py >= 0)
        data = recv_ref[jnp.where(there, px * ny + py, own)]
        return jnp.where(there, data, 0.0)

    def column(x, at):
        return jnp.broadcast_to(x[:, at : at + 1], (8, 128))

    total = jnp.sum(recv_ref[...], axis=0)
    misfit_ref[...] = total[:, 104:105] * (1.0 / voxels)
    total = jnp.broadcast_to(total, (8, 128))
    alpha = column(total, 105) / column(total, 106)
    row_low = face_of(block(-1, 0)) + jnp.where(lane == 0, column(face_of(block(-1, -1)), 16), 0.0)
    col_low = column_of(block(0, -1))[0]
    for kc in range(6):
        h = hess_ref[kc]
        h = h + jnp.where(sub == 0, jnp.broadcast_to(row_low[kc : kc + 1], (8, 128)), 0.0)
        h = h + jnp.where(lane == 0, column(col_low, kc), 0.0)
        prod_ref[kc // 2, kc % 2] = h[:, :16]
        step_ref[kc // 2, kc % 2] = (alpha * grad_ref[kc])[:, :16]


def swaps(count, first):
    pairs = [(i, i + 1) for i in range(first, count - 1, 2)]
    return pairs + [(j, i) for i, j in pairs]


def on_device(ref_image, def_image, shift_xy, shift_z, frac, connectivity):
    nx, ny = lax.axis_size("gx"), lax.axis_size("gy")
    peers = nx * ny
    sds = jax.ShapeDtypeStruct
    xa = lax.ppermute(def_image, "gx", swaps(nx, 0))
    xb = lax.ppermute(def_image, "gx", swaps(nx, 1))
    row = lax.broadcasted_iota(jnp.int32, (16, 128), 0)
    table = jnp.where(row == 10, shift_z[None], 0).astype(F32)
    for rows, at in ((connectivity, 0), (shift_xy, 8), (frac, 11)):
        table = table + jnp.pad(rows.astype(F32), ((at, 16 - at - rows.shape[0]), (0, 0)))
    idx, wgt, own = pl.pallas_call(
        index_kernel,
        out_shape=(sds((8, 128), jnp.int32), sds((8, 8, 128), F32), sds((8, 64, 128), BF16)),
        in_specs=[VMEM, VMEM],
        out_specs=(VMEM,) * 3,
        compiler_params=PARAMS,
        cost_estimate=pl.CostEstimate(flops=300000, bytes_accessed=262144, transcendentals=0),
        name="order_elements",
    )(table, def_image)
    packed = sds((4, SPAN, 128), BF16)
    to_b, to_a = pl.pallas_call(
        pack_kernel,
        out_shape=(packed, packed),
        in_specs=[VMEM] * 3,
        out_specs=(VMEM, VMEM),
        compiler_params=PARAMS,
        cost_estimate=pl.CostEstimate(flops=300000, bytes_accessed=524288, transcendentals=0),
        name="pack_halo",
    )(xb, own, xa)
    yb = lax.ppermute(to_b, "gy", swaps(ny, 1))
    ya = lax.ppermute(to_a, "gy", swaps(ny, 0))

    left, wy, expand, wyt = tables()
    arr = pl.pallas_call(
        early_kernel,
        out_shape=sds((16, 18, 8, 128), F32),
        in_specs=[SMEM] + [VMEM] * 3,
        out_specs=VMEM,
        scratch_shapes=[pltpu.VMEM((TILE_ROWS, 128), F32)],
        compiler_params=PARAMS,
        cost_estimate=pl.CostEstimate(flops=4000000, bytes_accessed=2000000, transcendentals=0),
        name="sample_early",
    )(idx, xb, own, xa)
    residual, slopes, nodes, send, square = pl.pallas_call(
        lambda *refs: late_kernel(nx, ny, *refs),
        out_shape=(
            sds((8, 64, 128), BF16),
            sds((3, 8, 8, 8, 128), F32),
            sds((64, 128), F32),
            sds((peers, 1, 128), F32),
            sds((8, 128), F32),
        ),
        in_specs=[SMEM] + [VMEM] * 10,
        out_specs=(VMEM,) * 5,
        scratch_shapes=[
            pltpu.VMEM((2 * TILE_ROWS, 128), F32),
            pltpu.VMEM((16, 18, 8, 128), F32),
            pltpu.VMEM((8, 8, 8, 128), F32),
            pltpu.VMEM((6, 8, 8, 128), F32),
        ],
        compiler_params=PARAMS,
        name="sample_and_gradient",
    )(idx, wgt, xb, own, xa, yb, ya, arr, ref_image, left, wy)
    recv = lax.all_to_all(send, ("gx", "gy"), 0, 0, tiled=True)
    grads, hess, send, residual = pl.pallas_call(
        lambda *refs: product_kernel(nx, ny, *refs),
        out_shape=(
            sds((6, 8, 128), F32),
            sds((6, 8, 128), F32),
            sds((peers, 1, 128), F32),
            sds((8, 64, 128), BF16),
        ),
        in_specs=[VMEM] * 9,
        out_specs=(VMEM,) * 3 + (pl.BlockSpec(memory_space=pl.ANY),),
        scratch_shapes=[
            pltpu.VMEM((6, 8, 8, 128), F32),
            pltpu.VMEM((6, 8, 8, 128), F32),
            pltpu.SemaphoreType.DMA,
        ],
        compiler_params=PARAMS,
        name="gauss_newton_product",
    )(recv, nodes, slopes, square, expand, wyt, left, wy, residual)
    recv = lax.all_to_all(send, ("gx", "gy"), 0, 0, tiled=True)
    voxels = 8 * 64 * 128 * peers
    step, product, misfit = pl.pallas_call(
        lambda *refs: finish_kernel(nx, ny, voxels, *refs),
        out_shape=(sds((3, 2, 8, 16), F32), sds((3, 2, 8, 16), F32), sds((1, 1), F32)),
        in_specs=[VMEM] * 3,
        out_specs=(VMEM,) * 3,
        compiler_params=PARAMS,
        name="finish",
    )(recv, grads, hess)
    return (residual, step, product, misfit[0, 0])


def solution(mesh):
    in_specs = (
        P(None, "gx", "gy"),
        P(None, "gx", "gy"),
        P(None, ("gx", "gy")),
        P(("gx", "gy")),
        P(None, ("gx", "gy")),
        P(None, ("gx", "gy")),
    )
    out_specs = (P(None, "gx", "gy"), P(None, None, "gx", "gy"), P(None, None, "gx", "gy"), P())
    return jax.shard_map(
        on_device, mesh=mesh, in_specs=in_specs, out_specs=out_specs, check_vma=False
    )
```

```python
import jax
import jax.numpy as jnp
import numpy as np
from jax import lax
from jax.experimental import pallas as pl
from jax.experimental.pallas import tpu as pltpu
from jax.sharding import PartitionSpec as P

HALO = 64
F32 = jnp.float32
BF16 = jnp.bfloat16
SPAN = 192
TILE_ROWS = 12 * SPAN
CHUNK = 16
VMEM = pl.BlockSpec(memory_space=pltpu.VMEM)
SMEM = pl.BlockSpec(memory_space=pltpu.SMEM)
PARAMS = pltpu.CompilerParams(vmem_limit_bytes=24 * 1024 * 1024)


def node_weights(count):
    w = np.zeros((count + 1, 8 * count), np.float32)
    for v in range(8 * count):
        s = (v % 8 + 0.5) / 8.0
        w[v // 8, v] = 1.0 - s
        w[v // 8 + 1, v] = s
    return w


def tables():
    wx = node_weights(8)
    left = np.zeros((64, 6, 64), np.float32)
    for kc in range(6):
        left[kc * 8 : kc * 8 + 8, kc] = wx[:8]
        left[48 + kc, kc] = wx[8]
        left[56 + kc, kc] = wx[0]
    left = left.reshape(64, 384)
    expand = left.T.copy()
    expand[:, 56:] = 0.0
    wy = np.zeros((128, 128), np.float32)
    wy[:, :17] = node_weights(16).T
    as_bf = lambda a: jnp.asarray(a, BF16)
    return as_bf(left / 512.0), as_bf(wy), as_bf(expand), as_bf(wy.T)


def split(x):
    hi = x.astype(BF16)
    return hi, (x - hi.astype(F32)).astype(BF16)


def dot(a, b):
    return jnp.dot(a, b, preferred_element_type=F32)


def dot_right(w, x):
    hi, lo = split(x)
    return dot(w, hi) + dot(w, lo)


def dot_left(x, w):
    hi, lo = split(x)
    return dot(hi, w) + dot(lo, w)


def pack_rows(src, dst_a, dst_b, at, even):
    left = lax.broadcasted_iota(jnp.int32, (64, 128), 1) < 64
    for p in range(4):
        a = src[p].astype(F32)
        c = src[p + 4].astype(F32)
        right = jnp.where(left, pltpu.roll(a, 64, 1), c)
        other = jnp.where(left, a, pltpu.roll(c, 64, 1))
        dst_a[p, pl.ds(at, 64)] = jnp.where(even, right, other).astype(BF16)
        dst_b[p, pl.ds(at, 64)] = jnp.where(even, other, right).astype(BF16)


def dot_rows(a, b):
    return lax.dot_general(a, b, (((1,), (1,)), ((), ())), preferred_element_type=F32)


def as_rows(rows):
    sub = lax.broadcasted_iota(jnp.int32, (8, 128), 0)
    out = jnp.zeros((8, 128), F32)
    for n, row in enumerate(rows):
        out = jnp.where(sub == n, jnp.broadcast_to(row.astype(F32), (8, 128)), out)
    return out


def index_kernel(row_ref, frac_ref, own_ref, idx_ref, wgt_ref, keep_ref):
    keep_ref[...] = own_ref[...]
    first = row_ref[0:1]
    col_x = (first * 241) >> 12
    col_y = first - 17 * col_x
    start_x = 8 * col_x + row_ref[8:9] + HALO
    start_y = 8 * col_y + row_ref[9:10] + HALO
    early = (start_y >= 64) & (start_y < 184)
    below = start_y < 64
    offset = jnp.where(early, start_y - 64, jnp.where(below, start_y, start_y - 128))
    base = (row_ref[10:11] + 2) * SPAN + start_x
    tile = jnp.where(early | below, 0, TILE_ROWS)
    shift = (8 * col_y - offset) & 127
    place = (col_y & 1) * 8 + col_x
    width = jnp.where(early, 0, 9)
    flag = early.astype(F32)
    row = lax.broadcasted_iota(jnp.int32, (128, 128), 0)
    lane = lax.broadcasted_iota(jnp.int32, (128, 128), 1)
    upto = dot(as_rows([flag]).astype(BF16), (row <= lane).astype(F32).astype(BF16))[0:1]
    count = jnp.sum(flag, axis=1, keepdims=True)
    rank = jnp.where(early, upto - 1.0, count + lane[0:1].astype(F32) - upto)
    order = (jnp.broadcast_to(rank, (128, 128)) == row.astype(F32)).astype(F32).astype(BF16)
    hi, lo = split(as_rows([base, shift, place, 8 * col_y, tile, width]))
    table = dot_rows(hi, order) + dot_rows(lo, order)
    sub = lax.broadcasted_iota(jnp.int32, (8, 128), 0)
    table = jnp.where(sub == 6, jnp.broadcast_to(count, (8, 128)), table)
    idx_ref[...] = table.astype(jnp.int32)
    value = as_rows([frac_ref[c : c + 1] for c in range(3)])
    hi, lo = split(value)
    rest = (value - hi.astype(F32) - lo.astype(F32)).astype(BF16)
    element = jnp.broadcast_to(col_x * 16 + col_y, (128, 128))
    for cx in range(8):
        spread = (element == cx * 16 + (row >> 3)).astype(F32).astype(BF16)
        wgt_ref[cx] = dot_rows(hi, spread) + dot_rows(lo, spread) + dot_rows(rest, spread)


def pack_kernel(xb_ref, own_ref, xa_ref, b_ref, a_ref):
    even = lax.axis_index("gy") % 2 == 0
    for n, ref in enumerate((xa_ref, own_ref, xb_ref)):
        pack_rows(ref, a_ref, b_ref, 64 * n, even)


def over_sublanes(x):
    return jnp.sum(x, axis=0, keepdims=True)


def lanes_of(x, idx):
    return jnp.take_along_axis(x, idx & 127, axis=1, mode="promise_in_bounds")


def face_row(face):
    return over_sublanes(pltpu.roll(face, 0, 1, stride=17, stride_axis=0))


def face_of(row):
    lane = lax.broadcasted_iota(jnp.int32, (8, 128), 1)
    sub = lax.broadcasted_iota(jnp.int32, (8, 128), 0)
    back = lanes_of(jnp.broadcast_to(row, (8, 128)), lane + 17 * sub)
    return jnp.where((lane < 17) & (sub < 6), back, 0.0)


def column_row(rows, face, at):
    lane = lax.broadcasted_iota(jnp.int32, (8, 128), 1)
    block = jnp.zeros((8, 128), F32)
    for kc in range(6):
        block = jnp.where(lane == kc, jnp.broadcast_to(rows[kc][:, at : at + 1], (8, 128)), block)
    edge = jnp.where(lane == 64, jnp.broadcast_to(face[:, at : at + 1], (8, 128)), 0.0)
    block = pltpu.roll(block, 0, 1, stride=8, stride_axis=0)
    edge = pltpu.roll(edge, 0, 1, stride=1, stride_axis=0)
    return over_sublanes(block + edge)


def column_of(row):
    lane = lax.broadcasted_iota(jnp.int32, (8, 128), 1)
    sub = lax.broadcasted_iota(jnp.int32, (8, 128), 0)
    row = jnp.broadcast_to(row, (8, 128))
    return lanes_of(row, lane + 8 * sub), lanes_of(row, lane + 64 + sub)


def place_of_a():
    return pl.multiple_of(jnp.where(lax.axis_index("gx") % 2 == 1, 0, 128), 64)


def clear_outside(img, tiles):
    zero = jnp.zeros((2 * SPAN, 128), F32)
    for k in range(tiles):
        img[pl.ds(k * TILE_ROWS, 2 * SPAN)] = zero
        img[pl.ds(k * TILE_ROWS + 10 * SPAN, 2 * SPAN)] = zero


def sample_element(img, arr, base, shift, place, first, width):
    lane = lax.broadcasted_iota(jnp.int32, (8, 128), 1)
    mask = ((lane - first) & 127) < width
    for z in range(9):
        for q in range(2):
            v = img[pl.ds(base + (z * SPAN + q), 8), :]
            pltpu.store(arr.at[place, z * 2 + q], pltpu.roll(v, shift, 1), mask=mask)


def early_kernel(idx_ref, xb_ref, own_ref, xa_ref, arr_ref, img):
    clear_outside(img, 1)
    at_a = place_of_a()
    for z in range(8):
        for ref, row in ((xa_ref, at_a), (own_ref, 64), (xb_ref, 128 - at_a)):
            img[pl.ds(pl.multiple_of((z + 2) * SPAN + row, 8), 64)] = ref[z].astype(F32)

    def chunk(n, carry):
        for m in range(CHUNK):
            e = n * CHUNK + m
            sample_element(
                img, arr_ref, idx_ref[0, e], idx_ref[1, e], idx_ref[2, e], idx_ref[3, e], 9
            )
        return carry

    lax.fori_loop(0, (idx_ref[6, 0] + (CHUNK - 1)) // CHUNK, chunk, 0)


def late_kernel(
    nx, ny, idx_ref, wgt, xb_ref, own_ref, xa_ref, yb_ref, ya_ref, arr_ref, ref_ref,
    left_ref, wy_ref, res_ref, slope_ref, node_ref, send_ref, sq_ref, img, arr, rsc, gsc,
):
    half = lax.broadcasted_iota(jnp.int32, (64, 128), 1) < 64
    clear_outside(img, 2)
    odd_y = lax.axis_index("gy") % 2 == 1
    at_a = place_of_a()
    segments = (
        (xa_ref, 0, at_a),
        (own_ref, 64, 64),
        (xb_ref, 128, 128 - at_a),
    )
    for p in range(4):
        for ref, at, row in segments:
            ra = pltpu.roll(ref[p].astype(F32), 64, 1)
            rc = pltpu.roll(ref[p + 4].astype(F32), 64, 1)
            from_a = ya_ref[p, pl.ds(at, 64)].astype(F32)
            from_b = yb_ref[p, pl.ds(at, 64)].astype(F32)
            lo = jnp.where(odd_y, from_a, from_b)
            hi = jnp.where(odd_y, from_b, from_a)
            at_row = lambda k, q: pl.ds(pl.multiple_of(k * TILE_ROWS + (q + 2) * SPAN + row, 8), 64)
            img[at_row(0, p)] = jnp.where(half, lo, ra)
            img[at_row(1, p)] = jnp.where(half, ra, pltpu.roll(hi, 64, 1))
            img[at_row(0, p + 4)] = jnp.where(half, pltpu.roll(lo, 64, 1), rc)
            img[at_row(1, p + 4)] = jnp.where(half, rc, hi)
    for z in range(8):
        rsc[z] = ref_ref[z].astype(F32).reshape(8, 8, 128)
    arr[...] = arr_ref[...]

    def chunk(n, carry):
        for m in range(CHUNK):
            e = n * CHUNK + m
            base = idx_ref[0, e] + idx_ref[4, e]
            sample_element(
                img, arr, base, idx_ref[1, e], idx_ref[2, e], idx_ref[3, e], idx_ref[5, e]
            )
        return carry

    lax.fori_loop(idx_ref[6, 0] // CHUNK, 128 // CHUNK, chunk, 0)

    lane = lax.broadcasted_iota(jnp.int32, (8, 128), 1)
    phase = lane & 15
    even = phase < 8
    even_next = (phase >= 1) & (phase <= 8)

    def interpolate(cx, square):
        wz, wx, wy = (jnp.broadcast_to(wgt[cx, c : c + 1], (8, 128)) for c in range(3))

        def pair(z, q):
            ev = arr[cx, z * 2 + q]
            od = arr[cx + 8, z * 2 + q]
            near = jnp.where(even, ev, od)
            far = pltpu.roll(jnp.where(even_next, ev, od), 127, 1)
            return near, far

        total = [None] * 3
        upper = [None] * 3
        prev = [pair(0, 0), pair(0, 1)]
        for z in range(8):
            cur = [pair(z + 1, 0), pair(z + 1, 1)]
            low, dzx, dx = [], [], []
            for y in range(2):
                d0 = cur[0][y] - prev[0][y]
                d1 = cur[1][y] - prev[1][y]
                l0 = prev[0][y] + wz * d0
                l1 = prev[1][y] + wz * d1
                dx.append(l1 - l0)
                low.append(l0 + wx * dx[y])
                dzx.append(d0 + wx * (d1 - d0))
            prev = cur
            slope_y = low[1] - low[0]
            value = low[0] + wy * slope_y
            slope_z = dzx[0] + wy * (dzx[1] - dzx[0])
            slope_x = dx[0] + wy * (dx[1] - dx[0])
            r = rsc[z, cx] - value
            rsc[z, cx] = r
            square = square + r * r
            for k, s in enumerate((slope_z, slope_x, slope_y)):
                slope_ref[k, z, cx] = s
                w = s * r
                u = w * ((z + 0.5) / 8.0)
                total[k] = w if z == 0 else total[k] + w
                upper[k] = u if z == 0 else upper[k] + u
        for k in range(3):
            gsc[2 * k, cx] = total[k] - upper[k]
            gsc[2 * k + 1, cx] = upper[k]
        return square

    sq_ref[...] = lax.fori_loop(0, 8, interpolate, jnp.zeros((8, 128), F32), unroll=4)
    res_ref[...] = rsc[...].reshape(8, 64, 128).astype(BF16)
    nodes = dot_left(dot_right(left_ref[...], gsc[...].reshape(384, 128)), wy_ref[...])
    node_ref[...] = nodes
    gx = lax.axis_index("gx")
    send_faces(send_ref, gx, nx, face_row(nodes[48:56]), face_row(nodes[56:64]))


def send_faces(send_ref, here, count, after, before):
    send_ref[...] = jnp.zeros(send_ref.shape, F32)

    @pl.when(here + 1 < count)
    def _():
        send_ref[here + 1] = after

    @pl.when(here > 0)
    def _():
        send_ref[here - 1] = before


def face_kernel(nx, ny, recv_ref, node_ref, sum_ref, send_ref):
    gx, gy = lax.axis_index("gx"), lax.axis_index("gy")
    sub = lax.broadcasted_iota(jnp.int32, (8, 128), 0)
    row_low = face_of(recv_ref[jnp.where(gx > 0, gx - 1, gx)])
    row_high = face_of(recv_ref[jnp.where(gx + 1 < nx, gx + 1, gx)])
    rows = []
    for kc in range(6):
        g = node_ref[kc * 8 : kc * 8 + 8]
        g = g + jnp.where(sub == 0, jnp.broadcast_to(row_low[kc : kc + 1], (8, 128)), 0.0)
        sum_ref[kc] = g
        rows.append(g)
    face = node_ref[48:56] + row_high
    sum_ref[6] = face
    send_faces(send_ref, gy, ny, column_row(rows, face, 16), column_row(rows, face, 0))


def product_kernel(
    nx, ny, recv_ref, node_ref, slope_ref, sq_ref, expand_ref, wyt_ref, left_ref, wy_ref, res_ref,
    grad_ref, hess_ref, send_ref, out_ref, msc, gsc, sem,
):
    copy_out = pltpu.make_async_copy(res_ref, out_ref, sem)
    copy_out.start()
    gx, gy = lax.axis_index("gx"), lax.axis_index("gy")
    lane = lax.broadcasted_iota(jnp.int32, (8, 128), 1)
    sub = lax.broadcasted_iota(jnp.int32, (8, 128), 0)

    def column(x, at):
        return jnp.broadcast_to(x[:, at : at + 1], (8, 128))

    keep_x = jnp.where(gx == nx - 1, 0.0, 1.0).astype(F32)
    keep_y = jnp.where(gy == ny - 1, 0.0, 1.0).astype(F32)
    keep_lane = jnp.where(lane == 16, keep_y, 1.0)
    col_low, edge_low = column_of(recv_ref[jnp.where(gy > 0, gy - 1, gy)])
    col_high, edge_high = column_of(recv_ref[jnp.where(gy + 1 < ny, gy + 1, gy)])
    grads = []
    square = jnp.zeros((8, 128), F32)
    for kc in range(6):
        g = node_ref[kc]
        g = g + jnp.where(lane == 0, column(col_low, kc), 0.0)
        g = g + jnp.where(lane == 16, column(col_high, kc), 0.0)
        g = g * keep_lane
        grads.append(g)
        grad_ref[kc] = g
        own_g = jnp.where(lane < 16, g, 0.0)
        square = square + own_g * own_g
    face = node_ref[6]
    face = face + jnp.where(lane == 0, column(edge_low, 0), 0.0)
    face = face + jnp.where(lane == 16, column(edge_high, 0), 0.0)
    face = jnp.where(sub < 6, face * keep_lane * keep_x, 0.0)
    full = jnp.concatenate(grads + [face, jnp.zeros((8, 128), F32)], axis=0)
    moved = dot_right(expand_ref[...], dot_left(full, wyt_ref[...]))
    msc[...] = moved.reshape(6, 8, 8, 128)

    def apply(cx, curve):
        m0 = [msc[2 * k, cx] for k in range(3)]
        dm = [msc[2 * k + 1, cx] - m0[k] for k in range(3)]
        total = [None] * 3
        upper = [None] * 3
        for z in range(8):
            sz = (z + 0.5) / 8.0
            s = [slope_ref[k, z, cx] for k in range(3)]
            along = s[0] * (m0[0] + sz * dm[0])
            for k in (1, 2):
                along = along + s[k] * (m0[k] + sz * dm[k])
            curve = curve + along * along
            for k in range(3):
                w = s[k] * along
                u = w * sz
                total[k] = w if z == 0 else total[k] + w
                upper[k] = u if z == 0 else upper[k] + u
        for k in range(3):
            gsc[2 * k, cx] = total[k] - upper[k]
            gsc[2 * k + 1, cx] = upper[k]
        return curve

    curve = lax.fori_loop(0, 8, apply, jnp.zeros((8, 128), F32), unroll=4)
    nodes = dot_left(dot_right(left_ref[...], gsc[...].reshape(384, 128)), wy_ref[...])
    rows = [nodes[kc * 8 : kc * 8 + 8] for kc in range(6)]
    for kc in range(6):
        hess_ref[kc] = rows[kc]
    high = face_row(nodes[48:56])
    spot = lane[:1]
    sums = jnp.where(spot == 104, jnp.sum(sq_ref[...]), 0.0)
    sums = jnp.where(spot == 105, jnp.sum(square), sums)
    sums = jnp.where(spot == 106, jnp.sum(curve) * (1.0 / 512.0), sums)
    send_ref[...] = jnp.broadcast_to(sums[None], send_ref.shape)

    @pl.when(gx + 1 < nx)
    def _():
        send_ref[gx + 1] = jnp.where(spot >= 104, sums, high)

    copy_out.wait()


def total_kernel(nx, ny, recv_ref, hess_ref, sum_ref, send_ref):
    gx, gy = lax.axis_index("gx"), lax.axis_index("gy")
    sub = lax.broadcasted_iota(jnp.int32, (8, 128), 0)
    spot = lax.broadcasted_iota(jnp.int32, (1, 128), 1)
    sums = jnp.where(spot >= 104, jnp.sum(recv_ref[...], axis=0), 0.0)
    row_low = face_of(recv_ref[jnp.where(gx > 0, gx - 1, gx)])
    row_low = jnp.where(gx > 0, row_low, 0.0)
    rows = []
    for kc in range(6):
        h = hess_ref[kc]
        h = h + jnp.where(sub == 0, jnp.broadcast_to(row_low[kc : kc + 1], (8, 128)), 0.0)
        sum_ref[kc] = h
        rows.append(h)
    col_high = column_row(rows, jnp.zeros((8, 128), F32), 16)
    send_ref[...] = jnp.broadcast_to(sums[None], send_ref.shape)

    @pl.when(gy + 1 < ny)
    def _():
        send_ref[gy + 1] = jnp.where(spot >= 104, sums, col_high)


def finish_kernel(nx, ny, voxels, recv_ref, grad_ref, hess_ref, step_ref, prod_ref, misfit_ref):
    gy = lax.axis_index("gy")
    lane = lax.broadcasted_iota(jnp.int32, (8, 128), 1)

    def column(x, at):
        return jnp.broadcast_to(x[:, at : at + 1], (8, 128))

    total = jnp.sum(recv_ref[...], axis=0)
    misfit_ref[...] = total[:, 104:105] * (1.0 / voxels)
    total = jnp.broadcast_to(total, (8, 128))
    alpha = column(total, 105) / column(total, 106)
    there = gy > 0
    col_low = column_of(recv_ref[jnp.where(there, gy - 1, gy)])[0]
    for kc in range(6):
        h = hess_ref[kc] + jnp.where(there & (lane == 0), column(col_low, kc), 0.0)
        prod_ref[kc // 2, kc % 2] = h[:, :16]
        step_ref[kc // 2, kc % 2] = (alpha * grad_ref[kc])[:, :16]


def swaps(count, first):
    pairs = [(i, i + 1) for i in range(first, count - 1, 2)]
    return pairs + [(j, i) for i, j in pairs]


def on_device(ref_image, def_image, shift_xy, shift_z, frac, connectivity):
    nx, ny = lax.axis_size("gx"), lax.axis_size("gy")
    peers = nx * ny
    sds = jax.ShapeDtypeStruct
    xa = lax.ppermute(def_image, "gx", swaps(nx, 0))
    xb = lax.ppermute(def_image, "gx", swaps(nx, 1))
    row = lax.broadcasted_iota(jnp.int32, (16, 128), 0)
    table = jnp.where(row == 10, shift_z[None], 0)
    table = table + jnp.pad(connectivity, ((0, 8), (0, 0))) + jnp.pad(shift_xy, ((8, 6), (0, 0)))
    idx, wgt, own = pl.pallas_call(
        index_kernel,
        out_shape=(sds((8, 128), jnp.int32), sds((8, 8, 128), F32), sds((8, 64, 128), BF16)),
        in_specs=[VMEM] * 3,
        out_specs=(VMEM,) * 3,
        compiler_params=PARAMS,
        cost_estimate=pl.CostEstimate(flops=300000, bytes_accessed=262144, transcendentals=0),
        name="order_elements",
    )(table, frac, def_image)
    packed = sds((4, SPAN, 128), BF16)
    to_b, to_a = pl.pallas_call(
        pack_kernel,
        out_shape=(packed, packed),
        in_specs=[VMEM] * 3,
        out_specs=(VMEM, VMEM),
        compiler_params=PARAMS,
        cost_estimate=pl.CostEstimate(flops=300000, bytes_accessed=524288, transcendentals=0),
        name="pack_halo",
    )(xb, own, xa)
    yb = lax.ppermute(to_b, "gy", swaps(ny, 1))
    ya = lax.ppermute(to_a, "gy", swaps(ny, 0))

    left, wy, expand, wyt = tables()
    arr = pl.pallas_call(
        early_kernel,
        out_shape=sds((16, 18, 8, 128), F32),
        in_specs=[SMEM] + [VMEM] * 3,
        out_specs=VMEM,
        scratch_shapes=[pltpu.VMEM((TILE_ROWS, 128), F32)],
        compiler_params=PARAMS,
        cost_estimate=pl.CostEstimate(flops=4000000, bytes_accessed=2000000, transcendentals=0),
        name="sample_early",
    )(idx, xb, own, xa)
    residual, slopes, nodes, send, square = pl.pallas_call(
        lambda *refs: late_kernel(nx, ny, *refs),
        out_shape=(
            sds((8, 64, 128), BF16),
            sds((3, 8, 8, 8, 128), F32),
            sds((64, 128), F32),
            sds((nx, 1, 128), F32),
            sds((8, 128), F32),
        ),
        in_specs=[SMEM] + [VMEM] * 10,
        out_specs=(VMEM,) * 5,
        scratch_shapes=[
            pltpu.VMEM((2 * TILE_ROWS, 128), F32),
            pltpu.VMEM((16, 18, 8, 128), F32),
            pltpu.VMEM((8, 8, 8, 128), F32),
            pltpu.VMEM((6, 8, 8, 128), F32),
        ],
        compiler_params=PARAMS,
        name="sample_and_gradient",
    )(idx, wgt, xb, own, xa, yb, ya, arr, ref_image, left, wy)
    recv = lax.all_to_all(send, "gx", 0, 0, tiled=True)
    nodes, send = pl.pallas_call(
        lambda *refs: face_kernel(nx, ny, *refs),
        out_shape=(sds((7, 8, 128), F32), sds((ny, 1, 128), F32)),
        in_specs=[VMEM] * 2,
        out_specs=(VMEM,) * 2,
        compiler_params=PARAMS,
        name="add_faces",
    )(recv, nodes)
    recv = lax.all_to_all(send, "gy", 0, 0, tiled=True)
    grads, hess, send, residual = pl.pallas_call(
        lambda *refs: product_kernel(nx, ny, *refs),
        out_shape=(
            sds((6, 8, 128), F32),
            sds((6, 8, 128), F32),
            sds((nx, 1, 128), F32),
            sds((8, 64, 128), BF16),
        ),
        in_specs=[VMEM] * 9,
        out_specs=(VMEM,) * 3 + (pl.BlockSpec(memory_space=pl.ANY),),
        scratch_shapes=[
            pltpu.VMEM((6, 8, 8, 128), F32),
            pltpu.VMEM((6, 8, 8, 128), F32),
            pltpu.SemaphoreType.DMA,
        ],
        compiler_params=PARAMS,
        name="gauss_newton_product",
    )(recv, nodes, slopes, square, expand, wyt, left, wy, residual)
    recv = lax.all_to_all(send, "gx", 0, 0, tiled=True)
    hess, send = pl.pallas_call(
        lambda *refs: total_kernel(nx, ny, *refs),
        out_shape=(sds((6, 8, 128), F32), sds((ny, 1, 128), F32)),
        in_specs=[VMEM] * 2,
        out_specs=(VMEM,) * 2,
        compiler_params=PARAMS,
        name="add_faces_and_sums",
    )(recv, hess)
    recv = lax.all_to_all(send, "gy", 0, 0, tiled=True)
    voxels = 8 * 64 * 128 * peers
    step, product, misfit = pl.pallas_call(
        lambda *refs: finish_kernel(nx, ny, voxels, *refs),
        out_shape=(sds((3, 2, 8, 16), F32), sds((3, 2, 8, 16), F32), sds((1, 1), F32)),
        in_specs=[VMEM] * 3,
        out_specs=(VMEM,) * 3,
        compiler_params=PARAMS,
        name="finish",
    )(recv, grads, hess)
    return (residual, step, product, misfit[0, 0])


def solution(mesh):
    in_specs = (
        P(None, "gx", "gy"),
        P(None, "gx", "gy"),
        P(None, ("gx", "gy")),
        P(("gx", "gy")),
        P(None, ("gx", "gy")),
        P(None, ("gx", "gy")),
    )
    out_specs = (P(None, "gx", "gy"), P(None, None, "gx", "gy"), P(None, None, "gx", "gy"), P())
    return jax.shard_map(
        on_device, mesh=mesh, in_specs=in_specs, out_specs=out_specs, check_vma=False
    )
```

```python
import jax
import jax.numpy as jnp
import numpy as np
from jax import lax
from jax.experimental import pallas as pl
from jax.experimental.pallas import tpu as pltpu
from jax.sharding import PartitionSpec as P

HALO = 64
F32 = jnp.float32
BF16 = jnp.bfloat16
SPAN = 192
TILE_ROWS = 12 * SPAN
CHUNK = 16
VMEM = pl.BlockSpec(memory_space=pltpu.VMEM)
SMEM = pl.BlockSpec(memory_space=pltpu.SMEM)
PARAMS = pltpu.CompilerParams(vmem_limit_bytes=24 * 1024 * 1024)


def node_weights(count):
    w = np.zeros((count + 1, 8 * count), np.float32)
    for v in range(8 * count):
        s = (v % 8 + 0.5) / 8.0
        w[v // 8, v] = 1.0 - s
        w[v // 8 + 1, v] = s
    return w


def tables():
    wx = node_weights(8)
    left = np.zeros((64, 6, 64), np.float32)
    for kc in range(6):
        left[kc * 8 : kc * 8 + 8, kc] = wx[:8]
        left[48 + kc, kc] = wx[8]
        left[56 + kc, kc] = wx[0]
    left = left.reshape(64, 384)
    expand = left.T.copy()
    expand[:, 56:] = 0.0
    wy = np.zeros((128, 128), np.float32)
    wy[:, :17] = node_weights(16).T
    as_bf = lambda a: jnp.asarray(a, BF16)
    return as_bf(left / 512.0), as_bf(wy), as_bf(expand), as_bf(wy.T)


def split(x):
    hi = x.astype(BF16)
    return hi, (x - hi.astype(F32)).astype(BF16)


def dot(a, b):
    return jnp.dot(a, b, preferred_element_type=F32)


def dot_right(w, x):
    hi, lo = split(x)
    return dot(w, hi) + dot(w, lo)


def dot_left(x, w):
    hi, lo = split(x)
    return dot(hi, w) + dot(lo, w)


def pack_rows(src, dst_a, dst_b, at, even):
    left = lax.broadcasted_iota(jnp.int32, (64, 128), 1) < 64
    for p in range(4):
        a = src[p].astype(F32)
        c = src[p + 4].astype(F32)
        right = jnp.where(left, pltpu.roll(a, 64, 1), c)
        other = jnp.where(left, a, pltpu.roll(c, 64, 1))
        dst_a[p, pl.ds(at, 64)] = jnp.where(even, right, other).astype(BF16)
        dst_b[p, pl.ds(at, 64)] = jnp.where(even, other, right).astype(BF16)


def dot_rows(a, b):
    return lax.dot_general(a, b, (((1,), (1,)), ((), ())), preferred_element_type=F32)


def as_rows(rows):
    sub = lax.broadcasted_iota(jnp.int32, (8, 128), 0)
    out = jnp.zeros((8, 128), F32)
    for n, row in enumerate(rows):
        out = jnp.where(sub == n, jnp.broadcast_to(row.astype(F32), (8, 128)), out)
    return out


def index_kernel(row_ref, frac_ref, own_ref, idx_ref, wgt_ref, keep_ref):
    keep_ref[...] = own_ref[...]
    first = row_ref[0:1]
    col_x = (first * 241) >> 12
    col_y = first - 17 * col_x
    start_x = 8 * col_x + row_ref[8:9] + HALO
    start_y = 8 * col_y + row_ref[9:10] + HALO
    early = (start_y >= 64) & (start_y < 184)
    below = start_y < 64
    offset = jnp.where(early, start_y - 64, jnp.where(below, start_y, start_y - 128))
    base = (row_ref[10:11] + 2) * SPAN + start_x
    tile = jnp.where(early | below, 0, TILE_ROWS)
    shift = (8 * col_y - offset) & 127
    place = (col_y & 1) * 8 + col_x
    width = jnp.where(early, 0, 9)
    flag = early.astype(F32)
    row = lax.broadcasted_iota(jnp.int32, (128, 128), 0)
    lane = lax.broadcasted_iota(jnp.int32, (128, 128), 1)
    upto = dot(as_rows([flag]).astype(BF16), (row <= lane).astype(F32).astype(BF16))[0:1]
    count = jnp.sum(flag, axis=1, keepdims=True)
    rank = jnp.where(early, upto - 1.0, count + lane[0:1].astype(F32) - upto)
    order = (jnp.broadcast_to(rank, (128, 128)) == row.astype(F32)).astype(F32).astype(BF16)
    hi, lo = split(as_rows([base, shift, place, 8 * col_y, tile, width]))
    table = dot_rows(hi, order) + dot_rows(lo, order)
    sub = lax.broadcasted_iota(jnp.int32, (8, 128), 0)
    table = jnp.where(sub == 6, jnp.broadcast_to(count, (8, 128)), table)
    idx_ref[...] = table.astype(jnp.int32)
    value = as_rows([frac_ref[c : c + 1] for c in range(3)])
    hi, lo = split(value)
    rest = (value - hi.astype(F32) - lo.astype(F32)).astype(BF16)
    element = jnp.broadcast_to(col_x * 16 + col_y, (128, 128))
    for cx in range(8):
        spread = (element == cx * 16 + (row >> 3)).astype(F32).astype(BF16)
        wgt_ref[cx] = dot_rows(hi, spread) + dot_rows(lo, spread) + dot_rows(rest, spread)


def pack_kernel(xb_ref, own_ref, xa_ref, b_ref, a_ref):
    even = lax.axis_index("gy") % 2 == 0
    for n, ref in enumerate((xa_ref, own_ref, xb_ref)):
        pack_rows(ref, a_ref, b_ref, 64 * n, even)


def over_sublanes(x):
    return jnp.sum(x, axis=0, keepdims=True)


def lanes_of(x, idx):
    return jnp.take_along_axis(x, idx & 127, axis=1, mode="promise_in_bounds")


def face_row(face):
    return over_sublanes(pltpu.roll(face, 0, 1, stride=17, stride_axis=0))


def face_of(row):
    lane = lax.broadcasted_iota(jnp.int32, (8, 128), 1)
    sub = lax.broadcasted_iota(jnp.int32, (8, 128), 0)
    back = lanes_of(jnp.broadcast_to(row, (8, 128)), lane + 17 * sub)
    return jnp.where((lane < 17) & (sub < 6), back, 0.0)


def column_row(rows, face, at):
    lane = lax.broadcasted_iota(jnp.int32, (8, 128), 1)
    block = jnp.zeros((8, 128), F32)
    for kc in range(6):
        block = jnp.where(lane == kc, jnp.broadcast_to(rows[kc][:, at : at + 1], (8, 128)), block)
    edge = jnp.where(lane == 64, jnp.broadcast_to(face[:, at : at + 1], (8, 128)), 0.0)
    block = pltpu.roll(block, 0, 1, stride=8, stride_axis=0)
    edge = pltpu.roll(edge, 0, 1, stride=1, stride_axis=0)
    return over_sublanes(block + edge)


def column_of(row):
    lane = lax.broadcasted_iota(jnp.int32, (8, 128), 1)
    sub = lax.broadcasted_iota(jnp.int32, (8, 128), 0)
    row = jnp.broadcast_to(row, (8, 128))
    return lanes_of(row, lane + 8 * sub), lanes_of(row, lane + 64 + sub)


def place_of_a():
    return pl.multiple_of(jnp.where(lax.axis_index("gx") % 2 == 1, 0, 128), 64)


def clear_outside(img, tiles):
    zero = jnp.zeros((2 * SPAN, 128), F32)
    for k in range(tiles):
        img[pl.ds(k * TILE_ROWS, 2 * SPAN)] = zero
        img[pl.ds(k * TILE_ROWS + 10 * SPAN, 2 * SPAN)] = zero


def sample_element(img, arr, base, shift, place, first, width):
    lane = lax.broadcasted_iota(jnp.int32, (8, 128), 1)
    mask = ((lane - first) & 127) < width
    for z in range(9):
        for q in range(2):
            v = img[pl.ds(base + (z * SPAN + q), 8), :]
            pltpu.store(arr.at[place, z * 2 + q], pltpu.roll(v, shift, 1), mask=mask)


def early_kernel(idx_ref, xb_ref, own_ref, xa_ref, arr_ref, img):
    clear_outside(img, 1)
    at_a = place_of_a()
    for z in range(8):
        for ref, row in ((xa_ref, at_a), (own_ref, 64), (xb_ref, 128 - at_a)):
            img[pl.ds(pl.multiple_of((z + 2) * SPAN + row, 8), 64)] = ref[z].astype(F32)

    def chunk(n, carry):
        for m in range(CHUNK):
            e = n * CHUNK + m
            sample_element(
                img, arr_ref, idx_ref[0, e], idx_ref[1, e], idx_ref[2, e], idx_ref[3, e], 9
            )
        return carry

    lax.fori_loop(0, (idx_ref[6, 0] + (CHUNK - 1)) // CHUNK, chunk, 0)


def late_kernel(
    nx, ny, idx_ref, wgt, xb_ref, own_ref, xa_ref, yb_ref, ya_ref, arr_ref, ref_ref,
    left_ref, wy_ref, res_ref, slope_ref, node_ref, b_ref, a_ref, sq_ref, img, arr, rsc, gsc,
):
    half = lax.broadcasted_iota(jnp.int32, (64, 128), 1) < 64
    clear_outside(img, 2)
    odd_y = lax.axis_index("gy") % 2 == 1
    at_a = place_of_a()
    segments = (
        (xa_ref, 0, at_a),
        (own_ref, 64, 64),
        (xb_ref, 128, 128 - at_a),
    )
    for p in range(4):
        for ref, at, row in segments:
            ra = pltpu.roll(ref[p].astype(F32), 64, 1)
            rc = pltpu.roll(ref[p + 4].astype(F32), 64, 1)
            from_a = ya_ref[p, pl.ds(at, 64)].astype(F32)
            from_b = yb_ref[p, pl.ds(at, 64)].astype(F32)
            lo = jnp.where(odd_y, from_a, from_b)
            hi = jnp.where(odd_y, from_b, from_a)
            at_row = lambda k, q: pl.ds(pl.multiple_of(k * TILE_ROWS + (q + 2) * SPAN + row, 8), 64)
            img[at_row(0, p)] = jnp.where(half, lo, ra)
            img[at_row(1, p)] = jnp.where(half, ra, pltpu.roll(hi, 64, 1))
            img[at_row(0, p + 4)] = jnp.where(half, pltpu.roll(lo, 64, 1), rc)
            img[at_row(1, p + 4)] = jnp.where(half, rc, hi)
    for z in range(8):
        rsc[z] = ref_ref[z].astype(F32).reshape(8, 8, 128)
    arr[...] = arr_ref[...]

    def chunk(n, carry):
        for m in range(CHUNK):
            e = n * CHUNK + m
            base = idx_ref[0, e] + idx_ref[4, e]
            sample_element(
                img, arr, base, idx_ref[1, e], idx_ref[2, e], idx_ref[3, e], idx_ref[5, e]
            )
        return carry

    lax.fori_loop(idx_ref[6, 0] // CHUNK, 128 // CHUNK, chunk, 0)

    lane = lax.broadcasted_iota(jnp.int32, (8, 128), 1)
    phase = lane & 15
    even = phase < 8
    even_next = (phase >= 1) & (phase <= 8)

    def interpolate(cx, square):
        wz, wx, wy = (jnp.broadcast_to(wgt[cx, c : c + 1], (8, 128)) for c in range(3))

        def pair(z, q):
            ev = arr[cx, z * 2 + q]
            od = arr[cx + 8, z * 2 + q]
            near = jnp.where(even, ev, od)
            far = pltpu.roll(jnp.where(even_next, ev, od), 127, 1)
            return near, far

        total = [None] * 3
        upper = [None] * 3
        prev = [pair(0, 0), pair(0, 1)]
        for z in range(8):
            cur = [pair(z + 1, 0), pair(z + 1, 1)]
            low, dzx, dx = [], [], []
            for y in range(2):
                d0 = cur[0][y] - prev[0][y]
                d1 = cur[1][y] - prev[1][y]
                l0 = prev[0][y] + wz * d0
                l1 = prev[1][y] + wz * d1
                dx.append(l1 - l0)
                low.append(l0 + wx * dx[y])
                dzx.append(d0 + wx * (d1 - d0))
            prev = cur
            slope_y = low[1] - low[0]
            value = low[0] + wy * slope_y
            slope_z = dzx[0] + wy * (dzx[1] - dzx[0])
            slope_x = dx[0] + wy * (dx[1] - dx[0])
            r = rsc[z, cx] - value
            rsc[z, cx] = r
            square = square + r * r
            for k, s in enumerate((slope_z, slope_x, slope_y)):
                slope_ref[k, z, cx] = s
                w = s * r
                u = w * ((z + 0.5) / 8.0)
                total[k] = w if z == 0 else total[k] + w
                upper[k] = u if z == 0 else upper[k] + u
        for k in range(3):
            gsc[2 * k, cx] = total[k] - upper[k]
            gsc[2 * k + 1, cx] = upper[k]
        return square

    sq_ref[...] = lax.fori_loop(0, 8, interpolate, jnp.zeros((8, 128), F32), unroll=4)
    res_ref[...] = rsc[...].reshape(8, 64, 128).astype(BF16)
    nodes = dot_left(dot_right(left_ref[...], gsc[...].reshape(384, 128)), wy_ref[...])
    node_ref[...] = nodes
    send_pairs(a_ref, b_ref, "gx", face_row(nodes[48:56]), face_row(nodes[56:64]))


def send_pairs(a_ref, b_ref, axis, after, before):
    even = lax.axis_index(axis) % 2 == 0
    a_ref[...] = jnp.where(even, after, before)
    b_ref[...] = jnp.where(even, before, after)


def from_pairs(a_ref, b_ref, axis):
    even = lax.axis_index(axis) % 2 == 0
    a, b = a_ref[...], b_ref[...]
    return jnp.where(even, b, a), jnp.where(even, a, b)


def face_kernel(xb_ref, xa_ref, node_ref, sum_ref, b_ref, a_ref):
    sub = lax.broadcasted_iota(jnp.int32, (8, 128), 0)
    row_low, row_high = (face_of(row) for row in from_pairs(xa_ref, xb_ref, "gx"))
    rows = []
    for kc in range(6):
        g = node_ref[kc * 8 : kc * 8 + 8]
        g = g + jnp.where(sub == 0, jnp.broadcast_to(row_low[kc : kc + 1], (8, 128)), 0.0)
        sum_ref[kc] = g
        rows.append(g)
    face = node_ref[48:56] + row_high
    sum_ref[6] = face
    send_pairs(a_ref, b_ref, "gy", column_row(rows, face, 16), column_row(rows, face, 0))


def product_kernel(
    nx, ny, yb_ref, ya_ref, node_ref, slope_ref, sq_ref, expand_ref, wyt_ref, left_ref, wy_ref, res_ref,
    grad_ref, hess_ref, send_ref, out_ref, msc, gsc, sem,
):
    copy_out = pltpu.make_async_copy(res_ref, out_ref, sem)
    copy_out.start()
    gx, gy = lax.axis_index("gx"), lax.axis_index("gy")
    lane = lax.broadcasted_iota(jnp.int32, (8, 128), 1)
    sub = lax.broadcasted_iota(jnp.int32, (8, 128), 0)

    def column(x, at):
        return jnp.broadcast_to(x[:, at : at + 1], (8, 128))

    keep_x = jnp.where(gx == nx - 1, 0.0, 1.0).astype(F32)
    keep_y = jnp.where(gy == ny - 1, 0.0, 1.0).astype(F32)
    keep_lane = jnp.where(lane == 16, keep_y, 1.0)
    before, after = from_pairs(ya_ref, yb_ref, "gy")
    col_low, edge_low = column_of(before)
    col_high, edge_high = column_of(after)
    grads = []
    square = jnp.zeros((8, 128), F32)
    for kc in range(6):
        g = node_ref[kc]
        g = g + jnp.where(lane == 0, column(col_low, kc), 0.0)
        g = g + jnp.where(lane == 16, column(col_high, kc), 0.0)
        g = g * keep_lane
        grads.append(g)
        grad_ref[kc] = g
        own_g = jnp.where(lane < 16, g, 0.0)
        square = square + own_g * own_g
    face = node_ref[6]
    face = face + jnp.where(lane == 0, column(edge_low, 0), 0.0)
    face = face + jnp.where(lane == 16, column(edge_high, 0), 0.0)
    face = jnp.where(sub < 6, face * keep_lane * keep_x, 0.0)
    full = jnp.concatenate(grads + [face, jnp.zeros((8, 128), F32)], axis=0)
    moved = dot_right(expand_ref[...], dot_left(full, wyt_ref[...]))
    msc[...] = moved.reshape(6, 8, 8, 128)

    def apply(cx, curve):
        m0 = [msc[2 * k, cx] for k in range(3)]
        dm = [msc[2 * k + 1, cx] - m0[k] for k in range(3)]
        total = [None] * 3
        upper = [None] * 3
        for z in range(8):
            sz = (z + 0.5) / 8.0
            s = [slope_ref[k, z, cx] for k in range(3)]
            along = s[0] * (m0[0] + sz * dm[0])
            for k in (1, 2):
                along = along + s[k] * (m0[k] + sz * dm[k])
            curve = curve + along * along
            for k in range(3):
                w = s[k] * along
                u = w * sz
                total[k] = w if z == 0 else total[k] + w
                upper[k] = u if z == 0 else upper[k] + u
        for k in range(3):
            gsc[2 * k, cx] = total[k] - upper[k]
            gsc[2 * k + 1, cx] = upper[k]
        return curve

    curve = lax.fori_loop(0, 8, apply, jnp.zeros((8, 128), F32), unroll=4)
    nodes = dot_left(dot_right(left_ref[...], gsc[...].reshape(384, 128)), wy_ref[...])
    rows = [nodes[kc * 8 : kc * 8 + 8] for kc in range(6)]
    for kc in range(6):
        hess_ref[kc] = rows[kc]
    col_high = column_row(rows, nodes[48:56], 16)
    high = face_row(nodes[48:56])
    spot = lane[:1]
    sums = jnp.where(spot == 104, jnp.sum(sq_ref[...]), 0.0)
    sums = jnp.where(spot == 105, jnp.sum(square), sums)
    sums = jnp.where(spot == 106, jnp.sum(curve) * (1.0 / 512.0), sums)
    tail = spot >= 104
    send_ref[...] = jnp.broadcast_to(sums[None], send_ref.shape)
    for dx, dy, data in ((1, 0, high), (1, 1, high), (0, 1, col_high)):
        px, py = gx + dx, gy + dy

        @pl.when((px < nx) & (py < ny))
        def _():
            send_ref[px * ny + py] = jnp.where(tail, sums, data)

    copy_out.wait()


def finish_kernel(nx, ny, voxels, recv_ref, grad_ref, hess_ref, step_ref, prod_ref, misfit_ref):
    gx, gy = lax.axis_index("gx"), lax.axis_index("gy")
    own = gx * ny + gy
    lane = lax.broadcasted_iota(jnp.int32, (8, 128), 1)
    sub = lax.broadcasted_iota(jnp.int32, (8, 128), 0)

    def block(dx, dy):
        px, py = gx + dx, gy + dy
        there = (px >= 0) & (py >= 0)
        data = recv_ref[jnp.where(there, px * ny + py, own)]
        return jnp.where(there, data, 0.0)

    def column(x, at):
        return jnp.broadcast_to(x[:, at : at + 1], (8, 128))

    total = jnp.sum(recv_ref[...], axis=0)
    misfit_ref[...] = total[:, 104:105] * (1.0 / voxels)
    total = jnp.broadcast_to(total, (8, 128))
    alpha = column(total, 105) / column(total, 106)
    row_low = face_of(block(-1, 0)) + jnp.where(lane == 0, column(face_of(block(-1, -1)), 16), 0.0)
    col_low = column_of(block(0, -1))[0]
    for kc in range(6):
        h = hess_ref[kc]
        h = h + jnp.where(sub == 0, jnp.broadcast_to(row_low[kc : kc + 1], (8, 128)), 0.0)
        h = h + jnp.where(lane == 0, column(col_low, kc), 0.0)
        prod_ref[kc // 2, kc % 2] = h[:, :16]
        step_ref[kc // 2, kc % 2] = (alpha * grad_ref[kc])[:, :16]


def swaps(count, first):
    pairs = [(i, i + 1) for i in range(first, count - 1, 2)]
    return pairs + [(j, i) for i, j in pairs]


def on_device(ref_image, def_image, shift_xy, shift_z, frac, connectivity):
    nx, ny = lax.axis_size("gx"), lax.axis_size("gy")
    peers = nx * ny
    sds = jax.ShapeDtypeStruct
    xa = lax.ppermute(def_image, "gx", swaps(nx, 0))
    xb = lax.ppermute(def_image, "gx", swaps(nx, 1))
    row = lax.broadcasted_iota(jnp.int32, (16, 128), 0)
    table = jnp.where(row == 10, shift_z[None], 0)
    table = table + jnp.pad(connectivity, ((0, 8), (0, 0))) + jnp.pad(shift_xy, ((8, 6), (0, 0)))
    idx, wgt, own = pl.pallas_call(
        index_kernel,
        out_shape=(sds((8, 128), jnp.int32), sds((8, 8, 128), F32), sds((8, 64, 128), BF16)),
        in_specs=[VMEM] * 3,
        out_specs=(VMEM,) * 3,
        compiler_params=PARAMS,
        cost_estimate=pl.CostEstimate(flops=300000, bytes_accessed=262144, transcendentals=0),
        name="order_elements",
    )(table, frac, def_image)
    packed = sds((4, SPAN, 128), BF16)
    to_b, to_a = pl.pallas_call(
        pack_kernel,
        out_shape=(packed, packed),
        in_specs=[VMEM] * 3,
        out_specs=(VMEM, VMEM),
        compiler_params=PARAMS,
        cost_estimate=pl.CostEstimate(flops=300000, bytes_accessed=524288, transcendentals=0),
        name="pack_halo",
    )(xb, own, xa)
    yb = lax.ppermute(to_b, "gy", swaps(ny, 1))
    ya = lax.ppermute(to_a, "gy", swaps(ny, 0))

    left, wy, expand, wyt = tables()
    arr = pl.pallas_call(
        early_kernel,
        out_shape=sds((16, 18, 8, 128), F32),
        in_specs=[SMEM] + [VMEM] * 3,
        out_specs=VMEM,
        scratch_shapes=[pltpu.VMEM((TILE_ROWS, 128), F32)],
        compiler_params=PARAMS,
        cost_estimate=pl.CostEstimate(flops=4000000, bytes_accessed=2000000, transcendentals=0),
        name="sample_early",
    )(idx, xb, own, xa)
    residual, slopes, nodes, to_b, to_a, square = pl.pallas_call(
        lambda *refs: late_kernel(nx, ny, *refs),
        out_shape=(
            sds((8, 64, 128), BF16),
            sds((3, 8, 8, 8, 128), F32),
            sds((64, 128), F32),
            sds((1, 128), F32),
            sds((1, 128), F32),
            sds((8, 128), F32),
        ),
        in_specs=[SMEM] + [VMEM] * 10,
        out_specs=(VMEM,) * 6,
        scratch_shapes=[
            pltpu.VMEM((2 * TILE_ROWS, 128), F32),
            pltpu.VMEM((16, 18, 8, 128), F32),
            pltpu.VMEM((8, 8, 8, 128), F32),
            pltpu.VMEM((6, 8, 8, 128), F32),
        ],
        compiler_params=PARAMS,
        name="sample_and_gradient",
    )(idx, wgt, xb, own, xa, yb, ya, arr, ref_image, left, wy)
    xa = lax.ppermute(to_a, "gx", swaps(nx, 0))
    xb = lax.ppermute(to_b, "gx", swaps(nx, 1))
    line = sds((1, 128), F32)
    nodes, to_b, to_a = pl.pallas_call(
        face_kernel,
        out_shape=(sds((7, 8, 128), F32), line, line),
        in_specs=[VMEM] * 3,
        out_specs=(VMEM,) * 3,
        compiler_params=PARAMS,
        name="add_faces",
    )(xb, xa, nodes)
    yb = lax.ppermute(to_b, "gy", swaps(ny, 1))
    ya = lax.ppermute(to_a, "gy", swaps(ny, 0))
    grads, hess, send, residual = pl.pallas_call(
        lambda *refs: product_kernel(nx, ny, *refs),
        out_shape=(
            sds((6, 8, 128), F32),
            sds((6, 8, 128), F32),
            sds((peers, 1, 128), F32),
            sds((8, 64, 128), BF16),
        ),
        in_specs=[VMEM] * 10,
        out_specs=(VMEM,) * 3 + (pl.BlockSpec(memory_space=pl.ANY),),
        scratch_shapes=[
            pltpu.VMEM((6, 8, 8, 128), F32),
            pltpu.VMEM((6, 8, 8, 128), F32),
            pltpu.SemaphoreType.DMA,
        ],
        compiler_params=PARAMS,
        name="gauss_newton_product",
    )(yb, ya, nodes, slopes, square, expand, wyt, left, wy, residual)
    recv = lax.all_to_all(send, ("gx", "gy"), 0, 0, tiled=True)
    voxels = 8 * 64 * 128 * peers
    step, product, misfit = pl.pallas_call(
        lambda *refs: finish_kernel(nx, ny, voxels, *refs),
        out_shape=(sds((3, 2, 8, 16), F32), sds((3, 2, 8, 16), F32), sds((1, 1), F32)),
        in_specs=[VMEM] * 3,
        out_specs=(VMEM,) * 3,
        compiler_params=PARAMS,
        name="finish",
    )(recv, grads, hess)
    return (residual, step, product, misfit[0, 0])


def solution(mesh):
    in_specs = (
        P(None, "gx", "gy"),
        P(None, "gx", "gy"),
        P(None, ("gx", "gy")),
        P(("gx", "gy")),
        P(None, ("gx", "gy")),
        P(None, ("gx", "gy")),
    )
    out_specs = (P(None, "gx", "gy"), P(None, None, "gx", "gy"), P(None, None, "gx", "gy"), P())
    return jax.shard_map(
        on_device, mesh=mesh, in_specs=in_specs, out_specs=out_specs, check_vma=False
    )
```

```python
import jax
import jax.numpy as jnp
import numpy as np
from jax import lax
from jax.experimental import pallas as pl
from jax.experimental.pallas import tpu as pltpu
from jax.sharding import PartitionSpec as P

HALO = 64
F32 = jnp.float32
BF16 = jnp.bfloat16
SPAN = 192
TILE_ROWS = 12 * SPAN
CHUNK = 16
VMEM = pl.BlockSpec(memory_space=pltpu.VMEM)
SMEM = pl.BlockSpec(memory_space=pltpu.SMEM)
PARAMS = pltpu.CompilerParams(vmem_limit_bytes=24 * 1024 * 1024)


def node_weights(count):
    w = np.zeros((count + 1, 8 * count), np.float32)
    for v in range(8 * count):
        s = (v % 8 + 0.5) / 8.0
        w[v // 8, v] = 1.0 - s
        w[v // 8 + 1, v] = s
    return w


def tables():
    wx = node_weights(8)
    left = np.zeros((64, 6, 64), np.float32)
    for kc in range(6):
        left[kc * 8 : kc * 8 + 8, kc] = wx[:8]
        left[48 + kc, kc] = wx[8]
        left[56 + kc, kc] = wx[0]
    left = left.reshape(64, 384)
    expand = left.T.copy()
    expand[:, 56:] = 0.0
    wy = np.zeros((128, 128), np.float32)
    wy[:, :17] = node_weights(16).T
    as_bf = lambda a: jnp.asarray(a, BF16)
    return as_bf(left / 512.0), as_bf(wy), as_bf(expand), as_bf(wy.T)


def split(x):
    hi = x.astype(BF16)
    return hi, (x - hi.astype(F32)).astype(BF16)


def dot(a, b):
    return jnp.dot(a, b, preferred_element_type=F32)


def dot_right(w, x):
    hi, lo = split(x)
    return dot(w, hi) + dot(w, lo)


def dot_left(x, w):
    hi, lo = split(x)
    return dot(hi, w) + dot(lo, w)


def pack_rows(src, dst_a, dst_b, at, even):
    left = lax.broadcasted_iota(jnp.int32, (64, 128), 1) < 64
    for p in range(4):
        a = src[p].astype(F32)
        c = src[p + 4].astype(F32)
        right = jnp.where(left, pltpu.roll(a, 64, 1), c)
        other = jnp.where(left, a, pltpu.roll(c, 64, 1))
        dst_a[p, pl.ds(at, 64)] = jnp.where(even, right, other).astype(BF16)
        dst_b[p, pl.ds(at, 64)] = jnp.where(even, other, right).astype(BF16)


def dot_rows(a, b):
    return lax.dot_general(a, b, (((1,), (1,)), ((), ())), preferred_element_type=F32)


def as_rows(rows):
    sub = lax.broadcasted_iota(jnp.int32, (8, 128), 0)
    out = jnp.zeros((8, 128), F32)
    for n, row in enumerate(rows):
        out = jnp.where(sub == n, jnp.broadcast_to(row.astype(F32), (8, 128)), out)
    return out


def index_kernel(row_ref, frac_ref, own_ref, idx_ref, wgt_ref, keep_ref):
    keep_ref[...] = own_ref[...]
    first = row_ref[0:1]
    col_x = (first * 241) >> 12
    col_y = first - 17 * col_x
    start_x = 8 * col_x + row_ref[8:9] + HALO
    start_y = 8 * col_y + row_ref[9:10] + HALO
    early = (start_y >= 64) & (start_y < 184)
    below = start_y < 64
    offset = jnp.where(early, start_y - 64, jnp.where(below, start_y, start_y - 128))
    base = (row_ref[10:11] + 2) * SPAN + start_x
    tile = jnp.where(early | below, 0, TILE_ROWS)
    shift = (8 * col_y - offset) & 127
    place = (col_y & 1) * 8 + col_x
    width = jnp.where(early, 0, 9)
    flag = early.astype(F32)
    row = lax.broadcasted_iota(jnp.int32, (128, 128), 0)
    lane = lax.broadcasted_iota(jnp.int32, (128, 128), 1)
    upto = dot(as_rows([flag]).astype(BF16), (row <= lane).astype(F32).astype(BF16))[0:1]
    count = jnp.sum(flag, axis=1, keepdims=True)
    rank = jnp.where(early, upto - 1.0, count + lane[0:1].astype(F32) - upto)
    order = (jnp.broadcast_to(rank, (128, 128)) == row.astype(F32)).astype(F32).astype(BF16)
    hi, lo = split(as_rows([base, shift, place, 8 * col_y, tile, width]))
    table = dot_rows(hi, order) + dot_rows(lo, order)
    sub = lax.broadcasted_iota(jnp.int32, (8, 128), 0)
    table = jnp.where(sub == 6, jnp.broadcast_to(count, (8, 128)), table)
    idx_ref[...] = table.astype(jnp.int32)
    value = as_rows([frac_ref[c : c + 1] for c in range(3)])
    hi, lo = split(value)
    rest = (value - hi.astype(F32) - lo.astype(F32)).astype(BF16)
    element = jnp.broadcast_to(col_x * 16 + col_y, (128, 128))
    for cx in range(8):
        spread = (element == cx * 16 + (row >> 3)).astype(F32).astype(BF16)
        wgt_ref[cx] = dot_rows(hi, spread) + dot_rows(lo, spread) + dot_rows(rest, spread)


def pack_kernel(xb_ref, own_ref, xa_ref, b_ref, a_ref):
    even = lax.axis_index("gy") % 2 == 0
    for n, ref in enumerate((xa_ref, own_ref, xb_ref)):
        pack_rows(ref, a_ref, b_ref, 64 * n, even)


def over_sublanes(x):
    return jnp.sum(x, axis=0, keepdims=True)


def lanes_of(x, idx):
    return jnp.take_along_axis(x, idx & 127, axis=1, mode="promise_in_bounds")


def face_row(face):
    return over_sublanes(pltpu.roll(face, 0, 1, stride=17, stride_axis=0))


def face_of(row):
    lane = lax.broadcasted_iota(jnp.int32, (8, 128), 1)
    sub = lax.broadcasted_iota(jnp.int32, (8, 128), 0)
    back = lanes_of(jnp.broadcast_to(row, (8, 128)), lane + 17 * sub)
    return jnp.where((lane < 17) & (sub < 6), back, 0.0)


def column_row(rows, face, at):
    lane = lax.broadcasted_iota(jnp.int32, (8, 128), 1)
    block = jnp.zeros((8, 128), F32)
    for kc in range(6):
        block = jnp.where(lane == kc, jnp.broadcast_to(rows[kc][:, at : at + 1], (8, 128)), block)
    edge = jnp.where(lane == 64, jnp.broadcast_to(face[:, at : at + 1], (8, 128)), 0.0)
    block = pltpu.roll(block, 0, 1, stride=8, stride_axis=0)
    edge = pltpu.roll(edge, 0, 1, stride=1, stride_axis=0)
    return over_sublanes(block + edge)


def column_of(row):
    lane = lax.broadcasted_iota(jnp.int32, (8, 128), 1)
    sub = lax.broadcasted_iota(jnp.int32, (8, 128), 0)
    row = jnp.broadcast_to(row, (8, 128))
    return lanes_of(row, lane + 8 * sub), lanes_of(row, lane + 64 + sub)


def place_of_a():
    return pl.multiple_of(jnp.where(lax.axis_index("gx") % 2 == 1, 0, 128), 64)


def clear_outside(img, tiles):
    zero = jnp.zeros((2 * SPAN, 128), F32)
    for k in range(tiles):
        img[pl.ds(k * TILE_ROWS, 2 * SPAN)] = zero
        img[pl.ds(k * TILE_ROWS + 10 * SPAN, 2 * SPAN)] = zero


def sample_element(img, arr, base, shift, place, first, width):
    lane = lax.broadcasted_iota(jnp.int32, (8, 128), 1)
    mask = ((lane - first) & 127) < width
    starts = [pl.ds(base + z * SPAN, 8) for z in range(9)]
    starts += [pl.ds(base + 8, 8, stride=SPAN), pl.ds(base + (8 * SPAN + 8), 8)]
    for n, start in enumerate(starts):
        pltpu.store(arr.at[place, n], pltpu.roll(img[start, :], shift, 1), mask=mask)


def early_kernel(idx_ref, xb_ref, own_ref, xa_ref, arr_ref, img):
    clear_outside(img, 1)
    at_a = place_of_a()
    for z in range(8):
        for ref, row in ((xa_ref, at_a), (own_ref, 64), (xb_ref, 128 - at_a)):
            img[pl.ds(pl.multiple_of((z + 2) * SPAN + row, 8), 64)] = ref[z].astype(F32)

    def chunk(n, carry):
        for m in range(CHUNK):
            e = n * CHUNK + m
            sample_element(
                img, arr_ref, idx_ref[0, e], idx_ref[1, e], idx_ref[2, e], idx_ref[3, e], 9
            )
        return carry

    lax.fori_loop(0, (idx_ref[6, 0] + (CHUNK - 1)) // CHUNK, chunk, 0)


def late_kernel(
    nx, ny, idx_ref, wgt, xb_ref, own_ref, xa_ref, yb_ref, ya_ref, arr_ref, ref_ref,
    left_ref, wy_ref, res_ref, slope_ref, node_ref, send_ref, sq_ref, img, arr, rsc, gsc,
):
    half = lax.broadcasted_iota(jnp.int32, (64, 128), 1) < 64
    clear_outside(img, 2)
    odd_y = lax.axis_index("gy") % 2 == 1
    at_a = place_of_a()
    segments = (
        (xa_ref, 0, at_a),
        (own_ref, 64, 64),
        (xb_ref, 128, 128 - at_a),
    )
    for p in range(4):
        for ref, at, row in segments:
            ra = pltpu.roll(ref[p].astype(F32), 64, 1)
            rc = pltpu.roll(ref[p + 4].astype(F32), 64, 1)
            from_a = ya_ref[p, pl.ds(at, 64)].astype(F32)
            from_b = yb_ref[p, pl.ds(at, 64)].astype(F32)
            lo = jnp.where(odd_y, from_a, from_b)
            hi = jnp.where(odd_y, from_b, from_a)
            at_row = lambda k, q: pl.ds(pl.multiple_of(k * TILE_ROWS + (q + 2) * SPAN + row, 8), 64)
            img[at_row(0, p)] = jnp.where(half, lo, ra)
            img[at_row(1, p)] = jnp.where(half, ra, pltpu.roll(hi, 64, 1))
            img[at_row(0, p + 4)] = jnp.where(half, pltpu.roll(lo, 64, 1), rc)
            img[at_row(1, p + 4)] = jnp.where(half, rc, hi)
    for z in range(8):
        rsc[z] = ref_ref[z].astype(F32).reshape(8, 8, 128)
    arr[...] = arr_ref[...]

    def chunk(n, carry):
        for m in range(CHUNK):
            e = n * CHUNK + m
            base = idx_ref[0, e] + idx_ref[4, e]
            sample_element(
                img, arr, base, idx_ref[1, e], idx_ref[2, e], idx_ref[3, e], idx_ref[5, e]
            )
        return carry

    lax.fori_loop(idx_ref[6, 0] // CHUNK, 128 // CHUNK, chunk, 0)

    lane = lax.broadcasted_iota(jnp.int32, (8, 128), 1)
    sub = lax.broadcasted_iota(jnp.int32, (8, 128), 0)
    phase = lane & 15
    even = phase < 8
    even_next = (phase >= 1) & (phase <= 8)

    def interpolate(cx, square):
        wz, wx, wy = (jnp.broadcast_to(wgt[cx, c : c + 1], (8, 128)) for c in range(3))

        def pair(n):
            ev = arr[cx, n]
            od = arr[cx + 8, n]
            near = jnp.where(even, ev, od)
            return near, pltpu.roll(jnp.where(even_next, ev, od), 127, 1)

        edge, corner = pair(9), pair(10)

        def both_rows(z):
            here = pair(z)
            last = [corner[y][0:1] if z == 8 else edge[y][z : z + 1] for y in range(2)]
            after = [
                jnp.where(sub == 7, jnp.broadcast_to(last[y], (8, 128)), pltpu.roll(here[y], 7, 0))
                for y in range(2)
            ]
            return here, after

        total = [None] * 3
        upper = [None] * 3
        prev = both_rows(0)
        for z in range(8):
            cur = both_rows(z + 1)
            low, dzx, dx = [], [], []
            for y in range(2):
                d0 = cur[0][y] - prev[0][y]
                d1 = cur[1][y] - prev[1][y]
                l0 = prev[0][y] + wz * d0
                l1 = prev[1][y] + wz * d1
                dx.append(l1 - l0)
                low.append(l0 + wx * dx[y])
                dzx.append(d0 + wx * (d1 - d0))
            prev = cur
            slope_y = low[1] - low[0]
            value = low[0] + wy * slope_y
            slope_z = dzx[0] + wy * (dzx[1] - dzx[0])
            slope_x = dx[0] + wy * (dx[1] - dx[0])
            r = rsc[z, cx] - value
            rsc[z, cx] = r
            square = square + r * r
            for k, s in enumerate((slope_z, slope_x, slope_y)):
                slope_ref[k, z, cx] = s
                w = s * r
                u = w * ((z + 0.5) / 8.0)
                total[k] = w if z == 0 else total[k] + w
                upper[k] = u if z == 0 else upper[k] + u
        for k in range(3):
            gsc[2 * k, cx] = total[k] - upper[k]
            gsc[2 * k + 1, cx] = upper[k]
        return square

    sq_ref[...] = lax.fori_loop(0, 8, interpolate, jnp.zeros((8, 128), F32), unroll=4)
    res_ref[...] = rsc[...].reshape(8, 64, 128).astype(BF16)
    nodes = dot_left(dot_right(left_ref[...], gsc[...].reshape(384, 128)), wy_ref[...])
    node_ref[...] = nodes
    rows = [nodes[kc * 8 : kc * 8 + 8] for kc in range(6)]
    high, low = nodes[48:56], nodes[56:64]
    col_high = column_row(rows, high, 16)
    col_low = column_row(rows, high, 0)
    high, low = face_row(high), face_row(low)
    gx, gy = lax.axis_index("gx"), lax.axis_index("gy")
    send_ref[...] = jnp.zeros(send_ref.shape, F32)
    for dx in (-1, 0, 1):
        for dy in (-1, 0, 1):
            if dx == 0 and dy == 0:
                continue
            block = high if dx == 1 else low if dx == -1 else col_high if dy == 1 else col_low
            px, py = gx + dx, gy + dy

            @pl.when((px >= 0) & (px < nx) & (py >= 0) & (py < ny))
            def _():
                send_ref[px * ny + py] = block


def product_kernel(
    nx, ny, recv_ref, node_ref, slope_ref, sq_ref, expand_ref, wyt_ref, left_ref, wy_ref, res_ref,
    grad_ref, hess_ref, send_ref, out_ref, msc, gsc, sem,
):
    copy_out = pltpu.make_async_copy(res_ref, out_ref, sem)
    copy_out.start()
    gx, gy = lax.axis_index("gx"), lax.axis_index("gy")
    own = gx * ny + gy
    lane = lax.broadcasted_iota(jnp.int32, (8, 128), 1)
    sub = lax.broadcasted_iota(jnp.int32, (8, 128), 0)

    def block(dx, dy):
        px, py = gx + dx, gy + dy
        there = (px >= 0) & (px < nx) & (py >= 0) & (py < ny)
        return recv_ref[jnp.where(there, px * ny + py, own)]

    def column(x, at):
        return jnp.broadcast_to(x[:, at : at + 1], (8, 128))

    def with_corners(dx):
        mid = face_of(block(dx, 0))
        mid = mid + jnp.where(lane == 0, column(face_of(block(dx, -1)), 16), 0.0)
        return mid + jnp.where(lane == 16, column(face_of(block(dx, 1)), 0), 0.0)

    keep_x = jnp.where(gx == nx - 1, 0.0, 1.0).astype(F32)
    keep_y = jnp.where(gy == ny - 1, 0.0, 1.0).astype(F32)
    keep_lane = jnp.where(lane == 16, keep_y, 1.0)
    row_low = with_corners(-1)
    row_high = with_corners(1)
    col_low, edge_low = column_of(block(0, -1))
    col_high, edge_high = column_of(block(0, 1))
    grads = []
    square = jnp.zeros((8, 128), F32)
    for kc in range(6):
        g = node_ref[kc * 8 : kc * 8 + 8]
        g = g + jnp.where(sub == 0, jnp.broadcast_to(row_low[kc : kc + 1], (8, 128)), 0.0)
        g = g + jnp.where(lane == 0, column(col_low, kc), 0.0)
        g = g + jnp.where(lane == 16, column(col_high, kc), 0.0)
        g = g * keep_lane
        grads.append(g)
        grad_ref[kc] = g
        own_g = jnp.where(lane < 16, g, 0.0)
        square = square + own_g * own_g
    face = node_ref[48:56] + row_high
    face = face + jnp.where(lane == 0, column(edge_low, 0), 0.0)
    face = face + jnp.where(lane == 16, column(edge_high, 0), 0.0)
    face = jnp.where(sub < 6, face * keep_lane * keep_x, 0.0)
    full = jnp.concatenate(grads + [face, jnp.zeros((8, 128), F32)], axis=0)
    moved = dot_right(expand_ref[...], dot_left(full, wyt_ref[...]))
    msc[...] = moved.reshape(6, 8, 8, 128)

    def apply(cx, curve):
        m0 = [msc[2 * k, cx] for k in range(3)]
        dm = [msc[2 * k + 1, cx] - m0[k] for k in range(3)]
        total = [None] * 3
        upper = [None] * 3
        for z in range(8):
            sz = (z + 0.5) / 8.0
            s = [slope_ref[k, z, cx] for k in range(3)]
            along = s[0] * (m0[0] + sz * dm[0])
            for k in (1, 2):
                along = along + s[k] * (m0[k] + sz * dm[k])
            curve = curve + along * along
            for k in range(3):
                w = s[k] * along
                u = w * sz
                total[k] = w if z == 0 else total[k] + w
                upper[k] = u if z == 0 else upper[k] + u
        for k in range(3):
            gsc[2 * k, cx] = total[k] - upper[k]
            gsc[2 * k + 1, cx] = upper[k]
        return curve

    curve = lax.fori_loop(0, 8, apply, jnp.zeros((8, 128), F32), unroll=4)
    nodes = dot_left(dot_right(left_ref[...], gsc[...].reshape(384, 128)), wy_ref[...])
    rows = [nodes[kc * 8 : kc * 8 + 8] for kc in range(6)]
    for kc in range(6):
        hess_ref[kc] = rows[kc]
    col_high = column_row(rows, nodes[48:56], 16)
    high = face_row(nodes[48:56])
    spot = lane[:1]
    sums = jnp.where(spot == 104, jnp.sum(sq_ref[...]), 0.0)
    sums = jnp.where(spot == 105, jnp.sum(square), sums)
    sums = jnp.where(spot == 106, jnp.sum(curve) * (1.0 / 512.0), sums)
    tail = spot >= 104
    send_ref[...] = jnp.broadcast_to(sums[None], send_ref.shape)
    for dx, dy, data in ((1, 0, high), (1, 1, high), (0, 1, col_high)):
        px, py = gx + dx, gy + dy

        @pl.when((px < nx) & (py < ny))
        def _():
            send_ref[px * ny + py] = jnp.where(tail, sums, data)

    copy_out.wait()


def finish_kernel(nx, ny, voxels, recv_ref, grad_ref, hess_ref, step_ref, prod_ref, misfit_ref):
    gx, gy = lax.axis_index("gx"), lax.axis_index("gy")
    own = gx * ny + gy
    lane = lax.broadcasted_iota(jnp.int32, (8, 128), 1)
    sub = lax.broadcasted_iota(jnp.int32, (8, 128), 0)

    def block(dx, dy):
        px, py = gx + dx, gy + dy
        there = (px >= 0) & (py >= 0)
        data = recv_ref[jnp.where(there, px * ny + py, own)]
        return jnp.where(there, data, 0.0)

    def column(x, at):
        return jnp.broadcast_to(x[:, at : at + 1], (8, 128))

    total = jnp.sum(recv_ref[...], axis=0)
    misfit_ref[...] = total[:, 104:105] * (1.0 / voxels)
    total = jnp.broadcast_to(total, (8, 128))
    alpha = column(total, 105) / column(total, 106)
    row_low = face_of(block(-1, 0)) + jnp.where(lane == 0, column(face_of(block(-1, -1)), 16), 0.0)
    col_low = column_of(block(0, -1))[0]
    for kc in range(6):
        h = hess_ref[kc]
        h = h + jnp.where(sub == 0, jnp.broadcast_to(row_low[kc : kc + 1], (8, 128)), 0.0)
        h = h + jnp.where(lane == 0, column(col_low, kc), 0.0)
        prod_ref[kc // 2, kc % 2] = h[:, :16]
        step_ref[kc // 2, kc % 2] = (alpha * grad_ref[kc])[:, :16]


def swaps(count, first):
    pairs = [(i, i + 1) for i in range(first, count - 1, 2)]
    return pairs + [(j, i) for i, j in pairs]


def on_device(ref_image, def_image, shift_xy, shift_z, frac, connectivity):
    nx, ny = lax.axis_size("gx"), lax.axis_size("gy")
    peers = nx * ny
    sds = jax.ShapeDtypeStruct
    xa = lax.ppermute(def_image, "gx", swaps(nx, 0))
    xb = lax.ppermute(def_image, "gx", swaps(nx, 1))
    row = lax.broadcasted_iota(jnp.int32, (16, 128), 0)
    table = jnp.where(row == 10, shift_z[None], 0)
    table = table + jnp.pad(connectivity, ((0, 8), (0, 0))) + jnp.pad(shift_xy, ((8, 6), (0, 0)))
    idx, wgt, own = pl.pallas_call(
        index_kernel,
        out_shape=(sds((8, 128), jnp.int32), sds((8, 8, 128), F32), sds((8, 64, 128), BF16)),
        in_specs=[VMEM] * 3,
        out_specs=(VMEM,) * 3,
        compiler_params=PARAMS,
        cost_estimate=pl.CostEstimate(flops=300000, bytes_accessed=262144, transcendentals=0),
        name="order_elements",
    )(table, frac, def_image)
    packed = sds((4, SPAN, 128), BF16)
    to_b, to_a = pl.pallas_call(
        pack_kernel,
        out_shape=(packed, packed),
        in_specs=[VMEM] * 3,
        out_specs=(VMEM, VMEM),
        compiler_params=PARAMS,
        cost_estimate=pl.CostEstimate(flops=300000, bytes_accessed=524288, transcendentals=0),
        name="pack_halo",
    )(xb, own, xa)
    yb = lax.ppermute(to_b, "gy", swaps(ny, 1))
    ya = lax.ppermute(to_a, "gy", swaps(ny, 0))

    left, wy, expand, wyt = tables()
    arr = pl.pallas_call(
        early_kernel,
        out_shape=sds((16, 11, 8, 128), F32),
        in_specs=[SMEM] + [VMEM] * 3,
        out_specs=VMEM,
        scratch_shapes=[pltpu.VMEM((TILE_ROWS + 8, 128), F32)],
        compiler_params=PARAMS,
        cost_estimate=pl.CostEstimate(flops=4000000, bytes_accessed=2000000, transcendentals=0),
        name="sample_early",
    )(idx, xb, own, xa)
    residual, slopes, nodes, send, square = pl.pallas_call(
        lambda *refs: late_kernel(nx, ny, *refs),
        out_shape=(
            sds((8, 64, 128), BF16),
            sds((3, 8, 8, 8, 128), F32),
            sds((64, 128), F32),
            sds((peers, 1, 128), F32),
            sds((8, 128), F32),
        ),
        in_specs=[SMEM] + [VMEM] * 10,
        out_specs=(VMEM,) * 5,
        scratch_shapes=[
            pltpu.VMEM((2 * TILE_ROWS + 8, 128), F32),
            pltpu.VMEM((16, 11, 8, 128), F32),
            pltpu.VMEM((8, 8, 8, 128), F32),
            pltpu.VMEM((6, 8, 8, 128), F32),
        ],
        compiler_params=PARAMS,
        name="sample_and_gradient",
    )(idx, wgt, xb, own, xa, yb, ya, arr, ref_image, left, wy)
    recv = lax.all_to_all(send, ("gx", "gy"), 0, 0, tiled=True)
    grads, hess, send, residual = pl.pallas_call(
        lambda *refs: product_kernel(nx, ny, *refs),
        out_shape=(
            sds((6, 8, 128), F32),
            sds((6, 8, 128), F32),
            sds((peers, 1, 128), F32),
            sds((8, 64, 128), BF16),
        ),
        in_specs=[VMEM] * 9,
        out_specs=(VMEM,) * 3 + (pl.BlockSpec(memory_space=pl.ANY),),
        scratch_shapes=[
            pltpu.VMEM((6, 8, 8, 128), F32),
            pltpu.VMEM((6, 8, 8, 128), F32),
            pltpu.SemaphoreType.DMA,
        ],
        compiler_params=PARAMS,
        name="gauss_newton_product",
    )(recv, nodes, slopes, square, expand, wyt, left, wy, residual)
    recv = lax.all_to_all(send, ("gx", "gy"), 0, 0, tiled=True)
    voxels = 8 * 64 * 128 * peers
    step, product, misfit = pl.pallas_call(
        lambda *refs: finish_kernel(nx, ny, voxels, *refs),
        out_shape=(sds((3, 2, 8, 16), F32), sds((3, 2, 8, 16), F32), sds((1, 1), F32)),
        in_specs=[VMEM] * 3,
        out_specs=(VMEM,) * 3,
        compiler_params=PARAMS,
        name="finish",
    )(recv, grads, hess)
    return (residual, step, product, misfit[0, 0])


def solution(mesh):
    in_specs = (
        P(None, "gx", "gy"),
        P(None, "gx", "gy"),
        P(None, ("gx", "gy")),
        P(("gx", "gy")),
        P(None, ("gx", "gy")),
        P(None, ("gx", "gy")),
    )
    out_specs = (P(None, "gx", "gy"), P(None, None, "gx", "gy"), P(None, None, "gx", "gy"), P())
    return jax.shard_map(
        on_device, mesh=mesh, in_specs=in_specs, out_specs=out_specs, check_vma=False
    )
```

```python
import jax
import jax.numpy as jnp
import numpy as np
from jax import lax
from jax.experimental import pallas as pl
from jax.experimental.pallas import tpu as pltpu
from jax.sharding import PartitionSpec as P

HALO = 64
F32 = jnp.float32
BF16 = jnp.bfloat16
SPAN = 192
TILE_ROWS = 12 * SPAN
CHUNK = 16
VMEM = pl.BlockSpec(memory_space=pltpu.VMEM)
SMEM = pl.BlockSpec(memory_space=pltpu.SMEM)
PARAMS = pltpu.CompilerParams(vmem_limit_bytes=24 * 1024 * 1024)


def node_weights(count):
    w = np.zeros((count + 1, 8 * count), np.float32)
    for v in range(8 * count):
        s = (v % 8 + 0.5) / 8.0
        w[v // 8, v] = 1.0 - s
        w[v // 8 + 1, v] = s
    return w


def tables():
    wx = node_weights(8)
    left = np.zeros((64, 6, 64), np.float32)
    for kc in range(6):
        left[kc * 8 : kc * 8 + 8, kc] = wx[:8]
        left[48 + kc, kc] = wx[8]
        left[56 + kc, kc] = wx[0]
    left = left.reshape(64, 384)
    wy = np.zeros((128, 128), np.float32)
    wy[:, :17] = node_weights(16).T
    as_bf = lambda a: jnp.asarray(a, BF16)
    return as_bf(left / 512.0), as_bf(wy), as_bf(wy.T)


def split(x):
    hi = x.astype(BF16)
    return hi, (x - hi.astype(F32)).astype(BF16)


def dot(a, b):
    return jnp.dot(a, b, preferred_element_type=F32)


def dot_right(w, x):
    hi, lo = split(x)
    return dot(w, hi) + dot(w, lo)


def dot_left(x, w):
    hi, lo = split(x)
    return dot(hi, w) + dot(lo, w)


def pack_rows(src, dst_a, dst_b, at, even):
    left = lax.broadcasted_iota(jnp.int32, (64, 128), 1) < 64
    for p in range(4):
        a = src[p].astype(F32)
        c = src[p + 4].astype(F32)
        right = jnp.where(left, pltpu.roll(a, 64, 1), c)
        other = jnp.where(left, a, pltpu.roll(c, 64, 1))
        dst_a[p, pl.ds(at, 64)] = jnp.where(even, right, other).astype(BF16)
        dst_b[p, pl.ds(at, 64)] = jnp.where(even, other, right).astype(BF16)


def dot_rows(a, b):
    return lax.dot_general(a, b, (((1,), (1,)), ((), ())), preferred_element_type=F32)


def as_rows(rows):
    sub = lax.broadcasted_iota(jnp.int32, (8, 128), 0)
    out = jnp.zeros((8, 128), F32)
    for n, row in enumerate(rows):
        out = jnp.where(sub == n, jnp.broadcast_to(row.astype(F32), (8, 128)), out)
    return out


def index_kernel(row_ref, frac_ref, own_ref, idx_ref, wgt_ref, keep_ref):
    keep_ref[...] = own_ref[...]
    first = row_ref[0:1]
    col_x = (first * 241) >> 12
    col_y = first - 17 * col_x
    start_x = 8 * col_x + row_ref[8:9] + HALO
    start_y = 8 * col_y + row_ref[9:10] + HALO
    early = (start_y >= 64) & (start_y < 184)
    below = start_y < 64
    offset = jnp.where(early, start_y - 64, jnp.where(below, start_y, start_y - 128))
    base = (row_ref[10:11] + 2) * SPAN + start_x
    tile = jnp.where(early | below, 0, TILE_ROWS)
    shift = (8 * col_y - offset) & 127
    place = (col_y & 1) * 8 + col_x
    width = jnp.where(early, 0, 9)
    flag = early.astype(F32)
    row = lax.broadcasted_iota(jnp.int32, (128, 128), 0)
    lane = lax.broadcasted_iota(jnp.int32, (128, 128), 1)
    upto = dot(as_rows([flag]).astype(BF16), (row <= lane).astype(F32).astype(BF16))[0:1]
    count = jnp.sum(flag, axis=1, keepdims=True)
    rank = jnp.where(early, upto - 1.0, count + lane[0:1].astype(F32) - upto)
    order = (jnp.broadcast_to(rank, (128, 128)) == row.astype(F32)).astype(F32).astype(BF16)
    hi, lo = split(as_rows([base, shift, place, 8 * col_y, tile, width]))
    table = dot_rows(hi, order) + dot_rows(lo, order)
    sub = lax.broadcasted_iota(jnp.int32, (8, 128), 0)
    table = jnp.where(sub == 6, jnp.broadcast_to(count, (8, 128)), table)
    idx_ref[...] = table.astype(jnp.int32)
    value = as_rows([frac_ref[c : c + 1] for c in range(3)])
    hi, lo = split(value)
    rest = (value - hi.astype(F32) - lo.astype(F32)).astype(BF16)
    element = jnp.broadcast_to(col_x * 16 + col_y, (128, 128))
    for cx in range(8):
        spread = (element == cx * 16 + (row >> 3)).astype(F32).astype(BF16)
        wgt_ref[cx] = dot_rows(hi, spread) + dot_rows(lo, spread) + dot_rows(rest, spread)


def pack_kernel(xb_ref, own_ref, xa_ref, b_ref, a_ref):
    even = lax.axis_index("gy") % 2 == 0
    for n, ref in enumerate((xa_ref, own_ref, xb_ref)):
        pack_rows(ref, a_ref, b_ref, 64 * n, even)


def over_sublanes(x):
    return jnp.sum(x, axis=0, keepdims=True)


def lanes_of(x, idx):
    return jnp.take_along_axis(x, idx & 127, axis=1, mode="promise_in_bounds")


def face_row(face):
    return over_sublanes(pltpu.roll(face, 0, 1, stride=17, stride_axis=0))


def face_of(row):
    lane = lax.broadcasted_iota(jnp.int32, (8, 128), 1)
    sub = lax.broadcasted_iota(jnp.int32, (8, 128), 0)
    back = lanes_of(jnp.broadcast_to(row, (8, 128)), lane + 17 * sub)
    return jnp.where((lane < 17) & (sub < 6), back, 0.0)


def column_row(rows, face, at):
    lane = lax.broadcasted_iota(jnp.int32, (8, 128), 1)
    block = jnp.zeros((8, 128), F32)
    for kc in range(6):
        block = jnp.where(lane == kc, jnp.broadcast_to(rows[kc][:, at : at + 1], (8, 128)), block)
    edge = jnp.where(lane == 64, jnp.broadcast_to(face[:, at : at + 1], (8, 128)), 0.0)
    block = pltpu.roll(block, 0, 1, stride=8, stride_axis=0)
    edge = pltpu.roll(edge, 0, 1, stride=1, stride_axis=0)
    return over_sublanes(block + edge)


def column_of(row):
    lane = lax.broadcasted_iota(jnp.int32, (8, 128), 1)
    sub = lax.broadcasted_iota(jnp.int32, (8, 128), 0)
    row = jnp.broadcast_to(row, (8, 128))
    return lanes_of(row, lane + 8 * sub), lanes_of(row, lane + 64 + sub)


def place_of_a():
    return pl.multiple_of(jnp.where(lax.axis_index("gx") % 2 == 1, 0, 128), 64)


def clear_outside(img, tiles):
    zero = jnp.zeros((2 * SPAN, 128), F32)
    for k in range(tiles):
        img[pl.ds(k * TILE_ROWS, 2 * SPAN)] = zero
        img[pl.ds(k * TILE_ROWS + 10 * SPAN, 2 * SPAN)] = zero


def sample_element(img, arr, base, shift, place, first, width):
    lane = lax.broadcasted_iota(jnp.int32, (8, 128), 1)
    mask = ((lane - first) & 127) < width
    starts = [pl.ds(base + z * SPAN, 8) for z in range(9)]
    starts += [pl.ds(base + 8, 8, stride=SPAN), pl.ds(base + (8 * SPAN + 8), 8)]
    for n, start in enumerate(starts):
        pltpu.store(arr.at[place, n], pltpu.roll(img[start, :], shift, 1), mask=mask)


def early_kernel(idx_ref, xb_ref, own_ref, xa_ref, arr_ref, img):
    clear_outside(img, 1)
    at_a = place_of_a()
    for z in range(8):
        for ref, row in ((xa_ref, at_a), (own_ref, 64), (xb_ref, 128 - at_a)):
            img[pl.ds(pl.multiple_of((z + 2) * SPAN + row, 8), 64)] = ref[z].astype(F32)

    def chunk(n, carry):
        for m in range(CHUNK):
            e = n * CHUNK + m
            sample_element(
                img, arr_ref, idx_ref[0, e], idx_ref[1, e], idx_ref[2, e], idx_ref[3, e], 9
            )
        return carry

    lax.fori_loop(0, (idx_ref[6, 0] + (CHUNK - 1)) // CHUNK, chunk, 0)


def late_kernel(
    nx, ny, idx_ref, wgt, xb_ref, own_ref, xa_ref, yb_ref, ya_ref, arr_ref, ref_ref,
    left_ref, wy_ref, res_ref, slope_ref, node_ref, send_ref, sq_ref, img, arr, rsc, gsc,
):
    half = lax.broadcasted_iota(jnp.int32, (64, 128), 1) < 64
    clear_outside(img, 2)
    odd_y = lax.axis_index("gy") % 2 == 1
    at_a = place_of_a()
    segments = (
        (xa_ref, 0, at_a),
        (own_ref, 64, 64),
        (xb_ref, 128, 128 - at_a),
    )
    for p in range(4):
        for ref, at, row in segments:
            ra = pltpu.roll(ref[p].astype(F32), 64, 1)
            rc = pltpu.roll(ref[p + 4].astype(F32), 64, 1)
            from_a = ya_ref[p, pl.ds(at, 64)].astype(F32)
            from_b = yb_ref[p, pl.ds(at, 64)].astype(F32)
            lo = jnp.where(odd_y, from_a, from_b)
            hi = jnp.where(odd_y, from_b, from_a)
            at_row = lambda k, q: pl.ds(pl.multiple_of(k * TILE_ROWS + (q + 2) * SPAN + row, 8), 64)
            img[at_row(0, p)] = jnp.where(half, lo, ra)
            img[at_row(1, p)] = jnp.where(half, ra, pltpu.roll(hi, 64, 1))
            img[at_row(0, p + 4)] = jnp.where(half, pltpu.roll(lo, 64, 1), rc)
            img[at_row(1, p + 4)] = jnp.where(half, rc, hi)
    for z in range(8):
        rsc[z] = ref_ref[z].astype(F32).reshape(8, 8, 128)
    arr[...] = arr_ref[...]

    def chunk(n, carry):
        for m in range(CHUNK):
            e = n * CHUNK + m
            base = idx_ref[0, e] + idx_ref[4, e]
            sample_element(
                img, arr, base, idx_ref[1, e], idx_ref[2, e], idx_ref[3, e], idx_ref[5, e]
            )
        return carry

    lax.fori_loop(idx_ref[6, 0] // CHUNK, 128 // CHUNK, chunk, 0)

    lane = lax.broadcasted_iota(jnp.int32, (8, 128), 1)
    sub = lax.broadcasted_iota(jnp.int32, (8, 128), 0)
    phase = lane & 15
    even = phase < 8
    even_next = (phase >= 1) & (phase <= 8)

    def interpolate(cx, square):
        wz, wx, wy = (jnp.broadcast_to(wgt[cx, c : c + 1], (8, 128)) for c in range(3))

        def pair(n):
            ev = arr[cx, n]
            od = arr[cx + 8, n]
            near = jnp.where(even, ev, od)
            return near, pltpu.roll(jnp.where(even_next, ev, od), 127, 1)

        edge, corner = pair(9), pair(10)

        def both_rows(z):
            here = pair(z)
            last = [corner[y][0:1] if z == 8 else edge[y][z : z + 1] for y in range(2)]
            after = [
                jnp.where(sub == 7, jnp.broadcast_to(last[y], (8, 128)), pltpu.roll(here[y], 7, 0))
                for y in range(2)
            ]
            return here, after

        total = [None] * 3
        upper = [None] * 3
        prev = both_rows(0)
        for z in range(8):
            cur = both_rows(z + 1)
            low, dzx, dx = [], [], []
            for y in range(2):
                d0 = cur[0][y] - prev[0][y]
                d1 = cur[1][y] - prev[1][y]
                l0 = prev[0][y] + wz * d0
                l1 = prev[1][y] + wz * d1
                dx.append(l1 - l0)
                low.append(l0 + wx * dx[y])
                dzx.append(d0 + wx * (d1 - d0))
            prev = cur
            slope_y = low[1] - low[0]
            value = low[0] + wy * slope_y
            slope_z = dzx[0] + wy * (dzx[1] - dzx[0])
            slope_x = dx[0] + wy * (dx[1] - dx[0])
            r = rsc[z, cx] - value
            rsc[z, cx] = r
            square = square + r * r
            for k, s in enumerate((slope_z, slope_x, slope_y)):
                slope_ref[k, z, cx] = s
                w = s * r
                u = w * ((z + 0.5) / 8.0)
                total[k] = w if z == 0 else total[k] + w
                upper[k] = u if z == 0 else upper[k] + u
        for k in range(3):
            gsc[2 * k, cx] = total[k] - upper[k]
            gsc[2 * k + 1, cx] = upper[k]
        return square

    square = jnp.zeros((8, 128), F32)
    for cx in range(8):
        square = interpolate(cx, square)
    sq_ref[...] = square
    res_ref[...] = rsc[...].reshape(8, 64, 128).astype(BF16)
    nodes = dot_left(dot_right(left_ref[...], gsc[...].reshape(384, 128)), wy_ref[...])
    node_ref[...] = nodes
    rows = [nodes[kc * 8 : kc * 8 + 8] for kc in range(6)]
    high, low = nodes[48:56], nodes[56:64]
    col_high = column_row(rows, high, 16)
    col_low = column_row(rows, high, 0)
    high, low = face_row(high), face_row(low)
    gx, gy = lax.axis_index("gx"), lax.axis_index("gy")
    send_ref[...] = jnp.zeros(send_ref.shape, F32)
    for dx in (-1, 0, 1):
        for dy in (-1, 0, 1):
            if dx == 0 and dy == 0:
                continue
            block = high if dx == 1 else low if dx == -1 else col_high if dy == 1 else col_low
            px, py = gx + dx, gy + dy

            @pl.when((px >= 0) & (px < nx) & (py >= 0) & (py < ny))
            def _():
                send_ref[px * ny + py] = block


def product_kernel(
    nx, ny, recv_ref, node_ref, slope_ref, sq_ref, wyt_ref, left_ref, wy_ref, res_ref,
    grad_ref, hess_ref, send_ref, out_ref, msc, gsc, sem,
):
    copy_out = pltpu.make_async_copy(res_ref, out_ref, sem)
    copy_out.start()
    gx, gy = lax.axis_index("gx"), lax.axis_index("gy")
    own = gx * ny + gy
    lane = lax.broadcasted_iota(jnp.int32, (8, 128), 1)
    sub = lax.broadcasted_iota(jnp.int32, (8, 128), 0)

    def block(dx, dy):
        px, py = gx + dx, gy + dy
        there = (px >= 0) & (px < nx) & (py >= 0) & (py < ny)
        return recv_ref[jnp.where(there, px * ny + py, own)]

    def column(x, at):
        return jnp.broadcast_to(x[:, at : at + 1], (8, 128))

    def with_corners(dx):
        mid = face_of(block(dx, 0))
        mid = mid + jnp.where(lane == 0, column(face_of(block(dx, -1)), 16), 0.0)
        return mid + jnp.where(lane == 16, column(face_of(block(dx, 1)), 0), 0.0)

    keep_x = jnp.where(gx == nx - 1, 0.0, 1.0).astype(F32)
    keep_y = jnp.where(gy == ny - 1, 0.0, 1.0).astype(F32)
    keep_lane = jnp.where(lane == 16, keep_y, 1.0)
    row_low = with_corners(-1)
    row_high = with_corners(1)
    col_low, edge_low = column_of(block(0, -1))
    col_high, edge_high = column_of(block(0, 1))
    grads = []
    square = jnp.zeros((8, 128), F32)
    for kc in range(6):
        g = node_ref[kc * 8 : kc * 8 + 8]
        g = g + jnp.where(sub == 0, jnp.broadcast_to(row_low[kc : kc + 1], (8, 128)), 0.0)
        g = g + jnp.where(lane == 0, column(col_low, kc), 0.0)
        g = g + jnp.where(lane == 16, column(col_high, kc), 0.0)
        g = g * keep_lane
        grads.append(g)
        grad_ref[kc] = g
        own_g = jnp.where(lane < 16, g, 0.0)
        square = square + own_g * own_g
    face = node_ref[48:56] + row_high
    face = face + jnp.where(lane == 0, column(edge_low, 0), 0.0)
    face = face + jnp.where(lane == 16, column(edge_high, 0), 0.0)
    face = jnp.where(sub < 6, face * keep_lane * keep_x, 0.0)
    full = jnp.concatenate(grads + [face, jnp.zeros((8, 128), F32)], axis=0)
    along_y = dot_left(full, wyt_ref[...])
    for kc in range(6):
        msc[kc, 0:8] = along_y[kc * 8 : kc * 8 + 8]
        msc[kc, 8:9] = along_y[48 + kc : 49 + kc]
    weight_x = (sub.astype(F32) + 0.5) / 8.0

    def along_x(kc, cx):
        low = jnp.broadcast_to(msc[kc, cx : cx + 1], (8, 128))
        high = jnp.broadcast_to(msc[kc, cx + 1 : cx + 2], (8, 128))
        return low + weight_x * (high - low)

    def apply(cx, curve):
        m0 = [along_x(2 * k, cx) for k in range(3)]
        dm = [along_x(2 * k + 1, cx) - m0[k] for k in range(3)]
        total = [None] * 3
        upper = [None] * 3
        for z in range(8):
            sz = (z + 0.5) / 8.0
            s = [slope_ref[k, z, cx] for k in range(3)]
            along = s[0] * (m0[0] + sz * dm[0])
            for k in (1, 2):
                along = along + s[k] * (m0[k] + sz * dm[k])
            curve = curve + along * along
            for k in range(3):
                w = s[k] * along
                u = w * sz
                total[k] = w if z == 0 else total[k] + w
                upper[k] = u if z == 0 else upper[k] + u
        for k in range(3):
            gsc[2 * k, cx] = total[k] - upper[k]
            gsc[2 * k + 1, cx] = upper[k]
        return curve

    curve = jnp.zeros((8, 128), F32)
    for cx in range(8):
        curve = apply(cx, curve)
    nodes = dot_left(dot_right(left_ref[...], gsc[...].reshape(384, 128)), wy_ref[...])
    rows = [nodes[kc * 8 : kc * 8 + 8] for kc in range(6)]
    for kc in range(6):
        hess_ref[kc] = rows[kc]
    col_high = column_row(rows, nodes[48:56], 16)
    high = face_row(nodes[48:56])
    spot = lane[:1]
    sums = jnp.where(spot == 104, jnp.sum(sq_ref[...]), 0.0)
    sums = jnp.where(spot == 105, jnp.sum(square), sums)
    sums = jnp.where(spot == 106, jnp.sum(curve) * (1.0 / 512.0), sums)
    tail = spot >= 104
    send_ref[...] = jnp.broadcast_to(sums[None], send_ref.shape)
    for dx, dy, data in ((1, 0, high), (1, 1, high), (0, 1, col_high)):
        px, py = gx + dx, gy + dy

        @pl.when((px < nx) & (py < ny))
        def _():
            send_ref[px * ny + py] = jnp.where(tail, sums, data)

    copy_out.wait()


def finish_kernel(nx, ny, voxels, recv_ref, grad_ref, hess_ref, step_ref, prod_ref, misfit_ref):
    gx, gy = lax.axis_index("gx"), lax.axis_index("gy")
    own = gx * ny + gy
    lane = lax.broadcasted_iota(jnp.int32, (8, 128), 1)
    sub = lax.broadcasted_iota(jnp.int32, (8, 128), 0)

    def block(dx, dy):
        px, py = gx + dx, gy + dy
        there = (px >= 0) & (py >= 0)
        data = recv_ref[jnp.where(there, px * ny + py, own)]
        return jnp.where(there, data, 0.0)

    def column(x, at):
        return jnp.broadcast_to(x[:, at : at + 1], (8, 128))

    total = jnp.sum(recv_ref[...], axis=0)
    misfit_ref[...] = total[:, 104:105] * (1.0 / voxels)
    total = jnp.broadcast_to(total, (8, 128))
    alpha = column(total, 105) / column(total, 106)
    row_low = face_of(block(-1, 0)) + jnp.where(lane == 0, column(face_of(block(-1, -1)), 16), 0.0)
    col_low = column_of(block(0, -1))[0]
    for kc in range(6):
        h = hess_ref[kc]
        h = h + jnp.where(sub == 0, jnp.broadcast_to(row_low[kc : kc + 1], (8, 128)), 0.0)
        h = h + jnp.where(lane == 0, column(col_low, kc), 0.0)
        prod_ref[kc // 2, kc % 2] = h[:, :16]
        step_ref[kc // 2, kc % 2] = (alpha * grad_ref[kc])[:, :16]


def swaps(count, first):
    pairs = [(i, i + 1) for i in range(first, count - 1, 2)]
    return pairs + [(j, i) for i, j in pairs]


def on_device(ref_image, def_image, shift_xy, shift_z, frac, connectivity):
    nx, ny = lax.axis_size("gx"), lax.axis_size("gy")
    peers = nx * ny
    sds = jax.ShapeDtypeStruct
    xa = lax.ppermute(def_image, "gx", swaps(nx, 0))
    xb = lax.ppermute(def_image, "gx", swaps(nx, 1))
    row = lax.broadcasted_iota(jnp.int32, (16, 128), 0)
    table = jnp.where(row == 10, shift_z[None], 0)
    table = table + jnp.pad(connectivity, ((0, 8), (0, 0))) + jnp.pad(shift_xy, ((8, 6), (0, 0)))
    idx, wgt, own = pl.pallas_call(
        index_kernel,
        out_shape=(sds((8, 128), jnp.int32), sds((8, 8, 128), F32), sds((8, 64, 128), BF16)),
        in_specs=[VMEM] * 3,
        out_specs=(VMEM,) * 3,
        compiler_params=PARAMS,
        cost_estimate=pl.CostEstimate(flops=300000, bytes_accessed=262144, transcendentals=0),
        name="order_elements",
    )(table, frac, def_image)
    packed = sds((4, SPAN, 128), BF16)
    to_b, to_a = pl.pallas_call(
        pack_kernel,
        out_shape=(packed, packed),
        in_specs=[VMEM] * 3,
        out_specs=(VMEM, VMEM),
        compiler_params=PARAMS,
        cost_estimate=pl.CostEstimate(flops=300000, bytes_accessed=524288, transcendentals=0),
        name="pack_halo",
    )(xb, own, xa)
    yb = lax.ppermute(to_b, "gy", swaps(ny, 1))
    ya = lax.ppermute(to_a, "gy", swaps(ny, 0))

    left, wy, wyt = tables()
    arr = pl.pallas_call(
        early_kernel,
        out_shape=sds((16, 11, 8, 128), F32),
        in_specs=[SMEM] + [VMEM] * 3,
        out_specs=VMEM,
        scratch_shapes=[pltpu.VMEM((TILE_ROWS + 8, 128), F32)],
        compiler_params=PARAMS,
        cost_estimate=pl.CostEstimate(flops=4000000, bytes_accessed=2000000, transcendentals=0),
        name="sample_early",
    )(idx, xb, own, xa)
    residual, slopes, nodes, send, square = pl.pallas_call(
        lambda *refs: late_kernel(nx, ny, *refs),
        out_shape=(
            sds((8, 64, 128), BF16),
            sds((3, 8, 8, 8, 128), F32),
            sds((64, 128), F32),
            sds((peers, 1, 128), F32),
            sds((8, 128), F32),
        ),
        in_specs=[SMEM] + [VMEM] * 10,
        out_specs=(VMEM,) * 5,
        scratch_shapes=[
            pltpu.VMEM((2 * TILE_ROWS + 8, 128), F32),
            pltpu.VMEM((16, 11, 8, 128), F32),
            pltpu.VMEM((8, 8, 8, 128), F32),
            pltpu.VMEM((6, 8, 8, 128), F32),
        ],
        compiler_params=PARAMS,
        name="sample_and_gradient",
    )(idx, wgt, xb, own, xa, yb, ya, arr, ref_image, left, wy)
    recv = lax.all_to_all(send, ("gx", "gy"), 0, 0, tiled=True)
    grads, hess, send, residual = pl.pallas_call(
        lambda *refs: product_kernel(nx, ny, *refs),
        out_shape=(
            sds((6, 8, 128), F32),
            sds((6, 8, 128), F32),
            sds((peers, 1, 128), F32),
            sds((8, 64, 128), BF16),
        ),
        in_specs=[VMEM] * 8,
        out_specs=(VMEM,) * 3 + (pl.BlockSpec(memory_space=pl.ANY),),
        scratch_shapes=[
            pltpu.VMEM((6, 16, 128), F32),
            pltpu.VMEM((6, 8, 8, 128), F32),
            pltpu.SemaphoreType.DMA,
        ],
        compiler_params=PARAMS,
        name="gauss_newton_product",
    )(recv, nodes, slopes, square, wyt, left, wy, residual)
    recv = lax.all_to_all(send, ("gx", "gy"), 0, 0, tiled=True)
    voxels = 8 * 64 * 128 * peers
    step, product, misfit = pl.pallas_call(
        lambda *refs: finish_kernel(nx, ny, voxels, *refs),
        out_shape=(sds((3, 2, 8, 16), F32), sds((3, 2, 8, 16), F32), sds((1, 1), F32)),
        in_specs=[VMEM] * 3,
        out_specs=(VMEM,) * 3,
        compiler_params=PARAMS,
        name="finish",
    )(recv, grads, hess)
    return (residual, step, product, misfit[0, 0])


def solution(mesh):
    in_specs = (
        P(None, "gx", "gy"),
        P(None, "gx", "gy"),
        P(None, ("gx", "gy")),
        P(("gx", "gy")),
        P(None, ("gx", "gy")),
        P(None, ("gx", "gy")),
    )
    out_specs = (P(None, "gx", "gy"), P(None, None, "gx", "gy"), P(None, None, "gx", "gy"), P())
    return jax.shard_map(
        on_device, mesh=mesh, in_specs=in_specs, out_specs=out_specs, check_vma=False
    )
```

```python
import jax
import jax.numpy as jnp
import numpy as np
from jax import lax
from jax.experimental import pallas as pl
from jax.experimental.pallas import tpu as pltpu
from jax.sharding import PartitionSpec as P

HALO = 64
F32 = jnp.float32
BF16 = jnp.bfloat16
SPAN = 192
TILE_ROWS = 12 * SPAN
CHUNK = 16
VMEM = pl.BlockSpec(memory_space=pltpu.VMEM)
SMEM = pl.BlockSpec(memory_space=pltpu.SMEM)
PARAMS = pltpu.CompilerParams(vmem_limit_bytes=24 * 1024 * 1024)


def node_weights(count):
    w = np.zeros((count + 1, 8 * count), np.float32)
    for v in range(8 * count):
        s = (v % 8 + 0.5) / 8.0
        w[v // 8, v] = 1.0 - s
        w[v // 8 + 1, v] = s
    return w


def tables():
    wx = node_weights(8)
    left = np.zeros((64, 6, 64), np.float32)
    for kc in range(6):
        left[kc * 8 : kc * 8 + 8, kc] = wx[:8]
        left[48 + kc, kc] = wx[8]
        left[56 + kc, kc] = wx[0]
    left = left.reshape(64, 384)
    expand = left.T.copy()
    expand[:, 56:] = 0.0
    wy = np.zeros((128, 128), np.float32)
    wy[:, :17] = node_weights(16).T
    as_bf = lambda a: jnp.asarray(a, BF16)
    return as_bf(left / 512.0), as_bf(wy), as_bf(expand), as_bf(wy.T)


def split(x):
    hi = x.astype(BF16)
    return hi, (x - hi.astype(F32)).astype(BF16)


def dot(a, b):
    return jnp.dot(a, b, preferred_element_type=F32)


def dot_right(w, x):
    hi, lo = split(x)
    return dot(w, hi) + dot(w, lo)


def dot_left(x, w):
    hi, lo = split(x)
    return dot(hi, w) + dot(lo, w)


def pack_rows(src, dst_a, dst_b, at, even):
    left = lax.broadcasted_iota(jnp.int32, (64, 128), 1) < 64
    for p in range(4):
        a = src[p].astype(F32)
        c = src[p + 4].astype(F32)
        right = jnp.where(left, pltpu.roll(a, 64, 1), c)
        other = jnp.where(left, a, pltpu.roll(c, 64, 1))
        dst_a[p, pl.ds(at, 64)] = jnp.where(even, right, other).astype(BF16)
        dst_b[p, pl.ds(at, 64)] = jnp.where(even, other, right).astype(BF16)


def dot_rows(a, b):
    return lax.dot_general(a, b, (((1,), (1,)), ((), ())), preferred_element_type=F32)


def as_rows(rows):
    sub = lax.broadcasted_iota(jnp.int32, (8, 128), 0)
    out = jnp.zeros((8, 128), F32)
    for n, row in enumerate(rows):
        out = jnp.where(sub == n, jnp.broadcast_to(row.astype(F32), (8, 128)), out)
    return out


def index_kernel(row_ref, frac_ref, own_ref, idx_ref, wgt_ref, keep_ref):
    keep_ref[...] = own_ref[...]
    first = row_ref[0:1]
    col_x = (first * 241) >> 12
    col_y = first - 17 * col_x
    start_x = 8 * col_x + row_ref[8:9] + HALO
    start_y = 8 * col_y + row_ref[9:10] + HALO
    early = (start_y >= 64) & (start_y < 184)
    below = start_y < 64
    offset = jnp.where(early, start_y - 64, jnp.where(below, start_y, start_y - 128))
    base = (row_ref[10:11] + 2) * SPAN + start_x
    tile = jnp.where(early | below, 0, TILE_ROWS)
    shift = (8 * col_y - offset) & 127
    place = (col_y & 1) * 8 + col_x
    width = jnp.where(early, 0, 9)
    flag = early.astype(F32)
    row = lax.broadcasted_iota(jnp.int32, (128, 128), 0)
    lane = lax.broadcasted_iota(jnp.int32, (128, 128), 1)
    upto = dot(as_rows([flag]).astype(BF16), (row <= lane).astype(F32).astype(BF16))[0:1]
    count = jnp.sum(flag, axis=1, keepdims=True)
    rank = jnp.where(early, upto - 1.0, count + lane[0:1].astype(F32) - upto)
    order = (jnp.broadcast_to(rank, (128, 128)) == row.astype(F32)).astype(F32).astype(BF16)
    hi, lo = split(as_rows([base, shift, place, 8 * col_y, tile, width]))
    table = dot_rows(hi, order) + dot_rows(lo, order)
    sub = lax.broadcasted_iota(jnp.int32, (8, 128), 0)
    table = jnp.where(sub == 6, jnp.broadcast_to(count, (8, 128)), table)
    idx_ref[...] = table.astype(jnp.int32)
    value = as_rows([frac_ref[c : c + 1] for c in range(3)])
    hi, lo = split(value)
    rest = (value - hi.astype(F32) - lo.astype(F32)).astype(BF16)
    element = jnp.broadcast_to(col_x * 16 + col_y, (128, 128))
    for cx in range(8):
        spread = (element == cx * 16 + (row >> 3)).astype(F32).astype(BF16)
        wgt_ref[cx] = dot_rows(hi, spread) + dot_rows(lo, spread) + dot_rows(rest, spread)


def pack_first_kernel(xa_ref, own_ref, b_ref, a_ref):
    even = lax.axis_index("gy") % 2 == 0
    pack_rows(xa_ref, a_ref, b_ref, 0, even)
    pack_rows(own_ref, a_ref, b_ref, 64, even)


def pack_second_kernel(xb_ref, after_ref, b_ref, a_ref):
    pack_rows(xb_ref, a_ref, b_ref, 0, lax.axis_index("gy") % 2 == 0)


def over_sublanes(x):
    return jnp.sum(x, axis=0, keepdims=True)


def lanes_of(x, idx):
    return jnp.take_along_axis(x, idx & 127, axis=1, mode="promise_in_bounds")


def face_row(face):
    return over_sublanes(pltpu.roll(face, 0, 1, stride=17, stride_axis=0))


def face_of(row):
    lane = lax.broadcasted_iota(jnp.int32, (8, 128), 1)
    sub = lax.broadcasted_iota(jnp.int32, (8, 128), 0)
    back = lanes_of(jnp.broadcast_to(row, (8, 128)), lane + 17 * sub)
    return jnp.where((lane < 17) & (sub < 6), back, 0.0)


def column_row(rows, face, at):
    lane = lax.broadcasted_iota(jnp.int32, (8, 128), 1)
    block = jnp.zeros((8, 128), F32)
    for kc in range(6):
        block = jnp.where(lane == kc, jnp.broadcast_to(rows[kc][:, at : at + 1], (8, 128)), block)
    edge = jnp.where(lane == 64, jnp.broadcast_to(face[:, at : at + 1], (8, 128)), 0.0)
    block = pltpu.roll(block, 0, 1, stride=8, stride_axis=0)
    edge = pltpu.roll(edge, 0, 1, stride=1, stride_axis=0)
    return over_sublanes(block + edge)


def column_of(row):
    lane = lax.broadcasted_iota(jnp.int32, (8, 128), 1)
    sub = lax.broadcasted_iota(jnp.int32, (8, 128), 0)
    row = jnp.broadcast_to(row, (8, 128))
    return lanes_of(row, lane + 8 * sub), lanes_of(row, lane + 64 + sub)


def place_of_a():
    return pl.multiple_of(jnp.where(lax.axis_index("gx") % 2 == 1, 0, 128), 64)


def clear_outside(img, tiles):
    zero = jnp.zeros((2 * SPAN, 128), F32)
    for k in range(tiles):
        img[pl.ds(k * TILE_ROWS, 2 * SPAN)] = zero
        img[pl.ds(k * TILE_ROWS + 10 * SPAN, 2 * SPAN)] = zero


def sample_element(img, arr, base, shift, place, first, width):
    lane = lax.broadcasted_iota(jnp.int32, (8, 128), 1)
    mask = ((lane - first) & 127) < width
    starts = [pl.ds(base + z * SPAN, 8) for z in range(9)]
    starts += [pl.ds(base + 8, 8, stride=SPAN), pl.ds(base + (8 * SPAN + 8), 8)]
    for n, start in enumerate(starts):
        pltpu.store(arr.at[place, n], pltpu.roll(img[start, :], shift, 1), mask=mask)


def early_kernel(idx_ref, xb_ref, own_ref, xa_ref, arr_ref, img):
    clear_outside(img, 1)
    at_a = place_of_a()
    for z in range(8):
        for ref, row in ((xa_ref, at_a), (own_ref, 64), (xb_ref, 128 - at_a)):
            img[pl.ds(pl.multiple_of((z + 2) * SPAN + row, 8), 64)] = ref[z].astype(F32)

    def chunk(n, carry):
        for m in range(CHUNK):
            e = n * CHUNK + m
            sample_element(
                img, arr_ref, idx_ref[0, e], idx_ref[1, e], idx_ref[2, e], idx_ref[3, e], 9
            )
        return carry

    lax.fori_loop(0, (idx_ref[6, 0] + (CHUNK - 1)) // CHUNK, chunk, 0)


def late_kernel(
    nx, ny, idx_ref, wgt, xb_ref, own_ref, xa_ref, yb_ref, ya_ref, yd_ref, yc_ref, arr_ref, ref_ref,
    left_ref, wy_ref, res_ref, slope_ref, node_ref, send_ref, sq_ref, img, arr, rsc, gsc,
):
    half = lax.broadcasted_iota(jnp.int32, (64, 128), 1) < 64
    clear_outside(img, 2)
    odd_y = lax.axis_index("gy") % 2 == 1
    at_a = place_of_a()
    segments = (
        (xa_ref, ya_ref, yb_ref, 0, at_a),
        (own_ref, ya_ref, yb_ref, 64, 64),
        (xb_ref, yc_ref, yd_ref, 0, 128 - at_a),
    )
    for p in range(4):
        for ref, pair_a, pair_b, at, row in segments:
            ra = pltpu.roll(ref[p].astype(F32), 64, 1)
            rc = pltpu.roll(ref[p + 4].astype(F32), 64, 1)
            from_a = pair_a[p, pl.ds(at, 64)].astype(F32)
            from_b = pair_b[p, pl.ds(at, 64)].astype(F32)
            lo = jnp.where(odd_y, from_a, from_b)
            hi = jnp.where(odd_y, from_b, from_a)
            at_row = lambda k, q: pl.ds(pl.multiple_of(k * TILE_ROWS + (q + 2) * SPAN + row, 8), 64)
            img[at_row(0, p)] = jnp.where(half, lo, ra)
            img[at_row(1, p)] = jnp.where(half, ra, pltpu.roll(hi, 64, 1))
            img[at_row(0, p + 4)] = jnp.where(half, pltpu.roll(lo, 64, 1), rc)
            img[at_row(1, p + 4)] = jnp.where(half, rc, hi)
    for z in range(8):
        rsc[z] = ref_ref[z].astype(F32).reshape(8, 8, 128)
    arr[...] = arr_ref[...]

    def chunk(n, carry):
        for m in range(CHUNK):
            e = n * CHUNK + m
            base = idx_ref[0, e] + idx_ref[4, e]
            sample_element(
                img, arr, base, idx_ref[1, e], idx_ref[2, e], idx_ref[3, e], idx_ref[5, e]
            )
        return carry

    lax.fori_loop(idx_ref[6, 0] // CHUNK, 128 // CHUNK, chunk, 0)

    lane = lax.broadcasted_iota(jnp.int32, (8, 128), 1)
    sub = lax.broadcasted_iota(jnp.int32, (8, 128), 0)
    phase = lane & 15
    even = phase < 8
    even_next = (phase >= 1) & (phase <= 8)

    def interpolate(cx, square):
        wz, wx, wy = (jnp.broadcast_to(wgt[cx, c : c + 1], (8, 128)) for c in range(3))

        def pair(n):
            ev = arr[cx, n]
            od = arr[cx + 8, n]
            near = jnp.where(even, ev, od)
            return near, pltpu.roll(jnp.where(even_next, ev, od), 127, 1)

        edge, corner = pair(9), pair(10)

        def both_rows(z):
            here = pair(z)
            last = [corner[y][0:1] if z == 8 else edge[y][z : z + 1] for y in range(2)]
            after = [
                jnp.where(sub == 7, jnp.broadcast_to(last[y], (8, 128)), pltpu.roll(here[y], 7, 0))
                for y in range(2)
            ]
            return here, after

        total = [None] * 3
        upper = [None] * 3
        prev = both_rows(0)
        for z in range(8):
            cur = both_rows(z + 1)
            low, dzx, dx = [], [], []
            for y in range(2):
                d0 = cur[0][y] - prev[0][y]
                d1 = cur[1][y] - prev[1][y]
                l0 = prev[0][y] + wz * d0
                l1 = prev[1][y] + wz * d1
                dx.append(l1 - l0)
                low.append(l0 + wx * dx[y])
                dzx.append(d0 + wx * (d1 - d0))
            prev = cur
            slope_y = low[1] - low[0]
            value = low[0] + wy * slope_y
            slope_z = dzx[0] + wy * (dzx[1] - dzx[0])
            slope_x = dx[0] + wy * (dx[1] - dx[0])
            r = rsc[z, cx] - value
            rsc[z, cx] = r
            square = square + r * r
            for k, s in enumerate((slope_z, slope_x, slope_y)):
                slope_ref[k, z, cx] = s
                w = s * r
                u = w * ((z + 0.5) / 8.0)
                total[k] = w if z == 0 else total[k] + w
                upper[k] = u if z == 0 else upper[k] + u
        for k in range(3):
            gsc[2 * k, cx] = total[k] - upper[k]
            gsc[2 * k + 1, cx] = upper[k]
        return square

    sq_ref[...] = lax.fori_loop(0, 8, interpolate, jnp.zeros((8, 128), F32), unroll=4)
    res_ref[...] = rsc[...].reshape(8, 64, 128).astype(BF16)
    nodes = dot_left(dot_right(left_ref[...], gsc[...].reshape(384, 128)), wy_ref[...])
    node_ref[...] = nodes
    rows = [nodes[kc * 8 : kc * 8 + 8] for kc in range(6)]
    high, low = nodes[48:56], nodes[56:64]
    col_high = column_row(rows, high, 16)
    col_low = column_row(rows, high, 0)
    high, low = face_row(high), face_row(low)
    gx, gy = lax.axis_index("gx"), lax.axis_index("gy")
    send_ref[...] = jnp.zeros(send_ref.shape, F32)
    for dx in (-1, 0, 1):
        for dy in (-1, 0, 1):
            if dx == 0 and dy == 0:
                continue
            block = high if dx == 1 else low if dx == -1 else col_high if dy == 1 else col_low
            px, py = gx + dx, gy + dy

            @pl.when((px >= 0) & (px < nx) & (py >= 0) & (py < ny))
            def _():
                send_ref[px * ny + py] = block


def product_kernel(
    nx, ny, recv_ref, node_ref, slope_ref, sq_ref, expand_ref, wyt_ref, left_ref, wy_ref, res_ref,
    grad_ref, hess_ref, send_ref, out_ref, msc, gsc, sem,
):
    copy_out = pltpu.make_async_copy(res_ref, out_ref, sem)
    copy_out.start()
    gx, gy = lax.axis_index("gx"), lax.axis_index("gy")
    own = gx * ny + gy
    lane = lax.broadcasted_iota(jnp.int32, (8, 128), 1)
    sub = lax.broadcasted_iota(jnp.int32, (8, 128), 0)

    def block(dx, dy):
        px, py = gx + dx, gy + dy
        there = (px >= 0) & (px < nx) & (py >= 0) & (py < ny)
        return recv_ref[jnp.where(there, px * ny + py, own)]

    def column(x, at):
        return jnp.broadcast_to(x[:, at : at + 1], (8, 128))

    def with_corners(dx):
        mid = face_of(block(dx, 0))
        mid = mid + jnp.where(lane == 0, column(face_of(block(dx, -1)), 16), 0.0)
        return mid + jnp.where(lane == 16, column(face_of(block(dx, 1)), 0), 0.0)

    keep_x = jnp.where(gx == nx - 1, 0.0, 1.0).astype(F32)
    keep_y = jnp.where(gy == ny - 1, 0.0, 1.0).astype(F32)
    keep_lane = jnp.where(lane == 16, keep_y, 1.0)
    row_low = with_corners(-1)
    row_high = with_corners(1)
    col_low, edge_low = column_of(block(0, -1))
    col_high, edge_high = column_of(block(0, 1))
    grads = []
    square = jnp.zeros((8, 128), F32)
    for kc in range(6):
        g = node_ref[kc * 8 : kc * 8 + 8]
        g = g + jnp.where(sub == 0, jnp.broadcast_to(row_low[kc : kc + 1], (8, 128)), 0.0)
        g = g + jnp.where(lane == 0, column(col_low, kc), 0.0)
        g = g + jnp.where(lane == 16, column(col_high, kc), 0.0)
        g = g * keep_lane
        grads.append(g)
        grad_ref[kc] = g
        own_g = jnp.where(lane < 16, g, 0.0)
        square = square + own_g * own_g
    face = node_ref[48:56] + row_high
    face = face + jnp.where(lane == 0, column(edge_low, 0), 0.0)
    face = face + jnp.where(lane == 16, column(edge_high, 0), 0.0)
    face = jnp.where(sub < 6, face * keep_lane * keep_x, 0.0)
    full = jnp.concatenate(grads + [face, jnp.zeros((8, 128), F32)], axis=0)
    moved = dot_right(expand_ref[...], dot_left(full, wyt_ref[...]))
    msc[...] = moved.reshape(6, 8, 8, 128)

    def apply(cx, curve):
        m0 = [msc[2 * k, cx] for k in range(3)]
        dm = [msc[2 * k + 1, cx] - m0[k] for k in range(3)]
        total = [None] * 3
        upper = [None] * 3
        for z in range(8):
            sz = (z + 0.5) / 8.0
            s = [slope_ref[k, z, cx] for k in range(3)]
            along = s[0] * (m0[0] + sz * dm[0])
            for k in (1, 2):
                along = along + s[k] * (m0[k] + sz * dm[k])
            curve = curve + along * along
            for k in range(3):
                w = s[k] * along
                u = w * sz
                total[k] = w if z == 0 else total[k] + w
                upper[k] = u if z == 0 else upper[k] + u
        for k in range(3):
            gsc[2 * k, cx] = total[k] - upper[k]
            gsc[2 * k + 1, cx] = upper[k]
        return curve

    curve = lax.fori_loop(0, 8, apply, jnp.zeros((8, 128), F32), unroll=4)
    nodes = dot_left(dot_right(left_ref[...], gsc[...].reshape(384, 128)), wy_ref[...])
    rows = [nodes[kc * 8 : kc * 8 + 8] for kc in range(6)]
    for kc in range(6):
        hess_ref[kc] = rows[kc]
    col_high = column_row(rows, nodes[48:56], 16)
    high = face_row(nodes[48:56])
    spot = lane[:1]
    sums = jnp.where(spot == 104, jnp.sum(sq_ref[...]), 0.0)
    sums = jnp.where(spot == 105, jnp.sum(square), sums)
    sums = jnp.where(spot == 106, jnp.sum(curve) * (1.0 / 512.0), sums)
    tail = spot >= 104
    send_ref[...] = jnp.broadcast_to(sums[None], send_ref.shape)
    for dx, dy, data in ((1, 0, high), (1, 1, high), (0, 1, col_high)):
        px, py = gx + dx, gy + dy

        @pl.when((px < nx) & (py < ny))
        def _():
            send_ref[px * ny + py] = jnp.where(tail, sums, data)

    copy_out.wait()


def finish_kernel(nx, ny, voxels, recv_ref, grad_ref, hess_ref, step_ref, prod_ref, misfit_ref):
    gx, gy = lax.axis_index("gx"), lax.axis_index("gy")
    own = gx * ny + gy
    lane = lax.broadcasted_iota(jnp.int32, (8, 128), 1)
    sub = lax.broadcasted_iota(jnp.int32, (8, 128), 0)

    def block(dx, dy):
        px, py = gx + dx, gy + dy
        there = (px >= 0) & (py >= 0)
        data = recv_ref[jnp.where(there, px * ny + py, own)]
        return jnp.where(there, data, 0.0)

    def column(x, at):
        return jnp.broadcast_to(x[:, at : at + 1], (8, 128))

    total = jnp.sum(recv_ref[...], axis=0)
    misfit_ref[...] = total[:, 104:105] * (1.0 / voxels)
    total = jnp.broadcast_to(total, (8, 128))
    alpha = column(total, 105) / column(total, 106)
    row_low = face_of(block(-1, 0)) + jnp.where(lane == 0, column(face_of(block(-1, -1)), 16), 0.0)
    col_low = column_of(block(0, -1))[0]
    for kc in range(6):
        h = hess_ref[kc]
        h = h + jnp.where(sub == 0, jnp.broadcast_to(row_low[kc : kc + 1], (8, 128)), 0.0)
        h = h + jnp.where(lane == 0, column(col_low, kc), 0.0)
        prod_ref[kc // 2, kc % 2] = h[:, :16]
        step_ref[kc // 2, kc % 2] = (alpha * grad_ref[kc])[:, :16]


def swaps(count, first):
    pairs = [(i, i + 1) for i in range(first, count - 1, 2)]
    return pairs + [(j, i) for i, j in pairs]


def on_device(ref_image, def_image, shift_xy, shift_z, frac, connectivity):
    nx, ny = lax.axis_size("gx"), lax.axis_size("gy")
    peers = nx * ny
    sds = jax.ShapeDtypeStruct
    xa = lax.ppermute(def_image, "gx", swaps(nx, 0))
    xb = lax.ppermute(def_image, "gx", swaps(nx, 1))
    row = lax.broadcasted_iota(jnp.int32, (16, 128), 0)
    table = jnp.where(row == 10, shift_z[None], 0)
    table = table + jnp.pad(connectivity, ((0, 8), (0, 0))) + jnp.pad(shift_xy, ((8, 6), (0, 0)))
    idx, wgt, own = pl.pallas_call(
        index_kernel,
        out_shape=(sds((8, 128), jnp.int32), sds((8, 8, 128), F32), sds((8, 64, 128), BF16)),
        in_specs=[VMEM] * 3,
        out_specs=(VMEM,) * 3,
        compiler_params=PARAMS,
        cost_estimate=pl.CostEstimate(flops=300000, bytes_accessed=262144, transcendentals=0),
        name="order_elements",
    )(table, frac, def_image)
    packed = sds((4, 128, 128), BF16)
    to_b, to_a = pl.pallas_call(
        pack_first_kernel,
        out_shape=(packed, packed),
        in_specs=[VMEM] * 2,
        out_specs=(VMEM, VMEM),
        compiler_params=PARAMS,
        cost_estimate=pl.CostEstimate(flops=300000, bytes_accessed=524288, transcendentals=0),
        name="pack_first_halo",
    )(xa, own)
    yb = lax.ppermute(to_b, "gy", swaps(ny, 1))
    ya = lax.ppermute(to_a, "gy", swaps(ny, 0))
    packed = sds((4, 64, 128), BF16)
    to_d, to_c = pl.pallas_call(
        pack_second_kernel,
        out_shape=(packed, packed),
        in_specs=[VMEM, pl.BlockSpec(memory_space=pl.ANY)],
        out_specs=(VMEM, VMEM),
        compiler_params=PARAMS,
        cost_estimate=pl.CostEstimate(flops=300000, bytes_accessed=524288, transcendentals=0),
        name="pack_second_halo",
    )(xb, to_a)
    yd = lax.ppermute(to_d, "gy", swaps(ny, 1))
    yc = lax.ppermute(to_c, "gy", swaps(ny, 0))

    left, wy, expand, wyt = tables()
    arr = pl.pallas_call(
        early_kernel,
        out_shape=sds((16, 11, 8, 128), F32),
        in_specs=[SMEM] + [VMEM] * 3,
        out_specs=VMEM,
        scratch_shapes=[pltpu.VMEM((TILE_ROWS + 8, 128), F32)],
        compiler_params=PARAMS,
        cost_estimate=pl.CostEstimate(flops=4000000, bytes_accessed=2000000, transcendentals=0),
        name="sample_early",
    )(idx, xb, own, xa)
    residual, slopes, nodes, send, square = pl.pallas_call(
        lambda *refs: late_kernel(nx, ny, *refs),
        out_shape=(
            sds((8, 64, 128), BF16),
            sds((3, 8, 8, 8, 128), F32),
            sds((64, 128), F32),
            sds((peers, 1, 128), F32),
            sds((8, 128), F32),
        ),
        in_specs=[SMEM] + [VMEM] * 12,
        out_specs=(VMEM,) * 5,
        scratch_shapes=[
            pltpu.VMEM((2 * TILE_ROWS + 8, 128), F32),
            pltpu.VMEM((16, 11, 8, 128), F32),
            pltpu.VMEM((8, 8, 8, 128), F32),
            pltpu.VMEM((6, 8, 8, 128), F32),
        ],
        compiler_params=PARAMS,
        name="sample_and_gradient",
    )(idx, wgt, xb, own, xa, yb, ya, yd, yc, arr, ref_image, left, wy)
    recv = lax.all_to_all(send, ("gx", "gy"), 0, 0, tiled=True)
    grads, hess, send, residual = pl.pallas_call(
        lambda *refs: product_kernel(nx, ny, *refs),
        out_shape=(
            sds((6, 8, 128), F32),
            sds((6, 8, 128), F32),
            sds((peers, 1, 128), F32),
            sds((8, 64, 128), BF16),
        ),
        in_specs=[VMEM] * 9,
        out_specs=(VMEM,) * 3 + (pl.BlockSpec(memory_space=pl.ANY),),
        scratch_shapes=[
            pltpu.VMEM((6, 8, 8, 128), F32),
            pltpu.VMEM((6, 8, 8, 128), F32),
            pltpu.SemaphoreType.DMA,
        ],
        compiler_params=PARAMS,
        name="gauss_newton_product",
    )(recv, nodes, slopes, square, expand, wyt, left, wy, residual)
    recv = lax.all_to_all(send, ("gx", "gy"), 0, 0, tiled=True)
    voxels = 8 * 64 * 128 * peers
    step, product, misfit = pl.pallas_call(
        lambda *refs: finish_kernel(nx, ny, voxels, *refs),
        out_shape=(sds((3, 2, 8, 16), F32), sds((3, 2, 8, 16), F32), sds((1, 1), F32)),
        in_specs=[VMEM] * 3,
        out_specs=(VMEM,) * 3,
        compiler_params=PARAMS,
        name="finish",
    )(recv, grads, hess)
    return (residual, step, product, misfit[0, 0])


def solution(mesh):
    in_specs = (
        P(None, "gx", "gy"),
        P(None, "gx", "gy"),
        P(None, ("gx", "gy")),
        P(("gx", "gy")),
        P(None, ("gx", "gy")),
        P(None, ("gx", "gy")),
    )
    out_specs = (P(None, "gx", "gy"), P(None, None, "gx", "gy"), P(None, None, "gx", "gy"), P())
    return jax.shard_map(
        on_device, mesh=mesh, in_specs=in_specs, out_specs=out_specs, check_vma=False
    )
```

```python
import jax
import jax.numpy as jnp
import numpy as np
from jax import lax
from jax.experimental import pallas as pl
from jax.experimental.pallas import tpu as pltpu
from jax.sharding import PartitionSpec as P

HALO = 64
F32 = jnp.float32
BF16 = jnp.bfloat16
SPAN = 192
TILE_ROWS = 12 * SPAN
CHUNK = 16
VMEM = pl.BlockSpec(memory_space=pltpu.VMEM)
SMEM = pl.BlockSpec(memory_space=pltpu.SMEM)
PARAMS = pltpu.CompilerParams(vmem_limit_bytes=24 * 1024 * 1024)


def node_weights(count):
    w = np.zeros((count + 1, 8 * count), np.float32)
    for v in range(8 * count):
        s = (v % 8 + 0.5) / 8.0
        w[v // 8, v] = 1.0 - s
        w[v // 8 + 1, v] = s
    return w


def tables():
    wx = node_weights(8)
    left = np.zeros((64, 6, 64), np.float32)
    for kc in range(6):
        left[kc * 8 : kc * 8 + 8, kc] = wx[:8]
        left[48 + kc, kc] = wx[8]
        left[56 + kc, kc] = wx[0]
    left = left.reshape(64, 384)
    expand = left.T.copy()
    expand[:, 56:] = 0.0
    wy = np.zeros((128, 128), np.float32)
    wy[:, :17] = node_weights(16).T
    as_bf = lambda a: jnp.asarray(a, BF16)
    return as_bf(left / 512.0), as_bf(wy), as_bf(expand), as_bf(wy.T)


def split(x):
    hi = x.astype(BF16)
    return hi, (x - hi.astype(F32)).astype(BF16)


def dot(a, b):
    return jnp.dot(a, b, preferred_element_type=F32)


def dot_right(w, x):
    hi, lo = split(x)
    return dot(w, hi) + dot(w, lo)


def dot_left(x, w):
    hi, lo = split(x)
    return dot(hi, w) + dot(lo, w)


def pack_rows(src, dst_a, dst_b, at, even):
    left = lax.broadcasted_iota(jnp.int32, (64, 128), 1) < 64
    for p in range(4):
        a = src[p].astype(F32)
        c = src[p + 4].astype(F32)
        right = jnp.where(left, pltpu.roll(a, 64, 1), c)
        other = jnp.where(left, a, pltpu.roll(c, 64, 1))
        dst_a[p, pl.ds(at, 64)] = jnp.where(even, right, other).astype(BF16)
        dst_b[p, pl.ds(at, 64)] = jnp.where(even, other, right).astype(BF16)


def dot_rows(a, b):
    return lax.dot_general(a, b, (((1,), (1,)), ((), ())), preferred_element_type=F32)


def as_rows(rows):
    sub = lax.broadcasted_iota(jnp.int32, (8, 128), 0)
    out = jnp.zeros((8, 128), F32)
    for n, row in enumerate(rows):
        out = jnp.where(sub == n, jnp.broadcast_to(row.astype(F32), (8, 128)), out)
    return out


def index_kernel(row_ref, frac_ref, after_ref, idx_ref, wgt_ref):
    first = row_ref[0:1]
    col_x = (first * 241) >> 12
    col_y = first - 17 * col_x
    start_x = 8 * col_x + row_ref[8:9] + HALO
    start_y = 8 * col_y + row_ref[9:10] + HALO
    early = (start_y >= 64) & (start_y < 184)
    below = start_y < 64
    offset = jnp.where(early, start_y - 64, jnp.where(below, start_y, start_y - 128))
    base = (row_ref[10:11] + 2) * SPAN + start_x
    tile = jnp.where(early | below, 0, TILE_ROWS)
    shift = (8 * col_y - offset) & 127
    place = (col_y & 1) * 8 + col_x
    width = jnp.where(early, 0, 9)
    flag = early.astype(F32)
    row = lax.broadcasted_iota(jnp.int32, (128, 128), 0)
    lane = lax.broadcasted_iota(jnp.int32, (128, 128), 1)
    upto = dot(as_rows([flag]).astype(BF16), (row <= lane).astype(F32).astype(BF16))[0:1]
    count = jnp.sum(flag, axis=1, keepdims=True)
    rank = jnp.where(early, upto - 1.0, count + lane[0:1].astype(F32) - upto)
    order = (jnp.broadcast_to(rank, (128, 128)) == row.astype(F32)).astype(F32).astype(BF16)
    hi, lo = split(as_rows([base, shift, place, 8 * col_y, tile, width]))
    table = dot_rows(hi, order) + dot_rows(lo, order)
    sub = lax.broadcasted_iota(jnp.int32, (8, 128), 0)
    table = jnp.where(sub == 6, jnp.broadcast_to(count, (8, 128)), table)
    idx_ref[...] = table.astype(jnp.int32)
    value = as_rows([frac_ref[c : c + 1] for c in range(3)])
    hi, lo = split(value)
    rest = (value - hi.astype(F32) - lo.astype(F32)).astype(BF16)
    element = jnp.broadcast_to(col_x * 16 + col_y, (128, 128))
    for cx in range(8):
        spread = (element == cx * 16 + (row >> 3)).astype(F32).astype(BF16)
        wgt_ref[cx] = dot_rows(hi, spread) + dot_rows(lo, spread) + dot_rows(rest, spread)


def pack_first_kernel(xa_ref, own_ref, b_ref, a_ref, keep_ref):
    keep_ref[...] = own_ref[...]
    even = lax.axis_index("gy") % 2 == 0
    pack_rows(xa_ref, a_ref, b_ref, 0, even)
    pack_rows(own_ref, a_ref, b_ref, 64, even)


def pack_second_kernel(xb_ref, after_ref, b_ref, a_ref):
    pack_rows(xb_ref, a_ref, b_ref, 0, lax.axis_index("gy") % 2 == 0)


def over_sublanes(x):
    return jnp.sum(x, axis=0, keepdims=True)


def lanes_of(x, idx):
    return jnp.take_along_axis(x, idx & 127, axis=1, mode="promise_in_bounds")


def face_row(face):
    return over_sublanes(pltpu.roll(face, 0, 1, stride=17, stride_axis=0))


def face_of(row):
    lane = lax.broadcasted_iota(jnp.int32, (8, 128), 1)
    sub = lax.broadcasted_iota(jnp.int32, (8, 128), 0)
    back = lanes_of(jnp.broadcast_to(row, (8, 128)), lane + 17 * sub)
    return jnp.where((lane < 17) & (sub < 6), back, 0.0)


def column_row(rows, face, at):
    lane = lax.broadcasted_iota(jnp.int32, (8, 128), 1)
    block = jnp.zeros((8, 128), F32)
    for kc in range(6):
        block = jnp.where(lane == kc, jnp.broadcast_to(rows[kc][:, at : at + 1], (8, 128)), block)
    edge = jnp.where(lane == 64, jnp.broadcast_to(face[:, at : at + 1], (8, 128)), 0.0)
    block = pltpu.roll(block, 0, 1, stride=8, stride_axis=0)
    edge = pltpu.roll(edge, 0, 1, stride=1, stride_axis=0)
    return over_sublanes(block + edge)


def column_of(row):
    lane = lax.broadcasted_iota(jnp.int32, (8, 128), 1)
    sub = lax.broadcasted_iota(jnp.int32, (8, 128), 0)
    row = jnp.broadcast_to(row, (8, 128))
    return lanes_of(row, lane + 8 * sub), lanes_of(row, lane + 64 + sub)


def place_of_a():
    return pl.multiple_of(jnp.where(lax.axis_index("gx") % 2 == 1, 0, 128), 64)


def clear_outside(img, tiles):
    zero = jnp.zeros((2 * SPAN, 128), F32)
    for k in range(tiles):
        img[pl.ds(k * TILE_ROWS, 2 * SPAN)] = zero
        img[pl.ds(k * TILE_ROWS + 10 * SPAN, 2 * SPAN)] = zero


def sample_element(img, arr, base, shift, place, first, width):
    lane = lax.broadcasted_iota(jnp.int32, (8, 128), 1)
    mask = ((lane - first) & 127) < width
    starts = [pl.ds(base + z * SPAN, 8) for z in range(9)]
    starts += [pl.ds(base + 8, 8, stride=SPAN), pl.ds(base + (8 * SPAN + 8), 8)]
    for n, start in enumerate(starts):
        pltpu.store(arr.at[place, n], pltpu.roll(img[start, :], shift, 1), mask=mask)


def early_kernel(idx_ref, xb_ref, own_ref, xa_ref, arr_ref, img):
    clear_outside(img, 1)
    at_a = place_of_a()
    for z in range(8):
        for ref, row in ((xa_ref, at_a), (own_ref, 64), (xb_ref, 128 - at_a)):
            img[pl.ds(pl.multiple_of((z + 2) * SPAN + row, 8), 64)] = ref[z].astype(F32)

    def chunk(n, carry):
        for m in range(CHUNK):
            e = n * CHUNK + m
            sample_element(
                img, arr_ref, idx_ref[0, e], idx_ref[1, e], idx_ref[2, e], idx_ref[3, e], 9
            )
        return carry

    lax.fori_loop(0, (idx_ref[6, 0] + (CHUNK - 1)) // CHUNK, chunk, 0)


def late_kernel(
    nx, ny, idx_ref, wgt, xb_ref, own_ref, xa_ref, yb_ref, ya_ref, yd_ref, yc_ref, arr_ref, ref_ref,
    left_ref, wy_ref, res_ref, slope_ref, node_ref, send_ref, sq_ref, img, arr, rsc, gsc,
):
    half = lax.broadcasted_iota(jnp.int32, (64, 128), 1) < 64
    clear_outside(img, 2)
    odd_y = lax.axis_index("gy") % 2 == 1
    at_a = place_of_a()
    segments = (
        (xa_ref, ya_ref, yb_ref, 0, at_a),
        (own_ref, ya_ref, yb_ref, 64, 64),
        (xb_ref, yc_ref, yd_ref, 0, 128 - at_a),
    )
    for p in range(4):
        for ref, pair_a, pair_b, at, row in segments:
            ra = pltpu.roll(ref[p].astype(F32), 64, 1)
            rc = pltpu.roll(ref[p + 4].astype(F32), 64, 1)
            from_a = pair_a[p, pl.ds(at, 64)].astype(F32)
            from_b = pair_b[p, pl.ds(at, 64)].astype(F32)
            lo = jnp.where(odd_y, from_a, from_b)
            hi = jnp.where(odd_y, from_b, from_a)
            at_row = lambda k, q: pl.ds(pl.multiple_of(k * TILE_ROWS + (q + 2) * SPAN + row, 8), 64)
            img[at_row(0, p)] = jnp.where(half, lo, ra)
            img[at_row(1, p)] = jnp.where(half, ra, pltpu.roll(hi, 64, 1))
            img[at_row(0, p + 4)] = jnp.where(half, pltpu.roll(lo, 64, 1), rc)
            img[at_row(1, p + 4)] = jnp.where(half, rc, hi)
    for z in range(8):
        rsc[z] = ref_ref[z].astype(F32).reshape(8, 8, 128)
    arr[...] = arr_ref[...]

    def chunk(n, carry):
        for m in range(CHUNK):
            e = n * CHUNK + m
            base = idx_ref[0, e] + idx_ref[4, e]
            sample_element(
                img, arr, base, idx_ref[1, e], idx_ref[2, e], idx_ref[3, e], idx_ref[5, e]
            )
        return carry

    lax.fori_loop(idx_ref[6, 0] // CHUNK, 128 // CHUNK, chunk, 0)

    lane = lax.broadcasted_iota(jnp.int32, (8, 128), 1)
    sub = lax.broadcasted_iota(jnp.int32, (8, 128), 0)
    phase = lane & 15
    even = phase < 8
    even_next = (phase >= 1) & (phase <= 8)

    def interpolate(cx, square):
        wz, wx, wy = (jnp.broadcast_to(wgt[cx, c : c + 1], (8, 128)) for c in range(3))

        def pair(n):
            ev = arr[cx, n]
            od = arr[cx + 8, n]
            near = jnp.where(even, ev, od)
            return near, pltpu.roll(jnp.where(even_next, ev, od), 127, 1)

        edge, corner = pair(9), pair(10)

        def both_rows(z):
            here = pair(z)
            last = [corner[y][0:1] if z == 8 else edge[y][z : z + 1] for y in range(2)]
            after = [
                jnp.where(sub == 7, jnp.broadcast_to(last[y], (8, 128)), pltpu.roll(here[y], 7, 0))
                for y in range(2)
            ]
            return here, after

        total = [None] * 3
        upper = [None] * 3
        prev = both_rows(0)
        for z in range(8):
            cur = both_rows(z + 1)
            low, dzx, dx = [], [], []
            for y in range(2):
                d0 = cur[0][y] - prev[0][y]
                d1 = cur[1][y] - prev[1][y]
                l0 = prev[0][y] + wz * d0
                l1 = prev[1][y] + wz * d1
                dx.append(l1 - l0)
                low.append(l0 + wx * dx[y])
                dzx.append(d0 + wx * (d1 - d0))
            prev = cur
            slope_y = low[1] - low[0]
            value = low[0] + wy * slope_y
            slope_z = dzx[0] + wy * (dzx[1] - dzx[0])
            slope_x = dx[0] + wy * (dx[1] - dx[0])
            r = rsc[z, cx] - value
            rsc[z, cx] = r
            square = square + r * r
            for k, s in enumerate((slope_z, slope_x, slope_y)):
                slope_ref[k, z, cx] = s
                w = s * r
                u = w * ((z + 0.5) / 8.0)
                total[k] = w if z == 0 else total[k] + w
                upper[k] = u if z == 0 else upper[k] + u
        for k in range(3):
            gsc[2 * k, cx] = total[k] - upper[k]
            gsc[2 * k + 1, cx] = upper[k]
        return square

    square = jnp.zeros((8, 128), F32)
    for cx in range(8):
        square = interpolate(cx, square)
    sq_ref[...] = square
    res_ref[...] = rsc[...].reshape(8, 64, 128).astype(BF16)
    nodes = dot_left(dot_right(left_ref[...], gsc[...].reshape(384, 128)), wy_ref[...])
    node_ref[...] = nodes
    rows = [nodes[kc * 8 : kc * 8 + 8] for kc in range(6)]
    high, low = nodes[48:56], nodes[56:64]
    col_high = column_row(rows, high, 16)
    col_low = column_row(rows, high, 0)
    high, low = face_row(high), face_row(low)
    gx, gy = lax.axis_index("gx"), lax.axis_index("gy")
    send_ref[...] = jnp.zeros(send_ref.shape, F32)
    for dx in (-1, 0, 1):
        for dy in (-1, 0, 1):
            if dx == 0 and dy == 0:
                continue
            block = high if dx == 1 else low if dx == -1 else col_high if dy == 1 else col_low
            px, py = gx + dx, gy + dy

            @pl.when((px >= 0) & (px < nx) & (py >= 0) & (py < ny))
            def _():
                send_ref[px * ny + py] = block


def product_kernel(
    nx, ny, recv_ref, node_ref, slope_ref, sq_ref, expand_ref, wyt_ref, left_ref, wy_ref, res_ref,
    grad_ref, hess_ref, send_ref, out_ref, msc, gsc, sem,
):
    copy_out = pltpu.make_async_copy(res_ref, out_ref, sem)
    copy_out.start()
    gx, gy = lax.axis_index("gx"), lax.axis_index("gy")
    own = gx * ny + gy
    lane = lax.broadcasted_iota(jnp.int32, (8, 128), 1)
    sub = lax.broadcasted_iota(jnp.int32, (8, 128), 0)

    def block(dx, dy):
        px, py = gx + dx, gy + dy
        there = (px >= 0) & (px < nx) & (py >= 0) & (py < ny)
        return recv_ref[jnp.where(there, px * ny + py, own)]

    def column(x, at):
        return jnp.broadcast_to(x[:, at : at + 1], (8, 128))

    def with_corners(dx):
        mid = face_of(block(dx, 0))
        mid = mid + jnp.where(lane == 0, column(face_of(block(dx, -1)), 16), 0.0)
        return mid + jnp.where(lane == 16, column(face_of(block(dx, 1)), 0), 0.0)

    keep_x = jnp.where(gx == nx - 1, 0.0, 1.0).astype(F32)
    keep_y = jnp.where(gy == ny - 1, 0.0, 1.0).astype(F32)
    keep_lane = jnp.where(lane == 16, keep_y, 1.0)
    row_low = with_corners(-1)
    row_high = with_corners(1)
    col_low, edge_low = column_of(block(0, -1))
    col_high, edge_high = column_of(block(0, 1))
    grads = []
    square = jnp.zeros((8, 128), F32)
    for kc in range(6):
        g = node_ref[kc * 8 : kc * 8 + 8]
        g = g + jnp.where(sub == 0, jnp.broadcast_to(row_low[kc : kc + 1], (8, 128)), 0.0)
        g = g + jnp.where(lane == 0, column(col_low, kc), 0.0)
        g = g + jnp.where(lane == 16, column(col_high, kc), 0.0)
        g = g * keep_lane
        grads.append(g)
        grad_ref[kc] = g
        own_g = jnp.where(lane < 16, g, 0.0)
        square = square + own_g * own_g
    face = node_ref[48:56] + row_high
    face = face + jnp.where(lane == 0, column(edge_low, 0), 0.0)
    face = face + jnp.where(lane == 16, column(edge_high, 0), 0.0)
    face = jnp.where(sub < 6, face * keep_lane * keep_x, 0.0)
    full = jnp.concatenate(grads + [face, jnp.zeros((8, 128), F32)], axis=0)
    moved = dot_right(expand_ref[...], dot_left(full, wyt_ref[...]))
    msc[...] = moved.reshape(6, 8, 8, 128)

    def apply(cx, curve):
        m0 = [msc[2 * k, cx] for k in range(3)]
        dm = [msc[2 * k + 1, cx] - m0[k] for k in range(3)]
        total = [None] * 3
        upper = [None] * 3
        for z in range(8):
            sz = (z + 0.5) / 8.0
            s = [slope_ref[k, z, cx] for k in range(3)]
            along = s[0] * (m0[0] + sz * dm[0])
            for k in (1, 2):
                along = along + s[k] * (m0[k] + sz * dm[k])
            curve = curve + along * along
            for k in range(3):
                w = s[k] * along
                u = w * sz
                total[k] = w if z == 0 else total[k] + w
                upper[k] = u if z == 0 else upper[k] + u
        for k in range(3):
            gsc[2 * k, cx] = total[k] - upper[k]
            gsc[2 * k + 1, cx] = upper[k]
        return curve

    curve = lax.fori_loop(0, 8, apply, jnp.zeros((8, 128), F32), unroll=4)
    nodes = dot_left(dot_right(left_ref[...], gsc[...].reshape(384, 128)), wy_ref[...])
    rows = [nodes[kc * 8 : kc * 8 + 8] for kc in range(6)]
    for kc in range(6):
        hess_ref[kc] = rows[kc]
    col_high = column_row(rows, nodes[48:56], 16)
    high = face_row(nodes[48:56])
    spot = lane[:1]
    sums = jnp.where(spot == 104, jnp.sum(sq_ref[...]), 0.0)
    sums = jnp.where(spot == 105, jnp.sum(square), sums)
    sums = jnp.where(spot == 106, jnp.sum(curve) * (1.0 / 512.0), sums)
    tail = spot >= 104
    send_ref[...] = jnp.broadcast_to(sums[None], send_ref.shape)
    for dx, dy, data in ((1, 0, high), (1, 1, high), (0, 1, col_high)):
        px, py = gx + dx, gy + dy

        @pl.when((px < nx) & (py < ny))
        def _():
            send_ref[px * ny + py] = jnp.where(tail, sums, data)

    copy_out.wait()


def finish_kernel(nx, ny, voxels, recv_ref, grad_ref, hess_ref, step_ref, prod_ref, misfit_ref):
    gx, gy = lax.axis_index("gx"), lax.axis_index("gy")
    own = gx * ny + gy
    lane = lax.broadcasted_iota(jnp.int32, (8, 128), 1)
    sub = lax.broadcasted_iota(jnp.int32, (8, 128), 0)

    def block(dx, dy):
        px, py = gx + dx, gy + dy
        there = (px >= 0) & (py >= 0)
        data = recv_ref[jnp.where(there, px * ny + py, own)]
        return jnp.where(there, data, 0.0)

    def column(x, at):
        return jnp.broadcast_to(x[:, at : at + 1], (8, 128))

    total = jnp.sum(recv_ref[...], axis=0)
    misfit_ref[...] = total[:, 104:105] * (1.0 / voxels)
    total = jnp.broadcast_to(total, (8, 128))
    alpha = column(total, 105) / column(total, 106)
    row_low = face_of(block(-1, 0)) + jnp.where(lane == 0, column(face_of(block(-1, -1)), 16), 0.0)
    col_low = column_of(block(0, -1))[0]
    for kc in range(6):
        h = hess_ref[kc]
        h = h + jnp.where(sub == 0, jnp.broadcast_to(row_low[kc : kc + 1], (8, 128)), 0.0)
        h = h + jnp.where(lane == 0, column(col_low, kc), 0.0)
        prod_ref[kc // 2, kc % 2] = h[:, :16]
        step_ref[kc // 2, kc % 2] = (alpha * grad_ref[kc])[:, :16]


def swaps(count, first):
    pairs = [(i, i + 1) for i in range(first, count - 1, 2)]
    return pairs + [(j, i) for i, j in pairs]


def on_device(ref_image, def_image, shift_xy, shift_z, frac, connectivity):
    nx, ny = lax.axis_size("gx"), lax.axis_size("gy")
    peers = nx * ny
    sds = jax.ShapeDtypeStruct
    xa = lax.ppermute(def_image, "gx", swaps(nx, 0))
    xb = lax.ppermute(def_image, "gx", swaps(nx, 1))
    packed = sds((4, 128, 128), BF16)
    to_b, to_a, own = pl.pallas_call(
        pack_first_kernel,
        out_shape=(packed, packed, sds((8, 64, 128), BF16)),
        in_specs=[VMEM] * 2,
        out_specs=(VMEM,) * 3,
        compiler_params=PARAMS,
        cost_estimate=pl.CostEstimate(flops=300000, bytes_accessed=524288, transcendentals=0),
        name="pack_first_halo",
    )(xa, def_image)
    yb = lax.ppermute(to_b, "gy", swaps(ny, 1))
    ya = lax.ppermute(to_a, "gy", swaps(ny, 0))
    row = lax.broadcasted_iota(jnp.int32, (16, 128), 0)
    table = jnp.where(row == 10, shift_z[None], 0)
    table = table + jnp.pad(connectivity, ((0, 8), (0, 0))) + jnp.pad(shift_xy, ((8, 6), (0, 0)))
    idx, wgt = pl.pallas_call(
        index_kernel,
        out_shape=(sds((8, 128), jnp.int32), sds((8, 8, 128), F32)),
        in_specs=[VMEM, VMEM, pl.BlockSpec(memory_space=pl.ANY)],
        out_specs=(VMEM, VMEM),
        compiler_params=PARAMS,
        cost_estimate=pl.CostEstimate(flops=300000, bytes_accessed=262144, transcendentals=0),
        name="order_elements",
    )(table, frac, to_b)
    packed = sds((4, 64, 128), BF16)
    to_d, to_c = pl.pallas_call(
        pack_second_kernel,
        out_shape=(packed, packed),
        in_specs=[VMEM, pl.BlockSpec(memory_space=pl.ANY)],
        out_specs=(VMEM, VMEM),
        compiler_params=PARAMS,
        cost_estimate=pl.CostEstimate(flops=300000, bytes_accessed=524288, transcendentals=0),
        name="pack_second_halo",
    )(xb, idx)
    yd = lax.ppermute(to_d, "gy", swaps(ny, 1))
    yc = lax.ppermute(to_c, "gy", swaps(ny, 0))

    left, wy, expand, wyt = tables()
    arr = pl.pallas_call(
        early_kernel,
        out_shape=sds((16, 11, 8, 128), F32),
        in_specs=[SMEM] + [VMEM] * 3,
        out_specs=VMEM,
        scratch_shapes=[pltpu.VMEM((TILE_ROWS + 8, 128), F32)],
        compiler_params=PARAMS,
        cost_estimate=pl.CostEstimate(flops=4000000, bytes_accessed=2000000, transcendentals=0),
        name="sample_early",
    )(idx, xb, own, xa)
    residual, slopes, nodes, send, square = pl.pallas_call(
        lambda *refs: late_kernel(nx, ny, *refs),
        out_shape=(
            sds((8, 64, 128), BF16),
            sds((3, 8, 8, 8, 128), F32),
            sds((64, 128), F32),
            sds((peers, 1, 128), F32),
            sds((8, 128), F32),
        ),
        in_specs=[SMEM] + [VMEM] * 12,
        out_specs=(VMEM,) * 5,
        scratch_shapes=[
            pltpu.VMEM((2 * TILE_ROWS + 8, 128), F32),
            pltpu.VMEM((16, 11, 8, 128), F32),
            pltpu.VMEM((8, 8, 8, 128), F32),
            pltpu.VMEM((6, 8, 8, 128), F32),
        ],
        compiler_params=PARAMS,
        name="sample_and_gradient",
    )(idx, wgt, xb, own, xa, yb, ya, yd, yc, arr, ref_image, left, wy)
    recv = lax.all_to_all(send, ("gx", "gy"), 0, 0, tiled=True)
    grads, hess, send, residual = pl.pallas_call(
        lambda *refs: product_kernel(nx, ny, *refs),
        out_shape=(
            sds((6, 8, 128), F32),
            sds((6, 8, 128), F32),
            sds((peers, 1, 128), F32),
            sds((8, 64, 128), BF16),
        ),
        in_specs=[VMEM] * 9,
        out_specs=(VMEM,) * 3 + (pl.BlockSpec(memory_space=pl.ANY),),
        scratch_shapes=[
            pltpu.VMEM((6, 8, 8, 128), F32),
            pltpu.VMEM((6, 8, 8, 128), F32),
            pltpu.SemaphoreType.DMA,
        ],
        compiler_params=PARAMS,
        name="gauss_newton_product",
    )(recv, nodes, slopes, square, expand, wyt, left, wy, residual)
    recv = lax.all_to_all(send, ("gx", "gy"), 0, 0, tiled=True)
    voxels = 8 * 64 * 128 * peers
    step, product, misfit = pl.pallas_call(
        lambda *refs: finish_kernel(nx, ny, voxels, *refs),
        out_shape=(sds((3, 2, 8, 16), F32), sds((3, 2, 8, 16), F32), sds((1, 1), F32)),
        in_specs=[VMEM] * 3,
        out_specs=(VMEM,) * 3,
        compiler_params=PARAMS,
        name="finish",
    )(recv, grads, hess)
    return (residual, step, product, misfit[0, 0])


def solution(mesh):
    in_specs = (
        P(None, "gx", "gy"),
        P(None, "gx", "gy"),
        P(None, ("gx", "gy")),
        P(("gx", "gy")),
        P(None, ("gx", "gy")),
        P(None, ("gx", "gy")),
    )
    out_specs = (P(None, "gx", "gy"), P(None, None, "gx", "gy"), P(None, None, "gx", "gy"), P())
    return jax.shard_map(
        on_device, mesh=mesh, in_specs=in_specs, out_specs=out_specs, check_vma=False
    )
```

```python
import jax
import jax.numpy as jnp
import numpy as np
from jax import lax
from jax.experimental import pallas as pl
from jax.experimental.pallas import tpu as pltpu
from jax.sharding import PartitionSpec as P

HALO = 64
F32 = jnp.float32
BF16 = jnp.bfloat16
SPAN = 192
TILE_ROWS = 12 * SPAN
CHUNK = 16
VMEM = pl.BlockSpec(memory_space=pltpu.VMEM)
SMEM = pl.BlockSpec(memory_space=pltpu.SMEM)
PARAMS = pltpu.CompilerParams(vmem_limit_bytes=24 * 1024 * 1024)


def node_weights(count):
    w = np.zeros((count + 1, 8 * count), np.float32)
    for v in range(8 * count):
        s = (v % 8 + 0.5) / 8.0
        w[v // 8, v] = 1.0 - s
        w[v // 8 + 1, v] = s
    return w


def tables():
    wx = node_weights(8)
    left = np.zeros((64, 6, 64), np.float32)
    for kc in range(6):
        left[kc * 8 : kc * 8 + 8, kc] = wx[:8]
        left[48 + kc, kc] = wx[8]
        left[56 + kc, kc] = wx[0]
    left = left.reshape(64, 384)
    expand = left.T.copy()
    expand[:, 56:] = 0.0
    wy = np.zeros((128, 128), np.float32)
    wy[:, :17] = node_weights(16).T
    as_bf = lambda a: jnp.asarray(a, BF16)
    return as_bf(left / 512.0), as_bf(wy), as_bf(expand), as_bf(wy.T)


def split(x):
    hi = x.astype(BF16)
    return hi, (x - hi.astype(F32)).astype(BF16)


def dot(a, b):
    return jnp.dot(a, b, preferred_element_type=F32)


def dot_right(w, x):
    hi, lo = split(x)
    return dot(w, hi) + dot(w, lo)


def dot_left(x, w):
    hi, lo = split(x)
    return dot(hi, w) + dot(lo, w)


def pack_rows(src, dst_a, dst_b, at, even):
    left = lax.broadcasted_iota(jnp.int32, (64, 128), 1) < 64
    for p in range(4):
        a = src[p].astype(F32)
        c = src[p + 4].astype(F32)
        right = jnp.where(left, pltpu.roll(a, 64, 1), c)
        other = jnp.where(left, a, pltpu.roll(c, 64, 1))
        dst_a[p, pl.ds(at, 64)] = jnp.where(even, right, other).astype(BF16)
        dst_b[p, pl.ds(at, 64)] = jnp.where(even, other, right).astype(BF16)


def dot_rows(a, b):
    return lax.dot_general(a, b, (((1,), (1,)), ((), ())), preferred_element_type=F32)


def as_rows(rows):
    sub = lax.broadcasted_iota(jnp.int32, (8, 128), 0)
    out = jnp.zeros((8, 128), F32)
    for n, row in enumerate(rows):
        out = jnp.where(sub == n, jnp.broadcast_to(row.astype(F32), (8, 128)), out)
    return out


def index_kernel(row_ref, frac_ref, own_ref, idx_ref, wgt_ref, keep_ref):
    keep_ref[...] = own_ref[...]
    first = row_ref[0:1]
    col_x = (first * 241) >> 12
    col_y = first - 17 * col_x
    start_x = 8 * col_x + row_ref[8:9] + HALO
    start_y = 8 * col_y + row_ref[9:10] + HALO
    early = (start_y >= 64) & (start_y < 184)
    below = start_y < 64
    offset = jnp.where(early, start_y - 64, jnp.where(below, start_y, start_y - 128))
    base = (row_ref[10:11] + 2) * SPAN + start_x
    tile = jnp.where(early | below, 0, TILE_ROWS)
    shift = (8 * col_y - offset) & 127
    place = (col_y & 1) * 8 + col_x
    width = jnp.where(early, 0, 9)
    flag = early.astype(F32)
    row = lax.broadcasted_iota(jnp.int32, (128, 128), 0)
    lane = lax.broadcasted_iota(jnp.int32, (128, 128), 1)
    upto = dot(as_rows([flag]).astype(BF16), (row <= lane).astype(F32).astype(BF16))[0:1]
    count = jnp.sum(flag, axis=1, keepdims=True)
    rank = jnp.where(early, upto - 1.0, count + lane[0:1].astype(F32) - upto)
    order = (jnp.broadcast_to(rank, (128, 128)) == row.astype(F32)).astype(F32).astype(BF16)
    hi, lo = split(as_rows([base, shift, place, 8 * col_y, tile, width]))
    table = dot_rows(hi, order) + dot_rows(lo, order)
    sub = lax.broadcasted_iota(jnp.int32, (8, 128), 0)
    table = jnp.where(sub == 6, jnp.broadcast_to(count, (8, 128)), table)
    idx_ref[...] = table.astype(jnp.int32)
    value = as_rows([frac_ref[c : c + 1] for c in range(3)])
    hi, lo = split(value)
    rest = (value - hi.astype(F32) - lo.astype(F32)).astype(BF16)
    element = jnp.broadcast_to(col_x * 16 + col_y, (128, 128))
    for cx in range(8):
        spread = (element == cx * 16 + (row >> 3)).astype(F32).astype(BF16)
        wgt_ref[cx] = dot_rows(hi, spread) + dot_rows(lo, spread) + dot_rows(rest, spread)


def pack_first_kernel(xa_ref, own_ref, b_ref, a_ref):
    even = lax.axis_index("gy") % 2 == 0
    pack_rows(xa_ref, a_ref, b_ref, 0, even)
    pack_rows(own_ref, a_ref, b_ref, 64, even)


def pack_second_kernel(xb_ref, after_ref, b_ref, a_ref):
    pack_rows(xb_ref, a_ref, b_ref, 0, lax.axis_index("gy") % 2 == 0)


def over_sublanes(x):
    return jnp.sum(x, axis=0, keepdims=True)


def lanes_of(x, idx):
    return jnp.take_along_axis(x, idx & 127, axis=1, mode="promise_in_bounds")


def face_row(face):
    return over_sublanes(pltpu.roll(face, 0, 1, stride=17, stride_axis=0))


def face_of(row):
    lane = lax.broadcasted_iota(jnp.int32, (8, 128), 1)
    sub = lax.broadcasted_iota(jnp.int32, (8, 128), 0)
    back = lanes_of(jnp.broadcast_to(row, (8, 128)), lane + 17 * sub)
    return jnp.where((lane < 17) & (sub < 6), back, 0.0)


def column_row(rows, face, at):
    lane = lax.broadcasted_iota(jnp.int32, (8, 128), 1)
    block = jnp.zeros((8, 128), F32)
    for kc in range(6):
        block = jnp.where(lane == kc, jnp.broadcast_to(rows[kc][:, at : at + 1], (8, 128)), block)
    edge = jnp.where(lane == 64, jnp.broadcast_to(face[:, at : at + 1], (8, 128)), 0.0)
    block = pltpu.roll(block, 0, 1, stride=8, stride_axis=0)
    edge = pltpu.roll(edge, 0, 1, stride=1, stride_axis=0)
    return over_sublanes(block + edge)


def column_of(row):
    lane = lax.broadcasted_iota(jnp.int32, (8, 128), 1)
    sub = lax.broadcasted_iota(jnp.int32, (8, 128), 0)
    row = jnp.broadcast_to(row, (8, 128))
    return lanes_of(row, lane + 8 * sub), lanes_of(row, lane + 64 + sub)


def place_of_a():
    return pl.multiple_of(jnp.where(lax.axis_index("gx") % 2 == 1, 0, 128), 64)


def clear_outside(img, tiles):
    zero = jnp.zeros((2 * SPAN, 128), F32)
    for k in range(tiles):
        img[pl.ds(k * TILE_ROWS, 2 * SPAN)] = zero
        img[pl.ds(k * TILE_ROWS + 10 * SPAN, 2 * SPAN)] = zero


def sample_element(img, arr, base, shift, place, first, width):
    lane = lax.broadcasted_iota(jnp.int32, (8, 128), 1)
    mask = ((lane - first) & 127) < width
    starts = [pl.ds(base + z * SPAN, 8) for z in range(9)]
    starts += [pl.ds(base + 8, 8, stride=SPAN), pl.ds(base + (8 * SPAN + 8), 8)]
    for n, start in enumerate(starts):
        pltpu.store(arr.at[place, n], pltpu.roll(img[start, :], shift, 1), mask=mask)


def early_kernel(idx_ref, xb_ref, own_ref, xa_ref, arr_ref, img):
    clear_outside(img, 1)
    at_a = place_of_a()
    for z in range(8):
        for ref, row in ((xa_ref, at_a), (own_ref, 64), (xb_ref, 128 - at_a)):
            img[pl.ds(pl.multiple_of((z + 2) * SPAN + row, 8), 64)] = ref[z].astype(F32)

    def chunk(n, carry):
        for m in range(CHUNK):
            e = n * CHUNK + m
            sample_element(
                img, arr_ref, idx_ref[0, e], idx_ref[1, e], idx_ref[2, e], idx_ref[3, e], 9
            )
        return carry

    lax.fori_loop(0, (idx_ref[6, 0] + (CHUNK - 1)) // CHUNK, chunk, 0)


def late_kernel(
    nx, ny, idx_ref, wgt, xb_ref, own_ref, xa_ref, yb_ref, ya_ref, yd_ref, yc_ref, arr_ref, ref_ref,
    left_ref, wy_ref, res_ref, slope_ref, node_ref, send_ref, sq_ref, img, arr, rsc, gsc,
):
    half = lax.broadcasted_iota(jnp.int32, (64, 128), 1) < 64
    clear_outside(img, 2)
    odd_y = lax.axis_index("gy") % 2 == 1
    at_a = place_of_a()
    segments = (
        (xa_ref, ya_ref, yb_ref, 0, at_a),
        (own_ref, ya_ref, yb_ref, 64, 64),
        (xb_ref, yc_ref, yd_ref, 0, 128 - at_a),
    )
    for p in range(4):
        for ref, pair_a, pair_b, at, row in segments:
            ra = pltpu.roll(ref[p].astype(F32), 64, 1)
            rc = pltpu.roll(ref[p + 4].astype(F32), 64, 1)
            from_a = pair_a[p, pl.ds(at, 64)].astype(F32)
            from_b = pair_b[p, pl.ds(at, 64)].astype(F32)
            lo = jnp.where(odd_y, from_a, from_b)
            hi = jnp.where(odd_y, from_b, from_a)
            at_row = lambda k, q: pl.ds(pl.multiple_of(k * TILE_ROWS + (q + 2) * SPAN + row, 8), 64)
            img[at_row(0, p)] = jnp.where(half, lo, ra)
            img[at_row(1, p)] = jnp.where(half, ra, pltpu.roll(hi, 64, 1))
            img[at_row(0, p + 4)] = jnp.where(half, pltpu.roll(lo, 64, 1), rc)
            img[at_row(1, p + 4)] = jnp.where(half, rc, hi)
    for z in range(8):
        rsc[z] = ref_ref[z].astype(F32).reshape(8, 8, 128)
    arr[...] = arr_ref[...]

    def chunk(n, carry):
        for m in range(CHUNK):
            e = n * CHUNK + m
            base = idx_ref[0, e] + idx_ref[4, e]
            sample_element(
                img, arr, base, idx_ref[1, e], idx_ref[2, e], idx_ref[3, e], idx_ref[5, e]
            )
        return carry

    lax.fori_loop(idx_ref[6, 0] // CHUNK, 128 // CHUNK, chunk, 0)

    lane = lax.broadcasted_iota(jnp.int32, (8, 128), 1)
    sub = lax.broadcasted_iota(jnp.int32, (8, 128), 0)
    phase = lane & 15
    even = phase < 8
    even_next = (phase >= 1) & (phase <= 8)

    def interpolate(cx, square):
        wz, wx, wy = (jnp.broadcast_to(wgt[cx, c : c + 1], (8, 128)) for c in range(3))

        def pair(n):
            ev = arr[cx, n]
            od = arr[cx + 8, n]
            near = jnp.where(even, ev, od)
            return near, pltpu.roll(jnp.where(even_next, ev, od), 127, 1)

        edge, corner = pair(9), pair(10)

        def both_rows(z):
            here = pair(z)
            last = [corner[y][0:1] if z == 8 else edge[y][z : z + 1] for y in range(2)]
            after = [
                jnp.where(sub == 7, jnp.broadcast_to(last[y], (8, 128)), pltpu.roll(here[y], 7, 0))
                for y in range(2)
            ]
            return here, after

        total = [None] * 3
        upper = [None] * 3
        prev = both_rows(0)
        for z in range(8):
            cur = both_rows(z + 1)
            low, dzx, dx = [], [], []
            for y in range(2):
                d0 = cur[0][y] - prev[0][y]
                d1 = cur[1][y] - prev[1][y]
                l0 = prev[0][y] + wz * d0
                l1 = prev[1][y] + wz * d1
                dx.append(l1 - l0)
                low.append(l0 + wx * dx[y])
                dzx.append(d0 + wx * (d1 - d0))
            prev = cur
            slope_y = low[1] - low[0]
            value = low[0] + wy * slope_y
            slope_z = dzx[0] + wy * (dzx[1] - dzx[0])
            slope_x = dx[0] + wy * (dx[1] - dx[0])
            r = rsc[z, cx] - value
            rsc[z, cx] = r
            square = square + r * r
            for k, s in enumerate((slope_z, slope_x, slope_y)):
                slope_ref[k, z, cx] = s
                w = s * r
                u = w * ((z + 0.5) / 8.0)
                total[k] = w if z == 0 else total[k] + w
                upper[k] = u if z == 0 else upper[k] + u
        for k in range(3):
            gsc[2 * k, cx] = total[k] - upper[k]
            gsc[2 * k + 1, cx] = upper[k]
        return square

    square = jnp.zeros((8, 128), F32)
    for cx in range(8):
        square = interpolate(cx, square)
    sq_ref[...] = square
    res_ref[...] = rsc[...].reshape(8, 64, 128).astype(BF16)
    nodes = dot_left(dot_right(left_ref[...], gsc[...].reshape(384, 128)), wy_ref[...])
    node_ref[...] = nodes
    rows = [nodes[kc * 8 : kc * 8 + 8] for kc in range(6)]
    high, low = nodes[48:56], nodes[56:64]
    col_high = column_row(rows, high, 16)
    col_low = column_row(rows, high, 0)
    high, low = face_row(high), face_row(low)
    gx, gy = lax.axis_index("gx"), lax.axis_index("gy")
    send_ref[...] = jnp.zeros(send_ref.shape, F32)
    for dx in (-1, 0, 1):
        for dy in (-1, 0, 1):
            if dx == 0 and dy == 0:
                continue
            block = high if dx == 1 else low if dx == -1 else col_high if dy == 1 else col_low
            px, py = gx + dx, gy + dy

            @pl.when((px >= 0) & (px < nx) & (py >= 0) & (py < ny))
            def _():
                send_ref[px * ny + py] = block


def product_kernel(
    nx, ny, recv_ref, node_ref, slope_ref, sq_ref, expand_ref, wyt_ref, left_ref, wy_ref, res_ref,
    grad_ref, hess_ref, send_ref, out_ref, msc, gsc, sem,
):
    copy_out = pltpu.make_async_copy(res_ref, out_ref, sem)
    copy_out.start()
    gx, gy = lax.axis_index("gx"), lax.axis_index("gy")
    own = gx * ny + gy
    lane = lax.broadcasted_iota(jnp.int32, (8, 128), 1)
    sub = lax.broadcasted_iota(jnp.int32, (8, 128), 0)

    def block(dx, dy):
        px, py = gx + dx, gy + dy
        there = (px >= 0) & (px < nx) & (py >= 0) & (py < ny)
        return recv_ref[jnp.where(there, px * ny + py, own)]

    def column(x, at):
        return jnp.broadcast_to(x[:, at : at + 1], (8, 128))

    def with_corners(dx):
        mid = face_of(block(dx, 0))
        mid = mid + jnp.where(lane == 0, column(face_of(block(dx, -1)), 16), 0.0)
        return mid + jnp.where(lane == 16, column(face_of(block(dx, 1)), 0), 0.0)

    keep_x = jnp.where(gx == nx - 1, 0.0, 1.0).astype(F32)
    keep_y = jnp.where(gy == ny - 1, 0.0, 1.0).astype(F32)
    keep_lane = jnp.where(lane == 16, keep_y, 1.0)
    row_low = with_corners(-1)
    row_high = with_corners(1)
    col_low, edge_low = column_of(block(0, -1))
    col_high, edge_high = column_of(block(0, 1))
    grads = []
    square = jnp.zeros((8, 128), F32)
    for kc in range(6):
        g = node_ref[kc * 8 : kc * 8 + 8]
        g = g + jnp.where(sub == 0, jnp.broadcast_to(row_low[kc : kc + 1], (8, 128)), 0.0)
        g = g + jnp.where(lane == 0, column(col_low, kc), 0.0)
        g = g + jnp.where(lane == 16, column(col_high, kc), 0.0)
        g = g * keep_lane
        grads.append(g)
        grad_ref[kc] = g
        own_g = jnp.where(lane < 16, g, 0.0)
        square = square + own_g * own_g
    face = node_ref[48:56] + row_high
    face = face + jnp.where(lane == 0, column(edge_low, 0), 0.0)
    face = face + jnp.where(lane == 16, column(edge_high, 0), 0.0)
    face = jnp.where(sub < 6, face * keep_lane * keep_x, 0.0)
    full = jnp.concatenate(grads + [face, jnp.zeros((8, 128), F32)], axis=0)
    moved = dot_right(expand_ref[...], dot_left(full, wyt_ref[...]))
    msc[...] = moved.reshape(6, 8, 8, 128)

    def apply(cx, curve):
        m0 = [msc[2 * k, cx] for k in range(3)]
        dm = [msc[2 * k + 1, cx] - m0[k] for k in range(3)]
        total = [None] * 3
        upper = [None] * 3
        for z in range(8):
            sz = (z + 0.5) / 8.0
            s = [slope_ref[k, z, cx] for k in range(3)]
            along = s[0] * (m0[0] + sz * dm[0])
            for k in (1, 2):
                along = along + s[k] * (m0[k] + sz * dm[k])
            curve = curve + along * along
            for k in range(3):
                w = s[k] * along
                u = w * sz
                total[k] = w if z == 0 else total[k] + w
                upper[k] = u if z == 0 else upper[k] + u
        for k in range(3):
            gsc[2 * k, cx] = total[k] - upper[k]
            gsc[2 * k + 1, cx] = upper[k]
        return curve

    curve = lax.fori_loop(0, 8, apply, jnp.zeros((8, 128), F32), unroll=4)
    nodes = dot_left(dot_right(left_ref[...], gsc[...].reshape(384, 128)), wy_ref[...])
    rows = [nodes[kc * 8 : kc * 8 + 8] for kc in range(6)]
    for kc in range(6):
        hess_ref[kc] = rows[kc]
    col_high = column_row(rows, nodes[48:56], 16)
    high = face_row(nodes[48:56])
    spot = lane[:1]
    sums = jnp.where(spot == 104, jnp.sum(sq_ref[...]), 0.0)
    sums = jnp.where(spot == 105, jnp.sum(square), sums)
    sums = jnp.where(spot == 106, jnp.sum(curve) * (1.0 / 512.0), sums)
    tail = spot >= 104
    send_ref[...] = jnp.broadcast_to(sums[None], send_ref.shape)
    for dx, dy, data in ((1, 0, high), (1, 1, high), (0, 1, col_high)):
        px, py = gx + dx, gy + dy

        @pl.when((px < nx) & (py < ny))
        def _():
            send_ref[px * ny + py] = jnp.where(tail, sums, data)

    copy_out.wait()


def finish_kernel(nx, ny, voxels, recv_ref, grad_ref, hess_ref, step_ref, prod_ref, misfit_ref):
    gx, gy = lax.axis_index("gx"), lax.axis_index("gy")
    own = gx * ny + gy
    lane = lax.broadcasted_iota(jnp.int32, (8, 128), 1)
    sub = lax.broadcasted_iota(jnp.int32, (8, 128), 0)

    def block(dx, dy):
        px, py = gx + dx, gy + dy
        there = (px >= 0) & (py >= 0)
        data = recv_ref[jnp.where(there, px * ny + py, own)]
        return jnp.where(there, data, 0.0)

    def column(x, at):
        return jnp.broadcast_to(x[:, at : at + 1], (8, 128))

    total = jnp.sum(recv_ref[...], axis=0)
    misfit_ref[...] = total[:, 104:105] * (1.0 / voxels)
    total = jnp.broadcast_to(total, (8, 128))
    alpha = column(total, 105) / column(total, 106)
    row_low = face_of(block(-1, 0)) + jnp.where(lane == 0, column(face_of(block(-1, -1)), 16), 0.0)
    col_low = column_of(block(0, -1))[0]
    for kc in range(6):
        h = hess_ref[kc]
        h = h + jnp.where(sub == 0, jnp.broadcast_to(row_low[kc : kc + 1], (8, 128)), 0.0)
        h = h + jnp.where(lane == 0, column(col_low, kc), 0.0)
        prod_ref[kc // 2, kc % 2] = h[:, :16]
        step_ref[kc // 2, kc % 2] = (alpha * grad_ref[kc])[:, :16]


def swaps(count, first):
    pairs = [(i, i + 1) for i in range(first, count - 1, 2)]
    return pairs + [(j, i) for i, j in pairs]


def on_device(ref_image, def_image, shift_xy, shift_z, frac, connectivity):
    nx, ny = lax.axis_size("gx"), lax.axis_size("gy")
    peers = nx * ny
    sds = jax.ShapeDtypeStruct
    xa = lax.ppermute(def_image, "gx", swaps(nx, 0))
    xb = lax.ppermute(def_image, "gx", swaps(nx, 1))
    row = lax.broadcasted_iota(jnp.int32, (16, 128), 0)
    table = jnp.where(row == 10, shift_z[None], 0)
    table = table + jnp.pad(connectivity, ((0, 8), (0, 0))) + jnp.pad(shift_xy, ((8, 6), (0, 0)))
    idx, wgt, own = pl.pallas_call(
        index_kernel,
        out_shape=(sds((8, 128), jnp.int32), sds((8, 8, 128), F32), sds((8, 64, 128), BF16)),
        in_specs=[VMEM] * 3,
        out_specs=(VMEM,) * 3,
        compiler_params=PARAMS,
        cost_estimate=pl.CostEstimate(flops=300000, bytes_accessed=262144, transcendentals=0),
        name="order_elements",
    )(table, frac, def_image)
    packed = sds((4, 128, 128), BF16)
    to_b, to_a = pl.pallas_call(
        pack_first_kernel,
        out_shape=(packed, packed),
        in_specs=[VMEM] * 2,
        out_specs=(VMEM, VMEM),
        compiler_params=PARAMS,
        cost_estimate=pl.CostEstimate(flops=300000, bytes_accessed=524288, transcendentals=0),
        name="pack_first_halo",
    )(xa, own)
    yb = lax.ppermute(to_b, "gy", swaps(ny, 1))
    ya = lax.ppermute(to_a, "gy", swaps(ny, 0))
    packed = sds((4, 64, 128), BF16)
    to_d, to_c = pl.pallas_call(
        pack_second_kernel,
        out_shape=(packed, packed),
        in_specs=[VMEM, pl.BlockSpec(memory_space=pl.ANY)],
        out_specs=(VMEM, VMEM),
        compiler_params=PARAMS,
        cost_estimate=pl.CostEstimate(flops=300000, bytes_accessed=524288, transcendentals=0),
        name="pack_second_halo",
    )(xb, to_a)
    yd = lax.ppermute(to_d, "gy", swaps(ny, 1))
    yc = lax.ppermute(to_c, "gy", swaps(ny, 0))

    left, wy, expand, wyt = tables()
    arr = pl.pallas_call(
        early_kernel,
        out_shape=sds((16, 11, 8, 128), F32),
        in_specs=[SMEM] + [VMEM] * 3,
        out_specs=VMEM,
        scratch_shapes=[pltpu.VMEM((TILE_ROWS + 8, 128), F32)],
        compiler_params=PARAMS,
        cost_estimate=pl.CostEstimate(flops=4000000, bytes_accessed=2000000, transcendentals=0),
        name="sample_early",
    )(idx, xb, own, xa)
    residual, slopes, nodes, send, square = pl.pallas_call(
        lambda *refs: late_kernel(nx, ny, *refs),
        out_shape=(
            sds((8, 64, 128), BF16),
            sds((3, 8, 8, 8, 128), F32),
            sds((64, 128), F32),
            sds((peers, 1, 128), F32),
            sds((8, 128), F32),
        ),
        in_specs=[SMEM] + [VMEM] * 12,
        out_specs=(VMEM,) * 5,
        scratch_shapes=[
            pltpu.VMEM((2 * TILE_ROWS + 8, 128), F32),
            pltpu.VMEM((16, 11, 8, 128), F32),
            pltpu.VMEM((8, 8, 8, 128), F32),
            pltpu.VMEM((6, 8, 8, 128), F32),
        ],
        compiler_params=PARAMS,
        name="sample_and_gradient",
    )(idx, wgt, xb, own, xa, yb, ya, yd, yc, arr, ref_image, left, wy)
    recv = lax.all_to_all(send, ("gx", "gy"), 0, 0, tiled=True)
    grads, hess, send, residual = pl.pallas_call(
        lambda *refs: product_kernel(nx, ny, *refs),
        out_shape=(
            sds((6, 8, 128), F32),
            sds((6, 8, 128), F32),
            sds((peers, 1, 128), F32),
            sds((8, 64, 128), BF16),
        ),
        in_specs=[VMEM] * 9,
        out_specs=(VMEM,) * 3 + (pl.BlockSpec(memory_space=pl.ANY),),
        scratch_shapes=[
            pltpu.VMEM((6, 8, 8, 128), F32),
            pltpu.VMEM((6, 8, 8, 128), F32),
            pltpu.SemaphoreType.DMA,
        ],
        compiler_params=PARAMS,
        name="gauss_newton_product",
    )(recv, nodes, slopes, square, expand, wyt, left, wy, residual)
    recv = lax.all_to_all(send, ("gx", "gy"), 0, 0, tiled=True)
    voxels = 8 * 64 * 128 * peers
    step, product, misfit = pl.pallas_call(
        lambda *refs: finish_kernel(nx, ny, voxels, *refs),
        out_shape=(sds((3, 2, 8, 16), F32), sds((3, 2, 8, 16), F32), sds((1, 1), F32)),
        in_specs=[VMEM] * 3,
        out_specs=(VMEM,) * 3,
        compiler_params=PARAMS,
        name="finish",
    )(recv, grads, hess)
    return (residual, step, product, misfit[0, 0])


def solution(mesh):
    in_specs = (
        P(None, "gx", "gy"),
        P(None, "gx", "gy"),
        P(None, ("gx", "gy")),
        P(("gx", "gy")),
        P(None, ("gx", "gy")),
        P(None, ("gx", "gy")),
    )
    out_specs = (P(None, "gx", "gy"), P(None, None, "gx", "gy"), P(None, None, "gx", "gy"), P())
    return jax.shard_map(
        on_device, mesh=mesh, in_specs=in_specs, out_specs=out_specs, check_vma=False
    )
```

```python
import jax
import jax.numpy as jnp
import numpy as np
from jax import lax
from jax.experimental import pallas as pl
from jax.experimental.pallas import tpu as pltpu
from jax.sharding import PartitionSpec as P

HALO = 64
F32 = jnp.float32
BF16 = jnp.bfloat16
SPAN = 192
TILE_ROWS = 12 * SPAN
CHUNK = 16
VMEM = pl.BlockSpec(memory_space=pltpu.VMEM)
SMEM = pl.BlockSpec(memory_space=pltpu.SMEM)
PARAMS = pltpu.CompilerParams(vmem_limit_bytes=24 * 1024 * 1024)


def node_weights(count):
    w = np.zeros((count + 1, 8 * count), np.float32)
    for v in range(8 * count):
        s = (v % 8 + 0.5) / 8.0
        w[v // 8, v] = 1.0 - s
        w[v // 8 + 1, v] = s
    return w


def tables():
    wx = node_weights(8)
    left = np.zeros((64, 6, 64), np.float32)
    for kc in range(6):
        left[kc * 8 : kc * 8 + 8, kc] = wx[:8]
        left[48 + kc, kc] = wx[8]
        left[56 + kc, kc] = wx[0]
    left = left.reshape(64, 384)
    expand = left.T.copy()
    expand[:, 56:] = 0.0
    wy = np.zeros((128, 128), np.float32)
    wy[:, :17] = node_weights(16).T
    as_bf = lambda a: jnp.asarray(a, BF16)
    return as_bf(left / 512.0), as_bf(wy), as_bf(expand), as_bf(wy.T)


def split(x):
    hi = x.astype(BF16)
    return hi, (x - hi.astype(F32)).astype(BF16)


def dot(a, b):
    return jnp.dot(a, b, preferred_element_type=F32)


def dot_right(w, x):
    hi, lo = split(x)
    return dot(w, hi) + dot(w, lo)


def dot_left(x, w):
    hi, lo = split(x)
    return dot(hi, w) + dot(lo, w)


def pack_rows(src, dst_a, dst_b, at, even):
    left = lax.broadcasted_iota(jnp.int32, (64, 128), 1) < 64
    for p in range(4):
        a = src[p].astype(F32)
        c = src[p + 4].astype(F32)
        right = jnp.where(left, pltpu.roll(a, 64, 1), c)
        other = jnp.where(left, a, pltpu.roll(c, 64, 1))
        dst_a[p, pl.ds(at, 64)] = jnp.where(even, right, other).astype(BF16)
        dst_b[p, pl.ds(at, 64)] = jnp.where(even, other, right).astype(BF16)


def dot_rows(a, b):
    return lax.dot_general(a, b, (((1,), (1,)), ((), ())), preferred_element_type=F32)


def as_rows(rows):
    sub = lax.broadcasted_iota(jnp.int32, (8, 128), 0)
    out = jnp.zeros((8, 128), F32)
    for n, row in enumerate(rows):
        out = jnp.where(sub == n, jnp.broadcast_to(row.astype(F32), (8, 128)), out)
    return out


def index_kernel(row_ref, frac_ref, own_ref, idx_ref, wgt_ref, keep_ref):
    keep_ref[...] = own_ref[...]
    first = row_ref[0:1]
    col_x = (first * 241) >> 12
    col_y = first - 17 * col_x
    start_x = 8 * col_x + row_ref[8:9] + HALO
    start_y = 8 * col_y + row_ref[9:10] + HALO
    early = (start_y >= 64) & (start_y < 184)
    below = start_y < 64
    offset = jnp.where(early, start_y - 64, jnp.where(below, start_y, start_y - 128))
    base = (row_ref[10:11] + 2) * SPAN + start_x
    tile = jnp.where(early | below, 0, TILE_ROWS)
    shift = (8 * col_y - offset) & 127
    place = (col_y & 1) * 8 + col_x
    width = jnp.where(early, 0, 9)
    flag = early.astype(F32)
    row = lax.broadcasted_iota(jnp.int32, (128, 128), 0)
    lane = lax.broadcasted_iota(jnp.int32, (128, 128), 1)
    upto = dot(as_rows([flag]).astype(BF16), (row <= lane).astype(F32).astype(BF16))[0:1]
    count = jnp.sum(flag, axis=1, keepdims=True)
    rank = jnp.where(early, upto - 1.0, count + lane[0:1].astype(F32) - upto)
    order = (jnp.broadcast_to(rank, (128, 128)) == row.astype(F32)).astype(F32).astype(BF16)
    hi, lo = split(as_rows([base, shift, place, 8 * col_y, tile, width]))
    table = dot_rows(hi, order) + dot_rows(lo, order)
    sub = lax.broadcasted_iota(jnp.int32, (8, 128), 0)
    table = jnp.where(sub == 6, jnp.broadcast_to(count, (8, 128)), table)
    idx_ref[...] = table.astype(jnp.int32)
    value = as_rows([frac_ref[c : c + 1] for c in range(3)])
    hi, lo = split(value)
    rest = (value - hi.astype(F32) - lo.astype(F32)).astype(BF16)
    element = jnp.broadcast_to(col_x * 16 + col_y, (128, 128))
    for cx in range(8):
        spread = (element == cx * 16 + (row >> 3)).astype(F32).astype(BF16)
        wgt_ref[cx] = dot_rows(hi, spread) + dot_rows(lo, spread) + dot_rows(rest, spread)


def pack_first_kernel(xa_ref, own_ref, b_ref, a_ref):
    even = lax.axis_index("gy") % 2 == 0
    pack_rows(xa_ref, a_ref, b_ref, 0, even)
    pack_rows(own_ref, a_ref, b_ref, 64, even)


def pack_second_kernel(xb_ref, after_ref, b_ref, a_ref):
    pack_rows(xb_ref, a_ref, b_ref, 0, lax.axis_index("gy") % 2 == 0)


def over_sublanes(x):
    return jnp.sum(x, axis=0, keepdims=True)


def lanes_of(x, idx):
    return jnp.take_along_axis(x, idx & 127, axis=1, mode="promise_in_bounds")


def face_row(face):
    return over_sublanes(pltpu.roll(face, 0, 1, stride=17, stride_axis=0))


def face_of(row):
    lane = lax.broadcasted_iota(jnp.int32, (8, 128), 1)
    sub = lax.broadcasted_iota(jnp.int32, (8, 128), 0)
    back = lanes_of(jnp.broadcast_to(row, (8, 128)), lane + 17 * sub)
    return jnp.where((lane < 17) & (sub < 6), back, 0.0)


def column_row(rows, face, at):
    lane = lax.broadcasted_iota(jnp.int32, (8, 128), 1)
    sub = lax.broadcasted_iota(jnp.int32, (8, 128), 0)
    out = jnp.where(lane == 64 + sub, jnp.broadcast_to(face[:, at : at + 1], (8, 128)), 0.0)
    for kc in range(6):
        col = jnp.broadcast_to(rows[kc][:, at : at + 1], (8, 128))
        out = jnp.where(lane == 8 * sub + kc, col, out)
    return over_sublanes(out)


def column_of(row):
    lane = lax.broadcasted_iota(jnp.int32, (8, 128), 1)
    sub = lax.broadcasted_iota(jnp.int32, (8, 128), 0)
    row = jnp.broadcast_to(row, (8, 128))
    return lanes_of(row, lane + 8 * sub), lanes_of(row, lane + 64 + sub)


def place_of_a():
    return pl.multiple_of(jnp.where(lax.axis_index("gx") % 2 == 1, 0, 128), 64)


def clear_outside(img, tiles):
    zero = jnp.zeros((2 * SPAN, 128), F32)
    for k in range(tiles):
        img[pl.ds(k * TILE_ROWS, 2 * SPAN)] = zero
        img[pl.ds(k * TILE_ROWS + 10 * SPAN, 2 * SPAN)] = zero


def sample_element(img, arr, base, shift, place, first, width):
    lane = lax.broadcasted_iota(jnp.int32, (8, 128), 1)
    mask = ((lane - first) & 127) < width
    starts = [pl.ds(base + z * SPAN, 8) for z in range(9)]
    starts += [pl.ds(base + 8, 8, stride=SPAN), pl.ds(base + (8 * SPAN + 8), 8)]
    for n, start in enumerate(starts):
        pltpu.store(arr.at[place, n], pltpu.roll(img[start, :], shift, 1), mask=mask)


def early_kernel(idx_ref, xb_ref, own_ref, xa_ref, arr_ref, img):
    clear_outside(img, 1)
    at_a = place_of_a()
    for z in range(8):
        for ref, row in ((xa_ref, at_a), (own_ref, 64), (xb_ref, 128 - at_a)):
            img[pl.ds(pl.multiple_of((z + 2) * SPAN + row, 8), 64)] = ref[z].astype(F32)

    def chunk(n, carry):
        for m in range(CHUNK):
            e = n * CHUNK + m
            sample_element(
                img, arr_ref, idx_ref[0, e], idx_ref[1, e], idx_ref[2, e], idx_ref[3, e], 9
            )
        return carry

    lax.fori_loop(0, (idx_ref[6, 0] + (CHUNK - 1)) // CHUNK, chunk, 0)


def late_kernel(
    nx, ny, idx_ref, wgt, xb_ref, own_ref, xa_ref, yb_ref, ya_ref, yd_ref, yc_ref, arr_ref, ref_ref,
    left_ref, wy_ref, res_ref, slope_ref, node_ref, send_ref, sq_ref, img, arr, rsc, gsc,
):
    half = lax.broadcasted_iota(jnp.int32, (64, 128), 1) < 64
    clear_outside(img, 2)
    odd_y = lax.axis_index("gy") % 2 == 1
    at_a = place_of_a()
    segments = (
        (xa_ref, ya_ref, yb_ref, 0, at_a),
        (own_ref, ya_ref, yb_ref, 64, 64),
        (xb_ref, yc_ref, yd_ref, 0, 128 - at_a),
    )
    for p in range(4):
        for ref, pair_a, pair_b, at, row in segments:
            ra = pltpu.roll(ref[p].astype(F32), 64, 1)
            rc = pltpu.roll(ref[p + 4].astype(F32), 64, 1)
            from_a = pair_a[p, pl.ds(at, 64)].astype(F32)
            from_b = pair_b[p, pl.ds(at, 64)].astype(F32)
            lo = jnp.where(odd_y, from_a, from_b)
            hi = jnp.where(odd_y, from_b, from_a)
            at_row = lambda k, q: pl.ds(pl.multiple_of(k * TILE_ROWS + (q + 2) * SPAN + row, 8), 64)
            img[at_row(0, p)] = jnp.where(half, lo, ra)
            img[at_row(1, p)] = jnp.where(half, ra, pltpu.roll(hi, 64, 1))
            img[at_row(0, p + 4)] = jnp.where(half, pltpu.roll(lo, 64, 1), rc)
            img[at_row(1, p + 4)] = jnp.where(half, rc, hi)
    for z in range(8):
        rsc[z] = ref_ref[z].astype(F32).reshape(8, 8, 128)
    arr[...] = arr_ref[...]

    def chunk(n, carry):
        for m in range(CHUNK):
            e = n * CHUNK + m
            base = idx_ref[0, e] + idx_ref[4, e]
            sample_element(
                img, arr, base, idx_ref[1, e], idx_ref[2, e], idx_ref[3, e], idx_ref[5, e]
            )
        return carry

    lax.fori_loop(idx_ref[6, 0] // CHUNK, 128 // CHUNK, chunk, 0)

    lane = lax.broadcasted_iota(jnp.int32, (8, 128), 1)
    sub = lax.broadcasted_iota(jnp.int32, (8, 128), 0)
    phase = lane & 15
    even = phase < 8
    even_next = (phase >= 1) & (phase <= 8)

    def interpolate(cx, square):
        wz, wx, wy = (jnp.broadcast_to(wgt[cx, c : c + 1], (8, 128)) for c in range(3))

        def pair(n):
            ev = arr[cx, n]
            od = arr[cx + 8, n]
            near = jnp.where(even, ev, od)
            return near, pltpu.roll(jnp.where(even_next, ev, od), 127, 1)

        edge, corner = pair(9), pair(10)

        def both_rows(z):
            here = pair(z)
            last = [corner[y][0:1] if z == 8 else edge[y][z : z + 1] for y in range(2)]
            after = [
                jnp.where(sub == 7, jnp.broadcast_to(last[y], (8, 128)), pltpu.roll(here[y], 7, 0))
                for y in range(2)
            ]
            return here, after

        total = [None] * 3
        upper = [None] * 3
        prev = both_rows(0)
        for z in range(8):
            cur = both_rows(z + 1)
            low, dzx, dx = [], [], []
            for y in range(2):
                d0 = cur[0][y] - prev[0][y]
                d1 = cur[1][y] - prev[1][y]
                l0 = prev[0][y] + wz * d0
                l1 = prev[1][y] + wz * d1
                dx.append(l1 - l0)
                low.append(l0 + wx * dx[y])
                dzx.append(d0 + wx * (d1 - d0))
            prev = cur
            slope_y = low[1] - low[0]
            value = low[0] + wy * slope_y
            slope_z = dzx[0] + wy * (dzx[1] - dzx[0])
            slope_x = dx[0] + wy * (dx[1] - dx[0])
            r = rsc[z, cx] - value
            rsc[z, cx] = r
            square = square + r * r
            for k, s in enumerate((slope_z, slope_x, slope_y)):
                slope_ref[k, z, cx] = s
                w = s * r
                u = w * ((z + 0.5) / 8.0)
                total[k] = w if z == 0 else total[k] + w
                upper[k] = u if z == 0 else upper[k] + u
        for k in range(3):
            gsc[2 * k, cx] = total[k] - upper[k]
            gsc[2 * k + 1, cx] = upper[k]
        return square

    sq_ref[...] = lax.fori_loop(0, 8, interpolate, jnp.zeros((8, 128), F32), unroll=4)
    res_ref[...] = rsc[...].reshape(8, 64, 128).astype(BF16)
    nodes = dot_left(dot_right(left_ref[...], gsc[...].reshape(384, 128)), wy_ref[...])
    node_ref[...] = nodes
    rows = [nodes[kc * 8 : kc * 8 + 8] for kc in range(6)]
    high, low = nodes[48:56], nodes[56:64]
    col_high = column_row(rows, high, 16)
    col_low = column_row(rows, high, 0)
    high, low = face_row(high), face_row(low)
    gx, gy = lax.axis_index("gx"), lax.axis_index("gy")
    send_ref[...] = jnp.zeros(send_ref.shape, F32)
    for dx in (-1, 0, 1):
        for dy in (-1, 0, 1):
            if dx == 0 and dy == 0:
                continue
            block = high if dx == 1 else low if dx == -1 else col_high if dy == 1 else col_low
            px, py = gx + dx, gy + dy

            @pl.when((px >= 0) & (px < nx) & (py >= 0) & (py < ny))
            def _():
                send_ref[px * ny + py] = block


def product_kernel(
    nx, ny, recv_ref, node_ref, slope_ref, sq_ref, expand_ref, wyt_ref, left_ref, wy_ref, res_ref,
    grad_ref, hess_ref, send_ref, out_ref, msc, gsc, sem,
):
    copy_out = pltpu.make_async_copy(res_ref, out_ref, sem)
    copy_out.start()
    gx, gy = lax.axis_index("gx"), lax.axis_index("gy")
    own = gx * ny + gy
    lane = lax.broadcasted_iota(jnp.int32, (8, 128), 1)
    sub = lax.broadcasted_iota(jnp.int32, (8, 128), 0)

    def block(dx, dy):
        px, py = gx + dx, gy + dy
        there = (px >= 0) & (px < nx) & (py >= 0) & (py < ny)
        return recv_ref[jnp.where(there, px * ny + py, own)]

    def column(x, at):
        return jnp.broadcast_to(x[:, at : at + 1], (8, 128))

    def with_corners(dx):
        mid = face_of(block(dx, 0))
        mid = mid + jnp.where(lane == 0, column(face_of(block(dx, -1)), 16), 0.0)
        return mid + jnp.where(lane == 16, column(face_of(block(dx, 1)), 0), 0.0)

    keep_x = jnp.where(gx == nx - 1, 0.0, 1.0).astype(F32)
    keep_y = jnp.where(gy == ny - 1, 0.0, 1.0).astype(F32)
    keep_lane = jnp.where(lane == 16, keep_y, 1.0)
    row_low = with_corners(-1)
    row_high = with_corners(1)
    col_low, edge_low = column_of(block(0, -1))
    col_high, edge_high = column_of(block(0, 1))
    grads = []
    square = jnp.zeros((8, 128), F32)
    for kc in range(6):
        g = node_ref[kc * 8 : kc * 8 + 8]
        g = g + jnp.where(sub == 0, jnp.broadcast_to(row_low[kc : kc + 1], (8, 128)), 0.0)
        g = g + jnp.where(lane == 0, column(col_low, kc), 0.0)
        g = g + jnp.where(lane == 16, column(col_high, kc), 0.0)
        g = g * keep_lane
        grads.append(g)
        grad_ref[kc] = g
        own_g = jnp.where(lane < 16, g, 0.0)
        square = square + own_g * own_g
    face = node_ref[48:56] + row_high
    face = face + jnp.where(lane == 0, column(edge_low, 0), 0.0)
    face = face + jnp.where(lane == 16, column(edge_high, 0), 0.0)
    face = jnp.where(sub < 6, face * keep_lane * keep_x, 0.0)
    full = jnp.concatenate(grads + [face, jnp.zeros((8, 128), F32)], axis=0)
    moved = dot_right(expand_ref[...], dot_left(full, wyt_ref[...]))
    msc[...] = moved.reshape(6, 8, 8, 128)

    def apply(cx, curve):
        m0 = [msc[2 * k, cx] for k in range(3)]
        dm = [msc[2 * k + 1, cx] - m0[k] for k in range(3)]
        total = [None] * 3
        upper = [None] * 3
        for z in range(8):
            sz = (z + 0.5) / 8.0
            s = [slope_ref[k, z, cx] for k in range(3)]
            along = s[0] * (m0[0] + sz * dm[0])
            for k in (1, 2):
                along = along + s[k] * (m0[k] + sz * dm[k])
            curve = curve + along * along
            for k in range(3):
                w = s[k] * along
                u = w * sz
                total[k] = w if z == 0 else total[k] + w
                upper[k] = u if z == 0 else upper[k] + u
        for k in range(3):
            gsc[2 * k, cx] = total[k] - upper[k]
            gsc[2 * k + 1, cx] = upper[k]
        return curve

    curve = lax.fori_loop(0, 8, apply, jnp.zeros((8, 128), F32), unroll=4)
    nodes = dot_left(dot_right(left_ref[...], gsc[...].reshape(384, 128)), wy_ref[...])
    rows = [nodes[kc * 8 : kc * 8 + 8] for kc in range(6)]
    for kc in range(6):
        hess_ref[kc] = rows[kc]
    col_high = column_row(rows, nodes[48:56], 16)
    high = face_row(nodes[48:56])
    spot = lane[:1]
    sums = jnp.where(spot == 104, jnp.sum(sq_ref[...]), 0.0)
    sums = jnp.where(spot == 105, jnp.sum(square), sums)
    sums = jnp.where(spot == 106, jnp.sum(curve) * (1.0 / 512.0), sums)
    tail = spot >= 104
    send_ref[...] = jnp.broadcast_to(sums[None], send_ref.shape)
    for dx, dy, data in ((1, 0, high), (1, 1, high), (0, 1, col_high)):
        px, py = gx + dx, gy + dy

        @pl.when((px < nx) & (py < ny))
        def _():
            send_ref[px * ny + py] = jnp.where(tail, sums, data)

    copy_out.wait()


def finish_kernel(nx, ny, voxels, recv_ref, grad_ref, hess_ref, step_ref, prod_ref, misfit_ref):
    gx, gy = lax.axis_index("gx"), lax.axis_index("gy")
    own = gx * ny + gy
    lane = lax.broadcasted_iota(jnp.int32, (8, 128), 1)
    sub = lax.broadcasted_iota(jnp.int32, (8, 128), 0)

    def block(dx, dy):
        px, py = gx + dx, gy + dy
        there = (px >= 0) & (py >= 0)
        data = recv_ref[jnp.where(there, px * ny + py, own)]
        return jnp.where(there, data, 0.0)

    def column(x, at):
        return jnp.broadcast_to(x[:, at : at + 1], (8, 128))

    total = jnp.sum(recv_ref[...], axis=0)
    misfit_ref[...] = total[:, 104:105] * (1.0 / voxels)
    total = jnp.broadcast_to(total, (8, 128))
    alpha = column(total, 105) / column(total, 106)
    row_low = face_of(block(-1, 0)) + jnp.where(lane == 0, column(face_of(block(-1, -1)), 16), 0.0)
    col_low = column_of(block(0, -1))[0]
    for kc in range(6):
        h = hess_ref[kc]
        h = h + jnp.where(sub == 0, jnp.broadcast_to(row_low[kc : kc + 1], (8, 128)), 0.0)
        h = h + jnp.where(lane == 0, column(col_low, kc), 0.0)
        prod_ref[kc // 2, kc % 2] = h[:, :16]
        step_ref[kc // 2, kc % 2] = (alpha * grad_ref[kc])[:, :16]


def swaps(count, first):
    pairs = [(i, i + 1) for i in range(first, count - 1, 2)]
    return pairs + [(j, i) for i, j in pairs]


def on_device(ref_image, def_image, shift_xy, shift_z, frac, connectivity):
    nx, ny = lax.axis_size("gx"), lax.axis_size("gy")
    peers = nx * ny
    sds = jax.ShapeDtypeStruct
    xa = lax.ppermute(def_image, "gx", swaps(nx, 0))
    xb = lax.ppermute(def_image, "gx", swaps(nx, 1))
    row = lax.broadcasted_iota(jnp.int32, (16, 128), 0)
    table = jnp.where(row == 10, shift_z[None], 0)
    table = table + jnp.pad(connectivity, ((0, 8), (0, 0))) + jnp.pad(shift_xy, ((8, 6), (0, 0)))
    idx, wgt, own = pl.pallas_call(
        index_kernel,
        out_shape=(sds((8, 128), jnp.int32), sds((8, 8, 128), F32), sds((8, 64, 128), BF16)),
        in_specs=[VMEM] * 3,
        out_specs=(VMEM,) * 3,
        compiler_params=PARAMS,
        cost_estimate=pl.CostEstimate(flops=300000, bytes_accessed=262144, transcendentals=0),
        name="order_elements",
    )(table, frac, def_image)
    packed = sds((4, 128, 128), BF16)
    to_b, to_a = pl.pallas_call(
        pack_first_kernel,
        out_shape=(packed, packed),
        in_specs=[VMEM] * 2,
        out_specs=(VMEM, VMEM),
        compiler_params=PARAMS,
        cost_estimate=pl.CostEstimate(flops=300000, bytes_accessed=524288, transcendentals=0),
        name="pack_first_halo",
    )(xa, own)
    yb = lax.ppermute(to_b, "gy", swaps(ny, 1))
    ya = lax.ppermute(to_a, "gy", swaps(ny, 0))
    packed = sds((4, 64, 128), BF16)
    to_d, to_c = pl.pallas_call(
        pack_second_kernel,
        out_shape=(packed, packed),
        in_specs=[VMEM, pl.BlockSpec(memory_space=pl.ANY)],
        out_specs=(VMEM, VMEM),
        compiler_params=PARAMS,
        cost_estimate=pl.CostEstimate(flops=300000, bytes_accessed=524288, transcendentals=0),
        name="pack_second_halo",
    )(xb, to_a)
    yd = lax.ppermute(to_d, "gy", swaps(ny, 1))
    yc = lax.ppermute(to_c, "gy", swaps(ny, 0))

    left, wy, expand, wyt = tables()
    arr = pl.pallas_call(
        early_kernel,
        out_shape=sds((16, 11, 8, 128), F32),
        in_specs=[SMEM] + [VMEM] * 3,
        out_specs=VMEM,
        scratch_shapes=[pltpu.VMEM((TILE_ROWS + 8, 128), F32)],
        compiler_params=PARAMS,
        cost_estimate=pl.CostEstimate(flops=4000000, bytes_accessed=2000000, transcendentals=0),
        name="sample_early",
    )(idx, xb, own, xa)
    residual, slopes, nodes, send, square = pl.pallas_call(
        lambda *refs: late_kernel(nx, ny, *refs),
        out_shape=(
            sds((8, 64, 128), BF16),
            sds((3, 8, 8, 8, 128), F32),
            sds((64, 128), F32),
            sds((peers, 1, 128), F32),
            sds((8, 128), F32),
        ),
        in_specs=[SMEM] + [VMEM] * 12,
        out_specs=(VMEM,) * 5,
        scratch_shapes=[
            pltpu.VMEM((2 * TILE_ROWS + 8, 128), F32),
            pltpu.VMEM((16, 11, 8, 128), F32),
            pltpu.VMEM((8, 8, 8, 128), F32),
            pltpu.VMEM((6, 8, 8, 128), F32),
        ],
        compiler_params=PARAMS,
        name="sample_and_gradient",
    )(idx, wgt, xb, own, xa, yb, ya, yd, yc, arr, ref_image, left, wy)
    recv = lax.all_to_all(send, ("gx", "gy"), 0, 0, tiled=True)
    grads, hess, send, residual = pl.pallas_call(
        lambda *refs: product_kernel(nx, ny, *refs),
        out_shape=(
            sds((6, 8, 128), F32),
            sds((6, 8, 128), F32),
            sds((peers, 1, 128), F32),
            sds((8, 64, 128), BF16),
        ),
        in_specs=[VMEM] * 9,
        out_specs=(VMEM,) * 3 + (pl.BlockSpec(memory_space=pl.ANY),),
        scratch_shapes=[
            pltpu.VMEM((6, 8, 8, 128), F32),
            pltpu.VMEM((6, 8, 8, 128), F32),
            pltpu.SemaphoreType.DMA,
        ],
        compiler_params=PARAMS,
        name="gauss_newton_product",
    )(recv, nodes, slopes, square, expand, wyt, left, wy, residual)
    recv = lax.all_to_all(send, ("gx", "gy"), 0, 0, tiled=True)
    voxels = 8 * 64 * 128 * peers
    step, product, misfit = pl.pallas_call(
        lambda *refs: finish_kernel(nx, ny, voxels, *refs),
        out_shape=(sds((3, 2, 8, 16), F32), sds((3, 2, 8, 16), F32), sds((1, 1), F32)),
        in_specs=[VMEM] * 3,
        out_specs=(VMEM,) * 3,
        compiler_params=PARAMS,
        name="finish",
    )(recv, grads, hess)
    return (residual, step, product, misfit[0, 0])


def solution(mesh):
    in_specs = (
        P(None, "gx", "gy"),
        P(None, "gx", "gy"),
        P(None, ("gx", "gy")),
        P(("gx", "gy")),
        P(None, ("gx", "gy")),
        P(None, ("gx", "gy")),
    )
    out_specs = (P(None, "gx", "gy"), P(None, None, "gx", "gy"), P(None, None, "gx", "gy"), P())
    return jax.shard_map(
        on_device, mesh=mesh, in_specs=in_specs, out_specs=out_specs, check_vma=False
    )
```

```python
import jax
import jax.numpy as jnp
import numpy as np
from jax import lax
from jax.experimental import pallas as pl
from jax.experimental.pallas import tpu as pltpu
from jax.sharding import PartitionSpec as P

HALO = 64
F32 = jnp.float32
BF16 = jnp.bfloat16
SPAN = 192
TILE_ROWS = 12 * SPAN
CHUNK = 16
EARLY_CHUNK = 32
VMEM = pl.BlockSpec(memory_space=pltpu.VMEM)
SMEM = pl.BlockSpec(memory_space=pltpu.SMEM)
PARAMS = pltpu.CompilerParams(vmem_limit_bytes=24 * 1024 * 1024)


def node_weights(count):
    w = np.zeros((count + 1, 8 * count), np.float32)
    for v in range(8 * count):
        s = (v % 8 + 0.5) / 8.0
        w[v // 8, v] = 1.0 - s
        w[v // 8 + 1, v] = s
    return w


def tables():
    wx = node_weights(8)
    left = np.zeros((64, 6, 64), np.float32)
    for kc in range(6):
        left[kc * 8 : kc * 8 + 8, kc] = wx[:8]
        left[48 + kc, kc] = wx[8]
        left[56 + kc, kc] = wx[0]
    left = left.reshape(64, 384)
    expand = left.T.copy()
    expand[:, 56:] = 0.0
    wy = np.zeros((128, 128), np.float32)
    wy[:, :17] = node_weights(16).T
    as_bf = lambda a: jnp.asarray(a, BF16)
    return as_bf(left / 512.0), as_bf(wy), as_bf(expand), as_bf(wy.T)


def split(x):
    hi = x.astype(BF16)
    return hi, (x - hi.astype(F32)).astype(BF16)


def dot(a, b):
    return jnp.dot(a, b, preferred_element_type=F32)


def dot_right(w, x):
    hi, lo = split(x)
    return dot(w, hi) + dot(w, lo)


def dot_left(x, w):
    hi, lo = split(x)
    return dot(hi, w) + dot(lo, w)


def pack_rows(src, dst_a, dst_b, at, even):
    left = lax.broadcasted_iota(jnp.int32, (64, 128), 1) < 64
    for p in range(4):
        a = src[p].astype(F32)
        c = src[p + 4].astype(F32)
        right = jnp.where(left, pltpu.roll(a, 64, 1), c)
        other = jnp.where(left, a, pltpu.roll(c, 64, 1))
        dst_a[p, pl.ds(at, 64)] = jnp.where(even, right, other).astype(BF16)
        dst_b[p, pl.ds(at, 64)] = jnp.where(even, other, right).astype(BF16)


def dot_rows(a, b):
    return lax.dot_general(a, b, (((1,), (1,)), ((), ())), preferred_element_type=F32)


def as_rows(rows):
    sub = lax.broadcasted_iota(jnp.int32, (8, 128), 0)
    out = jnp.zeros((8, 128), F32)
    for n, row in enumerate(rows):
        out = jnp.where(sub == n, jnp.broadcast_to(row.astype(F32), (8, 128)), out)
    return out


def index_kernel(row_ref, frac_ref, own_ref, idx_ref, wgt_ref, keep_ref):
    keep_ref[...] = own_ref[...]
    first = row_ref[0:1]
    col_x = (first * 241) >> 12
    col_y = first - 17 * col_x
    start_x = 8 * col_x + row_ref[8:9] + HALO
    start_y = 8 * col_y + row_ref[9:10] + HALO
    early = (start_y >= 64) & (start_y < 184)
    below = start_y < 64
    offset = jnp.where(early, start_y - 64, jnp.where(below, start_y, start_y - 128))
    base = (row_ref[10:11] + 2) * SPAN + start_x
    tile = jnp.where(early | below, 0, TILE_ROWS)
    shift = (8 * col_y - offset) & 127
    place = (col_y & 1) * 8 + col_x
    width = jnp.where(early, 0, 9)
    flag = early.astype(F32)
    row = lax.broadcasted_iota(jnp.int32, (128, 128), 0)
    lane = lax.broadcasted_iota(jnp.int32, (128, 128), 1)
    upto = dot(as_rows([flag]).astype(BF16), (row <= lane).astype(F32).astype(BF16))[0:1]
    count = jnp.sum(flag, axis=1, keepdims=True)
    rank = jnp.where(early, upto - 1.0, count + lane[0:1].astype(F32) - upto)
    order = (jnp.broadcast_to(rank, (128, 128)) == row.astype(F32)).astype(F32).astype(BF16)
    hi, lo = split(as_rows([base, shift, place, 8 * col_y, tile, width]))
    table = dot_rows(hi, order) + dot_rows(lo, order)
    sub = lax.broadcasted_iota(jnp.int32, (8, 128), 0)
    table = jnp.where(sub == 6, jnp.broadcast_to(count, (8, 128)), table)
    idx_ref[...] = table.astype(jnp.int32)
    value = as_rows([frac_ref[c : c + 1] for c in range(3)])
    hi, lo = split(value)
    rest = (value - hi.astype(F32) - lo.astype(F32)).astype(BF16)
    element = jnp.broadcast_to(col_x * 16 + col_y, (128, 128))
    for cx in range(8):
        spread = (element == cx * 16 + (row >> 3)).astype(F32).astype(BF16)
        wgt_ref[cx] = dot_rows(hi, spread) + dot_rows(lo, spread) + dot_rows(rest, spread)


def pack_first_kernel(xa_ref, own_ref, b_ref, a_ref):
    even = lax.axis_index("gy") % 2 == 0
    pack_rows(xa_ref, a_ref, b_ref, 0, even)
    pack_rows(own_ref, a_ref, b_ref, 64, even)


def pack_second_kernel(xb_ref, after_ref, b_ref, a_ref):
    pack_rows(xb_ref, a_ref, b_ref, 0, lax.axis_index("gy") % 2 == 0)


def over_sublanes(x):
    return jnp.sum(x, axis=0, keepdims=True)


def lanes_of(x, idx):
    return jnp.take_along_axis(x, idx & 127, axis=1, mode="promise_in_bounds")


def face_row(face):
    return over_sublanes(pltpu.roll(face, 0, 1, stride=17, stride_axis=0))


def face_of(row):
    lane = lax.broadcasted_iota(jnp.int32, (8, 128), 1)
    sub = lax.broadcasted_iota(jnp.int32, (8, 128), 0)
    back = lanes_of(jnp.broadcast_to(row, (8, 128)), lane + 17 * sub)
    return jnp.where((lane < 17) & (sub < 6), back, 0.0)


def column_row(rows, face, at):
    lane = lax.broadcasted_iota(jnp.int32, (8, 128), 1)
    block = jnp.zeros((8, 128), F32)
    for kc in range(6):
        block = jnp.where(lane == kc, jnp.broadcast_to(rows[kc][:, at : at + 1], (8, 128)), block)
    edge = jnp.where(lane == 64, jnp.broadcast_to(face[:, at : at + 1], (8, 128)), 0.0)
    block = pltpu.roll(block, 0, 1, stride=8, stride_axis=0)
    edge = pltpu.roll(edge, 0, 1, stride=1, stride_axis=0)
    return over_sublanes(block + edge)


def column_of(row):
    lane = lax.broadcasted_iota(jnp.int32, (8, 128), 1)
    sub = lax.broadcasted_iota(jnp.int32, (8, 128), 0)
    row = jnp.broadcast_to(row, (8, 128))
    return lanes_of(row, lane + 8 * sub), lanes_of(row, lane + 64 + sub)


def place_of_a():
    return pl.multiple_of(jnp.where(lax.axis_index("gx") % 2 == 1, 0, 128), 64)


def clear_outside(img, tiles):
    zero = jnp.zeros((2 * SPAN, 128), F32)
    for k in range(tiles):
        img[pl.ds(k * TILE_ROWS, 2 * SPAN)] = zero
        img[pl.ds(k * TILE_ROWS + 10 * SPAN, 2 * SPAN)] = zero


def sample_element(img, arr, base, shift, place, first, width):
    lane = lax.broadcasted_iota(jnp.int32, (8, 128), 1)
    mask = ((lane - first) & 127) < width
    starts = [pl.ds(base + z * SPAN, 8) for z in range(9)]
    starts += [pl.ds(base + 8, 8, stride=SPAN), pl.ds(base + (8 * SPAN + 8), 8)]
    for n, start in enumerate(starts):
        pltpu.store(arr.at[place, n], pltpu.roll(img[start, :], shift, 1), mask=mask)


def early_kernel(idx_ref, xb_ref, own_ref, xa_ref, arr_ref, img):
    clear_outside(img, 1)
    at_a = place_of_a()
    for z in range(8):
        for ref, row in ((xa_ref, at_a), (own_ref, 64), (xb_ref, 128 - at_a)):
            img[pl.ds(pl.multiple_of((z + 2) * SPAN + row, 8), 64)] = ref[z].astype(F32)

    def chunk(n, carry):
        for m in range(EARLY_CHUNK):
            e = n * EARLY_CHUNK + m
            sample_element(
                img, arr_ref, idx_ref[0, e], idx_ref[1, e], idx_ref[2, e], idx_ref[3, e], 9
            )
        return carry

    lax.fori_loop(0, (idx_ref[6, 0] + (EARLY_CHUNK - 1)) // EARLY_CHUNK, chunk, 0)


def late_kernel(
    nx, ny, idx_ref, wgt, xb_ref, own_ref, xa_ref, yb_ref, ya_ref, yd_ref, yc_ref, arr_ref, ref_ref,
    left_ref, wy_ref, res_ref, slope_ref, node_ref, send_ref, sq_ref, img, arr, rsc, gsc,
):
    half = lax.broadcasted_iota(jnp.int32, (64, 128), 1) < 64
    clear_outside(img, 2)
    odd_y = lax.axis_index("gy") % 2 == 1
    at_a = place_of_a()
    segments = (
        (xa_ref, ya_ref, yb_ref, 0, at_a),
        (own_ref, ya_ref, yb_ref, 64, 64),
        (xb_ref, yc_ref, yd_ref, 0, 128 - at_a),
    )
    for p in range(4):
        for ref, pair_a, pair_b, at, row in segments:
            ra = pltpu.roll(ref[p].astype(F32), 64, 1)
            rc = pltpu.roll(ref[p + 4].astype(F32), 64, 1)
            from_a = pair_a[p, pl.ds(at, 64)].astype(F32)
            from_b = pair_b[p, pl.ds(at, 64)].astype(F32)
            lo = jnp.where(odd_y, from_a, from_b)
            hi = jnp.where(odd_y, from_b, from_a)
            at_row = lambda k, q: pl.ds(pl.multiple_of(k * TILE_ROWS + (q + 2) * SPAN + row, 8), 64)
            img[at_row(0, p)] = jnp.where(half, lo, ra)
            img[at_row(1, p)] = jnp.where(half, ra, pltpu.roll(hi, 64, 1))
            img[at_row(0, p + 4)] = jnp.where(half, pltpu.roll(lo, 64, 1), rc)
            img[at_row(1, p + 4)] = jnp.where(half, rc, hi)
    for z in range(8):
        rsc[z] = ref_ref[z].astype(F32).reshape(8, 8, 128)
    arr[...] = arr_ref[...]

    def chunk(n, carry):
        for m in range(CHUNK):
            e = n * CHUNK + m
            base = idx_ref[0, e] + idx_ref[4, e]
            sample_element(
                img, arr, base, idx_ref[1, e], idx_ref[2, e], idx_ref[3, e], idx_ref[5, e]
            )
        return carry

    lax.fori_loop(idx_ref[6, 0] // CHUNK, 128 // CHUNK, chunk, 0)

    lane = lax.broadcasted_iota(jnp.int32, (8, 128), 1)
    sub = lax.broadcasted_iota(jnp.int32, (8, 128), 0)
    phase = lane & 15
    even = phase < 8
    even_next = (phase >= 1) & (phase <= 8)

    def interpolate(cx, square):
        wz, wx, wy = (jnp.broadcast_to(wgt[cx, c : c + 1], (8, 128)) for c in range(3))

        def pair(n):
            ev = arr[cx, n]
            od = arr[cx + 8, n]
            near = jnp.where(even, ev, od)
            return near, pltpu.roll(jnp.where(even_next, ev, od), 127, 1)

        edge, corner = pair(9), pair(10)

        def both_rows(z):
            here = pair(z)
            last = [corner[y][0:1] if z == 8 else edge[y][z : z + 1] for y in range(2)]
            after = [
                jnp.where(sub == 7, jnp.broadcast_to(last[y], (8, 128)), pltpu.roll(here[y], 7, 0))
                for y in range(2)
            ]
            return here, after

        total = [None] * 3
        upper = [None] * 3
        prev = both_rows(0)
        for z in range(8):
            cur = both_rows(z + 1)
            low, dzx, dx = [], [], []
            for y in range(2):
                d0 = cur[0][y] - prev[0][y]
                d1 = cur[1][y] - prev[1][y]
                l0 = prev[0][y] + wz * d0
                l1 = prev[1][y] + wz * d1
                dx.append(l1 - l0)
                low.append(l0 + wx * dx[y])
                dzx.append(d0 + wx * (d1 - d0))
            prev = cur
            slope_y = low[1] - low[0]
            value = low[0] + wy * slope_y
            slope_z = dzx[0] + wy * (dzx[1] - dzx[0])
            slope_x = dx[0] + wy * (dx[1] - dx[0])
            r = rsc[z, cx] - value
            rsc[z, cx] = r
            square = square + r * r
            for k, s in enumerate((slope_z, slope_x, slope_y)):
                slope_ref[k, z, cx] = s
                w = s * r
                u = w * ((z + 0.5) / 8.0)
                total[k] = w if z == 0 else total[k] + w
                upper[k] = u if z == 0 else upper[k] + u
        for k in range(3):
            gsc[2 * k, cx] = total[k] - upper[k]
            gsc[2 * k + 1, cx] = upper[k]
        return square

    sq_ref[...] = lax.fori_loop(0, 8, interpolate, jnp.zeros((8, 128), F32), unroll=4)
    res_ref[...] = rsc[...].reshape(8, 64, 128).astype(BF16)
    nodes = dot_left(dot_right(left_ref[...], gsc[...].reshape(384, 128)), wy_ref[...])
    node_ref[...] = nodes
    rows = [nodes[kc * 8 : kc * 8 + 8] for kc in range(6)]
    high, low = nodes[48:56], nodes[56:64]
    col_high = column_row(rows, high, 16)
    col_low = column_row(rows, high, 0)
    high, low = face_row(high), face_row(low)
    gx, gy = lax.axis_index("gx"), lax.axis_index("gy")
    send_ref[...] = jnp.zeros(send_ref.shape, F32)
    for dx in (-1, 0, 1):
        for dy in (-1, 0, 1):
            if dx == 0 and dy == 0:
                continue
            block = high if dx == 1 else low if dx == -1 else col_high if dy == 1 else col_low
            px, py = gx + dx, gy + dy

            @pl.when((px >= 0) & (px < nx) & (py >= 0) & (py < ny))
            def _():
                send_ref[px * ny + py] = block


def product_kernel(
    nx, ny, recv_ref, node_ref, slope_ref, sq_ref, expand_ref, wyt_ref, left_ref, wy_ref, res_ref,
    grad_ref, hess_ref, send_ref, out_ref, msc, gsc, sem,
):
    copy_out = pltpu.make_async_copy(res_ref, out_ref, sem)
    copy_out.start()
    gx, gy = lax.axis_index("gx"), lax.axis_index("gy")
    own = gx * ny + gy
    lane = lax.broadcasted_iota(jnp.int32, (8, 128), 1)
    sub = lax.broadcasted_iota(jnp.int32, (8, 128), 0)

    def block(dx, dy):
        px, py = gx + dx, gy + dy
        there = (px >= 0) & (px < nx) & (py >= 0) & (py < ny)
        return recv_ref[jnp.where(there, px * ny + py, own)]

    def column(x, at):
        return jnp.broadcast_to(x[:, at : at + 1], (8, 128))

    def with_corners(dx):
        mid = face_of(block(dx, 0))
        mid = mid + jnp.where(lane == 0, column(face_of(block(dx, -1)), 16), 0.0)
        return mid + jnp.where(lane == 16, column(face_of(block(dx, 1)), 0), 0.0)

    keep_x = jnp.where(gx == nx - 1, 0.0, 1.0).astype(F32)
    keep_y = jnp.where(gy == ny - 1, 0.0, 1.0).astype(F32)
    keep_lane = jnp.where(lane == 16, keep_y, 1.0)
    row_low = with_corners(-1)
    row_high = with_corners(1)
    col_low, edge_low = column_of(block(0, -1))
    col_high, edge_high = column_of(block(0, 1))
    grads = []
    square = jnp.zeros((8, 128), F32)
    for kc in range(6):
        g = node_ref[kc * 8 : kc * 8 + 8]
        g = g + jnp.where(sub == 0, jnp.broadcast_to(row_low[kc : kc + 1], (8, 128)), 0.0)
        g = g + jnp.where(lane == 0, column(col_low, kc), 0.0)
        g = g + jnp.where(lane == 16, column(col_high, kc), 0.0)
        g = g * keep_lane
        grads.append(g)
        grad_ref[kc] = g
        own_g = jnp.where(lane < 16, g, 0.0)
        square = square + own_g * own_g
    face = node_ref[48:56] + row_high
    face = face + jnp.where(lane == 0, column(edge_low, 0), 0.0)
    face = face + jnp.where(lane == 16, column(edge_high, 0), 0.0)
    face = jnp.where(sub < 6, face * keep_lane * keep_x, 0.0)
    full = jnp.concatenate(grads + [face, jnp.zeros((8, 128), F32)], axis=0)
    moved = dot_right(expand_ref[...], dot_left(full, wyt_ref[...]))
    msc[...] = moved.reshape(6, 8, 8, 128)

    def apply(cx, curve):
        m0 = [msc[2 * k, cx] for k in range(3)]
        dm = [msc[2 * k + 1, cx] - m0[k] for k in range(3)]
        total = [None] * 3
        upper = [None] * 3
        for z in range(8):
            sz = (z + 0.5) / 8.0
            s = [slope_ref[k, z, cx] for k in range(3)]
            along = s[0] * (m0[0] + sz * dm[0])
            for k in (1, 2):
                along = along + s[k] * (m0[k] + sz * dm[k])
            curve = curve + along * along
            for k in range(3):
                w = s[k] * along
                u = w * sz
                total[k] = w if z == 0 else total[k] + w
                upper[k] = u if z == 0 else upper[k] + u
        for k in range(3):
            gsc[2 * k, cx] = total[k] - upper[k]
            gsc[2 * k + 1, cx] = upper[k]
        return curve

    curve = lax.fori_loop(0, 8, apply, jnp.zeros((8, 128), F32), unroll=4)
    nodes = dot_left(dot_right(left_ref[...], gsc[...].reshape(384, 128)), wy_ref[...])
    rows = [nodes[kc * 8 : kc * 8 + 8] for kc in range(6)]
    for kc in range(6):
        hess_ref[kc] = rows[kc]
    col_high = column_row(rows, nodes[48:56], 16)
    high = face_row(nodes[48:56])
    spot = lane[:1]
    sums = jnp.where(spot == 104, jnp.sum(sq_ref[...]), 0.0)
    sums = jnp.where(spot == 105, jnp.sum(square), sums)
    sums = jnp.where(spot == 106, jnp.sum(curve) * (1.0 / 512.0), sums)
    tail = spot >= 104
    send_ref[...] = jnp.broadcast_to(sums[None], send_ref.shape)
    for dx, dy, data in ((1, 0, high), (1, 1, high), (0, 1, col_high)):
        px, py = gx + dx, gy + dy

        @pl.when((px < nx) & (py < ny))
        def _():
            send_ref[px * ny + py] = jnp.where(tail, sums, data)

    copy_out.wait()


def finish_kernel(nx, ny, voxels, recv_ref, grad_ref, hess_ref, step_ref, prod_ref, misfit_ref):
    gx, gy = lax.axis_index("gx"), lax.axis_index("gy")
    own = gx * ny + gy
    lane = lax.broadcasted_iota(jnp.int32, (8, 128), 1)
    sub = lax.broadcasted_iota(jnp.int32, (8, 128), 0)

    def block(dx, dy):
        px, py = gx + dx, gy + dy
        there = (px >= 0) & (py >= 0)
        data = recv_ref[jnp.where(there, px * ny + py, own)]
        return jnp.where(there, data, 0.0)

    def column(x, at):
        return jnp.broadcast_to(x[:, at : at + 1], (8, 128))

    total = jnp.sum(recv_ref[...], axis=0)
    misfit_ref[...] = total[:, 104:105] * (1.0 / voxels)
    total = jnp.broadcast_to(total, (8, 128))
    alpha = column(total, 105) / column(total, 106)
    row_low = face_of(block(-1, 0)) + jnp.where(lane == 0, column(face_of(block(-1, -1)), 16), 0.0)
    col_low = column_of(block(0, -1))[0]
    for kc in range(6):
        h = hess_ref[kc]
        h = h + jnp.where(sub == 0, jnp.broadcast_to(row_low[kc : kc + 1], (8, 128)), 0.0)
        h = h + jnp.where(lane == 0, column(col_low, kc), 0.0)
        prod_ref[kc // 2, kc % 2] = h[:, :16]
        step_ref[kc // 2, kc % 2] = (alpha * grad_ref[kc])[:, :16]


def swaps(count, first):
    pairs = [(i, i + 1) for i in range(first, count - 1, 2)]
    return pairs + [(j, i) for i, j in pairs]


def on_device(ref_image, def_image, shift_xy, shift_z, frac, connectivity):
    nx, ny = lax.axis_size("gx"), lax.axis_size("gy")
    peers = nx * ny
    sds = jax.ShapeDtypeStruct
    xa = lax.ppermute(def_image, "gx", swaps(nx, 0))
    xb = lax.ppermute(def_image, "gx", swaps(nx, 1))
    row = lax.broadcasted_iota(jnp.int32, (16, 128), 0)
    table = jnp.where(row == 10, shift_z[None], 0)
    table = table + jnp.pad(connectivity, ((0, 8), (0, 0))) + jnp.pad(shift_xy, ((8, 6), (0, 0)))
    idx, wgt, own = pl.pallas_call(
        index_kernel,
        out_shape=(sds((8, 128), jnp.int32), sds((8, 8, 128), F32), sds((8, 64, 128), BF16)),
        in_specs=[VMEM] * 3,
        out_specs=(VMEM,) * 3,
        compiler_params=PARAMS,
        cost_estimate=pl.CostEstimate(flops=300000, bytes_accessed=262144, transcendentals=0),
        name="order_elements",
    )(table, frac, def_image)
    packed = sds((4, 128, 128), BF16)
    to_b, to_a = pl.pallas_call(
        pack_first_kernel,
        out_shape=(packed, packed),
        in_specs=[VMEM] * 2,
        out_specs=(VMEM, VMEM),
        compiler_params=PARAMS,
        cost_estimate=pl.CostEstimate(flops=300000, bytes_accessed=524288, transcendentals=0),
        name="pack_first_halo",
    )(xa, own)
    yb = lax.ppermute(to_b, "gy", swaps(ny, 1))
    ya = lax.ppermute(to_a, "gy", swaps(ny, 0))
    packed = sds((4, 64, 128), BF16)
    to_d, to_c = pl.pallas_call(
        pack_second_kernel,
        out_shape=(packed, packed),
        in_specs=[VMEM, pl.BlockSpec(memory_space=pl.ANY)],
        out_specs=(VMEM, VMEM),
        compiler_params=PARAMS,
        cost_estimate=pl.CostEstimate(flops=300000, bytes_accessed=524288, transcendentals=0),
        name="pack_second_halo",
    )(xb, to_a)
    yd = lax.ppermute(to_d, "gy", swaps(ny, 1))
    yc = lax.ppermute(to_c, "gy", swaps(ny, 0))

    left, wy, expand, wyt = tables()
    arr = pl.pallas_call(
        early_kernel,
        out_shape=sds((16, 11, 8, 128), F32),
        in_specs=[SMEM] + [VMEM] * 3,
        out_specs=VMEM,
        scratch_shapes=[pltpu.VMEM((TILE_ROWS + 8, 128), F32)],
        compiler_params=PARAMS,
        cost_estimate=pl.CostEstimate(flops=4000000, bytes_accessed=2000000, transcendentals=0),
        name="sample_early",
    )(idx, xb, own, xa)
    residual, slopes, nodes, send, square = pl.pallas_call(
        lambda *refs: late_kernel(nx, ny, *refs),
        out_shape=(
            sds((8, 64, 128), BF16),
            sds((3, 8, 8, 8, 128), F32),
            sds((64, 128), F32),
            sds((peers, 1, 128), F32),
            sds((8, 128), F32),
        ),
        in_specs=[SMEM] + [VMEM] * 12,
        out_specs=(VMEM,) * 5,
        scratch_shapes=[
            pltpu.VMEM((2 * TILE_ROWS + 8, 128), F32),
            pltpu.VMEM((16, 11, 8, 128), F32),
            pltpu.VMEM((8, 8, 8, 128), F32),
            pltpu.VMEM((6, 8, 8, 128), F32),
        ],
        compiler_params=PARAMS,
        name="sample_and_gradient",
    )(idx, wgt, xb, own, xa, yb, ya, yd, yc, arr, ref_image, left, wy)
    recv = lax.all_to_all(send, ("gx", "gy"), 0, 0, tiled=True)
    grads, hess, send, residual = pl.pallas_call(
        lambda *refs: product_kernel(nx, ny, *refs),
        out_shape=(
            sds((6, 8, 128), F32),
            sds((6, 8, 128), F32),
            sds((peers, 1, 128), F32),
            sds((8, 64, 128), BF16),
        ),
        in_specs=[VMEM] * 9,
        out_specs=(VMEM,) * 3 + (pl.BlockSpec(memory_space=pl.ANY),),
        scratch_shapes=[
            pltpu.VMEM((6, 8, 8, 128), F32),
            pltpu.VMEM((6, 8, 8, 128), F32),
            pltpu.SemaphoreType.DMA,
        ],
        compiler_params=PARAMS,
        name="gauss_newton_product",
    )(recv, nodes, slopes, square, expand, wyt, left, wy, residual)
    recv = lax.all_to_all(send, ("gx", "gy"), 0, 0, tiled=True)
    voxels = 8 * 64 * 128 * peers
    step, product, misfit = pl.pallas_call(
        lambda *refs: finish_kernel(nx, ny, voxels, *refs),
        out_shape=(sds((3, 2, 8, 16), F32), sds((3, 2, 8, 16), F32), sds((1, 1), F32)),
        in_specs=[VMEM] * 3,
        out_specs=(VMEM,) * 3,
        compiler_params=PARAMS,
        name="finish",
    )(recv, grads, hess)
    return (residual, step, product, misfit[0, 0])


def solution(mesh):
    in_specs = (
        P(None, "gx", "gy"),
        P(None, "gx", "gy"),
        P(None, ("gx", "gy")),
        P(("gx", "gy")),
        P(None, ("gx", "gy")),
        P(None, ("gx", "gy")),
    )
    out_specs = (P(None, "gx", "gy"), P(None, None, "gx", "gy"), P(None, None, "gx", "gy"), P())
    return jax.shard_map(
        on_device, mesh=mesh, in_specs=in_specs, out_specs=out_specs, check_vma=False
    )
```
